32 devices in a mesh: dp: 4 (over y, x), seq: 8 (over z, core).
Axes of the slice: x: 2, y: 2, z: 4, core: 2. Of those that a mesh axis runs over, the one named last changes fastest.
Arguments:
- inputs: bfloat16 [32, 256, 768], P(('dp', 'seq')), may hold values from -6 to 6
- time_table: bfloat16 [1000, 768], replicated, may hold values from -6 to 6
- time_index: int32 [32], P(('dp', 'seq')), may hold values from 0 to 999
- token_keep: int32 [32, 256], P(('dp', 'seq')), may hold values from 0 to 1, as said below
- head_keep: int32 [32, 12], P(('dp', 'seq')), may hold values 0 or 1
- cotangent: bfloat16 [32, 256, 768], P(('dp', 'seq')), may hold values from -6 to 6
- w_ada: bfloat16 [768, 4608], P('dp'), may hold values from -0.21875 to 0.21875
- w_qkv: bfloat16 [768, 2304], P('dp'), may hold values from -0.21875 to 0.21875
- w_out: bfloat16 [768, 768], P('dp'), may hold values from -3.5 to 3.5
- w_up: bfloat16 [768, 3072], P('dp'), may hold values from -0.21875 to 0.21875
- w_down: bfloat16 [3072, 768], P('dp'), may hold values from -0.109375 to 0.109375
- w_head: bfloat16 [768, 12], P('dp'), may hold values from -0.21875 to 0.21875
- w_token: bfloat16 [768], P('dp'), may hold values from -0.21875 to 0.21875
Outputs:
- output: bfloat16 [32, 256, 768], P(('dp', 'seq'))
- grad_input: float32 [32, 256, 768], P(('dp', 'seq'))
- grad_w_ada: float32 [768, 4608], P(('dp', 'seq'))
- grad_w_qkv: float32 [768, 2304], P(('dp', 'seq'))
- grad_w_out: float32 [768, 768], P(('dp', 'seq'))
- grad_w_up: float32 [768, 3072], P(('dp', 'seq'))
- grad_w_down: float32 [3072, 768], P(('dp', 'seq'))
- grad_w_head: float32 [768, 12], P(('dp', 'seq'))
- grad_w_token: float32 [768], P(('dp', 'seq'))
The draws below stay inside these ranges and needn't reach their ends.
Inputs may be any that keep to these rules, and one draw needn't show every extreme that they name: `token_keep`: the 1 images of one device (consecutive images) keep anywhere from none to all of their tokens; in every group of 8 consecutive devices one device keeps all, and the group keeps exactly 1024 tokens together.
All inputs are finite; a program needn't handle non-finite values. No bound on the sum of `head_keep` on one device may be relied on, other than what follows from the above.
Results may differ from the reference program's by a relative error of at most 0.012.
Values may be sent and summed in bfloat16 or wider, within the bound.
A program may use at most 128 MiB of HBM per device.

```python
import math
import jax
import jax.numpy as jnp
from jax import lax

D = 768
HEADS = 12
FF = 3072
PATCHES = 256
NT = 1000
IMG_DEV = 1
IMAGES = 32
N_DP = 4
N_SEQ = 8


def shuffled(key, length, copies):

    def one_order(subkey):
        return jax.random.permutation(subkey, length)
    return jax.vmap(one_order)(jax.random.split(key, copies))


def draw_token_keep(key, part):
    key = jax.random.fold_in(key, 7)
    device_rows = IMG_DEV * PATCHES
    half_rows = device_rows // 2
    key_pairs, key_shift, key_rank = jax.random.split(key, 3)
    placing = shuffled(key_pairs, N_SEQ, N_DP)
    shifts = jax.random.randint(key_shift, (N_DP, N_SEQ // 2), 0, half_rows + 1)
    shifts = shifts.at[:, 0].set(half_rows)
    paired = jnp.stack([half_rows + shifts, half_rows - shifts], axis=2).reshape(N_DP, N_SEQ)
    group_index = jnp.arange(N_DP)[:, None]
    counts = jnp.zeros((N_DP, N_SEQ), jnp.int32).at[group_index, placing].set(paired.astype(jnp.int32))
    ranks = shuffled(key_rank, device_rows, N_DP * N_SEQ)
    keep = (ranks < counts.reshape(N_DP * N_SEQ, 1)).astype(jnp.int32)
    return keep.reshape(IMG_DEV * N_DP * N_SEQ, PATCHES)


def draw_cotangent(key, part):
    key = jax.random.fold_in(key, 11)
    key_common, key_noise = jax.random.split(key, 2)
    common = jax.random.normal(key_common, (IMAGES, 1, D), jnp.float32)
    noise = jax.random.normal(key_noise, (IMAGES, PATCHES, D), jnp.float32)
    values = 0.7 * common + 0.7 * noise
    return jnp.clip(values, -6.0, 6.0).astype(jnp.bfloat16)


def set_ends(values, own_key, smallest, high):
    longest = values.shape.index(max(values.shape))
    spots = []
    for shift in (0, 1):
        where = [jax.random.randint(jax.random.fold_in(own_key, axis), (), 0, length) for axis, length in enumerate(values.shape)]
        where[longest] = (where[longest] + shift) % values.shape[longest]
        spots.append(tuple(where))
    return values.at[spots[0]].set(smallest).at[spots[1]].set(high)


def shard_levels(key, dims, cuts, smallest, largest):
    factor_of = 1.0
    for dim, blocks in cuts:
        heights = jax.random.uniform(jax.random.fold_in(jax.random.fold_in(key, 6), dim), (blocks,), jnp.float32, smallest / len(cuts), largest / len(cuts))
        factor_of = factor_of * jnp.repeat(jnp.exp(heights), dims[dim] // blocks).reshape((-1,) + (1,) * (len(dims) - 1 - dim))
    return factor_of


def centred(stream_key, dims, width, limit, cuts=(), kind=jnp.bfloat16):
    entries = jax.random.normal(stream_key, dims, jnp.float32) * width
    if len(cuts) > 0:
        entries = shard_levels(stream_key, dims, cuts, -0.22, 0.18) * entries
    return jnp.clip(entries, min=-limit, max=limit).astype(kind)


def setup_inputs(seed: int = 0) -> dict:
    keys = jax.random.split(jax.random.key(seed), 14)
    inputs = centred(keys[0], (IMAGES, PATCHES, D), 1.0, 6.0, ((0, 32),))
    time_table = centred(keys[1], (NT, D), 1.0, 6.0)
    time_index = set_ends(jax.random.randint(keys[2], (IMAGES,), 0, NT), jax.random.fold_in(keys[2], 1), 0, NT - 1).astype(jnp.int32)
    token_keep = draw_token_keep(jax.random.fold_in(keys[13], 71), 0)
    head_keep = set_ends((jax.random.randint(keys[4], (IMAGES, HEADS), 0, 4) < 3).astype(jnp.int32), jax.random.fold_in(keys[4], 1), 0, 1)
    cotangent = draw_cotangent(jax.random.fold_in(keys[13], 71), 0)
    w_ada = centred(keys[6], (D, 6 * D), D ** -0.5, 0.21875, ((0, 4),))
    w_qkv = centred(keys[7], (D, 3 * D), D ** -0.5, 0.21875, ((0, 4),))
    w_out = centred(keys[8], (D, D), (max(1, D // PATCHES)) ** -0.5, 3.5, ((0, 4),))
    w_up = centred(keys[9], (D, FF), D ** -0.5, 0.21875, ((0, 4),))
    w_down = centred(keys[10], (FF, D), FF ** -0.5, 0.109375, ((0, 4),))
    w_head = centred(keys[11], (D, HEADS), D ** -0.5, 0.21875, ((0, 4),))
    w_token = centred(keys[12], (D,), D ** -0.5, 0.21875, ((0, 4),))
    return dict(inputs=inputs, time_table=time_table, time_index=time_index, token_keep=token_keep, head_keep=head_keep, cotangent=cotangent, w_ada=w_ada, w_qkv=w_qkv, w_out=w_out, w_up=w_up, w_down=w_down, w_head=w_head, w_token=w_token)


@jax.custom_vjp
def low(v):
    return lax.optimization_barrier(v.astype(jnp.bfloat16)).astype(jnp.float32)

@jax.custom_vjp
def low_back(v):
    return v

def low_keep(v):
    return (low(v), None)

def low_pass(kept, grad):
    return (grad,)

def back_keep(v):
    return (v, None)

def back_low(kept, grad):
    return (low(grad),)
low.defvjp(low_keep, low_pass)
low_back.defvjp(back_keep, back_low)
epsilon = 1e-06

def product(left, right):
    return jnp.matmul(left, right, precision=lax.Precision.HIGHEST)

def normalize(values):
    centre = values - lax.optimization_barrier(jnp.mean(values, axis=-1, keepdims=True))
    spread = lax.optimization_barrier(jnp.mean(centre * centre, axis=-1, keepdims=True))
    return centre * lax.rsqrt(spread + epsilon)

def block_forward(params, signal, cond_raw, head_mask, token_mask):
    w_ada, w_qkv, w_out, w_up, w_down, w_head, w_token = params
    images, patches, model_width = signal.shape
    head_count = head_mask.shape[1]
    head_size = model_width // head_count
    condition = low(jax.nn.silu(cond_raw))
    modulation = product(condition, w_ada).reshape(images, 6, model_width)
    shift_one = modulation[:, 0:1]
    scale_one = modulation[:, 1:2]
    gate_one = modulation[:, 2:3]
    shift_two = modulation[:, 3:4]
    scale_two = modulation[:, 4:5]
    gate_two = modulation[:, 5:6]
    head_gate = head_mask * jax.nn.sigmoid(product(condition, w_head))
    normed = low(normalize(signal) * (1.0 + scale_one) + shift_one)
    packed = low_back(low(product(normed, w_qkv))).reshape(images, patches, 3, head_count, head_size)
    queries = packed[:, :, 0]
    key_rows = packed[:, :, 1]
    value_rows = packed[:, :, 2]
    scores = low_back(jnp.einsum('bqhd,bkhd->bhqk', queries, key_rows, precision=lax.Precision.HIGHEST) * head_size ** (-0.5))
    probs_low = low(jax.nn.softmax(scores, axis=-1))
    attended = low_back(jnp.einsum('bhqk,bkhd->bqhd', probs_low, value_rows, precision=lax.Precision.HIGHEST))
    gated_heads = low((attended * head_gate[:, None, :, None]).reshape(images, patches, model_width))
    branch = low_back(product(gated_heads, w_out))
    middle = signal + gate_one * branch
    second = low(normalize(middle) * (1.0 + scale_two) + shift_two)
    router = jax.nn.sigmoid(product(second, w_token))
    up_proj = low_back(product(low_back(second), w_up))
    hidden = low(jax.nn.gelu(up_proj, approximate=True))
    produced = low_back(low(product(hidden, w_down)))
    return middle + gate_two * (token_mask * router)[:, :, None] * produced

def reference(inputs, time_table, time_index, token_keep, head_keep, cotangent, w_ada, w_qkv, w_out, w_up, w_down, w_head, w_token):
    params = tuple((weight.astype(jnp.float32) for weight in (w_ada, w_qkv, w_out, w_up, w_down, w_head, w_token)))
    image_count = inputs.shape[0]
    group_size = math.gcd(image_count, 16)
    blocks = image_count // group_size
    cond_raw = time_table.astype(jnp.float32)[time_index]
    head_mask = head_keep.astype(jnp.float32)
    token_mask = token_keep.astype(jnp.float32)
    stepper = jax.checkpoint(block_forward)

    def forward(signal, weights):

        def advance(state_carry, pieces):
            return (state_carry, stepper(weights, pieces[0], pieces[1], pieces[2], pieces[3]))
        stacked = (signal.reshape((blocks, group_size) + signal.shape[1:]), cond_raw.reshape(blocks, group_size, -1), head_mask.reshape(blocks, group_size, -1), token_mask.reshape(blocks, group_size, -1))
        _, outputs = lax.scan(advance, jnp.zeros((), jnp.float32), stacked)
        return outputs.reshape(signal.shape)
    result, pullback = jax.vjp(forward, inputs.astype(jnp.float32), params)
    grad_signal, grad_params = pullback(cotangent.astype(jnp.float32))
    return (result.astype(jnp.bfloat16), grad_signal, grad_params[0], grad_params[1], grad_params[2], grad_params[3], grad_params[4], grad_params[5], grad_params[6])
```

```python
import functools

import jax
import jax.numpy as jnp
from jax import lax
from jax.experimental import pallas as pl
from jax.experimental.pallas import tpu as pltpu
from jax.sharding import PartitionSpec as P

epsilon = 1e-06
MESH = pl.DeviceIdType.MESH
ANY = pl.BlockSpec(memory_space=pl.ANY)
VMEM = pl.BlockSpec(memory_space=pltpu.VMEM)
Z_CHIPS = 4
BLOCK = 2 * Z_CHIPS


def normalize(values):
    centre = values - jnp.mean(values, axis=-1, keepdims=True)
    spread = jnp.mean(centre * centre, axis=-1, keepdims=True)
    return centre * lax.rsqrt(spread + epsilon)


def modulate(values, scale_part, shift_part):
    return normalize(values) * (1.0 + scale_part) + shift_part


def gelu_tanh(values):
    return jax.nn.gelu(values, approximate=True)


class Place:
    def __init__(self):
        self.dp = lax.axis_index("dp")
        self.seq = lax.axis_index("seq")
        self.x = self.dp % 2
        self.y = self.dp // 2
        self.core = self.seq % 2
        self.z = (self.seq // 2) % Z_CHIPS
        self.outer = self.seq // BLOCK

    def z_of(self, step):
        return (self.z + step) % Z_CHIPS

    def peer_x(self):
        return (self.y * 2 + 1 - self.x, self.seq)

    def peer_y(self):
        return ((1 - self.y) * 2 + self.x, self.seq)

    def peer_d(self):
        return ((1 - self.y) * 2 + 1 - self.x, self.seq)

    def peer_core(self):
        return (self.dp, self.seq + 1 - 2 * self.core)

    def peer_z(self, step):
        return (self.dp, self.outer * BLOCK + self.z_of(step) * 2 + self.core)

    def all_peers(self):
        return [self.peer_x(), self.peer_y(), self.peer_d(), self.peer_core()] + [
            self.peer_z(k) for k in range(1, Z_CHIPS)
        ]

    def greet(self):
        barrier = pltpu.get_barrier_semaphore()
        peers = self.all_peers()
        for peer in peers:
            pl.semaphore_signal(barrier, inc=1, device_id=peer, device_id_type=MESH)
        pl.semaphore_wait(barrier, len(peers))


class Net:
    def __init__(self, send_sems, recv_sems):
        self.send_sems = send_sems
        self.recv_sems = recv_sems
        self.used = 0
        self.sent = []

    def send(self, src, dst, peer, landing=None):
        slot = self.used
        self.used += 1
        copy = pltpu.make_async_remote_copy(
            src_ref=src,
            dst_ref=dst,
            send_sem=self.send_sems.at[slot],
            recv_sem=self.recv_sems.at[slot],
            device_id=peer,
            device_id_type=MESH,
        )
        copy.start()
        self.sent.append(copy)
        arrival = copy
        if landing is not None:
            arrival = pltpu.make_async_remote_copy(
                src_ref=src,
                dst_ref=landing,
                send_sem=self.send_sems.at[slot],
                recv_sem=self.recv_sems.at[slot],
                device_id=peer,
                device_id_type=MESH,
            )
        return arrival.wait_recv

    def finish(self):
        for copy in self.sent:
            copy.wait_send()


def half(ref, core, *lead):
    width = ref.shape[-1] // 2
    columns = pl.ds(pl.multiple_of(core * width, 128), width)
    return ref.at[lead + (columns,)]


def gather_kernel(
    cond_ref, ada_ref, head_ref, wq, wo, wu, wd,
    mod_ref, fq, fo, fu, fd,
    cond_buf, part, part_buf, send_sems, recv_sems, local_sems,
):
    here = Place()
    here.greet()
    net = Net(send_sems, recv_sems)
    dp, core = here.dp, here.core
    every = slice(None)

    cond_waits = []
    for peer in (here.peer_x(), here.peer_y(), here.peer_d()):
        cond_waits.append(
            net.send(cond_ref.at[peer[0]], cond_buf.at[dp], peer, cond_buf.at[peer[0]])
        )
    pairs = ((wq, fq), (wo, fo), (wu, fu), (wd, fd))
    locals_ = []
    waits = []

    def start(index):
        own, full = pairs[index]
        depth = own.shape[0] // Z_CHIPS
        keep = pltpu.make_async_copy(own, full.at[dp], local_sems.at[index])
        keep.start()
        locals_.append(keep)
        found = {}
        for name, peer in (("x", here.peer_x()), ("y", here.peer_y())):
            found[name] = net.send(
                half(own, core, every),
                half(full, core, dp, every),
                peer,
                half(full, core, peer[0], every),
            )
        rows = pl.ds(pl.multiple_of(here.z * depth, 16), depth)
        peer = here.peer_d()
        found["d"] = net.send(
            half(own, core, rows),
            half(full, core, dp, rows),
            peer,
            half(full, core, peer[0], rows),
        )
        waits.append(found)

    start(0)
    own_cond = cond_ref[pl.ds(dp, 1)]
    cond_buf[pl.ds(dp, 1)] = own_cond
    for wait in cond_waits:
        wait()
    left = cond_buf[...].astype(jnp.bfloat16).reshape(32, cond_buf.shape[-1])
    width = part.shape[-1]
    for piece in range(6):
        product = jnp.dot(
            left, ada_ref[:, piece * width : (piece + 1) * width], preferred_element_type=jnp.float32
        )
        for image in range(4):
            part[image, piece : piece + 1, :] = product[image * 8 : image * 8 + 1]
    product = jnp.dot(left, head_ref[...], preferred_element_type=jnp.float32)
    part[:, 6:8, :] = jnp.zeros((4, 2, width), jnp.float32)
    for image in range(4):
        part[image, 6:7, 0:128] = product[image * 8 : image * 8 + 1]
    part_waits = []
    for index, peer in enumerate((here.peer_x(), here.peer_y(), here.peer_d())):
        part_waits.append(net.send(part.at[peer[0]], part_buf.at[index], peer))
    for index in range(1, len(pairs)):
        start(index)
    for wait in part_waits:
        wait()
    own_part = part[pl.ds(dp, 1)]
    mod_ref[...] = own_part[0] + part_buf[0] + part_buf[1] + part_buf[2]

    last = []
    for (own, full), found in zip(pairs, waits):
        depth = own.shape[0] // Z_CHIPS
        px, py, pd = here.peer_x(), here.peer_y(), here.peer_d()
        found["d"]()
        rows = pl.ds(pl.multiple_of(here.z * depth, 16), depth)
        found["z"] = []
        for step in range(1, Z_CHIPS):
            other = pl.ds(pl.multiple_of(here.z_of(Z_CHIPS - step) * depth, 16), depth)
            found["z"].append(
                net.send(
                    half(full, core, pd[0], rows),
                    half(full, core, pd[0], rows),
                    here.peer_z(step),
                    half(full, core, pd[0], other),
                )
            )
        for name, peer in (("x", px), ("y", py)):
            found[name]()
            last.append(
                net.send(
                    half(full, core, peer[0], every),
                    half(full, core, peer[0], every),
                    here.peer_core(),
                    half(full, 1 - core, peer[0], every),
                )
            )
    for (own, full), found in zip(pairs, waits):
        pd = here.peer_d()
        for wait in found["z"]:
            wait()
        last.append(
            net.send(
                half(full, core, pd[0], every),
                half(full, core, pd[0], every),
                here.peer_core(),
                half(full, 1 - core, pd[0], every),
            )
        )
    for wait in last:
        wait()
    for copy in locals_:
        copy.wait()
    net.finish()


def gather_weights(cond_rows, w_ada, w_head, wq, wo, wu, wd):
    width = cond_rows.shape[-1] * cond_rows.shape[0]
    copies = 3 + 3 + 4 * 9
    return pl.pallas_call(
        gather_kernel,
        out_shape=[jax.ShapeDtypeStruct((8, width), jnp.float32)]
        + [jax.ShapeDtypeStruct((4,) + w.shape, w.dtype) for w in (wq, wo, wu, wd)],
        in_specs=[VMEM] * 3 + [ANY] * 4,
        out_specs=[VMEM] + [ANY] * 4,
        scratch_shapes=[
            pltpu.VMEM(cond_rows.shape, jnp.float32),
            pltpu.VMEM((4, 8, width), jnp.float32),
            pltpu.VMEM((3, 8, width), jnp.float32),
            pltpu.SemaphoreType.DMA((copies,)),
            pltpu.SemaphoreType.DMA((copies,)),
            pltpu.SemaphoreType.DMA((4,)),
        ],
        compiler_params=pltpu.CompilerParams(
            collective_id=0, has_side_effects=True, vmem_limit_bytes=48 * 2**20
        ),
    )(cond_rows, w_ada, w_head, wq, wo, wu, wd)


def add_rows(total, extra):
    rows = total.shape[1]
    for lead in range(total.shape[0]):

        @pl.loop(0, rows // 16)
        def _(step):
            here = pl.ds(pl.multiple_of(step * 16, 16), 16)
            summed = total[lead, here, :].astype(jnp.float32) + extra[lead, here, :].astype(jnp.float32)
            total[lead, here, :] = summed.astype(total.dtype)


class Chunk:
    def __init__(self, net, here, grad, out, bufs, column, width):
        self.net, self.here, self.grad, self.out = net, here, grad, out
        self.column, self.width = column, width
        self.total, self.r0, self.r1a, self.r1b, self.r2a, self.r2b, self.r3, self.f32 = bufs

    def columns(self, core):
        start = core * (self.grad.shape[-1] // 2) + self.column
        return pl.ds(pl.multiple_of(start, 128), self.width)

    def begin(self, sem):
        here = self.here
        self.keep = pltpu.make_async_copy(
            self.grad.at[:, :, :, :, self.columns(here.core)], self.total, sem
        )
        self.keep.start()
        self.wait = self.net.send(
            self.grad.at[:, :, :, :, self.columns(1 - here.core)], self.r0, here.peer_core()
        )

    def pair(self):
        self.keep.wait()
        self.wait()
        rows = self.total.shape[3]

        @pl.loop(0, 16)
        def _(lead):
            for step in range(rows // 16):
                at = (lead // 8, (lead // 4) % 2, lead % 4, slice(step * 16, step * 16 + 16))
                summed = self.total[at].astype(jnp.float32) + self.r0[at].astype(jnp.float32)
                self.total[at] = summed.astype(jnp.bfloat16)

    def first(self):
        here, total = self.here, self.total
        self.wait_a = self.net.send(total.at[:, 1 - here.x, 0:2], self.r1a, here.peer_x())
        self.wait_b = self.net.send(total.at[1 - here.y, :, 2:4], self.r1b, here.peer_y())

    def second(self):
        here, total = self.here, self.total
        self.wait_a()
        add_rows(total.at[1 - here.y, here.x, 0:2], self.r1a.at[1 - here.y])
        next_a = self.net.send(total.at[1 - here.y, here.x, 0:2], self.r2a, here.peer_y())
        self.wait_b()
        add_rows(total.at[here.y, 1 - here.x, 2:4], self.r1b.at[1 - here.x])
        next_b = self.net.send(total.at[here.y, 1 - here.x, 2:4], self.r2b, here.peer_x())
        add_rows(total.at[here.y, here.x, 0:2], self.r1a.at[here.y])
        add_rows(total.at[here.y, here.x, 2:4], self.r1b.at[here.x])
        self.wait_a, self.wait_b = next_a, next_b

    def third(self):
        here, total = self.here, self.total
        self.wait_a()
        add_rows(total.at[here.y, here.x, 0:2], self.r2a)
        self.wait_b()
        add_rows(total.at[here.y, here.x, 2:4], self.r2b)
        self.waits = [
            self.net.send(total.at[here.y, here.x, here.z_of(k)], self.r3.at[k - 1], here.peer_z(k))
            for k in range(1, Z_CHIPS)
        ]

    def fourth(self):
        here, total = self.here, self.total
        for wait in self.waits:
            wait()
        rows = total.shape[3]

        @pl.loop(0, rows // 16)
        def _(step):
            at = pl.ds(pl.multiple_of(step * 16, 16), 16)
            summed = total[here.y, here.x, here.z, at, :].astype(jnp.float32)
            for k in range(Z_CHIPS - 1):
                summed += self.r3[k, at, :].astype(jnp.float32)
            self.f32[at, :] = summed

        part = rows // 2
        give = pl.ds(pl.multiple_of((1 - here.core) * part, 8), part)
        keep = pl.ds(pl.multiple_of(here.core * part, 8), part)
        self.wait = self.net.send(
            self.f32.at[give],
            self.out.at[:, self.columns(here.core)],
            here.peer_core(),
            self.out.at[:, self.columns(1 - here.core)],
        )
        self.out[:, self.columns(here.core)] = self.f32[keep, :]

    def end(self):
        self.wait()


def chunk_list(shapes):
    chunks = []
    for index in (3, 2, 1, 0):
        width = shapes[index][-1] // 2
        step = width if width % 256 else width // 2
        if width == 1152:
            step = 384
        if index == 1 or index == 3:
            step = width
        for column in range(0, width, step):
            chunks.append((index, column, step))
    return chunks


def scatter_kernel(chunks, vec_ref, g0, g1, g2, g3, vec_out, o0, o1, o2, o3, *scratch):
    send_sems, recv_sems, local_sems = scratch[:3]
    scratch = scratch[3:]
    here = Place()
    here.greet()
    net = Net(send_sems, recv_sems)
    grads, outs = (g0, g1, g2, g3), (o0, o1, o2, o3)
    pieces = []
    for number, (index, column, width) in enumerate(chunks):
        bufs = scratch[number * 8 : number * 8 + 8]
        pieces.append(Chunk(net, here, grads[index], outs[index], bufs, column, width))
    dp, z, core = here.dp, here.z, here.core
    vec_out[pl.ds(core, 1), pl.ds(z, 1), pl.ds(dp, 1)] = vec_ref[...][None, None, None]
    waits = []
    for peer in (here.peer_x(), here.peer_y(), here.peer_d()):
        waits.append(
            net.send(vec_ref, vec_out.at[core, z, dp], peer, vec_out.at[core, z, peer[0]])
        )
    for number, piece in enumerate(pieces):
        piece.begin(local_sems.at[number])
    for wait in waits:
        wait()
    waits = []
    for step in range(1, Z_CHIPS):
        waits.append(
            net.send(
                vec_out.at[core, z],
                vec_out.at[core, z],
                here.peer_z(step),
                vec_out.at[core, here.z_of(Z_CHIPS - step)],
            )
        )
    for piece in pieces:
        piece.pair()
        piece.first()
    for wait in waits:
        wait()
    wait = net.send(vec_out.at[core], vec_out.at[core], here.peer_core(), vec_out.at[1 - core])
    count = len(pieces)
    for step in range(count + 3):
        if step < count:
            pieces[step].second()
        if 0 <= step - 1 < count:
            pieces[step - 1].third()
        if 0 <= step - 2 < count:
            pieces[step - 2].fourth()
        if 0 <= step - 3 < count:
            pieces[step - 3].end()
    wait()
    net.finish()


def scatter_grads(vector, grads):
    split = [g.reshape(2, 2, Z_CHIPS, g.shape[0] // 16, g.shape[1]) for g in grads]
    chunks = chunk_list([g.shape for g in split])
    scratch = []
    copies = 3 + 3 + 1
    for index, _, width in chunks:
        rows = split[index].shape[3]
        scratch += [
            pltpu.VMEM((2, 2, Z_CHIPS, rows, width), jnp.bfloat16),
            pltpu.VMEM((2, 2, Z_CHIPS, rows, width), jnp.bfloat16),
            pltpu.VMEM((2, 2, rows, width), jnp.bfloat16),
            pltpu.VMEM((2, 2, rows, width), jnp.bfloat16),
            pltpu.VMEM((2, rows, width), jnp.bfloat16),
            pltpu.VMEM((2, rows, width), jnp.bfloat16),
            pltpu.VMEM((Z_CHIPS - 1, rows, width), jnp.bfloat16),
            pltpu.VMEM((rows, width), jnp.float32),
        ]
        copies += 1 + 2 + 2 + 3 + 1
    return pl.pallas_call(
        functools.partial(scatter_kernel, chunks),
        out_shape=[jax.ShapeDtypeStruct((2, Z_CHIPS, 4) + vector.shape, jnp.float32)]
        + [jax.ShapeDtypeStruct((g.shape[0] // 32, g.shape[1]), jnp.float32) for g in grads],
        in_specs=[VMEM] + [ANY] * 4,
        out_specs=[VMEM] * 5,
        scratch_shapes=[
            pltpu.SemaphoreType.DMA((copies,)),
            pltpu.SemaphoreType.DMA((copies,)),
            pltpu.SemaphoreType.DMA((len(chunks),)),
        ]
        + scratch,
        compiler_params=pltpu.CompilerParams(
            collective_id=1, has_side_effects=True, vmem_limit_bytes=56 * 2**20
        ),
    )(vector, *split)


def across_blocks(part, seq_size):
    blocks = seq_size // BLOCK
    if blocks == 1:
        return part
    groups = [[b * BLOCK + j for b in range(blocks)] for j in range(BLOCK)]
    mine = lax.psum_scatter(
        part, "seq", scatter_dimension=0, axis_index_groups=groups, tiled=True
    )
    moves = [(b * BLOCK + j, j * blocks + b) for b in range(blocks) for j in range(BLOCK)]
    return lax.ppermute(mine, "seq", moves)


def per_device(
    seq_size, inputs, time_table, time_index, token_keep, head_keep, cotangent,
    w_ada, w_qkv, w_out, w_up, w_down, w_head, w_token,
):
    images, patches, model_width = inputs.shape
    head_count = head_keep.shape[1]
    head_size = model_width // head_count
    factor = head_size ** (-0.5)
    quarter = model_width // 4
    condition = jax.nn.silu(time_table[time_index].astype(jnp.float32)).astype(jnp.bfloat16)
    cond_rows = jnp.broadcast_to(
        condition.astype(jnp.float32).reshape(4, 1, quarter), (4, 8, quarter)
    )
    head_wide = jnp.pad(w_head, ((0, 0), (0, 128 - head_count)))
    mod, fq, fo, fu, fd = gather_weights(cond_rows, w_ada, head_wide, w_qkv, w_out, w_up, w_down)
    fq, fo, fu, fd = (w.reshape(-1, w.shape[-1]) for w in (fq, fo, fu, fd))
    token_full = lax.all_gather(w_token, "dp", axis=0, tiled=True)
    shift_one, scale_one, gate_one, shift_two, scale_two, gate_two = (mod[i : i + 1] for i in range(6))
    head_sigmoid = jax.nn.sigmoid(mod[6, :head_count])
    head_mask = head_keep[0].astype(jnp.float32)
    head_gate = head_mask * head_sigmoid

    def dot(left, right, dims, dtype=jnp.float32):
        return lax.dot_general(
            left, right, (dims, ((), ())), preferred_element_type=jnp.float32
        ).astype(dtype)

    signal = inputs[0].astype(jnp.float32)
    normed = modulate(signal, scale_one, shift_one).astype(jnp.bfloat16)
    packed = dot(normed, fq, ((1,), (0,)), jnp.bfloat16)
    packed = packed.reshape(patches, 3, head_count, head_size)
    queries, key_rows, value_rows = packed[:, 0], packed[:, 1], packed[:, 2]
    scores = (
        jnp.einsum("qhd,khd->hqk", queries, key_rows, preferred_element_type=jnp.float32) * factor
    )
    probs = jax.nn.softmax(scores, axis=-1)
    probs_low = probs.astype(jnp.bfloat16)
    attended = jnp.einsum("hqk,khd->qhd", probs_low, value_rows, preferred_element_type=jnp.float32)
    gated = (attended * head_gate[None, :, None]).astype(jnp.bfloat16).reshape(patches, model_width)
    branch = dot(gated, fo, ((1,), (0,)))
    middle = signal + gate_one * branch
    second = modulate(middle, scale_two, shift_two).astype(jnp.bfloat16)
    router = jax.nn.sigmoid(dot(second, token_full[:, None], ((1,), (0,))))
    keep = token_keep[0].astype(jnp.float32)[:, None]
    up_proj = dot(second, fu, ((1,), (0,)))
    hidden, gelu_pull = jax.vjp(gelu_tanh, up_proj)
    hidden = hidden.astype(jnp.bfloat16)
    produced = dot(hidden, fd, ((1,), (0,)), jnp.bfloat16).astype(jnp.float32)
    scale_rows = keep * router
    output = (middle + gate_two * scale_rows * produced).astype(jnp.bfloat16)
    grad_out = cotangent[0].astype(jnp.float32)
    grad_gate_two = jnp.sum(grad_out * scale_rows * produced, axis=0, keepdims=True)
    grad_produced = (grad_out * gate_two * scale_rows).astype(jnp.bfloat16)
    grad_router = jnp.sum(grad_out * gate_two * produced, axis=-1, keepdims=True) * keep
    grad_logit = grad_router * router * (1.0 - router)
    grad_token = jnp.sum(grad_logit * second.astype(jnp.float32), axis=0, keepdims=True)
    grad_down = dot(hidden, grad_produced, ((0,), (0,)), jnp.bfloat16)
    grad_hidden = dot(grad_produced, fd, ((1,), (1,)))
    grad_up_proj = gelu_pull(grad_hidden)[0].astype(jnp.bfloat16)
    grad_up = dot(second, grad_up_proj, ((0,), (0,)), jnp.bfloat16)
    grad_second_mlp = dot(grad_up_proj, fu, ((1,), (1,)), jnp.bfloat16)
    grad_second = grad_second_mlp.astype(jnp.float32) + grad_logit * token_full.astype(jnp.float32)[None]
    middle_pull = jax.vjp(modulate, middle, scale_two, shift_two)[1]
    grad_middle_norm, grad_scale_two, grad_shift_two = middle_pull(grad_second)
    grad_middle = grad_out + grad_middle_norm
    grad_gate_one = jnp.sum(grad_middle * branch, axis=0, keepdims=True)
    grad_branch = (gate_one * grad_middle).astype(jnp.bfloat16)
    grad_out_proj = dot(gated, grad_branch, ((0,), (0,)), jnp.bfloat16)
    grad_gated = dot(grad_branch, fo, ((1,), (1,))).reshape(patches, head_count, head_size)
    grad_head_gate = jnp.sum(grad_gated * attended, axis=(0, 2))
    grad_head_logit = grad_head_gate * head_mask * head_sigmoid * (1.0 - head_sigmoid)
    grad_attended = (grad_gated * head_gate[None, :, None]).astype(jnp.bfloat16)
    grad_values = jnp.einsum("hqk,qhd->khd", probs_low, grad_attended, preferred_element_type=jnp.float32)
    grad_probs = jnp.einsum("qhd,khd->hqk", grad_attended, value_rows, preferred_element_type=jnp.float32)
    prob_delta = jnp.sum(probs * grad_probs, axis=-1, keepdims=True)
    grad_scores = (probs * (grad_probs - prob_delta)).astype(jnp.bfloat16)
    grad_queries = (
        jnp.einsum("hqk,khd->qhd", grad_scores, key_rows, preferred_element_type=jnp.float32) * factor
    )
    grad_keys = (
        jnp.einsum("hqk,qhd->khd", grad_scores, queries, preferred_element_type=jnp.float32) * factor
    )
    grad_packed = jnp.stack([grad_queries, grad_keys, grad_values], axis=1).astype(jnp.bfloat16)
    grad_packed = grad_packed.reshape(patches, 3 * model_width)
    grad_qkv = dot(normed, grad_packed, ((0,), (0,)), jnp.bfloat16)
    grad_normed = dot(grad_packed, fq, ((1,), (1,)))
    input_pull = jax.vjp(modulate, signal, scale_one, shift_one)[1]
    grad_signal_norm, grad_scale_one, grad_shift_one = input_pull(grad_normed)
    grad_input = grad_middle + grad_signal_norm
    head_row = jnp.pad(grad_head_logit, (0, model_width - head_count))[None]
    vector = jnp.concatenate(
        [
            grad_shift_one, grad_scale_one, grad_gate_one, grad_shift_two, grad_scale_two, grad_gate_two,
            head_row, grad_token, condition.astype(jnp.float32), jnp.zeros((7, model_width), jnp.float32),
        ],
        axis=0,
    )
    every, s_qkv, s_out, s_up, s_down = scatter_grads(
        vector, (grad_qkv, grad_out_proj, grad_up, grad_down)
    )
    every = every.reshape((32,) + vector.shape)
    share = model_width // 32
    inner = lax.axis_index("seq") % BLOCK
    start = lax.axis_index("dp") * quarter + inner * share
    cond_share = lax.dynamic_slice_in_dim(every[:, 8], start, share, 1)
    grad_ada = jnp.einsum(
        "ir,ikc->rkc", cond_share, every[:, :7], precision=lax.Precision.HIGHEST
    )
    grad_head = grad_ada[:, 6, :head_count]
    grad_ada = grad_ada[:, :6].reshape(share, 6 * model_width)
    grad_token_share = lax.dynamic_slice_in_dim(jnp.sum(every[:, 7], axis=0), start, share, 0)
    parts = (grad_ada, s_qkv, s_out, s_up, s_down, grad_head, grad_token_share)
    parts = tuple(across_blocks(part, seq_size) for part in parts)
    return (output[None], grad_input[None]) + parts


def solution(mesh):
    both = ("dp", "seq")
    in_specs = (
        P(both, None, None), P(), P(both), P(both, None), P(both, None), P(both, None, None),
        P("dp", None), P("dp", None), P("dp", None), P("dp", None), P("dp", None), P("dp", None), P("dp"),
    )
    out_specs = (P(both, None, None), P(both, None, None)) + (P(both, None),) * 6 + (P(both),)
    return jax.shard_map(
        functools.partial(per_device, mesh.shape["seq"]),
        mesh=mesh, in_specs=in_specs, out_specs=out_specs, check_vma=False,
    )
```

```python
import functools
import math
import types

import jax
import jax.numpy as jnp
from jax import lax
from jax.experimental import pallas as pl
from jax.experimental.pallas import tpu as pltpu
from jax.sharding import PartitionSpec as P

epsilon = 1e-06
MESH = pl.DeviceIdType.MESH
ANY = pl.BlockSpec(memory_space=pl.ANY)
VMEM = pl.BlockSpec(memory_space=pltpu.VMEM)
Z_CHIPS = 4
BLOCK = 2 * Z_CHIPS
F32, BF16 = jnp.float32, jnp.bfloat16
NN, NT, TN = ((1,), (0,)), ((1,), (1,)), ((0,), (0,))
ROWS = 32
SHARE = 24


def dot(left, right, dims, exact=False):
    return lax.dot_general(
        left, right, (dims, ((), ())), preferred_element_type=F32,
        precision=lax.Precision.HIGHEST if exact else None,
    )


def span(start, size, unit):
    return pl.ds(pl.multiple_of(start, unit), size)


def by_rows(total, body, step=ROWS):
    @pl.loop(0, total // step)
    def _(index):
        body(span(index * step, step, step))


def fold(values):
    return jnp.sum(values.reshape(-1, 8, values.shape[-1]), axis=0)


class Place:
    def __init__(self):
        self.dp = lax.axis_index("dp")
        self.seq = lax.axis_index("seq")
        self.x = self.dp % 2
        self.y = self.dp // 2
        self.core = self.seq % 2
        self.z = (self.seq // 2) % Z_CHIPS
        self.outer = self.seq // BLOCK

    def z_of(self, step):
        return (self.z + step) % Z_CHIPS

    def peer_x(self):
        return (self.y * 2 + 1 - self.x, self.seq)

    def peer_y(self):
        return ((1 - self.y) * 2 + self.x, self.seq)

    def peer_d(self):
        return ((1 - self.y) * 2 + 1 - self.x, self.seq)

    def peer_core(self):
        return (self.dp, self.seq + 1 - 2 * self.core)

    def peer_z(self, step):
        return (self.dp, self.outer * BLOCK + self.z_of(step) * 2 + self.core)

    def dp_peers(self):
        return (self.peer_x(), self.peer_y(), self.peer_d())

    def greet(self):
        barrier = pltpu.get_barrier_semaphore()
        peers = list(self.dp_peers()) + [self.peer_core()]
        peers += [self.peer_z(k) for k in range(1, Z_CHIPS)]
        for peer in peers:
            pl.semaphore_signal(barrier, inc=1, device_id=peer, device_id_type=MESH)
        pl.semaphore_wait(barrier, len(peers))


class Net:
    def __init__(self, send_sems, recv_sems):
        self.send_sems = send_sems
        self.recv_sems = recv_sems
        self.used = 0
        self.sent = []

    def send(self, src, dst, peer, landing=None):
        slot = self.used
        self.used += 1

        def copy_to(target):
            return pltpu.make_async_remote_copy(
                src_ref=src,
                dst_ref=target,
                send_sem=self.send_sems.at[slot],
                recv_sem=self.recv_sems.at[slot],
                device_id=peer,
                device_id_type=MESH,
            )

        copy = copy_to(dst)
        copy.start()
        self.sent.append(copy)
        arrival = copy if landing is None else copy_to(landing)
        return arrival.wait_recv

    def finish(self):
        for copy in self.sent:
            copy.wait_send()


class Weight:
    def __init__(self, net, here, own, full):
        self.net, self.here, self.own, self.full = net, here, own, full
        self.depth = own.shape[0]
        self.piece = self.depth // Z_CHIPS
        self.width = own.shape[1] // 2

    def columns(self, core):
        return span(core * self.width, self.width, 128)

    def quarter(self, dp):
        return span(dp * self.depth, self.depth, 16)

    def part(self, dp, z):
        return span(dp * self.depth + z * self.piece, self.piece, 16)

    def keep(self, sem):
        self.local = pltpu.make_async_copy(self.own, self.full.at[self.quarter(self.here.dp)], sem)
        self.local.start()

    def send_diagonal(self):
        here, columns = self.here, self.columns(self.here.core)
        peer = here.peer_d()
        self.wait_d = self.net.send(
            self.own.at[span(here.z * self.piece, self.piece, 16), columns],
            self.full.at[self.part(here.dp, here.z), columns],
            peer,
            self.full.at[self.part(peer[0], here.z), columns],
        )

    def send_straight(self):
        here, columns = self.here, self.columns(self.here.core)
        self.wait_xy = []
        for peer in (here.peer_x(), here.peer_y()):
            self.wait_xy.append(
                self.net.send(
                    self.own.at[:, columns],
                    self.full.at[self.quarter(here.dp), columns],
                    peer,
                    self.full.at[self.quarter(peer[0]), columns],
                )
            )
        self.last = []

    def spread(self):
        here, columns = self.here, self.columns(self.here.core)
        diagonal = here.peer_d()[0]
        self.wait_d()
        piece = self.full.at[self.part(diagonal, here.z), columns]
        self.wait_z = [
            self.net.send(
                piece, piece, here.peer_z(step),
                self.full.at[self.part(diagonal, here.z_of(Z_CHIPS - step)), columns],
            )
            for step in range(1, Z_CHIPS)
        ]

    def hand(self, dp):
        here = self.here
        block = self.full.at[self.quarter(dp), self.columns(here.core)]
        self.last.append(
            self.net.send(
                block, block, here.peer_core(),
                self.full.at[self.quarter(dp), self.columns(1 - here.core)],
            )
        )

    def share_straight(self):
        here = self.here
        for wait, peer in zip(self.wait_xy, (here.peer_x(), here.peer_y())):
            wait()
            self.hand(peer[0])

    def share_diagonal(self):
        for wait in self.wait_z:
            wait()
        self.hand(self.here.peer_d()[0])

    def ready(self):
        for wait in self.last:
            wait()
        self.local.wait()


class Chunk:
    def __init__(self, net, here, total, out, bufs, column, width):
        self.net, self.here, self.out = net, here, out
        self.total = total.at[:, span(column, width, 128)]
        self.block = total.shape[0] // 16
        self.column, self.width = column, width
        self.r1a, self.r1b, self.r2a, self.r2b, self.r3, self.f32 = bufs

    def columns(self, core):
        return span(core * (self.out.shape[1] // 2) + self.column, self.width, 128)

    def upper(self, dp):
        return self.total.at[span(dp * 4 * self.block, 2 * self.block, 16)]

    def lower(self, dp):
        return self.total.at[span(dp * 4 * self.block + 2 * self.block, 2 * self.block, 16)]

    def add(self, total, extra):
        def body(rows):
            total[rows, :] = (total[rows, :].astype(F32) + extra[rows, :].astype(F32)).astype(BF16)

        by_rows(2 * self.block, body, 16)

    def first(self):
        here = self.here
        self.wait_a, self.wait_b = [None, None], [None, None]
        for lead in range(2):
            self.wait_a[lead] = self.net.send(
                self.upper(lead * 2 + 1 - here.x), self.r1a.at[lead], here.peer_x()
            )
            self.wait_b[lead] = self.net.send(
                self.lower((1 - here.y) * 2 + lead), self.r1b.at[lead], here.peer_y()
            )

    def second(self):
        here = self.here
        for wait in self.wait_a:
            wait()
        away = self.upper((1 - here.y) * 2 + here.x)
        self.add(away, self.r1a.at[1 - here.y])
        next_a = self.net.send(away, self.r2a, here.peer_y())
        for wait in self.wait_b:
            wait()
        away = self.lower(here.y * 2 + 1 - here.x)
        self.add(away, self.r1b.at[1 - here.x])
        next_b = self.net.send(away, self.r2b, here.peer_x())
        self.add(self.upper(here.dp), self.r1a.at[here.y])
        self.add(self.lower(here.dp), self.r1b.at[here.x])
        self.wait_a, self.wait_b = next_a, next_b

    def mine(self, z):
        return self.total.at[span((here_dp(self.here) * 4 + z) * self.block, self.block, 16)]

    def third(self):
        here = self.here
        self.wait_a()
        self.add(self.upper(here.dp), self.r2a)
        self.wait_b()
        self.add(self.lower(here.dp), self.r2b)
        self.waits = [
            self.net.send(self.mine(here.z_of(k)), self.r3.at[k - 1], here.peer_z(k))
            for k in range(1, Z_CHIPS)
        ]

    def fourth(self):
        here = self.here
        for wait in self.waits:
            wait()
        own = self.mine(here.z)

        def body(rows):
            summed = own[rows, :].astype(F32)
            for k in range(Z_CHIPS - 1):
                summed += self.r3[k, rows, :].astype(F32)
            self.f32[rows, :] = summed

        by_rows(self.block, body, 16)
        part = self.block // 2
        self.wait = self.net.send(
            self.f32.at[span((1 - here.core) * part, part, 8)],
            self.out.at[:, self.columns(here.core)],
            here.peer_core(),
            self.out.at[:, self.columns(1 - here.core)],
        )
        self.out[:, self.columns(here.core)] = self.f32[span(here.core * part, part, 8), :]

    def end(self):
        self.wait()


def here_dp(here):
    return here.dp


def chunk_list(widths):
    chunks = []
    for index, pieces in ((3, 1), (2, 1), (1, 1), (0, 3)):
        step = widths[index] // 2 // pieces
        chunks += [(index, step * k, step) for k in range(pieces)]
    return chunks


def layer_kernel(names, chunks, sizes, *refs):
    v = types.SimpleNamespace(**dict(zip(names, refs)))
    tokens, width, heads, hidden_width = sizes
    quarter = width // 4
    size = width // heads
    factor = size ** (-0.5)
    here = Place()
    core, dp = here.core, here.dp
    net = Net(v.send_sems, v.recv_sems)
    mine, theirs = slice(0, tokens), slice(tokens, 2 * tokens)

    loads = []
    for number, (source, target) in enumerate(
        (
            (v.small, v.small_v), (v.w_head, v.head_v), (v.w_ada, v.ada_v),
            (v.inputs, v.x_v), (v.cotangent, v.g_v),
        )
    ):
        copy = pltpu.make_async_copy(source, target, v.local_sems.at[4 + number])
        copy.start()
        loads.append(copy)
    weights = [
        Weight(net, here, own, full)
        for own, full in ((v.wq, v.fq), (v.wo, v.fo), (v.wu, v.fu), (v.wd, v.fd))
    ]
    for number, weight in enumerate(weights):
        weight.keep(v.local_sems.at[number])
    w_q, w_o, w_u, w_d = weights
    here.greet()

    loads[0].wait()
    waits = [
        net.send(v.small_v, v.cond_buf.at[dp], peer, v.cond_buf.at[peer[0]])
        for peer in here.dp_peers()
    ]
    w_q.send_diagonal()
    w_q.send_straight()
    v.cond_buf[pl.ds(dp, 1)] = v.small_v[...][None]
    select = (
        lax.broadcasted_iota(jnp.int32, (width, quarter), 0)
        == lax.broadcasted_iota(jnp.int32, (width, quarter), 1) + dp * quarter
    ).astype(F32).astype(BF16)
    loads[1].wait()
    loads[2].wait()
    for wait in waits:
        wait()
    stacked = v.cond_buf[...].reshape(32, width).astype(BF16)
    left = dot(stacked, select, NN).astype(BF16)
    v.part[...] = jnp.zeros(v.part.shape, F32)
    for piece in range(7):
        if piece < 6:
            product = dot(left, v.ada_v[:, piece * width : (piece + 1) * width], NN)
        else:
            product = dot(left, v.head_v[...], NN)
        for image in range(4):
            v.part[image, piece : piece + 1, 0 : product.shape[1]] = product[image * 8 : image * 8 + 1]
    waits = [
        net.send(v.part.at[peer[0]], v.part_buf.at[index], peer)
        for index, peer in enumerate(here.dp_peers())
    ]
    w_o.send_diagonal()
    w_u.send_diagonal()
    w_o.send_straight()
    w_d.send_diagonal()
    w_u.send_straight()
    w_d.send_straight()
    v.token[...] = v.cond_buf[0, 1:2] + v.cond_buf[1, 1:2] + v.cond_buf[2, 1:2] + v.cond_buf[3, 1:2]
    keep_row = v.small_v[3:4, 0:tokens]
    diagonal = lax.broadcasted_iota(jnp.int32, (tokens, tokens), 0) == lax.broadcasted_iota(
        jnp.int32, (tokens, tokens), 1
    )
    v.keep[...] = jnp.sum(jnp.where(diagonal, keep_row, 0.0), axis=1, keepdims=True)
    head_of = lax.broadcasted_iota(jnp.int32, (128, width), 0) * size
    lane = lax.broadcasted_iota(jnp.int32, (128, width), 1)
    v.expand[...] = ((lane >= head_of) & (lane < head_of + size)).astype(F32)
    for wait in waits:
        wait()
    v.mod[...] = v.part[dp] + v.part_buf[0] + v.part_buf[1] + v.part_buf[2]
    head_sigmoid = jax.nn.sigmoid(v.mod[6:7, 0:128])
    head_mask = v.small_v[2:3, 0:128]
    gate = dot(jnp.broadcast_to(head_mask * head_sigmoid, (8, 128)), v.expand[...], NN, exact=True)
    v.gate_row[...] = gate[0:1]

    loads[3].wait()

    def first_norm(rows):
        values = v.x_v[rows, :].astype(F32)
        centre = values - jnp.mean(values, axis=1, keepdims=True)
        spread = jnp.mean(centre * centre, axis=1, keepdims=True)
        normal = centre * lax.rsqrt(spread + epsilon)
        v.nb[rows, :] = (normal * (1.0 + v.mod[1:2]) + v.mod[0:1]).astype(BF16)

    by_rows(tokens, first_norm)
    wait_normed = net.send(v.nb.at[mine], v.nb.at[theirs], here.peer_core())

    w_q.spread()
    w_q.share_straight()
    w_q.share_diagonal()
    w_q.ready()

    @pl.loop(0, 3 * width // 384)
    def _(index):
        columns = span(index * 384, 384, 128)
        v.packed[:, columns] = dot(v.nb[mine, :], v.fq[:, columns], NN).astype(BF16)

    w_o.spread()
    w_u.spread()

    lanes = lax.broadcasted_iota(jnp.int32, (1, 2 * size), 1)
    masks = ((lanes < size).astype(F32).astype(BF16), (lanes >= size).astype(F32).astype(BF16))
    low_lane = lax.broadcasted_iota(jnp.int32, (tokens, 2 * size), 1) < size

    def three(pair, block):
        return [block[:, span(part * width + pair * 2 * size, 2 * size, 128)] for part in range(3)]

    @pl.loop(0, heads // 2)
    def _(pair):
        queries, key_rows, value_rows = three(pair, v.packed)
        found = []
        for which in range(2):
            scores = dot(queries * masks[which], key_rows, NT) * factor
            powers = jnp.exp(scores - jnp.max(scores, axis=1, keepdims=True))
            probs = powers * (1.0 / jnp.sum(powers, axis=1, keepdims=True))
            v.probs[pair * 2 + which] = probs
            found.append(dot(probs.astype(BF16), value_rows, NN))
        attended = jnp.where(low_lane, found[0], found[1])
        columns = span(pair * 2 * size, 2 * size, 128)
        v.attended[:, columns] = attended
        v.gated[mine, columns] = (attended * v.gate_row[:, columns]).astype(BF16)

    wait_gated = net.send(v.gated.at[mine], v.gated.at[theirs], here.peer_core())
    w_o.share_straight()
    w_d.spread()
    w_o.share_diagonal()
    w_o.ready()

    @pl.loop(0, width // 256)
    def _(index):
        columns = span(index * 256, 256, 128)
        v.branch[:, columns] = dot(v.gated[mine, :], v.fo[:, columns], NN)

    loads[4].wait()

    def second_norm(rows):
        middle = v.x_v[rows, :].astype(F32) + v.mod[2:3] * v.branch[rows, :]
        v.middle[rows, :] = middle
        centre = middle - jnp.mean(middle, axis=1, keepdims=True)
        spread = jnp.mean(centre * centre, axis=1, keepdims=True)
        scale = lax.rsqrt(spread + epsilon)
        normal = centre * scale
        v.z2[rows, :] = normal
        v.scale2[rows, :] = scale
        second = (normal * (1.0 + v.mod[4:5]) + v.mod[3:4]).astype(BF16)
        v.second[rows, :] = second
        logit = jnp.sum(second.astype(F32) * v.token[...], axis=1, keepdims=True)
        router = jax.nn.sigmoid(logit)
        v.router[rows, :] = router
        weight = v.keep[rows, :] * router
        v.grad_prod[rows, :] = (v.g_v[rows, :].astype(F32) * v.mod[5:6] * weight).astype(BF16)

    by_rows(tokens, second_norm)
    wait_second = net.send(v.second.at[mine], v.second.at[theirs], here.peer_core())
    half = width // 2
    other = span((1 - core) * half, half, 128)
    own = span(core * half, half, 128)
    wait_dprod = net.send(v.grad_prod.at[:, other], v.dy_down.at[theirs], here.peer_core())
    v.dy_down[mine, :] = v.grad_prod[:, own]

    w_u.share_straight()
    w_u.share_diagonal()
    w_u.ready()
    inner = math.sqrt(2.0 / math.pi)

    @pl.loop(0, hidden_width // 512)
    def _(index):
        columns = span(index * 512, 512, 128)
        v.tmp[:, 0:512] = dot(v.second[mine, :], v.fu[:, columns], NN)

        def bend(rows):
            u = v.tmp[rows, 0:512]
            square = u * u
            t = jnp.tanh(inner * (u + 0.044715 * (square * u)))
            v.hidden[rows, columns] = (0.5 * u * (1.0 + t)).astype(BF16)
            v.slope[rows, columns] = 0.5 * (1.0 + t) + (0.5 * inner) * u * (1.0 - t * t) * (
                1.0 + (3.0 * 0.044715) * square
            )

        by_rows(tokens, bend)

    wait_hidden = net.send(v.hidden.at[mine], v.hidden.at[theirs], here.peer_core())
    pieces = []
    for number, (index, column, wide) in enumerate(chunks):
        total = (v.t_qkv, v.t_out, v.t_up, v.t_down)[index]
        out = (v.o_qkv, v.o_out, v.o_up, v.o_down)[index]
        bufs = [getattr(v, f"c{number}_{k}") for k in range(6)]
        pieces.append(Chunk(net, here, total, out, bufs, column, wide))
    c_down, c_up, c_out = pieces[:3]
    c_qkv = pieces[3:]

    def weight_grad(total, left, right, step):
        @pl.loop(0, total.shape[0] // step)
        def _(index):
            rows = span(index * step, step, 128)
            total[rows, :] = dot(left[:, rows], right[...], TN).astype(BF16)

    wait_hidden()
    wait_dprod()
    weight_grad(v.t_down, v.hidden, v.dy_down, 256)
    c_down.first()
    w_d.share_straight()
    w_d.share_diagonal()
    w_d.ready()

    wide_half = hidden_width // 2

    def bend_back(side):
        @pl.loop(0, wide_half // 512)
        def _(index):
            columns = span(side * wide_half + index * 512, 512, 128)
            back = dot(v.grad_prod[...], v.fd[columns, :], NT)
            v.grad_u[:, columns] = (back * v.slope[:, columns]).astype(BF16)

    bend_back(1 - core)
    wait_du = net.send(
        v.grad_u.at[:, span((1 - core) * wide_half, wide_half, 128)], v.dy_up.at[theirs], here.peer_core()
    )
    bend_back(core)
    v.dy_up[mine, :] = v.grad_u[:, span(core * wide_half, wide_half, 128)]
    wait_second()
    wait_du()
    weight_grad(v.t_up, v.second, v.dy_up, 256)
    c_up.first()

    @pl.loop(0, width // 256)
    def _(index):
        columns = span(index * 256, 256, 128)
        v.produced[:, columns] = dot(v.hidden[mine, :], v.fd[:, columns], NN).astype(BF16)

    c_down.second()
    v.sums[...] = jnp.zeros(v.sums.shape, F32)

    def finish(rows):
        produced = v.produced[rows, :].astype(F32)
        grad = v.g_v[rows, :].astype(F32)
        router, keep = v.router[rows, :], v.keep[rows, :]
        scaled = produced * (keep * router)
        v.output[rows, :] = (v.middle[rows, :] + v.mod[5:6] * scaled).astype(BF16)
        v.sums[0] += fold(grad * scaled)
        back = jnp.sum(grad * v.mod[5:6] * produced, axis=1, keepdims=True)
        v.logit[rows, :] = back * keep * router * (1.0 - router)

    by_rows(tokens, finish)

    @pl.loop(0, width // 256)
    def _(index):
        columns = span(index * 256, 256, 128)
        v.produced[:, columns] = dot(v.grad_u[...], v.fu[columns, :], NT).astype(BF16)

    def second_back(rows):
        logit = v.logit[rows, :]
        back = v.produced[rows, :].astype(F32) + logit * v.token[...]
        normal = v.z2[rows, :]
        v.sums[1] += fold(logit * v.second[rows, :].astype(F32))
        v.sums[2] += fold(back * normal)
        v.sums[3] += fold(back)
        inside = back * (1.0 + v.mod[4:5])
        level = jnp.mean(inside, axis=1, keepdims=True)
        slope = jnp.mean(inside * normal, axis=1, keepdims=True)
        grad = v.g_v[rows, :].astype(F32) + v.scale2[rows, :] * (inside - level - normal * slope)
        v.grad_mid[rows, :] = grad
        v.sums[4] += fold(grad * v.branch[rows, :])
        v.grad_branch[rows, :] = (v.mod[2:3] * grad).astype(BF16)

    by_rows(tokens, second_back)
    wait_dbranch = net.send(v.grad_branch.at[:, other], v.dy_out.at[theirs], here.peer_core())
    v.dy_out[mine, :] = v.grad_branch[:, own]

    @pl.loop(0, width // 256)
    def _(index):
        columns = span(index * 256, 256, 128)
        v.tmp[:, columns] = dot(v.grad_branch[...], v.fo[columns, :], NT)

    wait_gated()
    wait_dbranch()
    weight_grad(v.t_out, v.gated, v.dy_out, 256)
    c_out.first()
    c_up.second()

    def gate_back(rows):
        grad = v.tmp[rows, :]
        v.sums[5] += fold(grad * v.attended[rows, :])
        v.grad_att[rows, :] = (grad * v.gate_row[...]).astype(BF16)

    by_rows(tokens, gate_back)

    @pl.loop(0, heads // 2)
    def _(pair):
        queries, key_rows, value_rows = three(pair, v.packed)
        columns = span(pair * 2 * size, 2 * size, 128)
        grad_att = v.grad_att[:, columns]
        gq, gk, gv = [], [], []
        for which in range(2):
            probs = v.probs[pair * 2 + which]
            grad_probs = dot(grad_att * masks[which], value_rows, NT)
            level = jnp.sum(probs * grad_probs, axis=1, keepdims=True)
            grad_scores = (probs * (grad_probs - level)).astype(BF16)
            gq.append(dot(grad_scores, key_rows, NN))
            gk.append(dot(grad_scores, queries, TN))
            gv.append(dot(probs.astype(BF16), grad_att, TN))
        for part, (grads, scale) in enumerate(((gq, factor), (gk, factor), (gv, 1.0))):
            both = jnp.where(low_lane, grads[0], grads[1]) * scale
            v.grad_pack[:, span(part * width + pair * 2 * size, 2 * size, 128)] = both.astype(BF16)

    packed_half = 3 * width // 2
    wait_dpack = net.send(
        v.grad_pack.at[:, span((1 - core) * packed_half, packed_half, 128)],
        v.dy_qkv.at[theirs],
        here.peer_core(),
    )
    v.dy_qkv[mine, :] = v.grad_pack[:, span(core * packed_half, packed_half, 128)]
    c_down.third()
    c_out.second()
    wait_normed()
    wait_dpack()
    weight_grad(v.t_qkv, v.nb, v.dy_qkv, 256)
    for chunk in c_qkv:
        chunk.first()
    c_up.third()
    c_out.third()

    head_back = dot(
        jnp.broadcast_to(jnp.sum(v.sums[5], axis=0, keepdims=True), (8, width)), v.expand[...], NT, exact=True
    )
    head_back = head_back[0:1] * head_mask * head_sigmoid * (1.0 - head_sigmoid)
    v.early_out[...] = jnp.zeros(v.early_out.shape, F32)
    v.early_out[0:1, :] = jnp.sum(v.sums[4], axis=0, keepdims=True)
    v.early_out[1:2, :] = jnp.sum(v.sums[3], axis=0, keepdims=True)
    v.early_out[2:3, :] = jnp.sum(v.sums[2], axis=0, keepdims=True)
    v.early_out[3:4, :] = jnp.sum(v.sums[0], axis=0, keepdims=True)
    v.early_out[4:5, 0:128] = head_back
    v.early_out[5:6, :] = jnp.sum(v.sums[1], axis=0, keepdims=True)
    v.early_out[6:7, :] = v.small_v[0:1, :]

    def gather_start(piece, block):
        block[pl.ds(core, 1), pl.ds(here.z, 1), pl.ds(dp, 1)] = piece[...][None, None, None]
        return [
            net.send(piece, block.at[core, here.z, dp], peer, block.at[core, here.z, peer[0]])
            for peer in here.dp_peers()
        ]

    def gather_along(block, waits):
        for wait in waits:
            wait()
        return [
            net.send(
                block.at[core, here.z], block.at[core, here.z], here.peer_z(k),
                block.at[core, here.z_of(Z_CHIPS - k)],
            )
            for k in range(1, Z_CHIPS)
        ]

    def gather_pair(block, waits):
        for wait in waits:
            wait()
        return net.send(block.at[core], block.at[core], here.peer_core(), block.at[1 - core])

    early = gather_start(v.early_out, v.early)

    @pl.loop(0, width // 256)
    def _(index):
        columns = span(index * 256, 256, 128)
        v.tmp[:, columns] = dot(v.grad_pack[...], v.fq[columns, :], NT)

    def first_back(rows):
        back = v.tmp[rows, :]
        values = v.x_v[rows, :].astype(F32)
        centre = values - jnp.mean(values, axis=1, keepdims=True)
        spread = jnp.mean(centre * centre, axis=1, keepdims=True)
        scale = lax.rsqrt(spread + epsilon)
        normal = centre * scale
        v.sums[6] += fold(back * normal)
        v.sums[7] += fold(back)
        inside = back * (1.0 + v.mod[1:2])
        level = jnp.mean(inside, axis=1, keepdims=True)
        slope = jnp.mean(inside * normal, axis=1, keepdims=True)
        v.grad_input[rows, :] = v.grad_mid[rows, :] + scale * (inside - level - normal * slope)

    by_rows(tokens, first_back)
    shift = jnp.sum(v.sums[7], axis=0, keepdims=True)
    scale = jnp.sum(v.sums[6], axis=0, keepdims=True)
    v.late_out[...] = jnp.zeros(v.late_out.shape, F32)
    for k in range(width // 128):
        v.late_out[k : k + 1, :] = shift[:, k * 128 : (k + 1) * 128]
        v.late_out[8 + k : 9 + k, :] = scale[:, k * 128 : (k + 1) * 128]
    early = gather_along(v.early, early)
    late = gather_start(v.late_out, v.late)
    for chunk in c_qkv[:2]:
        chunk.second()
    late = gather_along(v.late, late)
    for chunk in c_qkv[2:]:
        chunk.second()
    c_down.fourth()
    c_up.fourth()
    c_out.fourth()
    early = gather_pair(v.early, early)
    c_qkv[0].third()
    late = gather_pair(v.late, late)
    for chunk in c_qkv[1:]:
        chunk.third()

    early()
    late()
    offset = dp * quarter + (here.seq % BLOCK) * SHARE
    pick = (
        lax.broadcasted_iota(jnp.int32, (width, SHARE), 0)
        == lax.broadcasted_iota(jnp.int32, (width, SHARE), 1) + offset
    ).astype(F32)
    every = v.early[...].reshape(32, 8, width)
    conditions = dot(every[:, 6, :].astype(BF16), pick.astype(BF16), NN)
    for slot, piece in enumerate((2, 3, 4, 5)):
        v.o_ada[:, piece * width : (piece + 1) * width] = dot(conditions, every[:, slot, :], TN, exact=True)
    v.o_head[...] = dot(conditions, every[:, 4, 0:128], TN, exact=True)[:, 0 : v.o_head.shape[1]]
    totals = jnp.sum(every[:, 5, :], axis=0, keepdims=True)
    v.o_token[...] = dot(jnp.broadcast_to(totals, (8, width)), pick, NN, exact=True)
    tail = v.late[...].reshape(32, 16, 128)
    for k in range(width // 128):
        v.o_ada[:, k * 128 : (k + 1) * 128] = dot(conditions, tail[:, k, :], TN, exact=True)
        v.o_ada[:, width + k * 128 : width + (k + 1) * 128] = dot(
            conditions, tail[:, 8 + k, :], TN, exact=True
        )
    for chunk in c_qkv:
        chunk.fourth()
    for chunk in pieces:
        chunk.end()
    net.finish()


def layer(small, inputs, cotangent, w_ada, w_head, wq, wo, wu, wd, heads):
    tokens, width = inputs.shape
    hidden_width = wu.shape[1]
    quarter = width // 4
    widths = [wq.shape[1], wo.shape[1], wu.shape[1], wd.shape[1]]
    depths = [4 * w.shape[0] for w in (wq, wo, wu, wd)]
    chunks = chunk_list(widths)
    operands = dict(
        small=small, inputs=inputs, cotangent=cotangent, w_ada=w_ada, w_head=w_head, wq=wq, wo=wo, wu=wu, wd=wd
    )
    results = dict(
        output=((tokens, width), BF16),
        grad_input=((tokens, width), F32),
        o_ada=((SHARE, 6 * width), F32),
        o_qkv=((depths[0] // 32, widths[0]), F32),
        o_out=((depths[1] // 32, widths[1]), F32),
        o_up=((depths[2] // 32, widths[2]), F32),
        o_down=((depths[3] // 32, widths[3]), F32),
        o_head=((SHARE, heads), F32),
        o_token=((8, SHARE), F32),
    )
    space = dict(
        small_v=(small.shape, F32),
        head_v=(w_head.shape, BF16),
        ada_v=(w_ada.shape, BF16),
        x_v=((tokens, width), BF16),
        g_v=((tokens, width), BF16),
        fq=((depths[0], widths[0]), BF16),
        fo=((depths[1], widths[1]), BF16),
        fu=((depths[2], widths[2]), BF16),
        fd=((depths[3], widths[3]), BF16),
        cond_buf=((4, 8, width), F32),
        part=((4, 8, width), F32),
        part_buf=((3, 8, width), F32),
        mod=((8, width), F32),
        token=((1, width), F32),
        keep=((tokens, 1), F32),
        expand=((128, width), F32),
        gate_row=((1, width), F32),
        nb=((2 * tokens, width), BF16),
        packed=((tokens, 3 * width), BF16),
        probs=((heads, tokens, tokens), F32),
        attended=((tokens, width), F32),
        gated=((2 * tokens, width), BF16),
        branch=((tokens, width), F32),
        middle=((tokens, width), F32),
        z2=((tokens, width), F32),
        scale2=((tokens, 1), F32),
        second=((2 * tokens, width), BF16),
        router=((tokens, 1), F32),
        logit=((tokens, 1), F32),
        grad_prod=((tokens, width), BF16),
        dy_down=((2 * tokens, width // 2), BF16),
        tmp=((tokens, width), F32),
        hidden=((2 * tokens, hidden_width), BF16),
        slope=((tokens, hidden_width), F32),
        grad_u=((tokens, hidden_width), BF16),
        dy_up=((2 * tokens, hidden_width // 2), BF16),
        produced=((tokens, width), BF16),
        grad_mid=((tokens, width), F32),
        grad_branch=((tokens, width), BF16),
        dy_out=((2 * tokens, width // 2), BF16),
        grad_att=((tokens, width), BF16),
        grad_pack=((tokens, 3 * width), BF16),
        dy_qkv=((2 * tokens, 3 * width // 2), BF16),
        sums=((8, 8, width), F32),
        early_out=((8, width), F32),
        early=((2, Z_CHIPS, 4, 8, width), F32),
        late_out=((16, 128), F32),
        late=((2, Z_CHIPS, 4, 16, 128), F32),
        t_qkv=((depths[0], widths[0] // 2), BF16),
        t_out=((depths[1], widths[1] // 2), BF16),
        t_up=((depths[2], widths[2] // 2), BF16),
        t_down=((depths[3], widths[3] // 2), BF16),
    )
    for number, (index, _, wide) in enumerate(chunks):
        rows = depths[index] // 16
        shapes = ((2, 2 * rows, wide), (2, 2 * rows, wide), (2 * rows, wide), (2 * rows, wide), (3, rows, wide))
        for k, shape in enumerate(shapes):
            space[f"c{number}_{k}"] = (shape, BF16)
        space[f"c{number}_5"] = ((rows, wide), F32)
    copies = 6 + 4 * 9 + 8 + len(chunks) * 10 + 14
    names = list(operands) + list(results) + list(space) + ["send_sems", "recv_sems", "local_sems"]
    return pl.pallas_call(
        functools.partial(layer_kernel, names, chunks, (tokens, width, heads, hidden_width)),
        out_shape=[jax.ShapeDtypeStruct(*r) for r in results.values()],
        in_specs=[ANY] * len(operands),
        out_specs=[VMEM] * len(results),
        scratch_shapes=[pltpu.VMEM(*s) for s in space.values()]
        + [
            pltpu.SemaphoreType.DMA((copies,)),
            pltpu.SemaphoreType.DMA((copies,)),
            pltpu.SemaphoreType.DMA((9,)),
        ],
        compiler_params=pltpu.CompilerParams(
            collective_id=0, has_side_effects=True, vmem_limit_bytes=64 * 2**20 - 2**16
        ),
    )(*operands.values())


def across_blocks(part, seq_size):
    blocks = seq_size // BLOCK
    if blocks == 1:
        return part
    groups = [[b * BLOCK + j for b in range(blocks)] for j in range(BLOCK)]
    mine = lax.psum_scatter(
        part, "seq", scatter_dimension=0, axis_index_groups=groups, tiled=True
    )
    moves = [(b * BLOCK + j, j * blocks + b) for b in range(blocks) for j in range(BLOCK)]
    return lax.ppermute(mine, "seq", moves)


def per_device(
    seq_size, inputs, time_table, time_index, token_keep, head_keep, cotangent,
    w_ada, w_qkv, w_out, w_up, w_down, w_head, w_token,
):
    _, patches, width = inputs.shape
    heads = head_keep.shape[1]
    quarter = width // 4
    condition = jax.nn.silu(time_table[time_index].astype(F32)).astype(BF16).astype(F32)
    place = jnp.arange(width) // quarter == lax.axis_index("dp")
    token_row = jnp.where(place, jnp.tile(w_token, 4).astype(F32), 0.0)[None]

    def row(values):
        return jnp.pad(values.astype(F32), ((0, 0), (0, width - values.shape[1])))

    small = jnp.concatenate(
        [condition, token_row, row(head_keep), row(token_keep), jnp.zeros((4, width), F32)], axis=0
    )
    out = layer(
        small, inputs[0], cotangent[0], w_ada, w_head, w_qkv, w_out, w_up, w_down, heads
    )
    output, grad_input, ada, qkv, outw, up, down, head, token = out
    parts = (ada, qkv, outw, up, down, head, token[0])
    parts = tuple(across_blocks(part, seq_size) for part in parts)
    return (output[None], grad_input[None]) + parts


def solution(mesh):
    both = ("dp", "seq")
    in_specs = (
        P(both, None, None), P(), P(both), P(both, None), P(both, None), P(both, None, None),
        P("dp", None), P("dp", None), P("dp", None), P("dp", None), P("dp", None), P("dp", None), P("dp"),
    )
    out_specs = (P(both, None, None), P(both, None, None)) + (P(both, None),) * 6 + (P(both),)
    return jax.shard_map(
        functools.partial(per_device, mesh.shape["seq"]),
        mesh=mesh, in_specs=in_specs, out_specs=out_specs, check_vma=False,
    )
```

```python
import functools
import math
import types

import jax
import jax.numpy as jnp
from jax import lax
from jax.experimental import pallas as pl
from jax.experimental.pallas import tpu as pltpu
from jax.sharding import PartitionSpec as P

epsilon = 1e-06
MESH = pl.DeviceIdType.MESH
ANY = pl.BlockSpec(memory_space=pl.ANY)
VMEM = pl.BlockSpec(memory_space=pltpu.VMEM)
Z_CHIPS = 4
BLOCK = 2 * Z_CHIPS
F32, BF16 = jnp.float32, jnp.bfloat16
NN, NT, TN = ((1,), (0,)), ((1,), (1,)), ((0,), (0,))
ROWS = 32
SHARE = 24


def dot(left, right, dims, exact=False):
    return lax.dot_general(
        left, right, (dims, ((), ())), preferred_element_type=F32,
        precision=lax.Precision.HIGHEST if exact else None,
    )


def span(start, size, unit):
    return pl.ds(pl.multiple_of(start, unit), size)


def by_rows(total, body, step=ROWS):
    @pl.loop(0, total // step)
    def _(index):
        body(span(index * step, step, step))


def fold(values):
    return jnp.sum(values.reshape(-1, 8, values.shape[-1]), axis=0)


class Place:
    def __init__(self):
        self.dp = lax.axis_index("dp")
        self.seq = lax.axis_index("seq")
        self.x = self.dp % 2
        self.y = self.dp // 2
        self.core = self.seq % 2
        self.z = (self.seq // 2) % Z_CHIPS
        self.outer = self.seq // BLOCK

    def z_of(self, step):
        return (self.z + step) % Z_CHIPS

    def peer_x(self):
        return (self.y * 2 + 1 - self.x, self.seq)

    def peer_y(self):
        return ((1 - self.y) * 2 + self.x, self.seq)

    def peer_d(self):
        return ((1 - self.y) * 2 + 1 - self.x, self.seq)

    def peer_core(self):
        return (self.dp, self.seq + 1 - 2 * self.core)

    def peer_z(self, step):
        return (self.dp, self.outer * BLOCK + self.z_of(step) * 2 + self.core)

    def peer_z1(self):
        return (self.dp, self.seq + 2 - 4 * (self.z % 2))

    def peer_z2(self):
        return (self.dp, self.seq + 4 - 8 * (self.z // 2))

    def dp_peers(self):
        return (self.peer_x(), self.peer_y(), self.peer_d())

    def greet(self):
        peers = list(self.dp_peers()) + [self.peer_core()]
        peers += [self.peer_z(k) for k in range(1, Z_CHIPS)]
        for peer in peers:
            pl.semaphore_signal(
                pltpu.get_barrier_semaphore(), inc=1, device_id=peer, device_id_type=MESH
            )
        self.peers = len(peers)

    def meet(self):
        pl.semaphore_wait(pltpu.get_barrier_semaphore(), self.peers)


class Net:
    def __init__(self, send_sems, recv_sems):
        self.send_sems = send_sems
        self.recv_sems = recv_sems
        self.used = 0
        self.sent = []

    def send(self, src, dst, peer, landing=None):
        slot = self.used
        self.used += 1

        def copy_to(target):
            return pltpu.make_async_remote_copy(
                src_ref=src,
                dst_ref=target,
                send_sem=self.send_sems.at[slot],
                recv_sem=self.recv_sems.at[slot],
                device_id=peer,
                device_id_type=MESH,
            )

        copy = copy_to(dst)
        copy.start()
        self.sent.append(copy)
        arrival = copy if landing is None else copy_to(landing)
        return arrival.wait_recv

    def finish(self):
        for copy in self.sent:
            copy.wait_send()


class Weight:
    def __init__(self, net, here, own, full):
        self.net, self.here, self.own, self.full = net, here, own, full
        self.depth = own.shape[0]
        self.piece = self.depth // Z_CHIPS
        self.width = own.shape[1] // 2

    def columns(self, core):
        return span(core * self.width, self.width, 128)

    def quarter(self, dp):
        return span(dp * self.depth, self.depth, 16)

    def part(self, dp, z):
        return span(dp * self.depth + z * self.piece, self.piece, 16)

    def keep(self, sem):
        self.local = pltpu.make_async_copy(self.own, self.full.at[self.quarter(self.here.dp)], sem)
        self.local.start()

    def send_diagonal(self):
        here, columns = self.here, self.columns(self.here.core)
        peer = here.peer_d()
        self.wait_d = self.net.send(
            self.own.at[span(here.z * self.piece, self.piece, 16), columns],
            self.full.at[self.part(here.dp, here.z), columns],
            peer,
            self.full.at[self.part(peer[0], here.z), columns],
        )

    def send_straight(self):
        here, columns = self.here, self.columns(self.here.core)
        self.wait_xy = []
        for peer in (here.peer_x(), here.peer_y()):
            self.wait_xy.append(
                self.net.send(
                    self.own.at[:, columns],
                    self.full.at[self.quarter(here.dp), columns],
                    peer,
                    self.full.at[self.quarter(peer[0]), columns],
                )
            )
        self.last = []

    def spread(self):
        here, columns = self.here, self.columns(self.here.core)
        diagonal = here.peer_d()[0]
        self.wait_d()
        piece = self.full.at[self.part(diagonal, here.z), columns]
        self.wait_z = [
            self.net.send(
                piece, piece, here.peer_z(step),
                self.full.at[self.part(diagonal, here.z_of(Z_CHIPS - step)), columns],
            )
            for step in range(1, Z_CHIPS)
        ]

    def hand(self, dp):
        here = self.here
        block = self.full.at[self.quarter(dp), self.columns(here.core)]
        self.last.append(
            self.net.send(
                block, block, here.peer_core(),
                self.full.at[self.quarter(dp), self.columns(1 - here.core)],
            )
        )

    def share_straight(self):
        here = self.here
        for wait, peer in zip(self.wait_xy, (here.peer_x(), here.peer_y())):
            wait()
            self.hand(peer[0])

    def share_diagonal(self):
        for wait in self.wait_z:
            wait()
        self.hand(self.here.peer_d()[0])

    def ready(self):
        for wait in self.last:
            wait()
        self.local.wait()


class Chunk:
    def __init__(self, net, here, total, out, bufs, column, width):
        self.net, self.here, self.out = net, here, out
        self.total = total.at[:, span(column, width, 128)]
        self.block = total.shape[0] // 16
        self.column, self.width = column, width
        self.r1a, self.r1b, self.r2a, self.r2b, self.r3a, self.r3b, self.f32 = bufs

    def columns(self, core):
        return span(core * (self.out.shape[1] // 2) + self.column, self.width, 128)

    def upper(self, dp):
        return self.total.at[span(dp * 4 * self.block, 2 * self.block, 16)]

    def lower(self, dp):
        return self.total.at[span(dp * 4 * self.block + 2 * self.block, 2 * self.block, 16)]

    def add(self, total, extra):
        def body(rows):
            total[rows, :] = (total[rows, :].astype(F32) + extra[rows, :].astype(F32)).astype(BF16)

        by_rows(total.shape[0], body, 16)

    def first_diagonal(self):
        here, dp = self.here, self.here.peer_d()[0]
        self.wait_a = [self.net.send(self.upper(dp), self.r1a.at[1 - here.y], here.peer_x())]
        self.wait_b = [self.net.send(self.lower(dp), self.r1b.at[1 - here.x], here.peer_y())]

    def first_x(self):
        here, peer = self.here, self.here.peer_x()
        self.wait_a.append(self.net.send(self.upper(peer[0]), self.r1a.at[here.y], peer))

    def first_y(self):
        here, peer = self.here, self.here.peer_y()
        self.wait_b.append(self.net.send(self.lower(peer[0]), self.r1b.at[here.x], peer))

    def first(self):
        self.first_diagonal()
        self.first_x()
        self.first_y()

    def second(self):
        here = self.here
        for wait in self.wait_a:
            wait()
        away = self.upper((1 - here.y) * 2 + here.x)
        self.add(away, self.r1a.at[1 - here.y])
        next_a = self.net.send(away, self.r2a, here.peer_y())
        for wait in self.wait_b:
            wait()
        away = self.lower(here.y * 2 + 1 - here.x)
        self.add(away, self.r1b.at[1 - here.x])
        next_b = self.net.send(away, self.r2b, here.peer_x())
        self.add(self.upper(here.dp), self.r1a.at[here.y])
        self.add(self.lower(here.dp), self.r1b.at[here.x])
        self.wait_a, self.wait_b = next_a, next_b

    def mine(self, z):
        return self.total.at[span((self.here.dp * 4 + z) * self.block, self.block, 16)]

    def third(self):
        here = self.here
        self.wait_a()
        self.add(self.upper(here.dp), self.r2a)
        self.wait_b()
        self.add(self.lower(here.dp), self.r2b)
        odd = 1 - here.z % 2
        self.waits = [
            self.net.send(self.mine(odd + 2 * k), self.r3a.at[k], here.peer_z1()) for k in range(2)
        ]

    def fourth(self):
        here = self.here
        far = (here.z + 2) % Z_CHIPS
        for wait in self.waits:
            wait()
        self.add(self.mine(far), self.r3a.at[far // 2])
        self.wait = self.net.send(self.mine(far), self.r3b, here.peer_z2())
        self.add(self.mine(here.z), self.r3a.at[here.z // 2])

    def fifth(self):
        here = self.here
        self.wait()
        own = self.mine(here.z)

        def body(rows):
            self.f32[rows, :] = own[rows, :].astype(F32) + self.r3b[rows, :].astype(F32)

        by_rows(self.block, body, 16)
        self.pass_on()

    def pass_on(self):
        here = self.here
        part = self.block // 2
        self.wait = self.net.send(
            self.f32.at[span((1 - here.core) * part, part, 8)],
            self.out.at[:, self.columns(here.core)],
            here.peer_core(),
            self.out.at[:, self.columns(1 - here.core)],
        )
        self.out[:, self.columns(here.core)] = self.f32[span(here.core * part, part, 8), :]

    def end(self):
        self.wait()


class EarlyChunk(Chunk):
    def __init__(self, net, here, total, out, bufs, column, width):
        super().__init__(net, here, total, out, bufs, column, width)
        if width == 128:
            half = self.block // 2
            self.halves = ((span(0, half, 16), span(0, width, 128)), (span(half, half, 16), span(0, width, 128)))
        else:
            half = width // 2
            rows = span(0, self.block, 16)
            self.halves = ((rows, span(0, half, 128)), (rows, span(half, half, 128)))

    def at(self, dp, z):
        return self.total.at[span((dp * 4 + z) * self.block, self.block, 16)]

    def upper(self, dp):
        return self.at(dp, self.here.z).at[self.halves[0]]

    def lower(self, dp):
        return self.at(dp, self.here.z).at[self.halves[1]]

    def near(self):
        here = self.here
        odd = 1 - here.z % 2
        self.waits = [
            self.net.send(self.at(dp, odd + 2 * k), self.r3a.at[k, dp], here.peer_z1())
            for k in range(2)
            for dp in range(4)
        ]

    def far(self):
        here = self.here
        far = (here.z + 2) % Z_CHIPS
        for wait in self.waits:
            wait()
        self.waits = []
        for dp in range(4):
            self.add(self.at(dp, far), self.r3a.at[far // 2, dp])
            self.waits.append(self.net.send(self.at(dp, far), self.r3b.at[dp], here.peer_z2()))
        for dp in range(4):
            self.add(self.at(dp, here.z), self.r3a.at[here.z // 2, dp])

    def first(self):
        for wait in self.waits:
            wait()
        for dp in range(4):
            self.add(self.at(dp, self.here.z), self.r3b.at[dp])
        super().first()

    def fifth(self):
        here = self.here
        self.wait_a()
        self.wait_b()
        own = self.at(here.dp, here.z)
        for where, extra in zip(self.halves, (self.r2a, self.r2b)):
            part, target = own.at[where], self.f32.at[where]

            def body(rows):
                target[rows, :] = part[rows, :].astype(F32) + extra[rows, :].astype(F32)

            by_rows(part.shape[0], body, 16)
        self.pass_on()


def chunk_list(widths):
    down = widths[3] // 2
    chunks = [(3, 0, down - 128, False), (3, down - 128, 128, True)]
    for index, pieces in ((2, 2), (1, 1), (0, 3)):
        step = widths[index] // 2 // pieces
        chunks += [(index, step * k, step, False) for k in range(pieces)]
    return chunks


def layer_kernel(names, chunks, sizes, *refs):
    v = types.SimpleNamespace(**dict(zip(names, refs)))
    tokens, width, heads, hidden_width = sizes
    quarter = width // 4
    size = width // heads
    factor = size ** (-0.5)
    here = Place()
    core, dp = here.core, here.dp
    net = Net(v.send_sems, v.recv_sems)
    mine, theirs = slice(0, tokens), slice(tokens, 2 * tokens)

    here.greet()
    loads = []
    for number, (source, target) in enumerate(
        (
            (v.cond, v.cond_v), (v.w_token, v.token_v), (v.w_head, v.head_v), (v.w_ada, v.ada_v),
            (v.token_keep, v.keep_v), (v.head_keep, v.head_keep_v), (v.inputs, v.x_v), (v.cotangent, v.g_v),
        )
    ):
        copy = pltpu.make_async_copy(source, target, v.local_sems.at[4 + number])
        copy.start()
        loads.append(copy)
    weights = [
        Weight(net, here, own, full)
        for own, full in ((v.wq, v.fq), (v.wo, v.fo), (v.wu, v.fu), (v.wd, v.fd))
    ]
    for number, weight in enumerate(weights):
        weight.keep(v.local_sems.at[number])
    w_q, w_o, w_u, w_d = weights
    select = (
        lax.broadcasted_iota(jnp.int32, (width, quarter), 0)
        == lax.broadcasted_iota(jnp.int32, (width, quarter), 1) + dp * quarter
    ).astype(F32).astype(BF16)
    loads[0].wait()
    loads[1].wait()
    token = jnp.broadcast_to(v.token_v[...].astype(F32).reshape(1, quarter), (16, quarter))
    placed = dot(token.astype(BF16), select, NT)
    v.small_v[...] = jnp.zeros(v.small_v.shape, F32)
    v.small_v[0:1, :] = v.cond_v[...]
    v.small_v[1:2, :] = placed[0:1]
    here.meet()

    waits = [
        net.send(v.small_v, v.cond_buf.at[dp], peer, v.cond_buf.at[peer[0]])
        for peer in here.dp_peers()
    ]
    w_q.send_diagonal()
    w_q.send_straight()
    v.cond_buf[pl.ds(dp, 1)] = v.small_v[...][None]
    head_of = lax.broadcasted_iota(jnp.int32, (128, width), 0) * size
    lane = lax.broadcasted_iota(jnp.int32, (128, width), 1)
    v.expand[...] = ((lane >= head_of) & (lane < head_of + size)).astype(F32)
    for load in loads[2:6]:
        load.wait()
    diagonal = lax.broadcasted_iota(jnp.int32, (tokens, tokens), 0) == lax.broadcasted_iota(
        jnp.int32, (tokens, tokens), 1
    )
    v.keep[...] = jnp.sum(jnp.where(diagonal, v.keep_v[...].astype(F32), 0.0), axis=1, keepdims=True)
    v.head_mask[...] = jnp.zeros(v.head_mask.shape, F32)
    v.head_mask[:, 0:heads] = v.head_keep_v[...].astype(F32)
    v.part[...] = jnp.zeros(v.part.shape, F32)
    for wait in waits:
        wait()
    stacked = v.cond_buf[...].reshape(32, width).astype(BF16)
    left = dot(stacked, select, NN).astype(BF16)
    for piece in range(7):
        if piece < 6:
            product = dot(left, v.ada_v[:, piece * width : (piece + 1) * width], NN)
        else:
            product = dot(left, v.head_v[...], NT)
        for image in range(4):
            v.part[image, piece : piece + 1, 0 : product.shape[1]] = product[image * 8 : image * 8 + 1]
    waits = [
        net.send(v.part.at[peer[0]], v.part_buf.at[index], peer)
        for index, peer in enumerate(here.dp_peers())
    ]
    for weight in weights[1:]:
        weight.send_diagonal()
    w_q.spread()
    v.token[...] = v.cond_buf[0, 1:2] + v.cond_buf[1, 1:2] + v.cond_buf[2, 1:2] + v.cond_buf[3, 1:2]
    w_q.share_straight()
    for weight in weights[1:]:
        weight.send_straight()
    w_o.spread()
    for wait in waits:
        wait()
    v.mod[...] = v.part[dp] + v.part_buf[0] + v.part_buf[1] + v.part_buf[2]
    head_sigmoid = jax.nn.sigmoid(v.mod[6:7, 0:128])
    head_mask = v.head_mask[...]
    gate = dot(jnp.broadcast_to(head_mask * head_sigmoid, (8, 128)), v.expand[...], NN, exact=True)
    v.gate_row[...] = gate[0:1]

    loads[6].wait()

    def first_norm(rows):
        values = v.x_v[rows, :].astype(F32)
        centre = values - jnp.mean(values, axis=1, keepdims=True)
        spread = jnp.mean(centre * centre, axis=1, keepdims=True)
        normal = centre * lax.rsqrt(spread + epsilon)
        v.nb[rows, :] = (normal * (1.0 + v.mod[1:2]) + v.mod[0:1]).astype(BF16)

    by_rows(tokens, first_norm)
    wait_normed = net.send(v.nb.at[mine], v.nb.at[theirs], here.peer_core())

    w_q.share_diagonal()
    w_u.spread()
    w_q.ready()

    @pl.loop(0, 3 * width // 384)
    def _(index):
        columns = span(index * 384, 384, 128)
        v.packed[:, columns] = dot(v.nb[mine, :], v.fq[:, columns], NN).astype(BF16)

    w_d.spread()

    lanes = lax.broadcasted_iota(jnp.int32, (1, 2 * size), 1)
    masks = ((lanes < size).astype(F32).astype(BF16), (lanes >= size).astype(F32).astype(BF16))
    scaled_masks = tuple(mask * jnp.asarray(factor, BF16) for mask in masks)
    low_lane = lax.broadcasted_iota(jnp.int32, (tokens, 2 * size), 1) < size

    def three(pair, block):
        return [block[:, span(part * width + pair * 2 * size, 2 * size, 128)] for part in range(3)]

    @pl.loop(0, heads // 2)
    def _(pair):
        queries, key_rows, value_rows = three(pair, v.packed)
        found = []
        for which in range(2):
            scores = dot(queries * scaled_masks[which], key_rows, NT)
            powers = jnp.exp(scores - jnp.max(scores, axis=1, keepdims=True))
            probs = powers * (1.0 / jnp.sum(powers, axis=1, keepdims=True))
            v.probs[pair * 2 + which] = probs
            found.append(dot(probs.astype(BF16), value_rows, NN))
        attended = jnp.where(low_lane, found[0], found[1])
        columns = span(pair * 2 * size, 2 * size, 128)
        v.attended[:, columns] = attended
        v.gated[mine, columns] = (attended * v.gate_row[:, columns]).astype(BF16)

    wait_gated = net.send(v.gated.at[mine], v.gated.at[theirs], here.peer_core())
    w_o.share_straight()
    w_o.share_diagonal()
    w_o.ready()

    @pl.loop(0, width // 256)
    def _(index):
        columns = span(index * 256, 256, 128)
        v.branch[:, columns] = dot(v.gated[mine, :], v.fo[:, columns], NN)

    loads[7].wait()

    def second_norm(rows):
        middle = v.x_v[rows, :].astype(F32) + v.mod[2:3] * v.branch[rows, :]
        v.middle[rows, :] = middle
        centre = middle - jnp.mean(middle, axis=1, keepdims=True)
        spread = jnp.mean(centre * centre, axis=1, keepdims=True)
        scale = lax.rsqrt(spread + epsilon)
        normal = centre * scale
        v.z2[rows, :] = normal
        v.scale2[rows, :] = scale
        second = (normal * (1.0 + v.mod[4:5]) + v.mod[3:4]).astype(BF16)
        v.second[rows, :] = second
        logit = jnp.sum(second.astype(F32) * v.token[...], axis=1, keepdims=True)
        router = jax.nn.sigmoid(logit)
        v.router[rows, :] = router
        weight = v.keep[rows, :] * router
        v.grad_prod[rows, :] = (v.g_v[rows, :].astype(F32) * v.mod[5:6] * weight).astype(BF16)

    by_rows(tokens, second_norm)
    wait_second = net.send(v.second.at[mine], v.second.at[theirs], here.peer_core())
    half = width // 2
    other = span((1 - core) * half, half, 128)
    own = span(core * half, half, 128)
    wait_dprod = net.send(v.grad_prod.at[:, other], v.dy_down.at[theirs], here.peer_core())
    v.dy_down[mine, :] = v.grad_prod[:, own]

    w_u.share_diagonal()
    w_u.share_straight()
    w_u.ready()
    inner = math.sqrt(2.0 / math.pi)

    wait_hidden = []
    for index in range(hidden_width // 512):
        columns = slice(index * 512, index * 512 + 512)
        v.tmp[:, 0:512] = dot(v.second[mine, :], v.fu[:, columns], NN)

        def bend(rows):
            u = v.tmp[rows, 0:512]
            square = u * u
            t = jnp.tanh(u * (inner + (inner * 0.044715) * square))
            a = 0.5 + 0.5 * t
            value = u * a
            v.hidden[rows, columns] = value.astype(BF16)
            v.slope[rows, columns] = a + value * (1.0 - a) * (2.0 * inner + (6.0 * inner * 0.044715) * square)

        by_rows(tokens, bend)
        if index % 2:
            done = slice(index * 512 - 512, index * 512 + 512)
            wait_hidden.append(
                net.send(v.hidden.at[mine, done], v.hidden.at[theirs, done], here.peer_core())
            )

    pieces = []
    for number, (index, column, wide, early) in enumerate(chunks):
        total = (v.t_qkv, v.t_out, v.t_up, v.t_down)[index]
        out = (v.o_qkv, v.o_out, v.o_up, v.o_down)[index]
        bufs = [getattr(v, f"c{number}_{k}") for k in range(7)]
        kind = EarlyChunk if early else Chunk
        pieces.append(kind(net, here, total, out, bufs, column, wide))
    c_down, c_early, c_up, c_more, c_out = pieces[:5]
    c_qkv = pieces[5:]

    def weight_grad(total, left, right, step):
        @pl.loop(0, total.shape[0] // step)
        def _(index):
            rows = span(index * step, step, 128)
            total[rows, :] = dot(left[:, rows], right[...], TN).astype(BF16)

    for wait in wait_hidden:
        wait()
    wait_dprod()

    def down_quarter(place):
        @pl.loop(0, 3)
        def _(index):
            rows = span(place * width + index * 256, 256, 256)
            v.t_down[rows, :] = dot(v.hidden[:, rows], v.dy_down[...], TN).astype(BF16)

    down_quarter(here.peer_d()[0])
    c_down.first_diagonal()
    down_quarter(here.peer_x()[0])
    c_down.first_x()
    down_quarter(here.peer_y()[0])
    c_down.first_y()
    down_quarter(dp)
    c_early.near()
    w_d.share_diagonal()
    w_d.share_straight()
    w_d.ready()

    wide_half = hidden_width // 2

    def bend_back(side):
        @pl.loop(0, wide_half // 512)
        def _(index):
            columns = span(side * wide_half + index * 512, 512, 128)
            back = dot(v.grad_prod[...], v.fd[columns, :], NT)
            v.grad_u[:, columns] = (back * v.slope[:, columns]).astype(BF16)

    bend_back(1 - core)
    wait_du = net.send(
        v.grad_u.at[:, span((1 - core) * wide_half, wide_half, 128)], v.dy_up.at[theirs], here.peer_core()
    )
    bend_back(core)
    v.dy_up[mine, :] = v.grad_u[:, span(core * wide_half, wide_half, 128)]
    wait_second()
    wait_du()
    weight_grad(v.t_up, v.second, v.dy_up, 256)
    c_down.second()
    c_up.first()
    c_more.first()

    @pl.loop(0, width // 256)
    def _(index):
        columns = span(index * 256, 256, 128)
        v.produced[:, columns] = dot(v.hidden[mine, :], v.fd[:, columns], NN).astype(BF16)

    v.sums[...] = jnp.zeros(v.sums.shape, F32)

    def finish(rows):
        produced = v.produced[rows, :].astype(F32)
        grad = v.g_v[rows, :].astype(F32)
        router, keep = v.router[rows, :], v.keep[rows, :]
        scaled = produced * (keep * router)
        v.output_v[rows, :] = (v.middle[rows, :] + v.mod[5:6] * scaled).astype(BF16)
        v.sums[0] += fold(grad * scaled)
        back = jnp.sum(grad * v.mod[5:6] * produced, axis=1, keepdims=True)
        v.logit[rows, :] = back * keep * router * (1.0 - router)

    by_rows(tokens, finish)
    out_copy = [pltpu.make_async_copy(v.output_v, v.output, v.local_sems.at[12])]
    out_copy[0].start()
    c_early.far()

    @pl.loop(0, width // 256)
    def _(index):
        columns = span(index * 256, 256, 128)
        v.produced[:, columns] = dot(v.grad_u[...], v.fu[columns, :], NT).astype(BF16)

    def second_back(rows):
        logit = v.logit[rows, :]
        back = v.produced[rows, :].astype(F32) + logit * v.token[...]
        normal = v.z2[rows, :]
        v.sums[1] += fold(logit * v.second[rows, :].astype(F32))
        v.sums[2] += fold(back * normal)
        v.sums[3] += fold(back)
        inside = back * (1.0 + v.mod[4:5])
        level = jnp.mean(inside, axis=1, keepdims=True)
        slope = jnp.mean(inside * normal, axis=1, keepdims=True)
        grad = v.g_v[rows, :].astype(F32) + v.scale2[rows, :] * (inside - level - normal * slope)
        v.grad_mid[rows, :] = grad
        v.sums[4] += fold(grad * v.branch[rows, :])
        v.grad_branch[rows, :] = (v.mod[2:3] * grad).astype(BF16)

    by_rows(tokens, second_back)
    wait_dbranch = net.send(v.grad_branch.at[:, other], v.dy_out.at[theirs], here.peer_core())
    v.dy_out[mine, :] = v.grad_branch[:, own]

    @pl.loop(0, width // 256)
    def _(index):
        columns = span(index * 256, 256, 128)
        v.tmp[:, columns] = dot(v.grad_branch[...], v.fo[columns, :], NT)

    wait_gated()
    wait_dbranch()
    weight_grad(v.t_out, v.gated, v.dy_out, 256)
    c_out.first()

    def gate_back(rows):
        grad = v.tmp[rows, :]
        v.sums[5] += fold(grad * v.attended[rows, :])
        v.grad_att[rows, :] = (grad * v.gate_row[...]).astype(BF16)

    by_rows(tokens, gate_back)

    def gather_start(piece, block):
        block[pl.ds(core, 1), pl.ds(here.z, 1), pl.ds(dp, 1)] = piece[...][None, None, None]
        return [
            net.send(piece, block.at[core, here.z, dp], peer, block.at[core, here.z, peer[0]])
            for peer in here.dp_peers()
        ]

    def gather_far(block, waits):
        for wait in waits:
            wait()
        far = (here.z + 2) % Z_CHIPS
        return [
            net.send(block.at[core, here.z], block.at[core, here.z], here.peer_z2(), block.at[core, far])
        ]

    def gather_near(block, waits):
        for wait in waits:
            wait()
        near = here.z + 1 - 2 * (here.z % 2)
        moves = []
        for k in range(2):
            z, other = (here.z + 2 * k) % Z_CHIPS, (near + 2 * k) % Z_CHIPS
            moves.append(
                net.send(block.at[core, z], block.at[core, z], here.peer_z1(), block.at[core, other])
            )
        return moves

    def gather_pair(block, waits):
        for wait in waits:
            wait()
        return net.send(block.at[core], block.at[core], here.peer_core(), block.at[1 - core])

    head_back = dot(
        jnp.broadcast_to(jnp.sum(v.sums[5], axis=0, keepdims=True), (8, width)), v.expand[...], NT, exact=True
    )
    head_back = head_back[0:1] * head_mask * head_sigmoid * (1.0 - head_sigmoid)
    v.early_f[...] = jnp.zeros(v.early_f.shape, F32)
    rows_out = [jnp.sum(v.sums[k], axis=0, keepdims=True) for k in (4, 3, 2, 0, 1)]
    cut = width // 2
    for slot, values in zip((0, 1, 2, 3, 5, 6), (*rows_out, v.small_v[0:1, :])):
        v.early_f[2 * slot : 2 * slot + 1, :] = values[:, 0:cut]
        v.early_f[2 * slot + 1 : 2 * slot + 2, :] = values[:, cut:width]
    v.early_f[8:9, 0:128] = head_back
    v.early_out[...] = v.early_f[...].astype(BF16)
    early = gather_start(v.early_out, v.early)
    c_down.third()
    c_up.second()

    def back_pair(pair):
        queries, key_rows, value_rows = three(pair, v.packed)
        columns = span(pair * 2 * size, 2 * size, 128)
        grad_att = v.grad_att[:, columns]
        gq, gk, gv = [], [], []
        for which in range(2):
            probs = v.probs[pair * 2 + which]
            grad_probs = dot(grad_att * masks[which], value_rows, NT)
            level = jnp.sum(probs * grad_probs, axis=1, keepdims=True)
            grad_scores = (probs * (grad_probs - level)).astype(BF16)
            gq.append(dot(grad_scores, key_rows, NN))
            gk.append(dot(grad_scores, queries, TN))
            gv.append(dot(probs.astype(BF16), grad_att, TN))
        for part, (grads, scale) in enumerate(((gq, factor), (gk, factor), (gv, 1.0))):
            both = jnp.where(low_lane, grads[0], grads[1]) * scale
            v.grad_pack[:, span(part * width + pair * 2 * size, 2 * size, 128)] = both.astype(BF16)

    pl.loop(0, heads // 2)(back_pair)
    packed_half = 3 * width // 2
    wait_dpack = net.send(
        v.grad_pack.at[:, span((1 - core) * packed_half, packed_half, 128)],
        v.dy_qkv.at[theirs],
        here.peer_core(),
    )
    v.dy_qkv[mine, :] = v.grad_pack[:, span(core * packed_half, packed_half, 128)]
    c_early.first()
    c_more.second()
    wait_normed()
    wait_dpack()
    weight_grad(v.t_qkv, v.nb, v.dy_qkv, 256)
    c_qkv[0].first()
    c_qkv[1].first()
    c_down.fourth()
    early = gather_far(v.early, early)


    @pl.loop(0, width // 256)
    def _(index):
        columns = span(index * 256, 256, 128)
        v.tmp[:, columns] = dot(v.grad_pack[...], v.fq[columns, :], NT)

    def first_back(rows):
        back = v.tmp[rows, :]
        values = v.x_v[rows, :].astype(F32)
        centre = values - jnp.mean(values, axis=1, keepdims=True)
        spread = jnp.mean(centre * centre, axis=1, keepdims=True)
        scale = lax.rsqrt(spread + epsilon)
        normal = centre * scale
        v.sums[6] += fold(back * normal)
        v.sums[7] += fold(back)
        inside = back * (1.0 + v.mod[1:2])
        level = jnp.mean(inside, axis=1, keepdims=True)
        slope = jnp.mean(inside * normal, axis=1, keepdims=True)
        v.grad_input_v[rows, :] = v.grad_mid[rows, :] + scale * (inside - level - normal * slope)

    by_rows(tokens, first_back)
    shift = jnp.sum(v.sums[7], axis=0, keepdims=True)
    scale = jnp.sum(v.sums[6], axis=0, keepdims=True)
    v.late_f[...] = jnp.zeros(v.late_f.shape, F32)
    for k in range(width // 128):
        v.late_f[k : k + 1, :] = shift[:, k * 128 : (k + 1) * 128]
        v.late_f[8 + k : 9 + k, :] = scale[:, k * 128 : (k + 1) * 128]
    v.late_out[...] = v.late_f[...].astype(BF16)
    late = gather_start(v.late_out, v.late)
    c_qkv[2].first()
    out_copy.append(pltpu.make_async_copy(v.grad_input_v, v.grad_input, v.local_sems.at[13]))
    out_copy[1].start()
    c_up.third()
    c_early.second()
    c_out.second()
    c_more.third()
    early = gather_near(v.early, early)
    c_qkv[0].second()
    c_up.fourth()
    c_qkv[1].second()
    c_more.fourth()
    late = gather_far(v.late, late)
    c_qkv[2].second()
    c_out.third()
    c_down.fifth()
    early = gather_pair(v.early, early)
    c_early.fifth()
    c_qkv[0].third()
    c_up.fifth()
    c_qkv[1].third()
    c_out.fourth()
    late = gather_near(v.late, late)
    c_qkv[2].third()
    c_more.fifth()
    c_qkv[0].fourth()
    c_qkv[1].fourth()
    late = gather_pair(v.late, late)

    early()
    offset = dp * quarter + (here.seq % BLOCK) * SHARE
    pick = (
        lax.broadcasted_iota(jnp.int32, (width, SHARE), 0)
        == lax.broadcasted_iota(jnp.int32, (width, SHARE), 1) + offset
    ).astype(F32)
    every = v.early[...].reshape(512, cut).astype(F32).reshape(32, 16, cut)
    conditions = (
        dot(every[:, 12, :].astype(BF16), pick[0:cut].astype(BF16), NN)
        + dot(every[:, 13, :].astype(BF16), pick[cut:width].astype(BF16), NN)
    ).astype(BF16)
    for slot, piece in enumerate((2, 3, 4, 5)):
        for side in range(2):
            start = piece * width + side * cut
            v.o_ada[:, start : start + cut] = dot(
                conditions, every[:, 2 * slot + side, :].astype(BF16), TN
            )
    v.o_head[...] = dot(every[:, 8, 0:128].astype(BF16), conditions, TN)[0:heads]
    totals = [jnp.sum(every[:, 10 + side, :], axis=0, keepdims=True) for side in range(2)]
    v.o_token[...] = (
        dot(jnp.broadcast_to(totals[0], (8, cut)), pick[0:cut], NN, exact=True)
        + dot(jnp.broadcast_to(totals[1], (8, cut)), pick[cut:width], NN, exact=True)
    )[0:1]

    def emit(number, source, target):
        copy = pltpu.make_async_copy(source, target, v.local_sems.at[14 + number])
        copy.start()
        out_copy.append(copy)

    c_qkv[2].fourth()
    c_out.fifth()
    c_qkv[0].fifth()
    c_qkv[1].fifth()
    for chunk in (c_down, c_early, c_up, c_more):
        chunk.end()
    for number, name in enumerate(("head", "token", "up", "down")):
        emit(number, getattr(v, "o_" + name), getattr(v, "out_" + name))
    late()
    tail = v.late[...].reshape(512, 128).astype(F32).reshape(32, 16, 128)
    for base in (0, 8):
        row = jnp.concatenate([tail[:, base + k, :] for k in range(width // 128)], axis=1)
        start = base // 8 * width
        v.o_ada[:, start : start + width] = dot(conditions, row.astype(BF16), TN)
    emit(4, v.o_ada, v.out_ada)
    c_qkv[2].fifth()
    for chunk in (c_out, *c_qkv):
        chunk.end()
    emit(5, v.o_out, v.out_out)
    emit(6, v.o_qkv, v.out_qkv)
    for copy in out_copy:
        copy.wait()
    net.finish()


def layer(cond, w_token, w_head, token_keep, head_keep, inputs, cotangent, w_ada, wq, wo, wu, wd):
    tokens, width = inputs.shape
    hidden_width = wu.shape[1]
    heads = head_keep.shape[1]
    widths = [wq.shape[1], wo.shape[1], wu.shape[1], wd.shape[1]]
    depths = [4 * w.shape[0] for w in (wq, wo, wu, wd)]
    chunks = chunk_list(widths)
    operands = dict(
        cond=cond, w_token=w_token, w_head=w_head, token_keep=token_keep, head_keep=head_keep,
        inputs=inputs, cotangent=cotangent, w_ada=w_ada, wq=wq, wo=wo, wu=wu, wd=wd,
    )
    outs = dict(
        ada=((SHARE, 6 * width), F32),
        qkv=((depths[0] // 32, widths[0]), F32),
        out=((depths[1] // 32, widths[1]), F32),
        up=((depths[2] // 32, widths[2]), F32),
        down=((depths[3] // 32, widths[3]), F32),
        head=((heads, SHARE), F32),
        token=((1, SHARE), F32),
    )
    results = dict(output=((tokens, width), BF16), grad_input=((tokens, width), F32))
    results.update({"out_" + k: s for k, s in outs.items()})
    space = dict(
        cond_v=(cond.shape, F32),
        small_v=((8, width), F32),
        token_v=(w_token.shape, BF16),
        keep_v=(token_keep.shape, jnp.int32),
        head_keep_v=(head_keep.shape, jnp.int32),
        head_mask=((1, 128), F32),
        output_v=((tokens, width), BF16),
        grad_input_v=((tokens, width), F32),
        head_v=(w_head.shape, BF16),
        ada_v=(w_ada.shape, BF16),
        x_v=((tokens, width), BF16),
        g_v=((tokens, width), BF16),
        fq=((depths[0], widths[0]), BF16),
        fo=((depths[1], widths[1]), BF16),
        fu=((depths[2], widths[2]), BF16),
        fd=((depths[3], widths[3]), BF16),
        cond_buf=((4, 8, width), F32),
        part=((4, 8, width), F32),
        part_buf=((3, 8, width), F32),
        mod=((8, width), F32),
        token=((1, width), F32),
        keep=((tokens, 1), F32),
        expand=((128, width), F32),
        gate_row=((1, width), F32),
        nb=((2 * tokens, width), BF16),
        packed=((tokens, 3 * width), BF16),
        probs=((heads, tokens, tokens), F32),
        attended=((tokens, width), F32),
        gated=((2 * tokens, width), BF16),
        branch=((tokens, width), F32),
        middle=((tokens, width), F32),
        z2=((tokens, width), F32),
        scale2=((tokens, 1), F32),
        second=((2 * tokens, width), BF16),
        router=((tokens, 1), F32),
        logit=((tokens, 1), F32),
        grad_prod=((tokens, width), BF16),
        dy_down=((2 * tokens, width // 2), BF16),
        tmp=((tokens, width), F32),
        hidden=((2 * tokens, hidden_width), BF16),
        slope=((tokens, hidden_width), F32),
        grad_u=((tokens, hidden_width), BF16),
        dy_up=((2 * tokens, hidden_width // 2), BF16),
        produced=((tokens, width), BF16),
        grad_mid=((tokens, width), F32),
        grad_branch=((tokens, width), BF16),
        dy_out=((2 * tokens, width // 2), BF16),
        grad_att=((tokens, width), BF16),
        grad_pack=((tokens, 3 * width), BF16),
        dy_qkv=((2 * tokens, 3 * width // 2), BF16),
        sums=((8, 8, width), F32),
        early_f=((16, width // 2), F32),
        early_out=((16, width // 2), BF16),
        early=((2, Z_CHIPS, 4, 16, width // 2), BF16),
        late_f=((16, 128), F32),
        late_out=((16, 128), BF16),
        late=((2, Z_CHIPS, 4, 16, 128), BF16),
        t_qkv=((depths[0], widths[0] // 2), BF16),
        t_out=((depths[1], widths[1] // 2), BF16),
        t_up=((depths[2], widths[2] // 2), BF16),
        t_down=((depths[3], widths[3] // 2), BF16),
    )
    space.update({"o_" + k: s for k, s in outs.items()})
    for number, (index, _, wide, early) in enumerate(chunks):
        rows = depths[index] // 16
        part, span_of = 2 * rows, wide
        if early and wide == 128:
            part = rows // 2
        elif early:
            part, span_of = rows, wide // 2
        shapes = ((2, part, span_of), (2, part, span_of), (part, span_of), (part, span_of))
        shapes += ((2, 4, rows, wide), (4, rows, wide)) if early else ((2, rows, wide), (rows, wide))
        for k, shape in enumerate(shapes):
            space[f"c{number}_{k}"] = (shape, BF16)
        space[f"c{number}_6"] = ((rows, wide), F32)
    copies = 6 + 4 * 9 + 12 + len(chunks) * 12 + 2 * 12 + 14
    names = list(operands) + list(results) + list(space) + ["send_sems", "recv_sems", "local_sems"]
    return pl.pallas_call(
        functools.partial(layer_kernel, names, chunks, (tokens, width, heads, hidden_width)),
        out_shape=[jax.ShapeDtypeStruct(*r) for r in results.values()],
        in_specs=[ANY] * len(operands),
        out_specs=[ANY] * len(results),
        scratch_shapes=[pltpu.VMEM(*s) for s in space.values()]
        + [
            pltpu.SemaphoreType.DMA((copies,)),
            pltpu.SemaphoreType.DMA((copies,)),
            pltpu.SemaphoreType.DMA((21,)),
        ],
        compiler_params=pltpu.CompilerParams(
            collective_id=0, has_side_effects=True, vmem_limit_bytes=64 * 2**20 - 2**16
        ),
    )(*operands.values())


def copy_kernel(count, *refs):
    ins, outs, space = refs[:count], refs[count : 2 * count], refs[2 * count : 3 * count]
    sems = refs[3 * count]
    loads = [pltpu.make_async_copy(ins[k], space[k], sems.at[k]) for k in range(count)]
    stores = [pltpu.make_async_copy(space[k], outs[k], sems.at[count + k]) for k in range(count)]
    for load in loads:
        load.start()
    for load, store in zip(loads, stores):
        load.wait()
        store.start()
    for store in stores:
        store.wait()


def copy_all(arrays):
    count = len(arrays)
    return pl.pallas_call(
        functools.partial(copy_kernel, count),
        out_shape=[jax.ShapeDtypeStruct(a.shape, a.dtype) for a in arrays],
        in_specs=[ANY] * count,
        out_specs=[ANY] * count,
        scratch_shapes=[pltpu.VMEM(a.shape, a.dtype) for a in arrays]
        + [pltpu.SemaphoreType.DMA((2 * count,))],
        compiler_params=pltpu.CompilerParams(vmem_limit_bytes=64 * 2**20 - 2**16),
    )(*arrays)


def across_blocks(part, seq_size):
    blocks = seq_size // BLOCK
    if blocks == 1:
        return part
    groups = [[b * BLOCK + j for b in range(blocks)] for j in range(BLOCK)]
    mine = lax.psum_scatter(
        part, "seq", scatter_dimension=0, axis_index_groups=groups, tiled=True
    )
    moves = [(b * BLOCK + j, j * blocks + b) for b in range(blocks) for j in range(BLOCK)]
    return lax.ppermute(mine, "seq", moves)


def per_device(
    seq_size, inputs, time_table, time_index, token_keep, head_keep, cotangent,
    w_ada, w_qkv, w_out, w_up, w_down, w_head, w_token,
):
    width = inputs.shape[2]
    row = lax.dynamic_slice(time_table, (time_index[0], 0), (1, width)).astype(F32)
    condition = jax.nn.silu(row).astype(BF16).astype(F32)
    out = layer(
        condition, w_token, w_head.T, token_keep, head_keep,
        inputs[0], cotangent[0], w_ada, w_qkv, w_out, w_up, w_down,
    )
    output, grad_input, ada, qkv, outw, up, down, head, token = copy_all(out)
    parts = (ada, qkv, outw, up, down, head.T, token[0])
    parts = tuple(across_blocks(part, seq_size) for part in parts)
    return (output[None], grad_input[None]) + parts


def solution(mesh):
    both = ("dp", "seq")
    in_specs = (
        P(both, None, None), P(), P(both), P(both, None), P(both, None), P(both, None, None),
        P("dp", None), P("dp", None), P("dp", None), P("dp", None), P("dp", None), P("dp", None), P("dp"),
    )
    out_specs = (P(both, None, None), P(both, None, None)) + (P(both, None),) * 6 + (P(both),)
    return jax.shard_map(
        functools.partial(per_device, mesh.shape["seq"]),
        mesh=mesh, in_specs=in_specs, out_specs=out_specs, check_vma=False,
    )
```

```python
import functools
import math
import types

import jax
import jax.numpy as jnp
from jax import lax
from jax.experimental import pallas as pl
from jax.experimental.pallas import tpu as pltpu
from jax.sharding import PartitionSpec as P

epsilon = 1e-06
MESH = pl.DeviceIdType.MESH
ANY = pl.BlockSpec(memory_space=pl.ANY)
VMEM = pl.BlockSpec(memory_space=pltpu.VMEM)
Z_CHIPS = 4
BLOCK = 2 * Z_CHIPS
F32, BF16 = jnp.float32, jnp.bfloat16
NN, NT, TN = ((1,), (0,)), ((1,), (1,)), ((0,), (0,))
ROWS = 32
SHARE = 24


def dot(left, right, dims, exact=False):
    return lax.dot_general(
        left, right, (dims, ((), ())), preferred_element_type=F32,
        precision=lax.Precision.HIGHEST if exact else None,
    )


def span(start, size, unit):
    return pl.ds(pl.multiple_of(start, unit), size)


def by_rows(total, body, step=ROWS):
    @pl.loop(0, total // step)
    def _(index):
        body(span(index * step, step, step))


def fold(values):
    return jnp.sum(values.reshape(-1, 8, values.shape[-1]), axis=0)


class Place:
    def __init__(self):
        self.dp = lax.axis_index("dp")
        self.seq = lax.axis_index("seq")
        self.x = self.dp % 2
        self.y = self.dp // 2
        self.core = self.seq % 2
        self.z = (self.seq // 2) % Z_CHIPS
        self.outer = self.seq // BLOCK

    def z_of(self, step):
        return (self.z + step) % Z_CHIPS

    def peer_x(self):
        return (self.y * 2 + 1 - self.x, self.seq)

    def peer_y(self):
        return ((1 - self.y) * 2 + self.x, self.seq)

    def peer_d(self):
        return ((1 - self.y) * 2 + 1 - self.x, self.seq)

    def peer_core(self):
        return (self.dp, self.seq + 1 - 2 * self.core)

    def peer_z(self, step):
        return (self.dp, self.outer * BLOCK + self.z_of(step) * 2 + self.core)

    def peer_z1(self):
        return (self.dp, self.seq + 2 - 4 * (self.z % 2))

    def peer_z2(self):
        return (self.dp, self.seq + 4 - 8 * (self.z // 2))

    def dp_peers(self):
        return (self.peer_x(), self.peer_y(), self.peer_d())

    def greet(self):
        peers = list(self.dp_peers()) + [self.peer_core()]
        peers += [self.peer_z(k) for k in range(1, Z_CHIPS)]
        for peer in peers:
            pl.semaphore_signal(
                pltpu.get_barrier_semaphore(), inc=1, device_id=peer, device_id_type=MESH
            )
        self.peers = len(peers)

    def meet(self):
        pl.semaphore_wait(pltpu.get_barrier_semaphore(), self.peers)


class Net:
    def __init__(self, send_sems, recv_sems):
        self.send_sems = send_sems
        self.recv_sems = recv_sems
        self.used = 0
        self.sent = []

    def send(self, src, dst, peer, landing=None):
        slot = self.used
        self.used += 1

        def copy_to(target):
            return pltpu.make_async_remote_copy(
                src_ref=src,
                dst_ref=target,
                send_sem=self.send_sems.at[slot],
                recv_sem=self.recv_sems.at[slot],
                device_id=peer,
                device_id_type=MESH,
            )

        copy = copy_to(dst)
        copy.start()
        self.sent.append(copy)
        arrival = copy if landing is None else copy_to(landing)
        return arrival.wait_recv

    def finish(self):
        for copy in self.sent:
            copy.wait_send()


class Weight:
    def __init__(self, net, here, own, full):
        self.net, self.here, self.own, self.full = net, here, own, full
        self.depth = own.shape[0]
        self.piece = self.depth // Z_CHIPS
        self.width = own.shape[1] // 2

    def columns(self, core):
        return span(core * self.width, self.width, 128)

    def quarter(self, dp):
        return span(dp * self.depth, self.depth, 16)

    def part(self, dp, z):
        return span(dp * self.depth + z * self.piece, self.piece, 16)

    def keep(self, sem):
        self.local = pltpu.make_async_copy(self.own, self.full.at[self.quarter(self.here.dp)], sem)
        self.local.start()

    def send_diagonal(self):
        here, columns = self.here, self.columns(self.here.core)
        peer = here.peer_d()
        self.wait_d = self.net.send(
            self.own.at[span(here.z * self.piece, self.piece, 16), columns],
            self.full.at[self.part(here.dp, here.z), columns],
            peer,
            self.full.at[self.part(peer[0], here.z), columns],
        )

    def rows(self, dp, side):
        half = self.depth // 2
        return span(dp * self.depth + side * half, half, 16)

    def send_straight(self):
        here, columns = self.here, self.columns(self.here.core)
        self.wait_xy = [
            [
                self.net.send(
                    self.own.at[self.rows(0, side), columns],
                    self.full.at[self.rows(here.dp, side), columns],
                    peer,
                    self.full.at[self.rows(peer[0], side), columns],
                )
                for peer in (here.peer_x(), here.peer_y())
            ]
            for side in range(2)
        ]
        self.last = []

    def spread(self):
        here, columns = self.here, self.columns(self.here.core)
        diagonal = here.peer_d()[0]
        self.wait_d()
        piece = self.full.at[self.part(diagonal, here.z), columns]
        self.wait_z = [
            self.net.send(
                piece, piece, here.peer_z(step),
                self.full.at[self.part(diagonal, here.z_of(Z_CHIPS - step)), columns],
            )
            for step in range(1, Z_CHIPS)
        ]

    def hand(self, rows):
        here = self.here
        block = self.full.at[rows, self.columns(here.core)]
        landing = self.full.at[rows, self.columns(1 - here.core)]
        self.last.append(self.net.send(block, block, here.peer_core(), landing))

    def share_straight(self, side):
        here = self.here
        for wait, peer in zip(self.wait_xy[side], (here.peer_x(), here.peer_y())):
            wait()
            self.hand(self.rows(peer[0], side))

    def share_diagonal(self):
        for wait in self.wait_z:
            wait()
        self.hand(self.quarter(self.here.peer_d()[0]))

    def ready(self):
        for wait in self.last:
            wait()
        self.local.wait()


class Chunk:
    @staticmethod
    def shapes(rows, wide):
        return ((2, 2 * rows, wide),) * 2 + ((2 * rows, wide),) * 2 + ((2, rows, wide), (rows, wide))

    def __init__(self, net, here, total, out, bufs, column, width):
        self.net, self.here, self.out = net, here, out
        self.total = total.at[:, span(column, width, 128)]
        self.block = total.shape[0] // 16
        self.column, self.width = column, width
        self.r1a, self.r1b, self.r2a, self.r2b, self.r3a, self.r3b, self.f32 = bufs

    def columns(self, core):
        return span(core * (self.out.shape[1] // 2) + self.column, self.width, 128)

    def upper(self, dp):
        return self.total.at[span(dp * 4 * self.block, 2 * self.block, 16)]

    def lower(self, dp):
        return self.total.at[span(dp * 4 * self.block + 2 * self.block, 2 * self.block, 16)]

    def add(self, total, extra):
        def body(rows):
            total[rows, :] = (total[rows, :].astype(F32) + extra[rows, :].astype(F32)).astype(BF16)

        by_rows(total.shape[0], body, 16)

    def first_diagonal(self):
        here, dp = self.here, self.here.peer_d()[0]
        self.wait_a = [self.net.send(self.upper(dp), self.r1a.at[1 - here.y], here.peer_x())]
        self.wait_b = [self.net.send(self.lower(dp), self.r1b.at[1 - here.x], here.peer_y())]

    def first_x(self):
        here, peer = self.here, self.here.peer_x()
        self.wait_a.append(self.net.send(self.upper(peer[0]), self.r1a.at[here.y], peer))

    def first_y(self):
        here, peer = self.here, self.here.peer_y()
        self.wait_b.append(self.net.send(self.lower(peer[0]), self.r1b.at[here.x], peer))

    def first(self):
        self.first_diagonal()
        self.first_x()
        self.first_y()

    def second(self):
        here = self.here
        for wait in self.wait_a:
            wait()
        away = self.upper((1 - here.y) * 2 + here.x)
        self.add(away, self.r1a.at[1 - here.y])
        next_a = self.net.send(away, self.r2a, here.peer_y())
        for wait in self.wait_b:
            wait()
        away = self.lower(here.y * 2 + 1 - here.x)
        self.add(away, self.r1b.at[1 - here.x])
        next_b = self.net.send(away, self.r2b, here.peer_x())
        self.add(self.upper(here.dp), self.r1a.at[here.y])
        self.add(self.lower(here.dp), self.r1b.at[here.x])
        self.wait_a, self.wait_b = next_a, next_b

    def mine(self, z):
        return self.total.at[span((self.here.dp * 4 + z) * self.block, self.block, 16)]

    def third(self):
        here = self.here
        self.wait_a()
        self.add(self.upper(here.dp), self.r2a)
        self.wait_b()
        self.add(self.lower(here.dp), self.r2b)
        odd = 1 - here.z % 2
        self.waits = [
            self.net.send(self.mine(odd + 2 * k), self.r3a.at[k], here.peer_z1()) for k in range(2)
        ]

    def fourth(self):
        here = self.here
        far = (here.z + 2) % Z_CHIPS
        for wait in self.waits:
            wait()
        self.add(self.mine(far), self.r3a.at[far // 2])
        self.wait = self.net.send(self.mine(far), self.r3b, here.peer_z2())
        self.add(self.mine(here.z), self.r3a.at[here.z // 2])

    def fifth(self):
        here = self.here
        self.wait()
        own = self.mine(here.z)

        def body(rows):
            self.f32[rows, :] = own[rows, :].astype(F32) + self.r3b[rows, :].astype(F32)

        by_rows(self.block, body, 16)
        self.pass_on()

    def pass_on(self):
        here = self.here
        part = self.block // 2
        self.wait = self.net.send(
            self.f32.at[span((1 - here.core) * part, part, 8)],
            self.out.at[:, self.columns(here.core)],
            here.peer_core(),
            self.out.at[:, self.columns(1 - here.core)],
        )
        self.out[:, self.columns(here.core)] = self.f32[span(here.core * part, part, 8), :]

    def end(self):
        self.wait()


class LastChunk(Chunk):
    @staticmethod
    def shapes(rows, wide):
        return ((2, 2 * rows, wide),) * 2 + ((2 * rows, wide),) * 2 + ((3, rows, wide), (16, 128))

    def third(self):
        here = self.here
        self.wait_a()
        self.add(self.upper(here.dp), self.r2a)
        self.wait_b()
        self.add(self.lower(here.dp), self.r2b)
        self.waits = [
            self.net.send(self.mine(here.z_of(k)), self.r3a.at[k - 1], here.peer_z(k))
            for k in range(1, Z_CHIPS)
        ]

    def fifth(self):
        for wait in self.waits:
            wait()
        own = self.mine(self.here.z)

        def body(rows):
            total = own[rows, :].astype(F32)
            for k in range(Z_CHIPS - 1):
                total += self.r3a[k, rows, :].astype(F32)
            self.f32[rows, :] = total

        by_rows(self.block, body, 16)
        self.pass_on()


class EarlyChunk(Chunk):
    @staticmethod
    def shapes(rows, wide):
        part = rows // 2
        return ((2, part, wide),) * 2 + ((part, wide),) * 2 + ((2, 4, rows, wide), (4, rows, wide))

    def __init__(self, net, here, total, out, bufs, column, width):
        super().__init__(net, here, total, out, bufs, column, width)
        half = self.block // 2
        self.halves = tuple((span(k * half, half, 16), slice(None)) for k in range(2))

    def at(self, dp, z):
        return self.total.at[span((dp * 4 + z) * self.block, self.block, 16)]

    def upper(self, dp):
        return self.at(dp, self.here.z).at[self.halves[0]]

    def lower(self, dp):
        return self.at(dp, self.here.z).at[self.halves[1]]

    def near(self):
        here = self.here
        odd = 1 - here.z % 2
        self.waits = [
            self.net.send(self.at(dp, odd + 2 * k), self.r3a.at[k, dp], here.peer_z1())
            for k in range(2)
            for dp in range(4)
        ]

    def far(self):
        here = self.here
        far = (here.z + 2) % Z_CHIPS
        for wait in self.waits:
            wait()
        self.waits = []
        for dp in range(4):
            self.add(self.at(dp, far), self.r3a.at[far // 2, dp])
            self.waits.append(self.net.send(self.at(dp, far), self.r3b.at[dp], here.peer_z2()))
        for dp in range(4):
            self.add(self.at(dp, here.z), self.r3a.at[here.z // 2, dp])

    def first(self):
        for wait in self.waits:
            wait()
        for dp in range(4):
            self.add(self.at(dp, self.here.z), self.r3b.at[dp])
        super().first()

    def fifth(self):
        here = self.here
        self.wait_a()
        self.wait_b()
        own = self.at(here.dp, here.z)
        for where, extra in zip(self.halves, (self.r2a, self.r2b)):
            part, target = own.at[where], self.f32.at[where]

            def body(rows):
                target[rows, :] = part[rows, :].astype(F32) + extra[rows, :].astype(F32)

            by_rows(part.shape[0], body, 16)
        self.pass_on()


def chunk_list(widths):
    cuts = (
        (3, (128, 128, 128), (Chunk, Chunk, EarlyChunk)),
        (2, (768, 768), (Chunk, Chunk)),
        (1, (384,), (Chunk,)),
        (0, (384, 384, 384), (LastChunk, LastChunk, LastChunk)),
    )
    chunks = []
    for index, parts, kinds in cuts:
        column = 0
        for part, kind in zip(parts, kinds):
            chunks.append((index, column, part, kind))
            column += part
        assert 2 * column == widths[index]
    return chunks


def layer_kernel(names, chunks, sizes, *refs):
    v = types.SimpleNamespace(**dict(zip(names, refs)))
    tokens, width, heads, hidden_width = sizes
    quarter = width // 4
    size = width // heads
    factor = size ** (-0.5)
    here = Place()
    core, dp = here.core, here.dp
    net = Net(v.send_sems, v.recv_sems)
    mine, theirs = slice(0, tokens), slice(tokens, 2 * tokens)

    here.greet()
    loads = []
    for number, (source, target) in enumerate(
        (
            (v.cond, v.cond_v), (v.w_token, v.token_v), (v.w_head, v.head_v), (v.w_ada, v.ada_v),
            (v.token_keep, v.keep_v), (v.head_keep, v.head_keep_v), (v.inputs, v.x_v), (v.cotangent, v.g_v),
        )
    ):
        copy = pltpu.make_async_copy(source, target, v.local_sems.at[4 + number])
        copy.start()
        loads.append(copy)
    weights = [
        Weight(net, here, own, full)
        for own, full in ((v.wq, v.fq), (v.wo, v.fo), (v.wu, v.fu), (v.wd, v.fd))
    ]
    for number, weight in enumerate(weights):
        weight.keep(v.local_sems.at[number])
    w_q, w_o, w_u, w_d = weights
    select = (
        lax.broadcasted_iota(jnp.int32, (width, quarter), 0)
        == lax.broadcasted_iota(jnp.int32, (width, quarter), 1) + dp * quarter
    ).astype(F32).astype(BF16)
    loads[0].wait()
    loads[1].wait()
    token = jnp.broadcast_to(v.token_v[...].astype(F32).reshape(1, quarter), (16, quarter))
    placed = dot(token.astype(BF16), select, NT)
    v.small_v[...] = jnp.zeros(v.small_v.shape, F32)
    v.small_v[0:1, :] = v.cond_v[...]
    v.small_v[1:2, :] = placed[0:1]
    here.meet()

    waits = [
        net.send(v.small_v, v.cond_buf.at[dp], peer, v.cond_buf.at[peer[0]])
        for peer in here.dp_peers()
    ]
    w_q.send_diagonal()
    w_q.send_straight()
    v.cond_buf[pl.ds(dp, 1)] = v.small_v[...][None]
    head_of = lax.broadcasted_iota(jnp.int32, (128, width), 0) * size
    lane = lax.broadcasted_iota(jnp.int32, (128, width), 1)
    v.expand[...] = ((lane >= head_of) & (lane < head_of + size)).astype(F32)
    for load in loads[2:6]:
        load.wait()
    diagonal = lax.broadcasted_iota(jnp.int32, (tokens, tokens), 0) == lax.broadcasted_iota(
        jnp.int32, (tokens, tokens), 1
    )
    v.keep[...] = jnp.sum(jnp.where(diagonal, v.keep_v[...].astype(F32), 0.0), axis=1, keepdims=True)
    v.head_mask[...] = jnp.zeros(v.head_mask.shape, F32)
    v.head_mask[:, 0:heads] = v.head_keep_v[...].astype(F32)
    v.part[...] = jnp.zeros(v.part.shape, F32)
    for wait in waits:
        wait()
    stacked = v.cond_buf[...].reshape(32, width).astype(BF16)
    left = dot(stacked, select, NN).astype(BF16)
    for piece in range(7):
        if piece < 6:
            product = dot(left, v.ada_v[:, piece * width : (piece + 1) * width], NN)
        else:
            product = dot(left, v.head_v[...], NT)
        for image in range(4):
            v.part[image, piece : piece + 1, 0 : product.shape[1]] = product[image * 8 : image * 8 + 1]
    waits = [
        net.send(v.part.at[peer[0]], v.part_buf.at[index], peer)
        for index, peer in enumerate(here.dp_peers())
    ]
    for weight in weights[1:]:
        weight.send_diagonal()
    w_q.spread()
    v.token[...] = v.cond_buf[0, 1:2] + v.cond_buf[1, 1:2] + v.cond_buf[2, 1:2] + v.cond_buf[3, 1:2]
    w_q.share_straight(0)
    w_q.share_straight(1)
    for weight in weights[1:]:
        weight.send_straight()
    w_o.spread()
    for wait in waits:
        wait()
    v.mod[...] = v.part[dp] + v.part_buf[0] + v.part_buf[1] + v.part_buf[2]
    head_sigmoid = jax.nn.sigmoid(v.mod[6:7, 0:128])
    head_mask = v.head_mask[...]
    gate = dot(jnp.broadcast_to(head_mask * head_sigmoid, (8, 128)), v.expand[...], NN, exact=True)
    v.gate_row[...] = gate[0:1]

    loads[6].wait()

    def first_norm(rows):
        values = v.x_v[rows, :].astype(F32)
        centre = values - jnp.mean(values, axis=1, keepdims=True)
        spread = jnp.mean(centre * centre, axis=1, keepdims=True)
        normal = centre * lax.rsqrt(spread + epsilon)
        v.nb[rows, :] = (normal * (1.0 + v.mod[1:2]) + v.mod[0:1]).astype(BF16)

    by_rows(tokens, first_norm)
    wait_normed = net.send(v.nb.at[mine], v.nb.at[theirs], here.peer_core())

    w_q.share_diagonal()
    w_u.spread()
    w_q.ready()

    @pl.loop(0, 3 * width // 384)
    def _(index):
        columns = span(index * 384, 384, 128)
        v.packed[:, columns] = dot(v.nb[mine, :], v.fq[:, columns], NN).astype(BF16)

    w_d.spread()

    lanes = lax.broadcasted_iota(jnp.int32, (1, 2 * size), 1)
    masks = ((lanes < size).astype(F32).astype(BF16), (lanes >= size).astype(F32).astype(BF16))
    scaled_masks = tuple(mask * jnp.asarray(factor, BF16) for mask in masks)
    low_lane = lax.broadcasted_iota(jnp.int32, (tokens, 2 * size), 1) < size

    def three(pair, block):
        return [block[:, span(part * width + pair * 2 * size, 2 * size, 128)] for part in range(3)]

    @pl.loop(0, heads // 2)
    def _(pair):
        queries, key_rows, value_rows = three(pair, v.packed)
        found = []
        for which in range(2):
            scores = dot(queries * scaled_masks[which], key_rows, NT)
            powers = jnp.exp(scores - jnp.max(scores, axis=1, keepdims=True))
            probs = powers * (1.0 / jnp.sum(powers, axis=1, keepdims=True))
            v.probs[pair * 2 + which] = probs
            found.append(dot(probs.astype(BF16), value_rows, NN))
        attended = jnp.where(low_lane, found[0], found[1])
        columns = span(pair * 2 * size, 2 * size, 128)
        v.attended[:, columns] = attended
        v.gated[mine, columns] = (attended * v.gate_row[:, columns]).astype(BF16)

    wait_gated = net.send(v.gated.at[mine], v.gated.at[theirs], here.peer_core())
    w_o.share_straight(0)
    w_o.share_straight(1)
    w_o.share_diagonal()
    w_o.ready()

    @pl.loop(0, width // 256)
    def _(index):
        columns = span(index * 256, 256, 128)
        v.branch[:, columns] = dot(v.gated[mine, :], v.fo[:, columns], NN)

    loads[7].wait()

    def second_norm(rows):
        middle = v.x_v[rows, :].astype(F32) + v.mod[2:3] * v.branch[rows, :]
        v.middle[rows, :] = middle
        centre = middle - jnp.mean(middle, axis=1, keepdims=True)
        spread = jnp.mean(centre * centre, axis=1, keepdims=True)
        scale = lax.rsqrt(spread + epsilon)
        normal = centre * scale
        v.z2[rows, :] = normal
        v.scale2[rows, :] = scale
        second = (normal * (1.0 + v.mod[4:5]) + v.mod[3:4]).astype(BF16)
        v.second[rows, :] = second
        logit = jnp.sum(second.astype(F32) * v.token[...], axis=1, keepdims=True)
        router = jax.nn.sigmoid(logit)
        v.router[rows, :] = router
        weight = v.keep[rows, :] * router
        v.grad_prod[rows, :] = (v.g_v[rows, :].astype(F32) * v.mod[5:6] * weight).astype(BF16)

    by_rows(tokens, second_norm)
    wait_second = net.send(v.second.at[mine], v.second.at[theirs], here.peer_core())
    half = width // 2
    other = span((1 - core) * half, half, 128)
    own = span(core * half, half, 128)
    wait_dprod = net.send(v.grad_prod.at[:, other], v.dy_down.at[theirs], here.peer_core())
    v.dy_down[mine, :] = v.grad_prod[:, own]

    w_u.share_straight(0)
    w_u.share_diagonal()
    w_u.share_straight(1)
    w_u.ready()
    inner = math.sqrt(2.0 / math.pi)

    wait_hidden = []
    for index in range(hidden_width // 512):
        columns = slice(index * 512, index * 512 + 512)
        v.tmp[:, 0:512] = dot(v.second[mine, :], v.fu[:, columns], NN)

        def bend(rows):
            u = v.tmp[rows, 0:512]
            square = u * u
            t = jnp.tanh(u * (inner + (inner * 0.044715) * square))
            a = 0.5 + 0.5 * t
            value = u * a
            v.hidden[rows, columns] = value.astype(BF16)
            v.slope[rows, columns] = a + value * (1.0 - a) * (2.0 * inner + (6.0 * inner * 0.044715) * square)

        by_rows(tokens, bend)
        if index % 2:
            done = slice(index * 512 - 512, index * 512 + 512)
            wait_hidden.append(
                net.send(v.hidden.at[mine, done], v.hidden.at[theirs, done], here.peer_core())
            )

    pieces = []
    for number, (index, column, wide, kind) in enumerate(chunks):
        total = (v.t_qkv, v.t_out, v.t_up, v.t_down)[index]
        out = (v.o_qkv, v.o_out, v.o_up, v.o_down)[index]
        bufs = [getattr(v, f"c{number}_{k}") for k in range(7)]
        pieces.append(kind(net, here, total, out, bufs, column, wide))
    c_down, c_next, c_early, c_up, c_more, c_out = pieces[:6]
    c_qkv = pieces[6:]

    def weight_grad(total, left, right, step):
        @pl.loop(0, total.shape[0] // step)
        def _(index):
            rows = span(index * step, step, 128)
            total[rows, :] = dot(left[:, rows], right[...], TN).astype(BF16)

    w_d.share_straight(0)
    for wait in wait_hidden:
        wait()
    wait_dprod()

    def down_quarter(place):
        @pl.loop(0, 3)
        def _(index):
            rows = span(place * width + index * 256, 256, 256)
            v.t_down[rows, :] = dot(v.hidden[:, rows], v.dy_down[...], TN).astype(BF16)

    down_quarter(here.peer_d()[0])
    c_down.first_diagonal()
    c_next.first_diagonal()
    down_quarter(here.peer_x()[0])
    c_down.first_x()
    c_next.first_x()
    down_quarter(here.peer_y()[0])
    c_down.first_y()
    c_next.first_y()
    down_quarter(dp)
    c_early.near()
    w_d.share_diagonal()
    w_d.share_straight(1)
    w_d.ready()

    wide_half = hidden_width // 2

    def bend_back(side):
        @pl.loop(0, wide_half // 512)
        def _(index):
            columns = span(side * wide_half + index * 512, 512, 128)
            back = dot(v.grad_prod[...], v.fd[columns, :], NT)
            v.grad_u[:, columns] = (back * v.slope[:, columns]).astype(BF16)

    bend_back(1 - core)
    wait_du = net.send(
        v.grad_u.at[:, span((1 - core) * wide_half, wide_half, 128)], v.dy_up.at[theirs], here.peer_core()
    )
    bend_back(core)
    v.dy_up[mine, :] = v.grad_u[:, span(core * wide_half, wide_half, 128)]
    c_down.second()
    c_next.second()
    wait_second()
    wait_du()
    weight_grad(v.t_up, v.second, v.dy_up, 256)
    c_up.first()
    c_more.first()

    @pl.loop(0, width // 256)
    def _(index):
        columns = span(index * 256, 256, 128)
        v.produced[:, columns] = dot(v.hidden[mine, :], v.fd[:, columns], NN).astype(BF16)

    v.sums[...] = jnp.zeros(v.sums.shape, F32)

    def finish(rows):
        produced = v.produced[rows, :].astype(F32)
        grad = v.g_v[rows, :].astype(F32)
        router, keep = v.router[rows, :], v.keep[rows, :]
        scaled = produced * (keep * router)
        v.output_v[rows, :] = (v.middle[rows, :] + v.mod[5:6] * scaled).astype(BF16)
        v.sums[0] += fold(grad * scaled)
        back = jnp.sum(grad * v.mod[5:6] * produced, axis=1, keepdims=True)
        v.logit[rows, :] = back * keep * router * (1.0 - router)

    by_rows(tokens, finish)
    out_copy = [pltpu.make_async_copy(v.output_v, v.output, v.local_sems.at[12])]
    out_copy[0].start()
    c_early.far()
    c_down.third()
    c_next.third()

    @pl.loop(0, width // 256)
    def _(index):
        columns = span(index * 256, 256, 128)
        v.produced[:, columns] = dot(v.grad_u[...], v.fu[columns, :], NT).astype(BF16)

    def second_back(rows):
        logit = v.logit[rows, :]
        back = v.produced[rows, :].astype(F32) + logit * v.token[...]
        normal = v.z2[rows, :]
        v.sums[1] += fold(logit * v.second[rows, :].astype(F32))
        v.sums[2] += fold(back * normal)
        v.sums[3] += fold(back)
        inside = back * (1.0 + v.mod[4:5])
        level = jnp.mean(inside, axis=1, keepdims=True)
        slope = jnp.mean(inside * normal, axis=1, keepdims=True)
        grad = v.g_v[rows, :].astype(F32) + v.scale2[rows, :] * (inside - level - normal * slope)
        v.grad_mid[rows, :] = grad
        v.sums[4] += fold(grad * v.branch[rows, :])
        v.grad_branch[rows, :] = (v.mod[2:3] * grad).astype(BF16)

    by_rows(tokens, second_back)
    wait_dbranch = net.send(v.grad_branch.at[:, other], v.dy_out.at[theirs], here.peer_core())
    v.dy_out[mine, :] = v.grad_branch[:, own]

    @pl.loop(0, width // 256)
    def _(index):
        columns = span(index * 256, 256, 128)
        v.tmp[:, columns] = dot(v.grad_branch[...], v.fo[columns, :], NT)

    wait_gated()
    wait_dbranch()
    weight_grad(v.t_out, v.gated, v.dy_out, 256)
    c_out.first()

    def gate_back(rows):
        grad = v.tmp[rows, :]
        v.sums[5] += fold(grad * v.attended[rows, :])
        v.grad_att[rows, :] = (grad * v.gate_row[...]).astype(BF16)

    by_rows(tokens, gate_back)

    def gather_far(piece, block):
        block[pl.ds(core, 1), pl.ds(here.z, 1), pl.ds(dp, 1)] = piece[...][None, None, None]
        far = (here.z + 2) % Z_CHIPS
        return [net.send(piece, block.at[core, here.z, dp], here.peer_z2(), block.at[core, far, dp])]

    def gather_near(block, waits):
        for wait in waits:
            wait()
        near = here.z + 1 - 2 * (here.z % 2)
        moves = []
        for k in range(2):
            z, other = (here.z + 2 * k) % Z_CHIPS, (near + 2 * k) % Z_CHIPS
            tile = block.at[core, z, dp]
            moves.append(net.send(tile, tile, here.peer_z1(), block.at[core, other, dp]))
        return moves

    def gather_dp(block, waits):
        for wait in waits:
            wait()
        tiles = block.at[core, pl.ds(0, Z_CHIPS), dp]
        return [
            net.send(tiles, tiles, peer, block.at[core, pl.ds(0, Z_CHIPS), peer[0]])
            for peer in here.dp_peers()
        ]

    def gather_pair(block, waits):
        for wait in waits:
            wait()
        return net.send(block.at[core], block.at[core], here.peer_core(), block.at[1 - core])

    head_back = dot(
        jnp.broadcast_to(jnp.sum(v.sums[5], axis=0, keepdims=True), (8, width)), v.expand[...], NT, exact=True
    )
    head_back = head_back[0:1] * head_mask * head_sigmoid * (1.0 - head_sigmoid)
    v.early_f[...] = jnp.zeros(v.early_f.shape, F32)
    rows_out = [jnp.sum(v.sums[k], axis=0, keepdims=True) for k in (4, 3, 2, 0, 1)]
    cut = width // 2
    for slot, values in zip((0, 1, 2, 3, 5, 6), (*rows_out, v.small_v[0:1, :])):
        v.early_f[2 * slot : 2 * slot + 1, :] = values[:, 0:cut]
        v.early_f[2 * slot + 1 : 2 * slot + 2, :] = values[:, cut:width]
    v.early_f[8:9, 0:128] = head_back
    v.early_out[...] = v.early_f[...].astype(BF16)
    early = gather_far(v.early_out, v.early)
    c_up.second()

    def back_pair(pair):
        queries, key_rows, value_rows = three(pair, v.packed)
        columns = span(pair * 2 * size, 2 * size, 128)
        grad_att = v.grad_att[:, columns]
        gq, gk, gv = [], [], []
        for which in range(2):
            probs = v.probs[pair * 2 + which]
            grad_probs = dot(grad_att * masks[which], value_rows, NT)
            level = jnp.sum(probs * grad_probs, axis=1, keepdims=True)
            grad_scores = (probs * (grad_probs - level)).astype(BF16)
            gq.append(dot(grad_scores, key_rows, NN))
            gk.append(dot(grad_scores, queries, TN))
            gv.append(dot(probs.astype(BF16), grad_att, TN))
        for part, (grads, scale) in enumerate(((gq, factor), (gk, factor), (gv, 1.0))):
            both = jnp.where(low_lane, grads[0], grads[1]) * scale
            v.grad_pack[:, span(part * width + pair * 2 * size, 2 * size, 128)] = both.astype(BF16)

    pl.loop(0, heads // 2)(back_pair)
    packed_half = 3 * width // 2
    wait_dpack = net.send(
        v.grad_pack.at[:, span((1 - core) * packed_half, packed_half, 128)],
        v.dy_qkv.at[theirs],
        here.peer_core(),
    )
    v.dy_qkv[mine, :] = v.grad_pack[:, span(core * packed_half, packed_half, 128)]
    c_early.first()
    c_more.second()
    early = gather_near(v.early, early)
    wait_normed()
    wait_dpack()
    weight_grad(v.t_qkv, v.nb, v.dy_qkv, 256)
    c_out.second()
    early = gather_dp(v.early, early)
    c_qkv[0].first()
    c_qkv[1].first()
    c_down.fourth()
    c_next.fourth()


    @pl.loop(0, width // 256)
    def _(index):
        columns = span(index * 256, 256, 128)
        v.tmp[:, columns] = dot(v.grad_pack[...], v.fq[columns, :], NT)

    c_up.third()

    def first_back(rows):
        back = v.tmp[rows, :]
        values = v.x_v[rows, :].astype(F32)
        centre = values - jnp.mean(values, axis=1, keepdims=True)
        spread = jnp.mean(centre * centre, axis=1, keepdims=True)
        scale = lax.rsqrt(spread + epsilon)
        normal = centre * scale
        v.sums[6] += fold(back * normal)
        v.sums[7] += fold(back)
        inside = back * (1.0 + v.mod[1:2])
        level = jnp.mean(inside, axis=1, keepdims=True)
        slope = jnp.mean(inside * normal, axis=1, keepdims=True)
        v.grad_input_v[rows, :] = v.grad_mid[rows, :] + scale * (inside - level - normal * slope)

    by_rows(tokens, first_back)
    shift = jnp.sum(v.sums[7], axis=0, keepdims=True)
    scale = jnp.sum(v.sums[6], axis=0, keepdims=True)
    v.late_f[...] = jnp.zeros(v.late_f.shape, F32)
    for k in range(width // 128):
        v.late_f[k : k + 1, :] = shift[:, k * 128 : (k + 1) * 128]
        v.late_f[8 + k : 9 + k, :] = scale[:, k * 128 : (k + 1) * 128]
    v.late_out[...] = v.late_f[...].astype(BF16)
    late = gather_far(v.late_out, v.late)
    out_copy.append(pltpu.make_async_copy(v.grad_input_v, v.grad_input, v.local_sems.at[13]))
    out_copy[1].start()
    c_more.third()
    c_up.fourth()
    c_early.second()
    c_out.third()
    late = gather_near(v.late, late)
    c_more.fourth()
    early = gather_pair(v.early, early)
    c_qkv[0].second()
    c_qkv[2].first()
    c_out.fourth()
    late = gather_dp(v.late, late)
    c_down.fifth()
    c_next.fifth()
    c_qkv[1].second()
    c_up.fifth()
    c_early.fifth()
    c_qkv[2].second()
    c_more.fifth()
    c_out.fifth()
    early()
    offset = dp * quarter + (here.seq % BLOCK) * SHARE
    pick = (
        lax.broadcasted_iota(jnp.int32, (width, SHARE), 0)
        == lax.broadcasted_iota(jnp.int32, (width, SHARE), 1) + offset
    ).astype(F32)
    c_qkv[0].third()
    late = gather_pair(v.late, late)
    c_qkv[1].third()
    c_qkv[2].third()

    every = v.early[...].reshape(512, cut).astype(F32).reshape(32, 16, cut)
    conditions = (
        dot(every[:, 12, :].astype(BF16), pick[0:cut].astype(BF16), NN)
        + dot(every[:, 13, :].astype(BF16), pick[cut:width].astype(BF16), NN)
    ).astype(BF16)
    for slot, piece in enumerate((2, 3, 4, 5)):
        for side in range(2):
            start = piece * width + side * cut
            v.o_ada[:, start : start + cut] = dot(
                conditions, every[:, 2 * slot + side, :].astype(BF16), TN
            )
    v.o_head[...] = dot(every[:, 8, 0:128].astype(BF16), conditions, TN)[0:heads]
    totals = [jnp.sum(every[:, 10 + side, :], axis=0, keepdims=True) for side in range(2)]
    v.o_token[...] = (
        dot(jnp.broadcast_to(totals[0], (8, cut)), pick[0:cut], NN, exact=True)
        + dot(jnp.broadcast_to(totals[1], (8, cut)), pick[cut:width], NN, exact=True)
    )[0:1]

    def emit(number, source, target):
        copy = pltpu.make_async_copy(source, target, v.local_sems.at[14 + number])
        copy.start()
        out_copy.append(copy)

    c_qkv[0].fifth()
    c_qkv[1].fifth()
    for chunk in (c_down, c_next, c_early, c_up, c_more):
        chunk.end()
    for number, name in enumerate(("head", "token", "up", "down")):
        emit(number, getattr(v, "o_" + name), getattr(v, "out_" + name))
    late()
    tail = v.late[...].reshape(512, 128).astype(F32).reshape(32, 16, 128)
    for base in (0, 8):
        row = jnp.concatenate([tail[:, base + k, :] for k in range(width // 128)], axis=1)
        start = base // 8 * width
        v.o_ada[:, start : start + width] = dot(conditions, row.astype(BF16), TN)
    emit(4, v.o_ada, v.out_ada)
    c_qkv[2].fifth()
    for chunk in (c_out, *c_qkv):
        chunk.end()
    emit(5, v.o_out, v.out_out)
    emit(6, v.o_qkv, v.out_qkv)
    for copy in out_copy:
        copy.wait()
    net.finish()


def layer(cond, w_token, w_head, token_keep, head_keep, inputs, cotangent, w_ada, wq, wo, wu, wd):
    tokens, width = inputs.shape
    hidden_width = wu.shape[1]
    heads = head_keep.shape[1]
    widths = [wq.shape[1], wo.shape[1], wu.shape[1], wd.shape[1]]
    depths = [4 * w.shape[0] for w in (wq, wo, wu, wd)]
    chunks = chunk_list(widths)
    operands = dict(
        cond=cond, w_token=w_token, w_head=w_head, token_keep=token_keep, head_keep=head_keep,
        inputs=inputs, cotangent=cotangent, w_ada=w_ada, wq=wq, wo=wo, wu=wu, wd=wd,
    )
    outs = dict(
        ada=((SHARE, 6 * width), F32),
        qkv=((depths[0] // 32, widths[0]), F32),
        out=((depths[1] // 32, widths[1]), F32),
        up=((depths[2] // 32, widths[2]), F32),
        down=((depths[3] // 32, widths[3]), F32),
        head=((heads, SHARE), F32),
        token=((1, SHARE), F32),
    )
    results = dict(output=((tokens, width), BF16), grad_input=((tokens, width), F32))
    results.update({"out_" + k: s for k, s in outs.items()})
    space = dict(
        cond_v=(cond.shape, F32),
        small_v=((8, width), F32),
        token_v=(w_token.shape, BF16),
        keep_v=(token_keep.shape, jnp.int32),
        head_keep_v=(head_keep.shape, jnp.int32),
        head_mask=((1, 128), F32),
        output_v=((tokens, width), BF16),
        grad_input_v=((tokens, width), F32),
        head_v=(w_head.shape, BF16),
        ada_v=(w_ada.shape, BF16),
        x_v=((tokens, width), BF16),
        g_v=((tokens, width), BF16),
        fq=((depths[0], widths[0]), BF16),
        fo=((depths[1], widths[1]), BF16),
        fu=((depths[2], widths[2]), BF16),
        fd=((depths[3], widths[3]), BF16),
        cond_buf=((4, 8, width), F32),
        part=((4, 8, width), F32),
        part_buf=((3, 8, width), F32),
        mod=((8, width), F32),
        token=((1, width), F32),
        keep=((tokens, 1), F32),
        expand=((128, width), F32),
        gate_row=((1, width), F32),
        nb=((2 * tokens, width), BF16),
        packed=((tokens, 3 * width), BF16),
        probs=((heads, tokens, tokens), F32),
        attended=((tokens, width), F32),
        gated=((2 * tokens, width), BF16),
        branch=((tokens, width), F32),
        middle=((tokens, width), F32),
        z2=((tokens, width), F32),
        scale2=((tokens, 1), F32),
        second=((2 * tokens, width), BF16),
        router=((tokens, 1), F32),
        logit=((tokens, 1), F32),
        grad_prod=((tokens, width), BF16),
        dy_down=((2 * tokens, width // 2), BF16),
        tmp=((tokens, width), F32),
        hidden=((2 * tokens, hidden_width), BF16),
        slope=((tokens, hidden_width), F32),
        grad_u=((tokens, hidden_width), BF16),
        dy_up=((2 * tokens, hidden_width // 2), BF16),
        produced=((tokens, width), BF16),
        grad_mid=((tokens, width), F32),
        grad_branch=((tokens, width), BF16),
        dy_out=((2 * tokens, width // 2), BF16),
        grad_att=((tokens, width), BF16),
        grad_pack=((tokens, 3 * width), BF16),
        dy_qkv=((2 * tokens, 3 * width // 2), BF16),
        sums=((8, 8, width), F32),
        early_f=((16, width // 2), F32),
        early_out=((16, width // 2), BF16),
        early=((2, Z_CHIPS, 4, 16, width // 2), BF16),
        late_f=((16, 128), F32),
        late_out=((16, 128), BF16),
        late=((2, Z_CHIPS, 4, 16, 128), BF16),
        t_qkv=((depths[0], widths[0] // 2), BF16),
        t_out=((depths[1], widths[1] // 2), BF16),
        t_up=((depths[2], widths[2] // 2), BF16),
        t_down=((depths[3], widths[3] // 2), BF16),
    )
    space.update({"o_" + k: s for k, s in outs.items()})
    for number, (index, _, wide, kind) in enumerate(chunks):
        shapes = kind.shapes(depths[index] // 16, wide)
        for k, shape in enumerate(shapes):
            space[f"c{number}_{k}"] = (shape, BF16)
        space[f"c{number}_6"] = ((depths[index] // 16, wide), F32)
    copies = 6 + 4 * 13 + 12 + len(chunks) * 12 + 2 * 12 + 14
    names = list(operands) + list(results) + list(space) + ["send_sems", "recv_sems", "local_sems"]
    return pl.pallas_call(
        functools.partial(layer_kernel, names, chunks, (tokens, width, heads, hidden_width)),
        out_shape=[jax.ShapeDtypeStruct(*r) for r in results.values()],
        in_specs=[ANY] * len(operands),
        out_specs=[ANY] * len(results),
        scratch_shapes=[pltpu.VMEM(*s) for s in space.values()]
        + [
            pltpu.SemaphoreType.DMA((copies,)),
            pltpu.SemaphoreType.DMA((copies,)),
            pltpu.SemaphoreType.DMA((21,)),
        ],
        compiler_params=pltpu.CompilerParams(
            collective_id=0, has_side_effects=True, vmem_limit_bytes=64 * 2**20 - 2**16
        ),
    )(*operands.values())


def copy_kernel(cuts, *refs):
    count = len(cuts)
    ins, outs, space = refs[:count], refs[count : 2 * count], refs[2 * count : 3 * count]
    sems = refs[3 * count]
    moves, used = [], 0
    for k, cut in enumerate(cuts):
        rows = ins[k].shape[0] // cut
        for piece in range(cut):
            at = (pl.ds(piece * rows, rows), slice(None))
            moves.append(
                (
                    pltpu.make_async_copy(ins[k].at[at], space[k].at[at], sems.at[used]),
                    pltpu.make_async_copy(space[k].at[at], outs[k].at[at], sems.at[used + 1]),
                )
            )
            used += 2
    for load, _ in moves:
        load.start()
    for load, store in moves:
        load.wait()
        store.start()
    for _, store in moves:
        store.wait()


def copy_all(arrays):
    cuts = [max(1, a.size * a.dtype.itemsize >> 17) for a in arrays]
    cuts = [1 if a.shape[0] % (cut * 16) else cut for a, cut in zip(arrays, cuts)]
    return pl.pallas_call(
        functools.partial(copy_kernel, cuts),
        out_shape=[jax.ShapeDtypeStruct(a.shape, a.dtype) for a in arrays],
        in_specs=[ANY] * len(arrays),
        out_specs=[ANY] * len(arrays),
        scratch_shapes=[pltpu.VMEM(a.shape, a.dtype) for a in arrays]
        + [pltpu.SemaphoreType.DMA((2 * sum(cuts),))],
        compiler_params=pltpu.CompilerParams(vmem_limit_bytes=64 * 2**20 - 2**16),
    )(*arrays)


def across_blocks(part, seq_size):
    blocks = seq_size // BLOCK
    if blocks == 1:
        return part
    groups = [[b * BLOCK + j for b in range(blocks)] for j in range(BLOCK)]
    mine = lax.psum_scatter(
        part, "seq", scatter_dimension=0, axis_index_groups=groups, tiled=True
    )
    moves = [(b * BLOCK + j, j * blocks + b) for b in range(blocks) for j in range(BLOCK)]
    return lax.ppermute(mine, "seq", moves)


def per_device(
    seq_size, inputs, time_table, time_index, token_keep, head_keep, cotangent,
    w_ada, w_qkv, w_out, w_up, w_down, w_head, w_token,
):
    width = inputs.shape[2]
    row = lax.dynamic_slice(time_table, (time_index[0], 0), (1, width)).astype(F32)
    condition = jax.nn.silu(row).astype(BF16).astype(F32)
    out = layer(
        condition, w_token, w_head.T, token_keep, head_keep,
        inputs[0], cotangent[0], w_ada, w_qkv, w_out, w_up, w_down,
    )
    output, grad_input, ada, qkv, outw, up, down, head, token = copy_all(out)
    parts = (ada, qkv, outw, up, down, head.T, token[0])
    parts = tuple(across_blocks(part, seq_size) for part in parts)
    return (output[None], grad_input[None]) + parts


def solution(mesh):
    both = ("dp", "seq")
    in_specs = (
        P(both, None, None), P(), P(both), P(both, None), P(both, None), P(both, None, None),
        P("dp", None), P("dp", None), P("dp", None), P("dp", None), P("dp", None), P("dp", None), P("dp"),
    )
    out_specs = (P(both, None, None), P(both, None, None)) + (P(both, None),) * 6 + (P(both),)
    return jax.shard_map(
        functools.partial(per_device, mesh.shape["seq"]),
        mesh=mesh, in_specs=in_specs, out_specs=out_specs, check_vma=False,
    )
```

```python
import functools
import math
import types

import jax
import jax.numpy as jnp
from jax import lax
from jax.experimental import pallas as pl
from jax.experimental.pallas import tpu as pltpu
from jax.sharding import PartitionSpec as P

epsilon = 1e-06
MESH = pl.DeviceIdType.MESH
ANY = pl.BlockSpec(memory_space=pl.ANY)
VMEM = pl.BlockSpec(memory_space=pltpu.VMEM)
Z_CHIPS = 4
BLOCK = 2 * Z_CHIPS
F32, BF16 = jnp.float32, jnp.bfloat16
NN, NT, TN = ((1,), (0,)), ((1,), (1,)), ((0,), (0,))
ROWS = 32
SHARE = 24


def dot(left, right, dims, exact=False):
    return lax.dot_general(
        left, right, (dims, ((), ())), preferred_element_type=F32,
        precision=lax.Precision.HIGHEST if exact else None,
    )


def span(start, size, unit):
    return pl.ds(pl.multiple_of(start, unit), size)


def by_rows(total, body, step=ROWS):
    @pl.loop(0, total // step)
    def _(index):
        body(span(index * step, step, step))


def fold(values):
    return jnp.sum(values.reshape(-1, 8, values.shape[-1]), axis=0)


class Place:
    def __init__(self):
        self.dp = lax.axis_index("dp")
        self.seq = lax.axis_index("seq")
        self.x = self.dp % 2
        self.y = self.dp // 2
        self.core = self.seq % 2
        self.z = (self.seq // 2) % Z_CHIPS
        self.outer = self.seq // BLOCK

    def z_of(self, step):
        return (self.z + step) % Z_CHIPS

    def peer_x(self):
        return (self.y * 2 + 1 - self.x, self.seq)

    def peer_y(self):
        return ((1 - self.y) * 2 + self.x, self.seq)

    def peer_d(self):
        return ((1 - self.y) * 2 + 1 - self.x, self.seq)

    def peer_core(self):
        return (self.dp, self.seq + 1 - 2 * self.core)

    def peer_z(self, step):
        return (self.dp, self.outer * BLOCK + self.z_of(step) * 2 + self.core)

    def peer_z1(self):
        return (self.dp, self.seq + 2 - 4 * (self.z % 2))

    def peer_z2(self):
        return (self.dp, self.seq + 4 - 8 * (self.z // 2))

    def dp_peers(self):
        return (self.peer_x(), self.peer_y(), self.peer_d())

    def greet(self):
        peers = list(self.dp_peers()) + [self.peer_core()]
        peers += [self.peer_z(k) for k in range(1, Z_CHIPS)]
        for peer in peers:
            pl.semaphore_signal(
                pltpu.get_barrier_semaphore(), inc=1, device_id=peer, device_id_type=MESH
            )
        self.peers = len(peers)

    def meet(self):
        pl.semaphore_wait(pltpu.get_barrier_semaphore(), self.peers)


class Net:
    def __init__(self, send_sems, recv_sems):
        self.send_sems = send_sems
        self.recv_sems = recv_sems
        self.used = 0
        self.sent = []

    def send(self, src, dst, peer, landing=None):
        slot = self.used
        self.used += 1

        def copy_to(target):
            return pltpu.make_async_remote_copy(
                src_ref=src,
                dst_ref=target,
                send_sem=self.send_sems.at[slot],
                recv_sem=self.recv_sems.at[slot],
                device_id=peer,
                device_id_type=MESH,
            )

        copy = copy_to(dst)
        copy.start()
        self.sent.append(copy)
        arrival = copy if landing is None else copy_to(landing)
        return arrival.wait_recv

    def finish(self):
        for copy in self.sent:
            copy.wait_send()


class Weight:
    def __init__(self, net, here, own, full):
        self.net, self.here, self.own, self.full = net, here, own, full
        self.depth = own.shape[0]
        self.piece = self.depth // Z_CHIPS
        self.width = own.shape[1] // 2

    def columns(self, core):
        return span(core * self.width, self.width, 128)

    def quarter(self, dp):
        return span(dp * self.depth, self.depth, 16)

    def part(self, dp, z):
        return span(dp * self.depth + z * self.piece, self.piece, 16)

    def keep(self, sem):
        self.local = pltpu.make_async_copy(self.own, self.full.at[self.quarter(self.here.dp)], sem)
        self.local.start()

    def send_diagonal(self):
        here, columns = self.here, self.columns(self.here.core)
        peer = here.peer_d()
        self.wait_d = self.net.send(
            self.own.at[span(here.z * self.piece, self.piece, 16), columns],
            self.full.at[self.part(here.dp, here.z), columns],
            peer,
            self.full.at[self.part(peer[0], here.z), columns],
        )

    def rows(self, dp, side):
        half = self.depth // 2
        return span(dp * self.depth + side * half, half, 16)

    def send_straight(self):
        here, columns = self.here, self.columns(self.here.core)
        self.wait_xy = [
            [
                self.net.send(
                    self.own.at[self.rows(0, side), columns],
                    self.full.at[self.rows(here.dp, side), columns],
                    peer,
                    self.full.at[self.rows(peer[0], side), columns],
                )
                for peer in (here.peer_x(), here.peer_y())
            ]
            for side in range(2)
        ]
        self.last = []

    def spread(self):
        here, columns = self.here, self.columns(self.here.core)
        diagonal = here.peer_d()[0]
        self.wait_d()
        piece = self.full.at[self.part(diagonal, here.z), columns]
        self.wait_z = [
            self.net.send(
                piece, piece, here.peer_z(step),
                self.full.at[self.part(diagonal, here.z_of(Z_CHIPS - step)), columns],
            )
            for step in range(1, Z_CHIPS)
        ]

    def hand(self, rows):
        here = self.here
        block = self.full.at[rows, self.columns(here.core)]
        landing = self.full.at[rows, self.columns(1 - here.core)]
        self.last.append(self.net.send(block, block, here.peer_core(), landing))

    def share_straight(self, side):
        here = self.here
        for wait, peer in zip(self.wait_xy[side], (here.peer_x(), here.peer_y())):
            wait()
            self.hand(self.rows(peer[0], side))

    def share_diagonal(self):
        for wait in self.wait_z:
            wait()
        self.hand(self.quarter(self.here.peer_d()[0]))

    def ready(self):
        for wait in self.last:
            wait()
        self.local.wait()


class Chunk:
    @staticmethod
    def shapes(rows, wide):
        return ((2, 2 * rows, wide),) * 2 + ((2 * rows, wide),) * 2 + ((2, rows, wide), (rows, wide))

    def __init__(self, net, here, total, out, bufs, column, width):
        self.net, self.here, self.out = net, here, out
        self.total = total.at[:, span(column, width, 128)]
        self.block = total.shape[0] // 16
        self.column, self.width = column, width
        self.r1a, self.r1b, self.r2a, self.r2b, self.r3a, self.r3b, self.f32 = bufs

    def columns(self, core):
        return span(core * (self.out.shape[1] // 2) + self.column, self.width, 128)

    def upper(self, dp):
        return self.total.at[span(dp * 4 * self.block, 2 * self.block, 16)]

    def lower(self, dp):
        return self.total.at[span(dp * 4 * self.block + 2 * self.block, 2 * self.block, 16)]

    def add(self, total, extra):
        def body(rows):
            total[rows, :] = (total[rows, :].astype(F32) + extra[rows, :].astype(F32)).astype(BF16)

        by_rows(total.shape[0], body, 16)

    def first_diagonal(self):
        here, dp = self.here, self.here.peer_d()[0]
        self.wait_a = [self.net.send(self.upper(dp), self.r1a.at[1 - here.y], here.peer_x())]
        self.wait_b = [self.net.send(self.lower(dp), self.r1b.at[1 - here.x], here.peer_y())]

    def first_x(self):
        here, peer = self.here, self.here.peer_x()
        self.wait_a.append(self.net.send(self.upper(peer[0]), self.r1a.at[here.y], peer))

    def first_y(self):
        here, peer = self.here, self.here.peer_y()
        self.wait_b.append(self.net.send(self.lower(peer[0]), self.r1b.at[here.x], peer))

    def first(self):
        self.first_diagonal()
        self.first_x()
        self.first_y()

    def second(self):
        here = self.here
        for wait in self.wait_a:
            wait()
        away = self.upper((1 - here.y) * 2 + here.x)
        self.add(away, self.r1a.at[1 - here.y])
        next_a = self.net.send(away, self.r2a, here.peer_y())
        for wait in self.wait_b:
            wait()
        away = self.lower(here.y * 2 + 1 - here.x)
        self.add(away, self.r1b.at[1 - here.x])
        next_b = self.net.send(away, self.r2b, here.peer_x())
        self.add(self.upper(here.dp), self.r1a.at[here.y])
        self.add(self.lower(here.dp), self.r1b.at[here.x])
        self.wait_a, self.wait_b = next_a, next_b

    def mine(self, z):
        return self.total.at[span((self.here.dp * 4 + z) * self.block, self.block, 16)]

    def third(self):
        here = self.here
        self.wait_a()
        self.add(self.upper(here.dp), self.r2a)
        self.wait_b()
        self.add(self.lower(here.dp), self.r2b)
        odd = 1 - here.z % 2
        self.waits = [
            self.net.send(self.mine(odd + 2 * k), self.r3a.at[k], here.peer_z1()) for k in range(2)
        ]

    def fourth(self):
        here = self.here
        far = (here.z + 2) % Z_CHIPS
        for wait in self.waits:
            wait()
        self.add(self.mine(far), self.r3a.at[far // 2])
        self.wait = self.net.send(self.mine(far), self.r3b, here.peer_z2())
        self.add(self.mine(here.z), self.r3a.at[here.z // 2])

    def fifth(self):
        here = self.here
        self.wait()
        own = self.mine(here.z)

        def body(rows):
            self.f32[rows, :] = own[rows, :].astype(F32) + self.r3b[rows, :].astype(F32)

        by_rows(self.block, body, 16)
        self.pass_on()

    def pass_on(self):
        here = self.here
        part = self.block // 2
        self.wait = self.net.send(
            self.f32.at[span((1 - here.core) * part, part, 8)],
            self.out.at[:, self.columns(here.core)],
            here.peer_core(),
            self.out.at[:, self.columns(1 - here.core)],
        )
        self.out[:, self.columns(here.core)] = self.f32[span(here.core * part, part, 8), :]

    def end(self):
        self.wait()


class LastChunk(Chunk):
    @staticmethod
    def shapes(rows, wide):
        return ((2, 2 * rows, wide),) * 2 + ((2 * rows, wide),) * 2 + ((3, rows, wide), (16, 128))

    def third(self):
        here = self.here
        self.wait_a()
        self.add(self.upper(here.dp), self.r2a)
        self.wait_b()
        self.add(self.lower(here.dp), self.r2b)
        self.waits = [
            self.net.send(self.mine(here.z_of(k)), self.r3a.at[k - 1], here.peer_z(k))
            for k in range(1, Z_CHIPS)
        ]

    def fifth(self):
        for wait in self.waits:
            wait()
        own = self.mine(self.here.z)

        def body(rows):
            total = own[rows, :].astype(F32)
            for k in range(Z_CHIPS - 1):
                total += self.r3a[k, rows, :].astype(F32)
            self.f32[rows, :] = total

        by_rows(self.block, body, 16)
        self.pass_on()


class EarlyChunk(Chunk):
    @staticmethod
    def shapes(rows, wide):
        part = rows // 2
        return ((2, part, wide),) * 2 + ((part, wide),) * 2 + ((2, 4, rows, wide), (4, rows, wide))

    def __init__(self, net, here, total, out, bufs, column, width):
        super().__init__(net, here, total, out, bufs, column, width)
        half = self.block // 2
        self.halves = tuple((span(k * half, half, 16), slice(None)) for k in range(2))

    def at(self, dp, z):
        return self.total.at[span((dp * 4 + z) * self.block, self.block, 16)]

    def upper(self, dp):
        return self.at(dp, self.here.z).at[self.halves[0]]

    def lower(self, dp):
        return self.at(dp, self.here.z).at[self.halves[1]]

    def near(self):
        here = self.here
        odd = 1 - here.z % 2
        self.waits = [
            self.net.send(self.at(dp, odd + 2 * k), self.r3a.at[k, dp], here.peer_z1())
            for k in range(2)
            for dp in range(4)
        ]

    def far(self):
        here = self.here
        far = (here.z + 2) % Z_CHIPS
        for wait in self.waits:
            wait()
        self.waits = []
        for dp in range(4):
            self.add(self.at(dp, far), self.r3a.at[far // 2, dp])
            self.waits.append(self.net.send(self.at(dp, far), self.r3b.at[dp], here.peer_z2()))
        for dp in range(4):
            self.add(self.at(dp, here.z), self.r3a.at[here.z // 2, dp])

    def first(self):
        for wait in self.waits:
            wait()
        for dp in range(4):
            self.add(self.at(dp, self.here.z), self.r3b.at[dp])
        super().first()

    def fifth(self):
        here = self.here
        self.wait_a()
        self.wait_b()
        own = self.at(here.dp, here.z)
        for where, extra in zip(self.halves, (self.r2a, self.r2b)):
            part, target = own.at[where], self.f32.at[where]

            def body(rows):
                target[rows, :] = part[rows, :].astype(F32) + extra[rows, :].astype(F32)

            by_rows(part.shape[0], body, 16)
        self.pass_on()


def chunk_list(widths):
    cuts = (
        (3, (128, 128, 128), (Chunk, Chunk, EarlyChunk)),
        (2, (768, 768), (Chunk, Chunk)),
        (1, (384,), (Chunk,)),
        (0, (384, 384, 384), (LastChunk, LastChunk, LastChunk)),
    )
    chunks = []
    for index, parts, kinds in cuts:
        column = 0
        for part, kind in zip(parts, kinds):
            chunks.append((index, column, part, kind))
            column += part
        assert 2 * column == widths[index]
    return chunks


def layer_kernel(names, chunks, sizes, *refs):
    v = types.SimpleNamespace(**dict(zip(names, refs)))
    tokens, width, heads, hidden_width = sizes
    quarter = width // 4
    size = width // heads
    factor = size ** (-0.5)
    here = Place()
    core, dp = here.core, here.dp
    net = Net(v.send_sems, v.recv_sems)
    mine, theirs = slice(0, tokens), slice(tokens, 2 * tokens)

    here.greet()
    loads = []
    for number, (source, target) in enumerate(
        (
            (v.time_table, v.table_v), (v.w_token, v.token_v), (v.w_head, v.head_v), (v.w_ada, v.ada_v),
            (v.token_keep, v.keep_v), (v.head_keep, v.head_keep_v), (v.inputs, v.x_v), (v.cotangent, v.g_v),
            (v.time_index, v.index_v),
        )
    ):
        copy = pltpu.make_async_copy(source, target, v.local_sems.at[4 + number])
        copy.start()
        loads.append(copy)
    weights = [
        Weight(net, here, own, full)
        for own, full in ((v.wq, v.fq), (v.wo, v.fo), (v.wu, v.fu), (v.wd, v.fd))
    ]
    for number, weight in enumerate(weights):
        weight.keep(v.local_sems.at[number])
    w_q, w_o, w_u, w_d = weights
    select = (
        lax.broadcasted_iota(jnp.int32, (width, quarter), 0)
        == lax.broadcasted_iota(jnp.int32, (width, quarter), 1) + dp * quarter
    ).astype(F32).astype(BF16)
    loads[1].wait()
    token = jnp.broadcast_to(v.token_v[...].astype(F32).reshape(1, quarter), (16, quarter))
    placed = dot(token.astype(BF16), select, NT)
    loads[8].wait()
    loads[0].wait()
    rows = v.table_v.shape[0]
    whole = rows // 128 * 128
    index_row = jnp.broadcast_to(v.index_v[...], (16, whole))
    hot = (lax.broadcasted_iota(jnp.int32, (16, whole), 1) == index_row).astype(F32).astype(BF16)
    row = dot(hot, v.table_v[0:whole, :], NN)[0:1]
    rest = lax.broadcasted_iota(jnp.int32, (rows - whole, width), 0) + whole
    rest = jnp.where(
        rest == jnp.broadcast_to(v.index_v[...], rest.shape), v.table_v[whole:rows, :].astype(F32), 0.0
    )
    row += jnp.sum(rest, axis=0, keepdims=True)
    v.small_v[...] = jnp.zeros(v.small_v.shape, F32)
    v.small_v[0:1, :] = (row * jax.nn.sigmoid(row)).astype(BF16).astype(F32)
    v.small_v[1:2, :] = placed[0:1]
    here.meet()

    w_q.send_diagonal()
    waits = [
        net.send(v.small_v, v.cond_buf.at[dp], peer, v.cond_buf.at[peer[0]])
        for peer in here.dp_peers()
    ]
    w_q.send_straight()
    v.cond_buf[pl.ds(dp, 1)] = v.small_v[...][None]
    head_of = lax.broadcasted_iota(jnp.int32, (128, width), 0) * size
    lane = lax.broadcasted_iota(jnp.int32, (128, width), 1)
    v.expand[...] = ((lane >= head_of) & (lane < head_of + size)).astype(F32)
    for load in loads[2:6]:
        load.wait()
    diagonal = lax.broadcasted_iota(jnp.int32, (tokens, tokens), 0) == lax.broadcasted_iota(
        jnp.int32, (tokens, tokens), 1
    )
    v.keep[...] = jnp.sum(jnp.where(diagonal, v.keep_v[...].astype(F32), 0.0), axis=1, keepdims=True)
    v.head_mask[...] = jnp.zeros(v.head_mask.shape, F32)
    v.head_mask[:, 0:heads] = v.head_keep_v[...].astype(F32)
    v.part[...] = jnp.zeros(v.part.shape, F32)
    for wait in waits:
        wait()
    stacked = v.cond_buf[...].reshape(32, width).astype(BF16)
    left = dot(stacked, select, NN).astype(BF16)
    for piece in range(7):
        if piece < 6:
            product = dot(left, v.ada_v[:, piece * width : (piece + 1) * width], NN)
        else:
            product = dot(left, v.head_v[...], NT)
        for image in range(4):
            v.part[image, piece : piece + 1, 0 : product.shape[1]] = product[image * 8 : image * 8 + 1]
    waits = [
        net.send(v.part.at[peer[0]], v.part_buf.at[index], peer)
        for index, peer in enumerate(here.dp_peers())
    ]
    for weight in weights[1:]:
        weight.send_diagonal()
    w_q.spread()
    v.token[...] = v.cond_buf[0, 1:2] + v.cond_buf[1, 1:2] + v.cond_buf[2, 1:2] + v.cond_buf[3, 1:2]
    w_q.share_straight(0)
    w_q.share_straight(1)
    for weight in weights[1:]:
        weight.send_straight()
    w_o.spread()
    for wait in waits:
        wait()
    v.mod[...] = v.part[dp] + v.part_buf[0] + v.part_buf[1] + v.part_buf[2]
    head_sigmoid = jax.nn.sigmoid(v.mod[6:7, 0:128])
    head_mask = v.head_mask[...]
    gate = dot(jnp.broadcast_to(head_mask * head_sigmoid, (8, 128)), v.expand[...], NN, exact=True)
    v.gate_row[...] = gate[0:1]

    loads[6].wait()

    def first_norm(rows):
        values = v.x_v[rows, :].astype(F32)
        centre = values - jnp.mean(values, axis=1, keepdims=True)
        spread = jnp.mean(centre * centre, axis=1, keepdims=True)
        normal = centre * lax.rsqrt(spread + epsilon)
        v.nb[rows, :] = (normal * (1.0 + v.mod[1:2]) + v.mod[0:1]).astype(BF16)

    by_rows(tokens, first_norm)
    wait_normed = net.send(v.nb.at[mine], v.nb.at[theirs], here.peer_core())

    w_q.share_diagonal()
    w_u.spread()
    w_q.ready()

    @pl.loop(0, 3 * width // 384)
    def _(index):
        columns = span(index * 384, 384, 128)
        v.packed[:, columns] = dot(v.nb[mine, :], v.fq[:, columns], NN).astype(BF16)

    w_d.spread()

    lanes = lax.broadcasted_iota(jnp.int32, (1, 2 * size), 1)
    masks = ((lanes < size).astype(F32).astype(BF16), (lanes >= size).astype(F32).astype(BF16))
    scaled_masks = tuple(mask * jnp.asarray(factor, BF16) for mask in masks)
    low_lane = lax.broadcasted_iota(jnp.int32, (tokens, 2 * size), 1) < size

    def three(pair, block):
        return [block[:, span(part * width + pair * 2 * size, 2 * size, 128)] for part in range(3)]

    @pl.loop(0, heads // 2)
    def _(pair):
        queries, key_rows, value_rows = three(pair, v.packed)
        found = []
        for which in range(2):
            scores = dot(queries * scaled_masks[which], key_rows, NT)
            powers = jnp.exp(scores - jnp.max(scores, axis=1, keepdims=True))
            probs = powers * (1.0 / jnp.sum(powers, axis=1, keepdims=True))
            v.probs[pair * 2 + which] = probs
            found.append(dot(probs.astype(BF16), value_rows, NN))
        attended = jnp.where(low_lane, found[0], found[1])
        columns = span(pair * 2 * size, 2 * size, 128)
        v.attended[:, columns] = attended
        v.gated[mine, columns] = (attended * v.gate_row[:, columns]).astype(BF16)

    wait_gated = net.send(v.gated.at[mine], v.gated.at[theirs], here.peer_core())
    w_o.share_straight(0)
    w_o.share_straight(1)
    w_o.share_diagonal()
    w_o.ready()

    @pl.loop(0, width // 256)
    def _(index):
        columns = span(index * 256, 256, 128)
        v.branch[:, columns] = dot(v.gated[mine, :], v.fo[:, columns], NN)

    loads[7].wait()

    def second_norm(rows):
        middle = v.x_v[rows, :].astype(F32) + v.mod[2:3] * v.branch[rows, :]
        v.middle[rows, :] = middle
        centre = middle - jnp.mean(middle, axis=1, keepdims=True)
        spread = jnp.mean(centre * centre, axis=1, keepdims=True)
        scale = lax.rsqrt(spread + epsilon)
        normal = centre * scale
        v.z2[rows, :] = normal
        v.scale2[rows, :] = scale
        second = (normal * (1.0 + v.mod[4:5]) + v.mod[3:4]).astype(BF16)
        v.second[rows, :] = second
        logit = jnp.sum(second.astype(F32) * v.token[...], axis=1, keepdims=True)
        router = jax.nn.sigmoid(logit)
        v.router[rows, :] = router
        weight = v.keep[rows, :] * router
        v.grad_prod[rows, :] = (v.g_v[rows, :].astype(F32) * v.mod[5:6] * weight).astype(BF16)

    by_rows(tokens, second_norm)
    wait_second = net.send(v.second.at[mine], v.second.at[theirs], here.peer_core())
    half = width // 2
    other = span((1 - core) * half, half, 128)
    own = span(core * half, half, 128)
    wait_dprod = net.send(v.grad_prod.at[:, other], v.dy_down.at[theirs], here.peer_core())
    v.dy_down[mine, :] = v.grad_prod[:, own]

    w_u.share_straight(0)
    w_u.share_diagonal()
    w_u.share_straight(1)
    w_u.ready()
    inner = math.sqrt(2.0 / math.pi)

    wait_hidden = []
    for index in range(hidden_width // 512):
        columns = slice(index * 512, index * 512 + 512)
        v.tmp[:, 0:512] = dot(v.second[mine, :], v.fu[:, columns], NN)

        def bend(rows):
            u = v.tmp[rows, 0:512]
            square = u * u
            t = jnp.tanh(u * (inner + (inner * 0.044715) * square))
            a = 0.5 + 0.5 * t
            value = u * a
            v.hidden[rows, columns] = value.astype(BF16)
            v.slope[rows, columns] = a + value * (1.0 - a) * (2.0 * inner + (6.0 * inner * 0.044715) * square)

        by_rows(tokens, bend)
        if index % 2:
            done = slice(index * 512 - 512, index * 512 + 512)
            wait_hidden.append(
                net.send(v.hidden.at[mine, done], v.hidden.at[theirs, done], here.peer_core())
            )

    pieces = []
    for number, (index, column, wide, kind) in enumerate(chunks):
        total = (v.t_qkv, v.t_out, v.t_up, v.t_down)[index]
        out = (v.o_qkv, v.o_out, v.o_up, v.o_down)[index]
        bufs = [getattr(v, f"c{number}_{k}") for k in range(7)]
        pieces.append(kind(net, here, total, out, bufs, column, wide))
    c_down, c_next, c_early, c_up, c_more, c_out = pieces[:6]
    c_qkv = pieces[6:]

    def weight_grad(total, left, right, step):
        @pl.loop(0, total.shape[0] // step)
        def _(index):
            rows = span(index * step, step, 128)
            total[rows, :] = dot(left[:, rows], right[...], TN).astype(BF16)

    w_d.share_straight(0)
    for wait in wait_hidden:
        wait()
    wait_dprod()

    def down_quarter(place):
        @pl.loop(0, 3)
        def _(index):
            rows = span(place * width + index * 256, 256, 256)
            v.t_down[rows, :] = dot(v.hidden[:, rows], v.dy_down[...], TN).astype(BF16)

    down_quarter(here.peer_d()[0])
    c_down.first_diagonal()
    c_next.first_diagonal()
    down_quarter(here.peer_x()[0])
    c_down.first_x()
    c_next.first_x()
    down_quarter(here.peer_y()[0])
    c_down.first_y()
    c_next.first_y()
    down_quarter(dp)
    c_early.near()
    w_d.share_diagonal()
    w_d.share_straight(1)
    w_d.ready()

    wide_half = hidden_width // 2

    def bend_back(side):
        @pl.loop(0, wide_half // 512)
        def _(index):
            columns = span(side * wide_half + index * 512, 512, 128)
            back = dot(v.grad_prod[...], v.fd[columns, :], NT)
            v.grad_u[:, columns] = (back * v.slope[:, columns]).astype(BF16)

    bend_back(1 - core)
    wait_du = net.send(
        v.grad_u.at[:, span((1 - core) * wide_half, wide_half, 128)], v.dy_up.at[theirs], here.peer_core()
    )
    bend_back(core)
    v.dy_up[mine, :] = v.grad_u[:, span(core * wide_half, wide_half, 128)]
    c_down.second()
    c_next.second()
    wait_second()
    wait_du()
    weight_grad(v.t_up, v.second, v.dy_up, 256)
    c_up.first()
    c_more.first()

    @pl.loop(0, width // 256)
    def _(index):
        columns = span(index * 256, 256, 128)
        v.produced[:, columns] = dot(v.hidden[mine, :], v.fd[:, columns], NN).astype(BF16)

    v.sums[...] = jnp.zeros(v.sums.shape, F32)

    def finish(rows):
        produced = v.produced[rows, :].astype(F32)
        grad = v.g_v[rows, :].astype(F32)
        router, keep = v.router[rows, :], v.keep[rows, :]
        scaled = produced * (keep * router)
        v.output[rows, :] = (v.middle[rows, :] + v.mod[5:6] * scaled).astype(BF16)
        v.sums[0] += fold(grad * scaled)
        back = jnp.sum(grad * v.mod[5:6] * produced, axis=1, keepdims=True)
        v.logit[rows, :] = back * keep * router * (1.0 - router)

    by_rows(tokens, finish)
    c_early.far()
    c_down.third()
    c_next.third()

    @pl.loop(0, width // 256)
    def _(index):
        columns = span(index * 256, 256, 128)
        v.produced[:, columns] = dot(v.grad_u[...], v.fu[columns, :], NT).astype(BF16)

    def second_back(rows):
        logit = v.logit[rows, :]
        back = v.produced[rows, :].astype(F32) + logit * v.token[...]
        normal = v.z2[rows, :]
        v.sums[1] += fold(logit * v.second[rows, :].astype(F32))
        v.sums[2] += fold(back * normal)
        v.sums[3] += fold(back)
        inside = back * (1.0 + v.mod[4:5])
        level = jnp.mean(inside, axis=1, keepdims=True)
        slope = jnp.mean(inside * normal, axis=1, keepdims=True)
        grad = v.g_v[rows, :].astype(F32) + v.scale2[rows, :] * (inside - level - normal * slope)
        v.grad_mid[rows, :] = grad
        v.sums[4] += fold(grad * v.branch[rows, :])
        v.grad_branch[rows, :] = (v.mod[2:3] * grad).astype(BF16)

    by_rows(tokens, second_back)
    wait_dbranch = net.send(v.grad_branch.at[:, other], v.dy_out.at[theirs], here.peer_core())
    v.dy_out[mine, :] = v.grad_branch[:, own]

    @pl.loop(0, width // 256)
    def _(index):
        columns = span(index * 256, 256, 128)
        v.tmp[:, columns] = dot(v.grad_branch[...], v.fo[columns, :], NT)

    wait_gated()
    wait_dbranch()
    weight_grad(v.t_out, v.gated, v.dy_out, 256)
    c_out.first()

    def gate_back(rows):
        grad = v.tmp[rows, :]
        v.sums[5] += fold(grad * v.attended[rows, :])
        v.grad_att[rows, :] = (grad * v.gate_row[...]).astype(BF16)

    by_rows(tokens, gate_back)

    def gather_far(piece, block):
        block[pl.ds(core, 1), pl.ds(here.z, 1), pl.ds(dp, 1)] = piece[...][None, None, None]
        far = (here.z + 2) % Z_CHIPS
        return [net.send(piece, block.at[core, here.z, dp], here.peer_z2(), block.at[core, far, dp])]

    def gather_near(block, waits):
        for wait in waits:
            wait()
        near = here.z + 1 - 2 * (here.z % 2)
        moves = []
        for k in range(2):
            z, other = (here.z + 2 * k) % Z_CHIPS, (near + 2 * k) % Z_CHIPS
            tile = block.at[core, z, dp]
            moves.append(net.send(tile, tile, here.peer_z1(), block.at[core, other, dp]))
        return moves

    def gather_dp(block, waits):
        for wait in waits:
            wait()
        tiles = block.at[core, pl.ds(0, Z_CHIPS), dp]
        return [
            net.send(tiles, tiles, peer, block.at[core, pl.ds(0, Z_CHIPS), peer[0]])
            for peer in here.dp_peers()
        ]

    def gather_pair(block, waits):
        for wait in waits:
            wait()
        return net.send(block.at[core], block.at[core], here.peer_core(), block.at[1 - core])

    head_back = dot(
        jnp.broadcast_to(jnp.sum(v.sums[5], axis=0, keepdims=True), (8, width)), v.expand[...], NT, exact=True
    )
    head_back = head_back[0:1] * head_mask * head_sigmoid * (1.0 - head_sigmoid)
    v.early_f[...] = jnp.zeros(v.early_f.shape, F32)
    rows_out = [jnp.sum(v.sums[k], axis=0, keepdims=True) for k in (4, 3, 2, 0, 1)]
    cut = width // 2
    for slot, values in zip((0, 1, 2, 3, 5, 6), (*rows_out, v.small_v[0:1, :])):
        v.early_f[2 * slot : 2 * slot + 1, :] = values[:, 0:cut]
        v.early_f[2 * slot + 1 : 2 * slot + 2, :] = values[:, cut:width]
    v.early_f[8:9, 0:128] = head_back
    v.early_out[...] = v.early_f[...].astype(BF16)
    early = gather_far(v.early_out, v.early)
    c_up.second()

    def back_pair(pair):
        queries, key_rows, value_rows = three(pair, v.packed)
        columns = span(pair * 2 * size, 2 * size, 128)
        grad_att = v.grad_att[:, columns]
        gq, gk, gv = [], [], []
        for which in range(2):
            probs = v.probs[pair * 2 + which]
            grad_probs = dot(grad_att * masks[which], value_rows, NT)
            level = jnp.sum(probs * grad_probs, axis=1, keepdims=True)
            grad_scores = (probs * (grad_probs - level)).astype(BF16)
            gq.append(dot(grad_scores, key_rows, NN))
            gk.append(dot(grad_scores, queries, TN))
            gv.append(dot(probs.astype(BF16), grad_att, TN))
        for part, (grads, scale) in enumerate(((gq, factor), (gk, factor), (gv, 1.0))):
            both = jnp.where(low_lane, grads[0], grads[1]) * scale
            v.grad_pack[:, span(part * width + pair * 2 * size, 2 * size, 128)] = both.astype(BF16)

    pl.loop(0, heads // 2)(back_pair)
    packed_half = 3 * width // 2
    wait_dpack = net.send(
        v.grad_pack.at[:, span((1 - core) * packed_half, packed_half, 128)],
        v.dy_qkv.at[theirs],
        here.peer_core(),
    )
    v.dy_qkv[mine, :] = v.grad_pack[:, span(core * packed_half, packed_half, 128)]
    c_early.first()
    c_more.second()
    early = gather_near(v.early, early)
    wait_normed()
    wait_dpack()
    weight_grad(v.t_qkv, v.nb, v.dy_qkv, 256)
    c_out.second()
    early = gather_dp(v.early, early)
    c_qkv[0].first()
    c_qkv[1].first()
    c_down.fourth()
    c_next.fourth()


    @pl.loop(0, width // 256)
    def _(index):
        columns = span(index * 256, 256, 128)
        v.tmp[:, columns] = dot(v.grad_pack[...], v.fq[columns, :], NT)

    c_up.third()

    def first_back(rows):
        back = v.tmp[rows, :]
        values = v.x_v[rows, :].astype(F32)
        centre = values - jnp.mean(values, axis=1, keepdims=True)
        spread = jnp.mean(centre * centre, axis=1, keepdims=True)
        scale = lax.rsqrt(spread + epsilon)
        normal = centre * scale
        v.sums[6] += fold(back * normal)
        v.sums[7] += fold(back)
        inside = back * (1.0 + v.mod[1:2])
        level = jnp.mean(inside, axis=1, keepdims=True)
        slope = jnp.mean(inside * normal, axis=1, keepdims=True)
        v.grad_input[rows, :] = v.grad_mid[rows, :] + scale * (inside - level - normal * slope)

    by_rows(tokens, first_back)
    shift = jnp.sum(v.sums[7], axis=0, keepdims=True)
    scale = jnp.sum(v.sums[6], axis=0, keepdims=True)
    v.late_f[...] = jnp.zeros(v.late_f.shape, F32)
    for k in range(width // 128):
        v.late_f[k : k + 1, :] = shift[:, k * 128 : (k + 1) * 128]
        v.late_f[8 + k : 9 + k, :] = scale[:, k * 128 : (k + 1) * 128]
    v.late_out[...] = v.late_f[...].astype(BF16)
    late = gather_far(v.late_out, v.late)
    c_more.third()
    c_up.fourth()
    c_early.second()
    c_out.third()
    late = gather_near(v.late, late)
    c_more.fourth()
    early = gather_pair(v.early, early)
    c_qkv[0].second()
    c_qkv[2].first()
    c_out.fourth()
    late = gather_dp(v.late, late)
    c_down.fifth()
    c_next.fifth()
    c_qkv[1].second()
    c_up.fifth()
    c_early.fifth()
    c_qkv[2].second()
    c_more.fifth()
    c_out.fifth()
    early()
    offset = dp * quarter + (here.seq % BLOCK) * SHARE
    pick = (
        lax.broadcasted_iota(jnp.int32, (width, SHARE), 0)
        == lax.broadcasted_iota(jnp.int32, (width, SHARE), 1) + offset
    ).astype(F32)
    c_qkv[0].third()
    late = gather_pair(v.late, late)
    c_qkv[1].third()
    c_qkv[2].third()

    every = v.early[...].reshape(512, cut).astype(F32).reshape(32, 16, cut)
    conditions = (
        dot(every[:, 12, :].astype(BF16), pick[0:cut].astype(BF16), NN)
        + dot(every[:, 13, :].astype(BF16), pick[cut:width].astype(BF16), NN)
    ).astype(BF16)
    for slot, piece in enumerate((2, 3, 4, 5)):
        for side in range(2):
            start = piece * width + side * cut
            v.o_ada[:, start : start + cut] = dot(
                conditions, every[:, 2 * slot + side, :].astype(BF16), TN
            )
    v.o_head[...] = dot(every[:, 8, 0:128].astype(BF16), conditions, TN)[0:heads]
    totals = [jnp.sum(every[:, 10 + side, :], axis=0, keepdims=True) for side in range(2)]
    v.o_token[...] = (
        dot(jnp.broadcast_to(totals[0], (8, cut)), pick[0:cut], NN, exact=True)
        + dot(jnp.broadcast_to(totals[1], (8, cut)), pick[cut:width], NN, exact=True)
    )[0:1]

    c_qkv[0].fifth()
    c_qkv[1].fifth()
    for chunk in (c_down, c_next, c_early, c_up, c_more):
        chunk.end()
    late()
    tail = v.late[...].reshape(512, 128).astype(F32).reshape(32, 16, 128)
    for base in (0, 8):
        row = jnp.concatenate([tail[:, base + k, :] for k in range(width // 128)], axis=1)
        start = base // 8 * width
        v.o_ada[:, start : start + width] = dot(conditions, row.astype(BF16), TN)
    c_qkv[2].fifth()
    for chunk in (c_out, *c_qkv):
        chunk.end()
    net.finish()


def layer(time_table, time_index, w_token, w_head, token_keep, head_keep, inputs, cotangent, w_ada, wq, wo, wu, wd):
    tokens, width = inputs.shape
    hidden_width = wu.shape[1]
    heads = head_keep.shape[1]
    widths = [wq.shape[1], wo.shape[1], wu.shape[1], wd.shape[1]]
    depths = [4 * w.shape[0] for w in (wq, wo, wu, wd)]
    chunks = chunk_list(widths)
    operands = dict(
        time_table=time_table, time_index=time_index, w_token=w_token, w_head=w_head, token_keep=token_keep, head_keep=head_keep,
        inputs=inputs, cotangent=cotangent, w_ada=w_ada, wq=wq, wo=wo, wu=wu, wd=wd,
    )
    outs = dict(
        ada=((SHARE, 6 * width), F32),
        qkv=((depths[0] // 32, widths[0]), F32),
        out=((depths[1] // 32, widths[1]), F32),
        up=((depths[2] // 32, widths[2]), F32),
        down=((depths[3] // 32, widths[3]), F32),
        head=((heads, SHARE), F32),
        token=((1, SHARE), F32),
    )
    results = dict(output=((tokens, width), BF16), grad_input=((tokens, width), F32))
    results.update({"o_" + k: s for k, s in outs.items()})
    space = dict(
        table_v=(time_table.shape, BF16),
        index_v=(time_index.shape, jnp.int32),
        small_v=((8, width), F32),
        token_v=(w_token.shape, BF16),
        keep_v=(token_keep.shape, jnp.int32),
        head_keep_v=(head_keep.shape, jnp.int32),
        head_mask=((1, 128), F32),
        head_v=(w_head.shape, BF16),
        ada_v=(w_ada.shape, BF16),
        x_v=((tokens, width), BF16),
        g_v=((tokens, width), BF16),
        fq=((depths[0], widths[0]), BF16),
        fo=((depths[1], widths[1]), BF16),
        fu=((depths[2], widths[2]), BF16),
        fd=((depths[3], widths[3]), BF16),
        cond_buf=((4, 8, width), F32),
        part=((4, 8, width), F32),
        part_buf=((3, 8, width), F32),
        mod=((8, width), F32),
        token=((1, width), F32),
        keep=((tokens, 1), F32),
        expand=((128, width), F32),
        gate_row=((1, width), F32),
        nb=((2 * tokens, width), BF16),
        packed=((tokens, 3 * width), BF16),
        probs=((heads, tokens, tokens), F32),
        attended=((tokens, width), F32),
        gated=((2 * tokens, width), BF16),
        branch=((tokens, width), F32),
        middle=((tokens, width), F32),
        z2=((tokens, width), F32),
        scale2=((tokens, 1), F32),
        second=((2 * tokens, width), BF16),
        router=((tokens, 1), F32),
        logit=((tokens, 1), F32),
        grad_prod=((tokens, width), BF16),
        dy_down=((2 * tokens, width // 2), BF16),
        tmp=((tokens, width), F32),
        hidden=((2 * tokens, hidden_width), BF16),
        slope=((tokens, hidden_width), F32),
        grad_u=((tokens, hidden_width), BF16),
        dy_up=((2 * tokens, hidden_width // 2), BF16),
        produced=((tokens, width), BF16),
        grad_mid=((tokens, width), F32),
        grad_branch=((tokens, width), BF16),
        dy_out=((2 * tokens, width // 2), BF16),
        grad_att=((tokens, width), BF16),
        grad_pack=((tokens, 3 * width), BF16),
        dy_qkv=((2 * tokens, 3 * width // 2), BF16),
        sums=((8, 8, width), F32),
        early_f=((16, width // 2), F32),
        early_out=((16, width // 2), BF16),
        early=((2, Z_CHIPS, 4, 16, width // 2), BF16),
        late_f=((16, 128), F32),
        late_out=((16, 128), BF16),
        late=((2, Z_CHIPS, 4, 16, 128), BF16),
        t_qkv=((depths[0], widths[0] // 2), BF16),
        t_out=((depths[1], widths[1] // 2), BF16),
        t_up=((depths[2], widths[2] // 2), BF16),
        t_down=((depths[3], widths[3] // 2), BF16),
    )
    for number, (index, _, wide, kind) in enumerate(chunks):
        shapes = kind.shapes(depths[index] // 16, wide)
        for k, shape in enumerate(shapes):
            space[f"c{number}_{k}"] = (shape, BF16)
        space[f"c{number}_6"] = ((depths[index] // 16, wide), F32)
    copies = 6 + 4 * 13 + 12 + len(chunks) * 12 + 2 * 12 + 14
    names = list(operands) + list(results) + list(space) + ["send_sems", "recv_sems", "local_sems"]
    return pl.pallas_call(
        functools.partial(layer_kernel, names, chunks, (tokens, width, heads, hidden_width)),
        out_shape=[pltpu.VMEM(*r) for r in results.values()],
        in_specs=[ANY] * len(operands),
        out_specs=[VMEM] * len(results),
        scratch_shapes=[pltpu.VMEM(*s) for s in space.values()]
        + [
            pltpu.SemaphoreType.DMA((copies,)),
            pltpu.SemaphoreType.DMA((copies,)),
            pltpu.SemaphoreType.DMA((13,)),
        ],
        compiler_params=pltpu.CompilerParams(
            collective_id=0, has_side_effects=True, vmem_limit_bytes=61 * 2**20
        ),
    )(*operands.values())


def copy_kernel(count, *refs):
    copies = [
        pltpu.make_async_copy(refs[k], refs[count + k], refs[2 * count].at[k]) for k in range(count)
    ]
    for copy in copies:
        copy.start()
    for copy in copies:
        copy.wait()


def copy_all(arrays):
    count = len(arrays)
    return pl.pallas_call(
        functools.partial(copy_kernel, count),
        out_shape=[jax.ShapeDtypeStruct(a.shape, a.dtype) for a in arrays],
        in_specs=[VMEM] * count,
        out_specs=[ANY] * count,
        scratch_shapes=[pltpu.SemaphoreType.DMA((count,))],
        compiler_params=pltpu.CompilerParams(vmem_limit_bytes=16 * 2**20),
    )(*(pltpu.with_memory_space_constraint(a, pltpu.VMEM) for a in arrays))


def across_blocks(part, seq_size):
    blocks = seq_size // BLOCK
    if blocks == 1:
        return part
    groups = [[b * BLOCK + j for b in range(blocks)] for j in range(BLOCK)]
    mine = lax.psum_scatter(
        part, "seq", scatter_dimension=0, axis_index_groups=groups, tiled=True
    )
    moves = [(b * BLOCK + j, j * blocks + b) for b in range(blocks) for j in range(BLOCK)]
    return lax.ppermute(mine, "seq", moves)


def per_device(
    seq_size, inputs, time_table, time_index, token_keep, head_keep, cotangent,
    w_ada, w_qkv, w_out, w_up, w_down, w_head, w_token,
):
    out = layer(
        time_table, time_index[None], w_token, w_head.T, token_keep, head_keep,
        inputs[0], cotangent[0], w_ada, w_qkv, w_out, w_up, w_down,
    )
    output, grad_input, ada, qkv, outw, up, down, head, token = copy_all(out)
    parts = (ada, qkv, outw, up, down, head.T, token[0])
    parts = tuple(across_blocks(part, seq_size) for part in parts)
    return (output[None], grad_input[None]) + parts


def solution(mesh):
    both = ("dp", "seq")
    in_specs = (
        P(both, None, None), P(), P(both), P(both, None), P(both, None), P(both, None, None),
        P("dp", None), P("dp", None), P("dp", None), P("dp", None), P("dp", None), P("dp", None), P("dp"),
    )
    out_specs = (P(both, None, None), P(both, None, None)) + (P(both, None),) * 6 + (P(both),)
    return jax.shard_map(
        functools.partial(per_device, mesh.shape["seq"]),
        mesh=mesh, in_specs=in_specs, out_specs=out_specs, check_vma=False,
    )
```

```python
import functools
import math
import types

import jax
import jax.numpy as jnp
from jax import lax
from jax.experimental import pallas as pl
from jax.experimental.pallas import tpu as pltpu
from jax.sharding import PartitionSpec as P

epsilon = 1e-06
MESH = pl.DeviceIdType.MESH
ANY = pl.BlockSpec(memory_space=pl.ANY)
VMEM = pl.BlockSpec(memory_space=pltpu.VMEM)
Z_CHIPS = 4
BLOCK = 2 * Z_CHIPS
F32, BF16 = jnp.float32, jnp.bfloat16
NN, NT, TN = ((1,), (0,)), ((1,), (1,)), ((0,), (0,))
ROWS = 32
SHARE = 24


def dot(left, right, dims, exact=False):
    return lax.dot_general(
        left, right, (dims, ((), ())), preferred_element_type=F32,
        precision=lax.Precision.HIGHEST if exact else None,
    )


def span(start, size, unit):
    return pl.ds(pl.multiple_of(start, unit), size)


def by_rows(total, body, step=ROWS):
    @pl.loop(0, total // step)
    def _(index):
        body(span(index * step, step, step))


def fold(values):
    return jnp.sum(values.reshape(-1, 8, values.shape[-1]), axis=0)


class Place:
    def __init__(self):
        self.dp = lax.axis_index("dp")
        self.seq = lax.axis_index("seq")
        self.x = self.dp % 2
        self.y = self.dp // 2
        self.core = self.seq % 2
        self.z = (self.seq // 2) % Z_CHIPS
        self.outer = self.seq // BLOCK

    def z_of(self, step):
        return (self.z + step) % Z_CHIPS

    def peer_x(self):
        return (self.y * 2 + 1 - self.x, self.seq)

    def peer_y(self):
        return ((1 - self.y) * 2 + self.x, self.seq)

    def peer_d(self):
        return ((1 - self.y) * 2 + 1 - self.x, self.seq)

    def peer_core(self):
        return (self.dp, self.seq + 1 - 2 * self.core)

    def peer_z(self, step):
        return (self.dp, self.outer * BLOCK + self.z_of(step) * 2 + self.core)

    def peer_z1(self):
        return (self.dp, self.seq + 2 - 4 * (self.z % 2))

    def peer_z2(self):
        return (self.dp, self.seq + 4 - 8 * (self.z // 2))

    def dp_peers(self):
        return (self.peer_x(), self.peer_y(), self.peer_d())

    def greet(self):
        peers = list(self.dp_peers()) + [self.peer_core()]
        peers += [self.peer_z(k) for k in range(1, Z_CHIPS)]
        for peer in peers:
            pl.semaphore_signal(
                pltpu.get_barrier_semaphore(), inc=1, device_id=peer, device_id_type=MESH
            )
        self.peers = len(peers)

    def meet(self):
        pl.semaphore_wait(pltpu.get_barrier_semaphore(), self.peers)


class Net:
    def __init__(self, send_sems, recv_sems):
        self.send_sems = send_sems
        self.recv_sems = recv_sems
        self.used = 0
        self.sent = []

    def send(self, src, dst, peer, landing=None):
        slot = self.used
        self.used += 1

        def copy_to(target):
            return pltpu.make_async_remote_copy(
                src_ref=src,
                dst_ref=target,
                send_sem=self.send_sems.at[slot],
                recv_sem=self.recv_sems.at[slot],
                device_id=peer,
                device_id_type=MESH,
            )

        copy = copy_to(dst)
        copy.start()
        self.sent.append(copy)
        arrival = copy if landing is None else copy_to(landing)
        return arrival.wait_recv

    def finish(self):
        for copy in self.sent:
            copy.wait_send()


class Weight:
    def __init__(self, net, here, own, full):
        self.net, self.here, self.own, self.full = net, here, own, full
        self.depth = own.shape[0]
        self.piece = self.depth // Z_CHIPS
        self.width = own.shape[1] // 2

    def columns(self, core):
        return span(core * self.width, self.width, 128)

    def quarter(self, dp):
        return span(dp * self.depth, self.depth, 16)

    def part(self, dp, z):
        return span(dp * self.depth + z * self.piece, self.piece, 16)

    def keep(self, sem):
        self.local = pltpu.make_async_copy(self.own, self.full.at[self.quarter(self.here.dp)], sem)
        self.local.start()

    def send_diagonal(self):
        here, columns = self.here, self.columns(self.here.core)
        peer = here.peer_d()
        self.wait_d = self.net.send(
            self.own.at[span(here.z * self.piece, self.piece, 16), columns],
            self.full.at[self.part(here.dp, here.z), columns],
            peer,
            self.full.at[self.part(peer[0], here.z), columns],
        )

    def rows(self, dp, side):
        half = self.depth // 2
        return span(dp * self.depth + side * half, half, 16)

    def send_straight(self):
        here, columns = self.here, self.columns(self.here.core)
        self.wait_xy = [
            [
                self.net.send(
                    self.own.at[self.rows(0, side), columns],
                    self.full.at[self.rows(here.dp, side), columns],
                    peer,
                    self.full.at[self.rows(peer[0], side), columns],
                )
                for peer in (here.peer_x(), here.peer_y())
            ]
            for side in range(2)
        ]
        self.last = []

    def spread(self):
        here, columns = self.here, self.columns(self.here.core)
        diagonal = here.peer_d()[0]
        self.wait_d()
        piece = self.full.at[self.part(diagonal, here.z), columns]
        self.wait_z = [
            self.net.send(
                piece, piece, here.peer_z(step),
                self.full.at[self.part(diagonal, here.z_of(Z_CHIPS - step)), columns],
            )
            for step in range(1, Z_CHIPS)
        ]

    def hand(self, rows):
        here = self.here
        block = self.full.at[rows, self.columns(here.core)]
        landing = self.full.at[rows, self.columns(1 - here.core)]
        self.last.append(self.net.send(block, block, here.peer_core(), landing))

    def share_straight(self, side):
        here = self.here
        for wait, peer in zip(self.wait_xy[side], (here.peer_x(), here.peer_y())):
            wait()
            self.hand(self.rows(peer[0], side))

    def share_diagonal(self):
        for wait in self.wait_z:
            wait()
        self.hand(self.quarter(self.here.peer_d()[0]))

    def ready(self):
        for wait in self.last:
            wait()
        self.local.wait()


class Chunk:
    @staticmethod
    def shapes(rows, wide):
        return ((2, 2 * rows, wide),) * 2 + ((2 * rows, wide),) * 2 + ((2, rows, wide), (rows, wide))

    def __init__(self, net, here, total, out, bufs, column, width):
        self.net, self.here, self.out = net, here, out
        self.total = total.at[:, span(column, width, 128)]
        self.block = total.shape[0] // 16
        self.column, self.width = column, width
        self.r1a, self.r1b, self.r2a, self.r2b, self.r3a, self.r3b, self.f32 = bufs

    def columns(self, core):
        return span(core * (self.out.shape[1] // 2) + self.column, self.width, 128)

    def upper(self, dp):
        return self.total.at[span(dp * 4 * self.block, 2 * self.block, 16)]

    def lower(self, dp):
        return self.total.at[span(dp * 4 * self.block + 2 * self.block, 2 * self.block, 16)]

    def add(self, total, extra):
        def body(rows):
            total[rows, :] = (total[rows, :].astype(F32) + extra[rows, :].astype(F32)).astype(BF16)

        by_rows(total.shape[0], body, 16)

    def first_diagonal(self):
        here, dp = self.here, self.here.peer_d()[0]
        self.wait_a = [self.net.send(self.upper(dp), self.r1a.at[1 - here.y], here.peer_x())]
        self.wait_b = [self.net.send(self.lower(dp), self.r1b.at[1 - here.x], here.peer_y())]

    def first_x(self):
        here, peer = self.here, self.here.peer_x()
        self.wait_a.append(self.net.send(self.upper(peer[0]), self.r1a.at[here.y], peer))

    def first_y(self):
        here, peer = self.here, self.here.peer_y()
        self.wait_b.append(self.net.send(self.lower(peer[0]), self.r1b.at[here.x], peer))

    def first(self):
        self.first_diagonal()
        self.first_x()
        self.first_y()

    def second(self):
        here = self.here
        for wait in self.wait_a:
            wait()
        away = self.upper((1 - here.y) * 2 + here.x)
        self.add(away, self.r1a.at[1 - here.y])
        next_a = self.net.send(away, self.r2a, here.peer_y())
        for wait in self.wait_b:
            wait()
        away = self.lower(here.y * 2 + 1 - here.x)
        self.add(away, self.r1b.at[1 - here.x])
        next_b = self.net.send(away, self.r2b, here.peer_x())
        self.add(self.upper(here.dp), self.r1a.at[here.y])
        self.add(self.lower(here.dp), self.r1b.at[here.x])
        self.wait_a, self.wait_b = next_a, next_b

    def mine(self, z):
        return self.total.at[span((self.here.dp * 4 + z) * self.block, self.block, 16)]

    def third(self):
        here = self.here
        self.wait_a()
        self.add(self.upper(here.dp), self.r2a)
        self.wait_b()
        self.add(self.lower(here.dp), self.r2b)
        odd = 1 - here.z % 2
        self.waits = [
            self.net.send(self.mine(odd + 2 * k), self.r3a.at[k], here.peer_z1()) for k in range(2)
        ]

    def fourth(self):
        here = self.here
        far = (here.z + 2) % Z_CHIPS
        for wait in self.waits:
            wait()
        self.add(self.mine(far), self.r3a.at[far // 2])
        self.wait = self.net.send(self.mine(far), self.r3b, here.peer_z2())
        self.add(self.mine(here.z), self.r3a.at[here.z // 2])

    def fifth(self):
        here = self.here
        self.wait()
        own = self.mine(here.z)

        def body(rows):
            self.f32[rows, :] = own[rows, :].astype(F32) + self.r3b[rows, :].astype(F32)

        by_rows(self.block, body, 16)
        self.pass_on()

    def pass_on(self):
        here = self.here
        part = self.block // 2
        self.wait = self.net.send(
            self.f32.at[span((1 - here.core) * part, part, 8)],
            self.out.at[:, self.columns(here.core)],
            here.peer_core(),
            self.out.at[:, self.columns(1 - here.core)],
        )
        self.out[:, self.columns(here.core)] = self.f32[span(here.core * part, part, 8), :]

    def end(self):
        self.wait()


class LastChunk(Chunk):
    @staticmethod
    def shapes(rows, wide):
        return ((2, 2 * rows, wide),) * 2 + ((2 * rows, wide),) * 2 + ((3, rows, wide), (16, 128))

    def third(self):
        here = self.here
        self.wait_a()
        self.add(self.upper(here.dp), self.r2a)
        self.wait_b()
        self.add(self.lower(here.dp), self.r2b)
        self.waits = [
            self.net.send(self.mine(here.z_of(k)), self.r3a.at[k - 1], here.peer_z(k))
            for k in range(1, Z_CHIPS)
        ]

    def fifth(self):
        for wait in self.waits:
            wait()
        own = self.mine(self.here.z)

        def body(rows):
            total = own[rows, :].astype(F32)
            for k in range(Z_CHIPS - 1):
                total += self.r3a[k, rows, :].astype(F32)
            self.f32[rows, :] = total

        by_rows(self.block, body, 16)
        self.pass_on()


class EarlyChunk(Chunk):
    @staticmethod
    def shapes(rows, wide):
        part = rows // 2
        return ((2, part, wide),) * 2 + ((part, wide),) * 2 + ((2, 4, rows, wide), (4, rows, wide))

    def __init__(self, net, here, total, out, bufs, column, width):
        super().__init__(net, here, total, out, bufs, column, width)
        half = self.block // 2
        self.halves = tuple((span(k * half, half, 16), slice(None)) for k in range(2))

    def at(self, dp, z):
        return self.total.at[span((dp * 4 + z) * self.block, self.block, 16)]

    def upper(self, dp):
        return self.at(dp, self.here.z).at[self.halves[0]]

    def lower(self, dp):
        return self.at(dp, self.here.z).at[self.halves[1]]

    def near(self):
        here = self.here
        odd = 1 - here.z % 2
        self.waits = [
            self.net.send(self.at(dp, odd + 2 * k), self.r3a.at[k, dp], here.peer_z1())
            for k in range(2)
            for dp in range(4)
        ]

    def far(self):
        here = self.here
        far = (here.z + 2) % Z_CHIPS
        for wait in self.waits:
            wait()
        self.waits = []
        for dp in range(4):
            self.add(self.at(dp, far), self.r3a.at[far // 2, dp])
            self.waits.append(self.net.send(self.at(dp, far), self.r3b.at[dp], here.peer_z2()))
        for dp in range(4):
            self.add(self.at(dp, here.z), self.r3a.at[here.z // 2, dp])

    def first(self):
        for wait in self.waits:
            wait()
        for dp in range(4):
            self.add(self.at(dp, self.here.z), self.r3b.at[dp])
        super().first()

    def fifth(self):
        here = self.here
        self.wait_a()
        self.wait_b()
        own = self.at(here.dp, here.z)
        for where, extra in zip(self.halves, (self.r2a, self.r2b)):
            part, target = own.at[where], self.f32.at[where]

            def body(rows):
                target[rows, :] = part[rows, :].astype(F32) + extra[rows, :].astype(F32)

            by_rows(part.shape[0], body, 16)
        self.pass_on()


def chunk_list(widths):
    cuts = (
        (3, (128, 128, 128), (Chunk, Chunk, EarlyChunk)),
        (2, (768, 768), (Chunk, Chunk)),
        (1, (384,), (Chunk,)),
        (0, (512, 384, 256), (LastChunk, LastChunk, LastChunk)),
    )
    chunks = []
    for index, parts, kinds in cuts:
        column = 0
        for part, kind in zip(parts, kinds):
            chunks.append((index, column, part, kind))
            column += part
        assert 2 * column == widths[index]
    return chunks


def layer_kernel(names, chunks, sizes, *refs):
    v = types.SimpleNamespace(**dict(zip(names, refs)))
    tokens, width, heads, hidden_width = sizes
    quarter = width // 4
    size = width // heads
    factor = size ** (-0.5)
    here = Place()
    core, dp = here.core, here.dp
    net = Net(v.send_sems, v.recv_sems)
    mine, theirs = slice(0, tokens), slice(tokens, 2 * tokens)

    here.greet()
    loads = []
    for number, (source, target) in enumerate(
        (
            (v.time_table, v.table_v), (v.w_token, v.token_v), (v.w_head, v.head_v), (v.w_ada, v.ada_v),
            (v.token_keep, v.keep_v), (v.head_keep, v.head_keep_v), (v.inputs, v.x_v), (v.cotangent, v.g_v),
            (v.time_index, v.index_v),
        )
    ):
        copy = pltpu.make_async_copy(source, target, v.local_sems.at[4 + number])
        copy.start()
        loads.append(copy)
    weights = [
        Weight(net, here, own, full)
        for own, full in ((v.wq, v.fq), (v.wo, v.fo), (v.wu, v.fu), (v.wd, v.fd))
    ]
    for number, weight in enumerate(weights):
        weight.keep(v.local_sems.at[number])
    w_q, w_o, w_u, w_d = weights
    select = (
        lax.broadcasted_iota(jnp.int32, (width, quarter), 0)
        == lax.broadcasted_iota(jnp.int32, (width, quarter), 1) + dp * quarter
    ).astype(F32).astype(BF16)
    loads[1].wait()
    token = jnp.broadcast_to(v.token_v[...].astype(F32).reshape(1, quarter), (16, quarter))
    placed = dot(token.astype(BF16), select, NT)
    loads[8].wait()
    loads[0].wait()
    rows = v.table_v.shape[0]
    whole = rows // 128 * 128
    index_row = jnp.broadcast_to(v.index_v[...], (16, whole))
    hot = (lax.broadcasted_iota(jnp.int32, (16, whole), 1) == index_row).astype(F32).astype(BF16)
    row = dot(hot, v.table_v[0:whole, :], NN)[0:1]
    rest = lax.broadcasted_iota(jnp.int32, (rows - whole, width), 0) + whole
    rest = jnp.where(
        rest == jnp.broadcast_to(v.index_v[...], rest.shape), v.table_v[whole:rows, :].astype(F32), 0.0
    )
    row += jnp.sum(rest, axis=0, keepdims=True)
    condition = (row * jax.nn.sigmoid(row)).astype(BF16).astype(F32)
    v.condition[...] = condition
    v.small_v[...] = jnp.zeros(v.small_v.shape, F32)
    for k in range(width // 128):
        v.small_v[k : k + 1, :] = condition[:, k * 128 : (k + 1) * 128]
        v.small_v[8 + k : 9 + k, :] = placed[0:1, k * 128 : (k + 1) * 128]
    here.meet()

    w_q.send_diagonal()
    waits = [
        net.send(v.small_v, v.cond_buf.at[dp], peer, v.cond_buf.at[peer[0]])
        for peer in here.dp_peers()
    ]
    w_q.send_straight()
    v.cond_buf[pl.ds(dp, 1)] = v.small_v[...][None]
    head_of = lax.broadcasted_iota(jnp.int32, (128, width), 0) * size
    lane = lax.broadcasted_iota(jnp.int32, (128, width), 1)
    v.expand[...] = ((lane >= head_of) & (lane < head_of + size)).astype(F32)
    for load in loads[2:6]:
        load.wait()
    diagonal = lax.broadcasted_iota(jnp.int32, (tokens, tokens), 0) == lax.broadcasted_iota(
        jnp.int32, (tokens, tokens), 1
    )
    v.keep[...] = jnp.sum(jnp.where(diagonal, v.keep_v[...].astype(F32), 0.0), axis=1, keepdims=True)
    v.head_mask[...] = jnp.zeros(v.head_mask.shape, F32)
    v.head_mask[:, 0:heads] = v.head_keep_v[...].astype(F32)
    v.part[...] = jnp.zeros(v.part.shape, F32)
    for wait in waits:
        wait()
    def wide(first):
        return jnp.concatenate([v.cond_buf[:, first + k, :] for k in range(width // 128)], axis=1)

    stacked = jnp.concatenate([wide(0), jnp.zeros((12, width), F32)], axis=0).astype(BF16)
    left = dot(stacked, select, NN).astype(BF16)
    for piece in range(7):
        if piece < 6:
            product = dot(left, v.ada_v[:, piece * width : (piece + 1) * width], NN)
        else:
            product = dot(left, v.head_v[...], NT)
        for image in range(4):
            v.part[image, piece : piece + 1, 0 : product.shape[1]] = product[image : image + 1]
    waits = [
        net.send(v.part.at[peer[0]], v.part_buf.at[index], peer)
        for index, peer in enumerate(here.dp_peers())
    ]
    for weight in weights[1:]:
        weight.send_diagonal()
    w_q.spread()
    v.token[...] = jnp.sum(wide(8), axis=0, keepdims=True)
    w_q.share_straight(0)
    w_q.share_straight(1)
    for weight in weights[1:]:
        weight.send_straight()
    w_o.spread()
    for wait in waits:
        wait()
    v.mod[...] = v.part[dp] + v.part_buf[0] + v.part_buf[1] + v.part_buf[2]
    head_sigmoid = jax.nn.sigmoid(v.mod[6:7, 0:128])
    head_mask = v.head_mask[...]
    gate = dot(jnp.broadcast_to(head_mask * head_sigmoid, (8, 128)), v.expand[...], NN, exact=True)
    v.gate_row[...] = gate[0:1]

    loads[6].wait()

    def first_norm(rows):
        values = v.x_v[rows, :].astype(F32)
        centre = values - jnp.mean(values, axis=1, keepdims=True)
        spread = jnp.mean(centre * centre, axis=1, keepdims=True)
        normal = centre * lax.rsqrt(spread + epsilon)
        v.nb[rows, :] = (normal * (1.0 + v.mod[1:2]) + v.mod[0:1]).astype(BF16)

    by_rows(tokens, first_norm)
    wait_normed = net.send(v.nb.at[mine], v.nb.at[theirs], here.peer_core())

    w_q.share_diagonal()
    w_u.spread()
    w_q.ready()

    @pl.loop(0, 3 * width // 384)
    def _(index):
        columns = span(index * 384, 384, 128)
        v.packed[:, columns] = dot(v.nb[mine, :], v.fq[:, columns], NN).astype(BF16)

    w_d.spread()

    lanes = lax.broadcasted_iota(jnp.int32, (1, 2 * size), 1)
    masks = ((lanes < size).astype(F32).astype(BF16), (lanes >= size).astype(F32).astype(BF16))
    scaled_masks = tuple(mask * jnp.asarray(factor, BF16) for mask in masks)
    low_lane = lax.broadcasted_iota(jnp.int32, (tokens, 2 * size), 1) < size

    def three(pair, block):
        return [block[:, span(part * width + pair * 2 * size, 2 * size, 128)] for part in range(3)]

    @pl.loop(0, heads // 2)
    def _(pair):
        queries, key_rows, value_rows = three(pair, v.packed)
        found = []
        for which in range(2):
            scores = dot(queries * scaled_masks[which], key_rows, NT)
            powers = jnp.exp(scores - jnp.max(scores, axis=1, keepdims=True))
            probs = powers * (1.0 / jnp.sum(powers, axis=1, keepdims=True))
            v.probs[pair * 2 + which] = probs
            found.append(dot(probs.astype(BF16), value_rows, NN))
        attended = jnp.where(low_lane, found[0], found[1])
        columns = span(pair * 2 * size, 2 * size, 128)
        v.attended[:, columns] = attended
        v.gated[mine, columns] = (attended * v.gate_row[:, columns]).astype(BF16)

    wait_gated = net.send(v.gated.at[mine], v.gated.at[theirs], here.peer_core())
    w_o.share_straight(0)
    w_o.share_straight(1)
    w_o.share_diagonal()
    w_o.ready()

    @pl.loop(0, width // 256)
    def _(index):
        columns = span(index * 256, 256, 128)
        v.branch[:, columns] = dot(v.gated[mine, :], v.fo[:, columns], NN)

    loads[7].wait()

    def second_norm(rows):
        middle = v.x_v[rows, :].astype(F32) + v.mod[2:3] * v.branch[rows, :]
        v.middle[rows, :] = middle
        centre = middle - jnp.mean(middle, axis=1, keepdims=True)
        spread = jnp.mean(centre * centre, axis=1, keepdims=True)
        scale = lax.rsqrt(spread + epsilon)
        normal = centre * scale
        v.z2[rows, :] = normal
        v.scale2[rows, :] = scale
        second = (normal * (1.0 + v.mod[4:5]) + v.mod[3:4]).astype(BF16)
        v.second[rows, :] = second
        logit = jnp.sum(second.astype(F32) * v.token[...], axis=1, keepdims=True)
        router = jax.nn.sigmoid(logit)
        v.router[rows, :] = router
        weight = v.keep[rows, :] * router
        v.grad_prod[rows, :] = (v.g_v[rows, :].astype(F32) * v.mod[5:6] * weight).astype(BF16)

    by_rows(tokens, second_norm)
    wait_second = net.send(v.second.at[mine], v.second.at[theirs], here.peer_core())
    half = width // 2
    other = span((1 - core) * half, half, 128)
    own = span(core * half, half, 128)
    wait_dprod = net.send(v.grad_prod.at[:, other], v.dy_down.at[theirs], here.peer_core())
    v.dy_down[mine, :] = v.grad_prod[:, own]

    w_u.share_straight(0)
    w_u.share_diagonal()
    w_u.share_straight(1)
    w_u.ready()
    inner = math.sqrt(2.0 / math.pi)

    wait_hidden = []
    for index in range(hidden_width // 512):
        columns = slice(index * 512, index * 512 + 512)
        v.tmp[:, 0:512] = dot(v.second[mine, :], v.fu[:, columns], NN)

        def bend(rows):
            u = v.tmp[rows, 0:512]
            square = u * u
            t = jnp.tanh(u * (inner + (inner * 0.044715) * square))
            a = 0.5 + 0.5 * t
            value = u * a
            v.hidden[rows, columns] = value.astype(BF16)
            v.slope[rows, columns] = a + value * (1.0 - a) * (2.0 * inner + (6.0 * inner * 0.044715) * square)

        by_rows(tokens, bend)
        if index % 2:
            done = slice(index * 512 - 512, index * 512 + 512)
            wait_hidden.append(
                net.send(v.hidden.at[mine, done], v.hidden.at[theirs, done], here.peer_core())
            )

    pieces = []
    for number, (index, column, wide, kind) in enumerate(chunks):
        total = (v.t_qkv, v.t_out, v.t_up, v.t_down)[index]
        out = (v.o_qkv, v.o_out, v.o_up, v.o_down)[index]
        bufs = [getattr(v, f"c{number}_{k}") for k in range(7)]
        pieces.append(kind(net, here, total, out, bufs, column, wide))
    c_down, c_next, c_early, c_up, c_more, c_out = pieces[:6]
    c_qkv = pieces[6:]

    def weight_grad(total, left, right, step):
        @pl.loop(0, total.shape[0] // step)
        def _(index):
            rows = span(index * step, step, 128)
            total[rows, :] = dot(left[:, rows], right[...], TN).astype(BF16)

    w_d.share_straight(0)
    for wait in wait_hidden:
        wait()
    wait_dprod()

    def down_quarter(place):
        @pl.loop(0, 3)
        def _(index):
            rows = span(place * width + index * 256, 256, 256)
            v.t_down[rows, :] = dot(v.hidden[:, rows], v.dy_down[...], TN).astype(BF16)

    down_quarter(here.peer_d()[0])
    c_down.first_diagonal()
    c_next.first_diagonal()
    down_quarter(here.peer_x()[0])
    c_down.first_x()
    c_next.first_x()
    down_quarter(here.peer_y()[0])
    c_down.first_y()
    c_next.first_y()
    down_quarter(dp)
    c_early.near()
    w_d.share_diagonal()
    w_d.share_straight(1)
    w_d.ready()

    wide_half = hidden_width // 2

    def bend_back(side):
        @pl.loop(0, wide_half // 512)
        def _(index):
            columns = span(side * wide_half + index * 512, 512, 128)
            back = dot(v.grad_prod[...], v.fd[columns, :], NT)
            v.grad_u[:, columns] = (back * v.slope[:, columns]).astype(BF16)

    bend_back(1 - core)
    wait_du = net.send(
        v.grad_u.at[:, span((1 - core) * wide_half, wide_half, 128)], v.dy_up.at[theirs], here.peer_core()
    )
    bend_back(core)
    v.dy_up[mine, :] = v.grad_u[:, span(core * wide_half, wide_half, 128)]
    c_down.second()
    c_next.second()
    wait_second()
    wait_du()
    weight_grad(v.t_up, v.second, v.dy_up, 256)
    c_up.first()
    c_more.first()

    @pl.loop(0, width // 256)
    def _(index):
        columns = span(index * 256, 256, 128)
        v.produced[:, columns] = dot(v.hidden[mine, :], v.fd[:, columns], NN).astype(BF16)

    v.sums[...] = jnp.zeros(v.sums.shape, F32)

    def finish(rows):
        produced = v.produced[rows, :].astype(F32)
        grad = v.g_v[rows, :].astype(F32)
        router, keep = v.router[rows, :], v.keep[rows, :]
        scaled = produced * (keep * router)
        v.output[rows, :] = (v.middle[rows, :] + v.mod[5:6] * scaled).astype(BF16)
        v.sums[0] += fold(grad * scaled)
        back = jnp.sum(grad * v.mod[5:6] * produced, axis=1, keepdims=True)
        v.logit[rows, :] = back * keep * router * (1.0 - router)

    by_rows(tokens, finish)
    c_early.far()
    c_down.third()
    c_next.third()

    @pl.loop(0, width // 256)
    def _(index):
        columns = span(index * 256, 256, 128)
        v.produced[:, columns] = dot(v.grad_u[...], v.fu[columns, :], NT).astype(BF16)

    def second_back(rows):
        logit = v.logit[rows, :]
        back = v.produced[rows, :].astype(F32) + logit * v.token[...]
        normal = v.z2[rows, :]
        v.sums[1] += fold(logit * v.second[rows, :].astype(F32))
        v.sums[2] += fold(back * normal)
        v.sums[3] += fold(back)
        inside = back * (1.0 + v.mod[4:5])
        level = jnp.mean(inside, axis=1, keepdims=True)
        slope = jnp.mean(inside * normal, axis=1, keepdims=True)
        grad = v.g_v[rows, :].astype(F32) + v.scale2[rows, :] * (inside - level - normal * slope)
        v.grad_mid[rows, :] = grad
        v.sums[4] += fold(grad * v.branch[rows, :])
        v.grad_branch[rows, :] = (v.mod[2:3] * grad).astype(BF16)

    by_rows(tokens, second_back)
    wait_dbranch = net.send(v.grad_branch.at[:, other], v.dy_out.at[theirs], here.peer_core())
    v.dy_out[mine, :] = v.grad_branch[:, own]

    @pl.loop(0, width // 256)
    def _(index):
        columns = span(index * 256, 256, 128)
        v.tmp[:, columns] = dot(v.grad_branch[...], v.fo[columns, :], NT)

    wait_gated()
    wait_dbranch()
    weight_grad(v.t_out, v.gated, v.dy_out, 256)
    c_out.first()

    def gate_back(rows):
        grad = v.tmp[rows, :]
        v.sums[5] += fold(grad * v.attended[rows, :])
        v.grad_att[rows, :] = (grad * v.gate_row[...]).astype(BF16)

    by_rows(tokens, gate_back)

    def gather_far(piece, block):
        block[pl.ds(core, 1), pl.ds(here.z, 1), pl.ds(dp, 1)] = piece[...][None, None, None]
        far = (here.z + 2) % Z_CHIPS
        return [net.send(piece, block.at[core, here.z, dp], here.peer_z2(), block.at[core, far, dp])]

    def gather_near(block, waits):
        for wait in waits:
            wait()
        near = here.z + 1 - 2 * (here.z % 2)
        moves = []
        for k in range(2):
            z, other = (here.z + 2 * k) % Z_CHIPS, (near + 2 * k) % Z_CHIPS
            tile = block.at[core, z, dp]
            moves.append(net.send(tile, tile, here.peer_z1(), block.at[core, other, dp]))
        return moves

    def gather_dp(block, waits):
        for wait in waits:
            wait()
        tiles = block.at[core, pl.ds(0, Z_CHIPS), dp]
        return [
            net.send(tiles, tiles, peer, block.at[core, pl.ds(0, Z_CHIPS), peer[0]])
            for peer in here.dp_peers()
        ]

    one_way = (dp + (1 - core) * (1 - 2 * here.x) + core * (2 - 4 * here.y), here.seq)
    other_way = (dp + core * (1 - 2 * here.x) + (1 - core) * (2 - 4 * here.y), here.seq)

    def gather_one(block, waits):
        for wait in waits:
            wait()
        tiles = block.at[core, pl.ds(0, Z_CHIPS), dp]
        return [net.send(tiles, tiles, one_way, block.at[core, pl.ds(0, Z_CHIPS), one_way[0]])]

    def gather_two(block, waits):
        for wait in waits:
            wait()
        moves = []
        for mine_dp, their_dp in ((dp, other_way[0]), (one_way[0], here.peer_d()[0])):
            tiles = block.at[core, pl.ds(0, Z_CHIPS), mine_dp]
            moves.append(
                net.send(tiles, tiles, other_way, block.at[core, pl.ds(0, Z_CHIPS), their_dp])
            )
        return moves

    def gather_pair(block, waits):
        for wait in waits:
            wait()
        return net.send(block.at[core], block.at[core], here.peer_core(), block.at[1 - core])

    head_back = dot(
        jnp.broadcast_to(jnp.sum(v.sums[5], axis=0, keepdims=True), (8, width)), v.expand[...], NT, exact=True
    )
    head_back = head_back[0:1] * head_mask * head_sigmoid * (1.0 - head_sigmoid)
    v.early_f[...] = jnp.zeros(v.early_f.shape, F32)
    rows_out = [jnp.sum(v.sums[k], axis=0, keepdims=True) for k in (4, 3, 2, 0, 1)]
    cut = width // 2
    for slot, values in zip((0, 1, 2, 3, 5, 6), (*rows_out, v.condition[...])):
        v.early_f[2 * slot : 2 * slot + 1, :] = values[:, 0:cut]
        v.early_f[2 * slot + 1 : 2 * slot + 2, :] = values[:, cut:width]
    v.early_f[8:9, 0:128] = head_back
    v.early_out[...] = v.early_f[...].astype(BF16)
    early = gather_far(v.early_out, v.early)
    c_up.second()

    def back_pair(pair):
        queries, key_rows, value_rows = three(pair, v.packed)
        columns = span(pair * 2 * size, 2 * size, 128)
        grad_att = v.grad_att[:, columns]
        gq, gk, gv = [], [], []
        for which in range(2):
            probs = v.probs[pair * 2 + which]
            grad_probs = dot(grad_att * masks[which], value_rows, NT)
            level = jnp.sum(probs * grad_probs, axis=1, keepdims=True)
            grad_scores = (probs * (grad_probs - level)).astype(BF16)
            gq.append(dot(grad_scores, key_rows, NN))
            gk.append(dot(grad_scores, queries, TN))
            gv.append(dot(probs.astype(BF16), grad_att, TN))
        for part, (grads, scale) in enumerate(((gq, factor), (gk, factor), (gv, 1.0))):
            both = jnp.where(low_lane, grads[0], grads[1]) * scale
            v.grad_pack[:, span(part * width + pair * 2 * size, 2 * size, 128)] = both.astype(BF16)

    pl.loop(0, heads // 2)(back_pair)
    packed_half = 3 * width // 2
    wait_dpack = net.send(
        v.grad_pack.at[:, span((1 - core) * packed_half, packed_half, 128)],
        v.dy_qkv.at[theirs],
        here.peer_core(),
    )
    v.dy_qkv[mine, :] = v.grad_pack[:, span(core * packed_half, packed_half, 128)]
    c_down.fourth()
    c_next.fourth()
    c_early.first()
    c_more.second()
    early = gather_near(v.early, early)
    wait_normed()
    wait_dpack()
    weight_grad(v.t_qkv, v.nb, v.dy_qkv, 256)
    c_out.second()
    early = gather_one(v.early, early)
    c_qkv[0].first()
    c_qkv[1].first()


    @pl.loop(0, width // 256)
    def _(index):
        columns = span(index * 256, 256, 128)
        v.tmp[:, columns] = dot(v.grad_pack[...], v.fq[columns, :], NT)

    c_up.third()

    def first_back(rows):
        back = v.tmp[rows, :]
        values = v.x_v[rows, :].astype(F32)
        centre = values - jnp.mean(values, axis=1, keepdims=True)
        spread = jnp.mean(centre * centre, axis=1, keepdims=True)
        scale = lax.rsqrt(spread + epsilon)
        normal = centre * scale
        v.sums[6] += fold(back * normal)
        v.sums[7] += fold(back)
        inside = back * (1.0 + v.mod[1:2])
        level = jnp.mean(inside, axis=1, keepdims=True)
        slope = jnp.mean(inside * normal, axis=1, keepdims=True)
        v.grad_input[rows, :] = v.grad_mid[rows, :] + scale * (inside - level - normal * slope)

    by_rows(tokens, first_back)
    shift = jnp.sum(v.sums[7], axis=0, keepdims=True)
    scale = jnp.sum(v.sums[6], axis=0, keepdims=True)
    v.late_f[...] = jnp.zeros(v.late_f.shape, F32)
    for k in range(width // 128):
        v.late_f[k : k + 1, :] = shift[:, k * 128 : (k + 1) * 128]
        v.late_f[8 + k : 9 + k, :] = scale[:, k * 128 : (k + 1) * 128]
    v.late_out[...] = v.late_f[...].astype(BF16)
    late = gather_far(v.late_out, v.late)
    c_more.third()
    early = gather_two(v.early, early)
    c_up.fourth()
    c_early.second()
    c_out.third()
    late = gather_near(v.late, late)
    c_more.fourth()
    c_qkv[0].second()
    c_qkv[2].first()
    c_out.fourth()
    early = gather_pair(v.early, early)
    late = gather_dp(v.late, late)
    c_down.fifth()
    c_next.fifth()
    c_qkv[1].second()
    c_up.fifth()
    c_early.fifth()
    c_qkv[0].third()
    c_qkv[2].second()
    c_more.fifth()
    c_out.fifth()
    early()
    offset = dp * quarter + (here.seq % BLOCK) * SHARE
    pick = (
        lax.broadcasted_iota(jnp.int32, (width, SHARE), 0)
        == lax.broadcasted_iota(jnp.int32, (width, SHARE), 1) + offset
    ).astype(F32)
    late = gather_pair(v.late, late)
    c_qkv[1].third()
    c_qkv[2].third()

    every = v.early[...].reshape(512, cut).astype(F32).reshape(32, 16, cut)
    conditions = (
        dot(every[:, 12, :].astype(BF16), pick[0:cut].astype(BF16), NN)
        + dot(every[:, 13, :].astype(BF16), pick[cut:width].astype(BF16), NN)
    ).astype(BF16)
    for slot, piece in enumerate((2, 3, 4, 5)):
        for side in range(2):
            start = piece * width + side * cut
            v.o_ada[:, start : start + cut] = dot(
                conditions, every[:, 2 * slot + side, :].astype(BF16), TN
            )
    v.o_head[...] = dot(every[:, 8, 0:128].astype(BF16), conditions, TN)[0:heads]
    totals = [jnp.sum(every[:, 10 + side, :], axis=0, keepdims=True) for side in range(2)]
    v.o_token[...] = (
        dot(jnp.broadcast_to(totals[0], (8, cut)), pick[0:cut], NN, exact=True)
        + dot(jnp.broadcast_to(totals[1], (8, cut)), pick[cut:width], NN, exact=True)
    )[0:1]

    c_qkv[0].fifth()
    c_qkv[1].fifth()
    for chunk in (c_down, c_next, c_early, c_up, c_more):
        chunk.end()
    late()
    tail = v.late[...].reshape(512, 128).astype(F32).reshape(32, 16, 128)
    for base in (0, 8):
        row = jnp.concatenate([tail[:, base + k, :] for k in range(width // 128)], axis=1)
        start = base // 8 * width
        v.o_ada[:, start : start + width] = dot(conditions, row.astype(BF16), TN)
    c_qkv[2].fifth()
    for chunk in (c_out, *c_qkv):
        chunk.end()
    net.finish()


def layer(time_table, time_index, w_token, w_head, token_keep, head_keep, inputs, cotangent, w_ada, wq, wo, wu, wd):
    tokens, width = inputs.shape
    hidden_width = wu.shape[1]
    heads = head_keep.shape[1]
    widths = [wq.shape[1], wo.shape[1], wu.shape[1], wd.shape[1]]
    depths = [4 * w.shape[0] for w in (wq, wo, wu, wd)]
    chunks = chunk_list(widths)
    operands = dict(
        time_table=time_table, time_index=time_index, w_token=w_token, w_head=w_head, token_keep=token_keep, head_keep=head_keep,
        inputs=inputs, cotangent=cotangent, w_ada=w_ada, wq=wq, wo=wo, wu=wu, wd=wd,
    )
    outs = dict(
        ada=((SHARE, 6 * width), F32),
        qkv=((depths[0] // 32, widths[0]), F32),
        out=((depths[1] // 32, widths[1]), F32),
        up=((depths[2] // 32, widths[2]), F32),
        down=((depths[3] // 32, widths[3]), F32),
        head=((heads, SHARE), F32),
        token=((1, SHARE), F32),
    )
    results = dict(output=((tokens, width), BF16), grad_input=((tokens, width), F32))
    results.update({"o_" + k: s for k, s in outs.items()})
    space = dict(
        table_v=(time_table.shape, BF16),
        index_v=(time_index.shape, jnp.int32),
        small_v=((16, 128), F32),
        condition=((1, width), F32),
        token_v=(w_token.shape, BF16),
        keep_v=(token_keep.shape, jnp.int32),
        head_keep_v=(head_keep.shape, jnp.int32),
        head_mask=((1, 128), F32),
        head_v=(w_head.shape, BF16),
        ada_v=(w_ada.shape, BF16),
        x_v=((tokens, width), BF16),
        g_v=((tokens, width), BF16),
        fq=((depths[0], widths[0]), BF16),
        fo=((depths[1], widths[1]), BF16),
        fu=((depths[2], widths[2]), BF16),
        fd=((depths[3], widths[3]), BF16),
        cond_buf=((4, 16, 128), F32),
        part=((4, 8, width), F32),
        part_buf=((3, 8, width), F32),
        mod=((8, width), F32),
        token=((1, width), F32),
        keep=((tokens, 1), F32),
        expand=((128, width), F32),
        gate_row=((1, width), F32),
        nb=((2 * tokens, width), BF16),
        packed=((tokens, 3 * width), BF16),
        probs=((heads, tokens, tokens), F32),
        attended=((tokens, width), F32),
        gated=((2 * tokens, width), BF16),
        branch=((tokens, width), F32),
        middle=((tokens, width), F32),
        z2=((tokens, width), F32),
        scale2=((tokens, 1), F32),
        second=((2 * tokens, width), BF16),
        router=((tokens, 1), F32),
        logit=((tokens, 1), F32),
        grad_prod=((tokens, width), BF16),
        dy_down=((2 * tokens, width // 2), BF16),
        tmp=((tokens, width), F32),
        hidden=((2 * tokens, hidden_width), BF16),
        slope=((tokens, hidden_width), F32),
        grad_u=((tokens, hidden_width), BF16),
        dy_up=((2 * tokens, hidden_width // 2), BF16),
        produced=((tokens, width), BF16),
        grad_mid=((tokens, width), F32),
        grad_branch=((tokens, width), BF16),
        dy_out=((2 * tokens, width // 2), BF16),
        grad_att=((tokens, width), BF16),
        grad_pack=((tokens, 3 * width), BF16),
        dy_qkv=((2 * tokens, 3 * width // 2), BF16),
        sums=((8, 8, width), F32),
        early_f=((16, width // 2), F32),
        early_out=((16, width // 2), BF16),
        early=((2, Z_CHIPS, 4, 16, width // 2), BF16),
        late_f=((16, 128), F32),
        late_out=((16, 128), BF16),
        late=((2, Z_CHIPS, 4, 16, 128), BF16),
        t_qkv=((depths[0], widths[0] // 2), BF16),
        t_out=((depths[1], widths[1] // 2), BF16),
        t_up=((depths[2], widths[2] // 2), BF16),
        t_down=((depths[3], widths[3] // 2), BF16),
    )
    for number, (index, _, wide, kind) in enumerate(chunks):
        shapes = kind.shapes(depths[index] // 16, wide)
        for k, shape in enumerate(shapes):
            space[f"c{number}_{k}"] = (shape, BF16)
        space[f"c{number}_6"] = ((depths[index] // 16, wide), F32)
    copies = 6 + 4 * 13 + 12 + len(chunks) * 12 + 2 * 12 + 14
    names = list(operands) + list(results) + list(space) + ["send_sems", "recv_sems", "local_sems"]
    return pl.pallas_call(
        functools.partial(layer_kernel, names, chunks, (tokens, width, heads, hidden_width)),
        out_shape=[pltpu.VMEM(*r) for r in results.values()],
        in_specs=[ANY] * len(operands),
        out_specs=[VMEM] * len(results),
        scratch_shapes=[pltpu.VMEM(*s) for s in space.values()]
        + [
            pltpu.SemaphoreType.DMA((copies,)),
            pltpu.SemaphoreType.DMA((copies,)),
            pltpu.SemaphoreType.DMA((13,)),
        ],
        compiler_params=pltpu.CompilerParams(
            collective_id=0, has_side_effects=True, vmem_limit_bytes=61 * 2**20
        ),
    )(*operands.values())


def copy_kernel(count, *refs):
    copies = [
        pltpu.make_async_copy(refs[k], refs[count + k], refs[2 * count].at[k]) for k in range(count)
    ]
    for copy in copies:
        copy.start()
    for copy in copies:
        copy.wait()


def copy_all(arrays):
    count = len(arrays)
    return pl.pallas_call(
        functools.partial(copy_kernel, count),
        out_shape=[jax.ShapeDtypeStruct(a.shape, a.dtype) for a in arrays],
        in_specs=[VMEM] * count,
        out_specs=[ANY] * count,
        scratch_shapes=[pltpu.SemaphoreType.DMA((count,))],
        compiler_params=pltpu.CompilerParams(vmem_limit_bytes=16 * 2**20),
    )(*(pltpu.with_memory_space_constraint(a, pltpu.VMEM) for a in arrays))


def across_blocks(part, seq_size):
    blocks = seq_size // BLOCK
    if blocks == 1:
        return part
    groups = [[b * BLOCK + j for b in range(blocks)] for j in range(BLOCK)]
    mine = lax.psum_scatter(
        part, "seq", scatter_dimension=0, axis_index_groups=groups, tiled=True
    )
    moves = [(b * BLOCK + j, j * blocks + b) for b in range(blocks) for j in range(BLOCK)]
    return lax.ppermute(mine, "seq", moves)


def per_device(
    seq_size, inputs, time_table, time_index, token_keep, head_keep, cotangent,
    w_ada, w_qkv, w_out, w_up, w_down, w_head, w_token,
):
    out = layer(
        time_table, time_index[None], w_token, w_head.T, token_keep, head_keep,
        inputs[0], cotangent[0], w_ada, w_qkv, w_out, w_up, w_down,
    )
    output, grad_input, ada, qkv, outw, up, down, head, token = copy_all(out)
    parts = (ada, qkv, outw, up, down, head.T, token[0])
    parts = tuple(across_blocks(part, seq_size) for part in parts)
    return (output[None], grad_input[None]) + parts


def solution(mesh):
    both = ("dp", "seq")
    in_specs = (
        P(both, None, None), P(), P(both), P(both, None), P(both, None), P(both, None, None),
        P("dp", None), P("dp", None), P("dp", None), P("dp", None), P("dp", None), P("dp", None), P("dp"),
    )
    out_specs = (P(both, None, None), P(both, None, None)) + (P(both, None),) * 6 + (P(both),)
    return jax.shard_map(
        functools.partial(per_device, mesh.shape["seq"]),
        mesh=mesh, in_specs=in_specs, out_specs=out_specs, check_vma=False,
    )
```

```python
import functools
import math
import types

import jax
import jax.numpy as jnp
from jax import lax
from jax.experimental import pallas as pl
from jax.experimental.pallas import tpu as pltpu
from jax.sharding import PartitionSpec as P

epsilon = 1e-06
MESH = pl.DeviceIdType.MESH
ANY = pl.BlockSpec(memory_space=pl.ANY)
VMEM = pl.BlockSpec(memory_space=pltpu.VMEM)
Z_CHIPS = 4
BLOCK = 2 * Z_CHIPS
F32, BF16 = jnp.float32, jnp.bfloat16
NN, NT, TN = ((1,), (0,)), ((1,), (1,)), ((0,), (0,))
ROWS = 32
SHARE = 24


def dot(left, right, dims, exact=False):
    return lax.dot_general(
        left, right, (dims, ((), ())), preferred_element_type=F32,
        precision=lax.Precision.HIGHEST if exact else None,
    )


def span(start, size, unit):
    return pl.ds(pl.multiple_of(start, unit), size)


def by_rows(total, body, step=ROWS):
    @pl.loop(0, total // step)
    def _(index):
        body(span(index * step, step, step))


def fold(values):
    return jnp.sum(values.reshape(-1, 8, values.shape[-1]), axis=0)


class Place:
    def __init__(self):
        self.dp = lax.axis_index("dp")
        self.seq = lax.axis_index("seq")
        self.x = self.dp % 2
        self.y = self.dp // 2
        self.core = self.seq % 2
        self.z = (self.seq // 2) % Z_CHIPS
        self.side = self.z % 2
        self.high = self.z // 2
        self.outer = self.seq // BLOCK

    def z_of(self, step):
        return (self.z + step) % Z_CHIPS

    def peer_x(self):
        return (self.y * 2 + 1 - self.x, self.seq)

    def peer_y(self):
        return ((1 - self.y) * 2 + self.x, self.seq)

    def peer_d(self):
        return ((1 - self.y) * 2 + 1 - self.x, self.seq)

    def peer_core(self):
        return (self.dp, self.seq + 1 - 2 * self.core)

    def peer_z(self, step):
        return (self.dp, self.outer * BLOCK + self.z_of(step) * 2 + self.core)

    def peer_z1(self):
        return (self.dp, self.seq + 2 - 4 * (self.z % 2))

    def peer_z2(self):
        return (self.dp, self.seq + 4 - 8 * (self.z // 2))

    def dp_peers(self):
        return (self.peer_x(), self.peer_y(), self.peer_d())

    def greet(self):
        peers = list(self.dp_peers()) + [self.peer_core()]
        for k in range(1, Z_CHIPS):
            same = self.peer_z(k)
            peers += [same, (same[0], same[1] + 1 - 2 * self.core)]
        for peer in peers:
            pl.semaphore_signal(
                pltpu.get_barrier_semaphore(), inc=1, device_id=peer, device_id_type=MESH
            )
        self.peers = len(peers)

    def meet(self):
        pl.semaphore_wait(pltpu.get_barrier_semaphore(), self.peers)


class Net:
    def __init__(self, send_sems, recv_sems):
        self.send_sems = send_sems
        self.recv_sems = recv_sems
        self.used = 0
        self.sent = []

    def send(self, src, dst, peer, landing=None):
        slot = self.used
        self.used += 1

        def copy_to(target):
            return pltpu.make_async_remote_copy(
                src_ref=src,
                dst_ref=target,
                send_sem=self.send_sems.at[slot],
                recv_sem=self.recv_sems.at[slot],
                device_id=peer,
                device_id_type=MESH,
            )

        copy = copy_to(dst)
        copy.start()
        self.sent.append(copy)
        arrival = copy if landing is None else copy_to(landing)
        return arrival.wait_recv

    def plan(self, src, dst, peer):
        slot = self.used
        self.used += 1
        return pltpu.make_async_remote_copy(
            src_ref=src,
            dst_ref=dst,
            send_sem=self.send_sems.at[slot],
            recv_sem=self.recv_sems.at[slot],
            device_id=peer,
            device_id_type=MESH,
        )

    def finish(self):
        for copy in self.sent:
            copy.wait_send()


class Weight:
    def __init__(self, net, here, own, full):
        self.net, self.here, self.own, self.full = net, here, own, full
        self.depth = own.shape[0]
        self.piece = self.depth // Z_CHIPS
        self.width = own.shape[1] // 2

    def columns(self, core):
        return span(core * self.width, self.width, 128)

    def quarter(self, dp):
        return span(dp * self.depth, self.depth, 16)

    def part(self, dp, z):
        return span(dp * self.depth + z * self.piece, self.piece, 16)

    def keep(self, sem):
        self.local = pltpu.make_async_copy(self.own, self.full.at[self.quarter(self.here.dp)], sem)
        self.local.start()

    def send_diagonal(self):
        here, columns = self.here, self.columns(self.here.core)
        peer = here.peer_d()
        self.wait_d = self.net.send(
            self.own.at[span(here.z * self.piece, self.piece, 16), columns],
            self.full.at[self.part(here.dp, here.z), columns],
            peer,
            self.full.at[self.part(peer[0], here.z), columns],
        )

    def rows(self, dp, side):
        half = self.depth // 2
        return span(dp * self.depth + side * half, half, 16)

    def send_straight(self):
        here, columns = self.here, self.columns(self.here.core)
        self.wait_xy = [
            [
                self.net.send(
                    self.own.at[self.rows(0, side), columns],
                    self.full.at[self.rows(here.dp, side), columns],
                    peer,
                    self.full.at[self.rows(peer[0], side), columns],
                )
                for peer in (here.peer_x(), here.peer_y())
            ]
            for side in range(2)
        ]
        self.last = []

    def spread(self):
        here, columns = self.here, self.columns(self.here.core)
        diagonal = here.peer_d()[0]
        self.wait_d()
        piece = self.full.at[self.part(diagonal, here.z), columns]
        self.wait_z = [
            self.net.send(
                piece, piece, here.peer_z(step),
                self.full.at[self.part(diagonal, here.z_of(Z_CHIPS - step)), columns],
            )
            for step in range(1, Z_CHIPS)
        ]

    def hand(self, rows):
        here = self.here
        block = self.full.at[rows, self.columns(here.core)]
        landing = self.full.at[rows, self.columns(1 - here.core)]
        self.last.append(self.net.send(block, block, here.peer_core(), landing))

    def share_straight(self, side):
        here = self.here
        for wait, peer in zip(self.wait_xy[side], (here.peer_x(), here.peer_y())):
            wait()
            self.hand(self.rows(peer[0], side))

    def share_diagonal(self):
        for wait in self.wait_z:
            wait()
        self.hand(self.quarter(self.here.peer_d()[0]))

    def ready(self):
        for wait in self.last:
            wait()
        self.local.wait()


class HalfWeight(Weight):
    def __init__(self, net, here, own, full, by_columns):
        self.net, self.here, self.own, self.full, self.by_columns = net, here, own, full, by_columns
        self.last = []

    def source(self, part):
        here = self.here
        if self.by_columns:
            return self.own.at[:, span((2 * here.core + part) * 768 + here.side * 384, 384, 128)]
        return self.own.at[span(here.side * 384 + part * 192, 192, 16), span(here.core * 384, 384, 128)]

    def block(self, dp, part, core):
        if self.by_columns:
            return self.full.at[span(dp * 192, 192, 16), span((2 * core + part) * 384, 384, 128)]
        return self.full.at[span(dp * 384 + part * 192, 192, 16), span(core * 384, 384, 128)]

    def whole(self, dp, core):
        if self.by_columns:
            return self.full.at[span(dp * 192, 192, 16), span(core * 768, 768, 128)]
        return self.full.at[span(dp * 384, 384, 16), span(core * 384, 384, 128)]

    def keep(self, sems):
        dp, side = self.here.dp, self.here.side
        if self.by_columns:
            moves = [
                (
                    self.own.at[:, span(k * 768 + side * 384, 384, 128)],
                    self.full.at[span(dp * 192, 192, 16), span(k * 384, 384, 128)],
                )
                for k in range(4)
            ]
        else:
            moves = [(self.own.at[span(side * 384, 384, 16)], self.full.at[span(dp * 384, 384, 16)])]
        self.locals = [
            pltpu.make_async_copy(source, target, sem) for (source, target), sem in zip(moves, sems)
        ]
        for copy in self.locals:
            copy.start()

    def send_diagonal(self):
        here = self.here
        peer = here.peer_d()
        self.wait_d = self.net.send(
            self.source(here.high),
            self.block(here.dp, here.high, here.core),
            peer,
            self.block(peer[0], here.high, here.core),
        )

    def send_straight(self):
        here = self.here
        self.wait_xy = [
            [
                self.net.send(
                    self.source(part),
                    self.block(here.dp, part, here.core),
                    peer,
                    self.block(peer[0], part, here.core),
                )
                for peer in (here.peer_x(), here.peer_y())
            ]
            for part in range(2)
        ]

    def spread(self):
        here = self.here
        diagonal = here.peer_d()[0]
        self.wait_d()
        piece = self.block(diagonal, here.high, here.core)
        self.wait_z = [
            self.net.send(
                piece, piece, here.peer_z2(), self.block(diagonal, 1 - here.high, here.core)
            )
        ]

    def pass_core(self, block, landing):
        self.last.append(self.net.send(block, block, self.here.peer_core(), landing))

    def share_straight(self, part):
        here = self.here
        for wait, peer in zip(self.wait_xy[part], (here.peer_x(), here.peer_y())):
            wait()
            self.pass_core(self.block(peer[0], part, here.core), self.block(peer[0], part, 1 - here.core))

    def share_diagonal(self):
        here = self.here
        diagonal = here.peer_d()[0]
        for wait in self.wait_z:
            wait()
        self.pass_core(self.whole(diagonal, here.core), self.whole(diagonal, 1 - here.core))

    def ready(self):
        for wait in self.last:
            wait()
        for copy in self.locals:
            copy.wait()


class Chunk:
    @staticmethod
    def shapes(rows, wide):
        return ((2, 2 * rows, wide),) * 2 + ((2 * rows, wide),) * 2 + ((2, rows, wide), (rows, wide))

    def __init__(self, net, here, total, out, bufs, column, width):
        self.net, self.here, self.out = net, here, out
        self.total = total.at[:, span(column, width, 128)]
        self.block = total.shape[0] // 16
        self.column, self.width = column, width
        self.r1a, self.r1b, self.r2a, self.r2b, self.r3a, self.r3b, self.f32 = bufs

    @staticmethod
    def sums(rows, wide):
        return (rows, wide)

    def columns(self, core):
        return span(core * (self.out.shape[1] // 2) + self.column, self.width, 128)

    def upper(self, dp):
        return self.total.at[span(dp * 4 * self.block, 2 * self.block, 16)]

    def lower(self, dp):
        return self.total.at[span(dp * 4 * self.block + 2 * self.block, 2 * self.block, 16)]

    def add(self, total, extra):
        def body(rows):
            total[rows, :] = (total[rows, :].astype(F32) + extra[rows, :].astype(F32)).astype(BF16)

        by_rows(total.shape[0], body, 16)

    def first_diagonal(self):
        here, dp = self.here, self.here.peer_d()[0]
        self.wait_a = [self.net.send(self.upper(dp), self.r1a.at[1 - here.y], here.peer_x())]
        self.wait_b = [self.net.send(self.lower(dp), self.r1b.at[1 - here.x], here.peer_y())]

    def first_x(self):
        here, peer = self.here, self.here.peer_x()
        self.wait_a.append(self.net.send(self.upper(peer[0]), self.r1a.at[here.y], peer))

    def first_y(self):
        here, peer = self.here, self.here.peer_y()
        self.wait_b.append(self.net.send(self.lower(peer[0]), self.r1b.at[here.x], peer))

    def first(self):
        self.first_diagonal()
        self.first_x()
        self.first_y()

    def second(self):
        here = self.here
        for wait in self.wait_a:
            wait()
        away = self.upper((1 - here.y) * 2 + here.x)
        self.add(away, self.r1a.at[1 - here.y])
        next_a = self.net.send(away, self.r2a.at[span(0, away.shape[0], 16)], here.peer_y())
        for wait in self.wait_b:
            wait()
        away = self.lower(here.y * 2 + 1 - here.x)
        self.add(away, self.r1b.at[1 - here.x])
        next_b = self.net.send(away, self.r2b, here.peer_x())
        self.add(self.upper(here.dp), self.r1a.at[here.y])
        self.add(self.lower(here.dp), self.r1b.at[here.x])
        self.wait_a, self.wait_b = next_a, next_b

    def mine(self, z):
        return self.total.at[span((self.here.dp * 4 + z) * self.block, self.block, 16)]

    def third(self):
        here = self.here
        self.wait_a()
        self.add(self.upper(here.dp), self.r2a)
        self.wait_b()
        self.add(self.lower(here.dp), self.r2b)
        odd = 1 - here.z % 2
        self.waits = [
            self.net.send(self.mine(odd + 2 * k), self.r3a.at[k], here.peer_z1()) for k in range(2)
        ]

    def fourth(self):
        here = self.here
        far = (here.z + 2) % Z_CHIPS
        for wait in self.waits:
            wait()
        self.add(self.mine(far), self.r3a.at[far // 2])
        self.wait = self.net.send(self.mine(far), self.r3b, here.peer_z2())
        self.add(self.mine(here.z), self.r3a.at[here.z // 2])

    def fifth(self):
        here = self.here
        self.wait()
        own = self.mine(here.z)

        def body(rows):
            self.f32[rows, :] = own[rows, :].astype(F32) + self.r3b[rows, :].astype(F32)

        by_rows(self.block, body, 16)
        self.pass_on()

    def pass_on(self):
        here = self.here
        part = self.block // 2
        self.wait = self.net.send(
            self.f32.at[span((1 - here.core) * part, part, 8)],
            self.out.at[:, self.columns(here.core)],
            here.peer_core(),
            self.out.at[:, self.columns(1 - here.core)],
        )
        self.out[:, self.columns(here.core)] = self.f32[span(here.core * part, part, 8), :]

    def end(self):
        self.wait()


class LastChunk(Chunk):
    @staticmethod
    def shapes(rows, wide):
        return ((2, 2 * rows, wide),) * 2 + ((2 * rows, wide),) * 2 + ((3, rows, wide), (16, 128))

    def third(self):
        here = self.here
        self.wait_a()
        self.add(self.upper(here.dp), self.r2a)
        self.wait_b()
        self.add(self.lower(here.dp), self.r2b)
        self.waits = [
            self.net.send(self.mine(here.z_of(k)), self.r3a.at[k - 1], here.peer_z(k))
            for k in range(1, Z_CHIPS)
        ]

    def fifth(self):
        for wait in self.waits:
            wait()
        own = self.mine(self.here.z)

        def body(rows):
            total = own[rows, :].astype(F32)
            for k in range(Z_CHIPS - 1):
                total += self.r3a[k, rows, :].astype(F32)
            self.f32[rows, :] = total

        by_rows(self.block, body, 16)
        self.pass_on()


class UpChunk(Chunk):
    @staticmethod
    def shapes(rows, wide):
        return ((2, 2 * rows, wide),) * 2 + ((2 * rows, wide),) * 2 + ((2, rows, wide), (2, rows, wide))

    @staticmethod
    def sums(rows, wide):
        return (2, rows, wide)

    def fourth(self):
        here = self.here
        far = (here.z + 2) % Z_CHIPS
        for wait in self.waits:
            wait()
        self.waits = [
            self.net.send(self.mine(far), self.r3b.at[0], here.peer_z2()),
            self.net.send(self.r3a.at[1 - here.high], self.r3b.at[1], here.peer_z2()),
        ]

    def place(self, core, side):
        return span((2 * core + self.column // self.width) * 768 + side * 384, 384, 128)

    def fifth(self):
        here = self.here
        for wait in self.waits:
            wait()
        part = self.block // 2
        self.waits = []
        for k, (own, side) in enumerate(
            ((self.mine(here.z), here.side), (self.r3a.at[here.high], 1 - here.side))
        ):

            def body(rows):
                self.f32[k, rows, :] = own[rows, :].astype(F32) + self.r3b[k, rows, :].astype(F32)

            by_rows(self.block, body, 16)
            self.waits.append(
                self.net.send(
                    self.f32.at[k, span((1 - here.core) * part, part, 8)],
                    self.out.at[:, self.place(here.core, side)],
                    here.peer_core(),
                    self.out.at[:, self.place(1 - here.core, side)],
                )
            )
            self.out[:, self.place(here.core, side)] = self.f32[k, span(here.core * part, part, 8), :]

    def end(self):
        for wait in self.waits:
            wait()


class DownChunk(Chunk):
    @staticmethod
    def shapes(rows, wide):
        return ((3, rows, wide), (2, rows, wide)) + ((2 * rows, wide), (rows, wide)) + ((16, 128), (rows, wide))

    def __init__(self, net, here, total, out, bufs, column, width):
        super().__init__(net, here, total, out, bufs, column, width)
        self.block = total.shape[0] // 8

    def part(self, dp, which):
        return self.total.at[span((dp * 2 + which) * self.block, self.block, 16)]

    def upper(self, dp):
        return self.part(dp, 0)

    def lower(self, dp):
        return self.part(dp, 1)

    def third(self):
        here = self.here
        self.wait_a()
        self.add(self.upper(here.dp), self.r2a)
        self.wait_b()
        self.add(self.lower(here.dp), self.r2b)
        self.wait = self.net.send(self.part(here.dp, 1 - here.high), self.r3b, here.peer_z2())

    def fifth(self):
        here, core = self.here, self.here.core
        self.wait()
        own = self.part(here.dp, here.high)

        def body(rows):
            self.f32[rows, :] = own[rows, :].astype(F32) + self.r3b[rows, :].astype(F32)

        by_rows(self.block, body, 16)
        size = self.block // 2
        mine, theirs = (span(c * size, size, 16) for c in (core, 1 - core))
        target = self.out.at[:, self.columns(core)]
        across = here.seq + 6 - 4 * here.z
        self.stay = (self.net.plan(self.f32.at[theirs], target, here.peer_core()),)
        self.swap = (
            self.net.plan(self.r2a.at[span(self.block + core * size, size, 16)], self.r1a.at[2, span(0, size, 16)], (here.dp, across)),
            self.net.plan(
                self.r2a.at[span(self.block + (1 - core) * size, size, 16)],
                self.r1a.at[2, span(size, size, 16)],
                (here.dp, across + 1 - 2 * core),
            ),
        )

        @pl.when(here.side == here.high)
        def _():
            self.stay[0].start()
            self.out[:, self.columns(core)] = self.f32[mine, :]

        @pl.when(here.side != here.high)
        def _():
            def lower(rows):
                self.r2a[span(self.block + rows.start, 16, 16), :] = self.f32[rows, :].astype(BF16)

            by_rows(self.block, lower, 16)
            for copy in self.swap:
                copy.start()

    def end(self):
        here, core = self.here, self.here.core
        size = self.block // 2

        @pl.when(here.side == here.high)
        def _():
            self.stay[0].wait()

        @pl.when(here.side != here.high)
        def _():
            for copy in self.swap:
                copy.wait()
            for side, owner in ((0, core), (1, 1 - core)):
                self.out[:, self.columns(owner)] = self.r1a[2, side * size : side * size + size, :].astype(F32)


def chunk_list(widths):
    cuts = (
        (3, (384,), (DownChunk,)),
        (2, (384, 384), (UpChunk, UpChunk)),
        (1, (384,), (Chunk,)),
        (0, (512, 384, 256), (Chunk, Chunk, LastChunk)),
    )
    chunks = []
    for index, parts, kinds in cuts:
        column = 0
        for part, kind in zip(parts, kinds):
            chunks.append((index, column, part, kind))
            column += part
    return chunks


def layer_kernel(names, chunks, sizes, *refs):
    v = types.SimpleNamespace(**dict(zip(names, refs)))
    tokens, width, heads, hidden_width = sizes
    quarter = width // 4
    size = width // heads
    factor = size ** (-0.5)
    here = Place()
    core, dp = here.core, here.dp
    net = Net(v.send_sems, v.recv_sems)
    mine, theirs = slice(0, tokens), slice(tokens, 2 * tokens)
    near_rows = theirs
    both, pair_both = slice(0, 2 * tokens), slice(2 * tokens, 4 * tokens)

    here.greet()
    loads = []
    for number, (source, target) in enumerate(
        (
            (v.time_table, v.table_v), (v.w_token, v.token_v), (v.w_head, v.head_v), (v.w_ada, v.ada_v),
            (v.token_keep, v.keep_v), (v.head_keep, v.head_keep_v), (v.inputs, v.x_v), (v.cotangent, v.g_v.at[mine]),
            (v.time_index, v.index_v),
        )
    ):
        copy = pltpu.make_async_copy(source, target, v.local_sems.at[7 + number])
        copy.start()
        loads.append(copy)
    w_q, w_o = Weight(net, here, v.wq, v.fq), Weight(net, here, v.wo, v.fo)
    w_u, w_d = HalfWeight(net, here, v.wu, v.fu, True), HalfWeight(net, here, v.wd, v.fd, False)
    weights = [w_q, w_o, w_u, w_d]
    w_q.keep(v.local_sems.at[0])
    w_o.keep(v.local_sems.at[1])
    w_u.keep([v.local_sems.at[2 + k] for k in range(4)])
    w_d.keep([v.local_sems.at[6]])
    select = (
        lax.broadcasted_iota(jnp.int32, (width, quarter), 0)
        == lax.broadcasted_iota(jnp.int32, (width, quarter), 1) + dp * quarter
    ).astype(F32).astype(BF16)
    loads[1].wait()
    token = jnp.broadcast_to(v.token_v[...].astype(F32).reshape(1, quarter), (16, quarter))
    placed = dot(token.astype(BF16), select, NT)
    loads[8].wait()
    loads[0].wait()
    rows = v.table_v.shape[0]
    whole = rows // 128 * 128
    index_row = jnp.broadcast_to(v.index_v[...], (16, whole))
    hot = (lax.broadcasted_iota(jnp.int32, (16, whole), 1) == index_row).astype(F32).astype(BF16)
    row = dot(hot, v.table_v[0:whole, :], NN)[0:1]
    rest = lax.broadcasted_iota(jnp.int32, (rows - whole, width), 0) + whole
    rest = jnp.where(
        rest == jnp.broadcast_to(v.index_v[...], rest.shape), v.table_v[whole:rows, :].astype(F32), 0.0
    )
    row += jnp.sum(rest, axis=0, keepdims=True)
    condition = (row * jax.nn.sigmoid(row)).astype(BF16).astype(F32)
    v.condition[...] = condition
    v.small_v[...] = jnp.zeros(v.small_v.shape, F32)
    for k in range(width // 128):
        v.small_v[k : k + 1, :] = condition[:, k * 128 : (k + 1) * 128]
        v.small_v[8 + k : 9 + k, :] = placed[0:1, k * 128 : (k + 1) * 128]
    here.meet()

    w_q.send_diagonal()
    wait_cotangent = net.send(v.cotangent, v.g_v.at[near_rows], here.peer_z1())
    waits = [
        net.send(v.small_v, v.cond_buf.at[dp], peer, v.cond_buf.at[peer[0]])
        for peer in here.dp_peers()
    ]
    w_q.send_straight()
    v.cond_buf[pl.ds(dp, 1)] = v.small_v[...][None]
    head_of = lax.broadcasted_iota(jnp.int32, (128, width), 0) * size
    lane = lax.broadcasted_iota(jnp.int32, (128, width), 1)
    v.expand[...] = ((lane >= head_of) & (lane < head_of + size)).astype(F32)
    for load in loads[2:6]:
        load.wait()
    diagonal = lax.broadcasted_iota(jnp.int32, (tokens, tokens), 0) == lax.broadcasted_iota(
        jnp.int32, (tokens, tokens), 1
    )
    v.keep[...] = jnp.sum(jnp.where(diagonal, v.keep_v[...].astype(F32), 0.0), axis=1, keepdims=True)
    v.head_mask[...] = jnp.zeros(v.head_mask.shape, F32)
    v.head_mask[:, 0:heads] = v.head_keep_v[...].astype(F32)
    v.part[...] = jnp.zeros(v.part.shape, F32)
    for wait in waits:
        wait()
    def wide(first):
        return jnp.concatenate([v.cond_buf[:, first + k, :] for k in range(width // 128)], axis=1)

    stacked = jnp.concatenate([wide(0), jnp.zeros((12, width), F32)], axis=0).astype(BF16)
    left = dot(stacked, select, NN).astype(BF16)
    for piece in range(7):
        if piece < 6:
            product = dot(left, v.ada_v[:, piece * width : (piece + 1) * width], NN)
        else:
            product = dot(left, v.head_v[...], NT)
        for image in range(4):
            v.part[image, piece : piece + 1, 0 : product.shape[1]] = product[image : image + 1]
    waits = [
        net.send(v.part.at[peer[0]], v.part_buf.at[index], peer)
        for index, peer in enumerate(here.dp_peers())
    ]
    for weight in weights[1:]:
        weight.send_diagonal()
    w_q.spread()
    v.token[...] = jnp.sum(wide(8), axis=0, keepdims=True)
    w_q.share_straight(0)
    w_q.share_straight(1)
    for weight in weights[1:]:
        weight.send_straight()
    w_o.spread()
    for wait in waits:
        wait()
    v.mod[...] = v.part[dp] + v.part_buf[0] + v.part_buf[1] + v.part_buf[2]
    v.mod[7:8, 0:tokens] = v.keep_v[...].astype(F32)
    wait_mod = net.send(v.mod, v.mod_near, here.peer_z1())
    head_sigmoid = jax.nn.sigmoid(v.mod[6:7, 0:128])
    head_mask = v.head_mask[...]
    gate = dot(jnp.broadcast_to(head_mask * head_sigmoid, (8, 128)), v.expand[...], NN, exact=True)
    v.gate_row[...] = gate[0:1]

    loads[6].wait()

    def first_norm(rows):
        values = v.x_v[rows, :].astype(F32)
        centre = values - jnp.mean(values, axis=1, keepdims=True)
        spread = jnp.mean(centre * centre, axis=1, keepdims=True)
        normal = centre * lax.rsqrt(spread + epsilon)
        v.nb[rows, :] = (normal * (1.0 + v.mod[1:2]) + v.mod[0:1]).astype(BF16)

    by_rows(tokens, first_norm)
    wait_normed = net.send(v.nb.at[mine], v.nb.at[theirs], here.peer_core())

    w_q.share_diagonal()
    w_u.spread()
    w_q.ready()

    @pl.loop(0, 3 * width // 384)
    def _(index):
        columns = span(index * 384, 384, 128)
        v.packed[:, columns] = dot(v.nb[mine, :], v.fq[:, columns], NN).astype(BF16)

    w_d.spread()

    lanes = lax.broadcasted_iota(jnp.int32, (1, 2 * size), 1)
    masks = ((lanes < size).astype(F32).astype(BF16), (lanes >= size).astype(F32).astype(BF16))
    scaled_masks = tuple(mask * jnp.asarray(factor, BF16) for mask in masks)
    low_lane = lax.broadcasted_iota(jnp.int32, (tokens, 2 * size), 1) < size

    def three(pair, block):
        return [block[:, span(part * width + pair * 2 * size, 2 * size, 128)] for part in range(3)]

    @pl.loop(0, heads // 2)
    def _(pair):
        queries, key_rows, value_rows = three(pair, v.packed)
        found = []
        for which in range(2):
            scores = dot(queries * scaled_masks[which], key_rows, NT)
            powers = jnp.exp(scores - jnp.max(scores, axis=1, keepdims=True))
            probs = powers * (1.0 / jnp.sum(powers, axis=1, keepdims=True))
            v.probs[pair * 2 + which] = probs
            found.append(dot(probs.astype(BF16), value_rows, NN))
        attended = jnp.where(low_lane, found[0], found[1])
        columns = span(pair * 2 * size, 2 * size, 128)
        v.attended[:, columns] = attended
        v.gated[mine, columns] = (attended * v.gate_row[:, columns]).astype(BF16)

    wait_gated = net.send(v.gated.at[mine], v.gated.at[theirs], here.peer_core())
    w_o.share_straight(0)
    w_o.share_straight(1)
    w_o.share_diagonal()
    w_o.ready()

    @pl.loop(0, width // 256)
    def _(index):
        columns = span(index * 256, 256, 128)
        v.branch[:, columns] = dot(v.gated[mine, :], v.fo[:, columns], NN)

    loads[7].wait()

    def weigh(rows, second, modulation, keep):
        logit = jnp.sum(second.astype(F32) * v.token[...], axis=1, keepdims=True)
        router = jax.nn.sigmoid(logit)
        weight = keep * router
        v.grad_prod[rows, :] = (v.g_v[rows, :].astype(F32) * modulation[5:6] * weight).astype(BF16)
        return router

    def second_norm(rows):
        middle = v.x_v[rows, :].astype(F32) + v.mod[2:3] * v.branch[rows, :]
        v.middle[rows, :] = middle
        centre = middle - jnp.mean(middle, axis=1, keepdims=True)
        spread = jnp.mean(centre * centre, axis=1, keepdims=True)
        scale = lax.rsqrt(spread + epsilon)
        normal = centre * scale
        v.z2[rows, :] = normal
        v.scale2[rows, :] = scale
        second = (normal * (1.0 + v.mod[4:5]) + v.mod[3:4]).astype(BF16)
        v.second[rows, :] = second
        v.router[rows, :] = weigh(rows, second, v.mod, v.keep[rows, :])

    def some_rows(start, count, body):
        @pl.loop(0, count // ROWS)
        def _(index):
            body(span(start + index * ROWS, ROWS, ROWS))

    bit = tokens // 2
    wait_near = []
    for k in range(2):
        some_rows(k * bit, bit, second_norm)
        block = slice(k * bit, k * bit + bit)
        landing = v.second.at[slice(tokens + k * bit, tokens + k * bit + bit)]
        wait_near.append(net.send(v.second.at[block], landing, here.peer_z1()))
        if k == 0:
            w_u.share_diagonal()
            w_u.share_straight(0)
            w_u.share_straight(1)
    half = width // 2
    other = span((1 - core) * half, half, 128)
    own = span(core * half, half, 128)
    wait_pair = [
        net.send(v.second.at[mine], v.second.at[slice(2 * tokens, 3 * tokens)], here.peer_core()),
        net.send(
            v.grad_prod.at[mine, other], v.dy_down.at[slice(2 * tokens, 3 * tokens)], here.peer_core()
        ),
    ]
    v.dy_down[mine, :] = v.grad_prod[mine, own]

    w_u.ready()
    inner = math.sqrt(2.0 / math.pi)
    units = hidden_width // 2

    def feed(start, count):
        tokens_of = slice(start, start + count)
        for index in range(units // 512):
            columns = slice(index * 512, index * 512 + 512)
            v.tmp[0:count, 0:512] = dot(v.second[tokens_of, :], v.fu[:, columns], NN)

            @pl.loop(0, count // ROWS)
            def _(step):
                rows = span(step * ROWS, ROWS, ROWS)
                there = span(start + step * ROWS, ROWS, ROWS)
                u = v.tmp[rows, 0:512]
                square = u * u
                t = jnp.tanh(u * (inner + (inner * 0.044715) * square))
                a = 0.5 + 0.5 * t
                value = u * a
                v.hidden[there, columns] = value.astype(BF16)
                v.slope[there, columns] = a + value * (1.0 - a) * (
                    2.0 * inner + (6.0 * inner * 0.044715) * square
                )

    def feed_back(start, count):
        tokens_of = slice(start, start + count)

        @pl.loop(0, units // 512)
        def _(index):
            columns = span(index * 512, 512, 128)
            back = dot(v.grad_prod[tokens_of, :], v.fd[columns, :], NT)
            v.grad_u[tokens_of, columns] = (back * v.slope[tokens_of, columns]).astype(BF16)

    def down(start, count, target, at, kind):
        @pl.loop(0, width // 256)
        def _(index):
            columns = span(index * 256, 256, 128)
            target[at, columns] = dot(v.hidden[start : start + count, :], v.fd[:, columns], NN).astype(kind)

    def up_back(start, count, target, at, kind):
        @pl.loop(0, width // 256)
        def _(index):
            columns = span(index * 256, 256, 128)
            target[at, columns] = dot(v.grad_u[start : start + count, :], v.fu[columns, :], NT).astype(kind)

    quarter_units = units // 2
    other_units = span((1 - core) * quarter_units, quarter_units, 128)
    own_units = span(core * quarter_units, quarter_units, 128)

    def hand_over(block, landing):
        wait_pair.append(net.send(v.grad_u.at[block, other_units], v.dy_up.at[landing], here.peer_core()))
        v.dy_up[block, :] = v.grad_u[block, own_units]

    feed(0, tokens)
    wait_pair.append(
        net.send(v.hidden.at[mine], v.hidden.at[slice(2 * tokens, 3 * tokens)], here.peer_core())
    )
    pieces = []
    for number, (index, column, wide, kind) in enumerate(chunks):
        total = (v.t_qkv, v.t_out, v.t_up, v.t_down)[index]
        out = (v.o_qkv, v.o_out, v.o_up, v.o_down)[index]
        bufs = [getattr(v, f"c{number}_{k}") for k in range(7)]
        pieces.append(kind(net, here, total, out, bufs, column, wide))
    c_down, c_up, c_more, c_out = pieces[:4]
    c_qkv = pieces[4:]

    def weight_grad(total, left, right, step):
        @pl.loop(0, total.shape[0] // step)
        def _(index):
            rows = span(index * step, step, 128)
            total[rows, :] = dot(left[:, rows], right[...], TN).astype(BF16)

    w_d.share_straight(0)
    w_d.share_diagonal()
    w_d.share_straight(1)
    w_d.ready()
    feed_back(0, tokens)
    hand_over(mine, slice(2 * tokens, 3 * tokens))
    wait_cotangent()
    wait_mod()
    v.keep_near[...] = jnp.sum(
        jnp.where(diagonal, v.mod_near[7:8, 0:tokens], 0.0), axis=1, keepdims=True
    )
    up_back(0, tokens, v.own_back, mine, F32)
    for wait in wait_near:
        wait()

    def weigh_near(rows):
        kept = v.keep_near[span(rows.start - tokens, ROWS, ROWS), :]
        weigh(rows, v.second[rows, :], v.mod_near, kept)

    some_rows(tokens, tokens, weigh_near)
    feed(tokens, tokens)
    last_rows = slice(3 * tokens, 4 * tokens)
    wait_pair.append(net.send(v.hidden.at[near_rows], v.hidden.at[last_rows], here.peer_core()))
    wait_pair.append(net.send(v.second.at[near_rows], v.second.at[last_rows], here.peer_core()))
    wait_pair.append(net.send(v.grad_prod.at[near_rows, other], v.dy_down.at[last_rows], here.peer_core()))
    feed_back(tokens, tokens)
    hand_over(near_rows, last_rows)
    wait_back = []
    for k in range(width // 256):
        columns = slice(k * 256, k * 256 + 256)
        v.near_back[:, columns] = dot(v.grad_u[near_rows, :], v.fu[columns, :], NT).astype(BF16)
        wait_back.append(
            net.send(v.near_back.at[:, columns], v.got_back.at[:, columns], here.peer_z1())
        )
    v.dy_down[near_rows, :] = v.grad_prod[near_rows, own]
    for wait in wait_pair:
        wait()

    def down_quarter(place):
        rows = span(place * 384, 384, 128)
        v.t_down[rows, :] = dot(v.hidden[:, rows], v.dy_down[...], TN).astype(BF16)

    down_quarter(here.peer_d()[0])
    c_down.first_diagonal()
    down_quarter(here.peer_x()[0])
    c_down.first_x()
    down_quarter(here.peer_y()[0])
    c_down.first_y()
    down_quarter(dp)
    down(tokens, tokens, v.near_prod, mine, BF16)

    def near_level(rows):
        grad = v.g_v[span(rows.start + tokens, ROWS, ROWS), :].astype(F32)
        produced = v.near_prod[rows, :].astype(F32)
        v.level[rows, :] = jnp.sum(grad * v.mod_near[5:6] * produced, axis=1, keepdims=True)

    by_rows(tokens, near_level)
    v.level_out[...] = jnp.broadcast_to(
        jnp.sum(jnp.where(diagonal, v.level[...], 0.0), axis=0, keepdims=True), v.level_out.shape
    )
    wait_level = net.send(v.level_out, v.level_in, here.peer_z1())
    wait_prod = net.send(v.near_prod, v.got_prod, here.peer_z1())
    weight_grad(v.t_up, v.second, v.dy_up, 256)
    c_up.first()
    c_more.first()
    down(0, tokens, v.own_prod, mine, F32)

    def own_level(rows):
        grad = v.g_v[rows, :].astype(F32)
        v.level[rows, :] = jnp.sum(grad * v.mod[5:6] * v.own_prod[rows, :], axis=1, keepdims=True)

    by_rows(tokens, own_level)
    c_down.second()

    v.sums[...] = jnp.zeros(v.sums.shape, F32)
    wait_level()
    got = jnp.sum(jnp.where(diagonal, v.level_in[0:1, :], 0.0), axis=1, keepdims=True)
    router, keep = v.router[...], v.keep[...]
    v.logit[...] = (v.level[...] + got) * keep * router * (1.0 - router)

    def second_back(rows):
        logit = v.logit[rows, :]
        back = (v.own_back[rows, :] + v.got_back[rows, :].astype(F32)).astype(BF16).astype(F32)
        back += logit * v.token[...]
        normal = v.z2[rows, :]
        v.sums[1] += fold(logit * v.second[rows, :].astype(F32))
        v.sums[2] += fold(back * normal)
        v.sums[3] += fold(back)
        inside = back * (1.0 + v.mod[4:5])
        level = jnp.mean(inside, axis=1, keepdims=True)
        slope = jnp.mean(inside * normal, axis=1, keepdims=True)
        grad = v.g_v[rows, :].astype(F32) + v.scale2[rows, :] * (inside - level - normal * slope)
        v.grad_mid[rows, :] = grad
        v.sums[4] += fold(grad * v.branch[rows, :])
        v.grad_branch[rows, :] = (v.mod[2:3] * grad).astype(BF16)

    for wait in wait_back:
        wait()
    by_rows(tokens, second_back)
    wait_dbranch = net.send(v.grad_branch.at[:, other], v.dy_out.at[theirs], here.peer_core())
    v.dy_out[mine, :] = v.grad_branch[:, own]

    @pl.loop(0, width // 256)
    def _(index):
        columns = span(index * 256, 256, 128)
        v.tmp[:, columns] = dot(v.grad_branch[...], v.fo[columns, :], NT)


    def gate_back(rows):
        grad = v.tmp[rows, :]
        v.sums[5] += fold(grad * v.attended[rows, :])
        v.grad_att[rows, :] = (grad * v.gate_row[...]).astype(BF16)

    by_rows(tokens, gate_back)
    c_up.second()

    def gather_far(piece, block):
        block[pl.ds(core, 1), pl.ds(here.z, 1), pl.ds(dp, 1)] = piece[...][None, None, None]
        far = (here.z + 2) % Z_CHIPS
        return [net.send(piece, block.at[core, here.z, dp], here.peer_z2(), block.at[core, far, dp])]

    def gather_near(block, waits):
        for wait in waits:
            wait()
        near = here.z + 1 - 2 * (here.z % 2)
        moves = []
        for k in range(2):
            z, other = (here.z + 2 * k) % Z_CHIPS, (near + 2 * k) % Z_CHIPS
            tile = block.at[core, z, dp]
            moves.append(net.send(tile, tile, here.peer_z1(), block.at[core, other, dp]))
        return moves

    def gather_dp(block, waits):
        for wait in waits:
            wait()
        tiles = block.at[core, pl.ds(0, Z_CHIPS), dp]
        return [
            net.send(tiles, tiles, peer, block.at[core, pl.ds(0, Z_CHIPS), peer[0]])
            for peer in here.dp_peers()
        ]

    one_way = (dp + (1 - core) * (1 - 2 * here.x) + core * (2 - 4 * here.y), here.seq)
    other_way = (dp + core * (1 - 2 * here.x) + (1 - core) * (2 - 4 * here.y), here.seq)

    def gather_one(block, waits):
        for wait in waits:
            wait()
        tiles = block.at[core, pl.ds(0, Z_CHIPS), dp]
        return [net.send(tiles, tiles, one_way, block.at[core, pl.ds(0, Z_CHIPS), one_way[0]])]

    def gather_two(block, waits):
        for wait in waits:
            wait()
        moves = []
        for mine_dp, their_dp in ((dp, other_way[0]), (one_way[0], here.peer_d()[0])):
            tiles = block.at[core, pl.ds(0, Z_CHIPS), mine_dp]
            moves.append(
                net.send(tiles, tiles, other_way, block.at[core, pl.ds(0, Z_CHIPS), their_dp])
            )
        return moves

    def gather_pair(block, waits):
        for wait in waits:
            wait()
        return net.send(block.at[core], block.at[core], here.peer_core(), block.at[1 - core])

    def back_pair(pair):
        queries, key_rows, value_rows = three(pair, v.packed)
        columns = span(pair * 2 * size, 2 * size, 128)
        grad_att = v.grad_att[:, columns]
        gq, gk, gv = [], [], []
        for which in range(2):
            probs = v.probs[pair * 2 + which]
            grad_probs = dot(grad_att * masks[which], value_rows, NT)
            level = jnp.sum(probs * grad_probs, axis=1, keepdims=True)
            grad_scores = (probs * (grad_probs - level)).astype(BF16)
            gq.append(dot(grad_scores, key_rows, NN))
            gk.append(dot(grad_scores, queries, TN))
            gv.append(dot(probs.astype(BF16), grad_att, TN))
        for part, (grads, scale) in enumerate(((gq, factor), (gk, factor), (gv, 1.0))):
            both = jnp.where(low_lane, grads[0], grads[1]) * scale
            v.grad_pack[:, span(part * width + pair * 2 * size, 2 * size, 128)] = both.astype(BF16)

    pl.loop(0, heads // 4)(back_pair)
    wait_gated()
    wait_dbranch()
    weight_grad(v.t_out, v.gated, v.dy_out, 256)
    c_out.first()
    pl.loop(heads // 4, heads // 2)(back_pair)
    packed_half = 3 * width // 2
    wait_dpack = net.send(
        v.grad_pack.at[:, span((1 - core) * packed_half, packed_half, 128)],
        v.dy_qkv.at[theirs],
        here.peer_core(),
    )
    v.dy_qkv[mine, :] = v.grad_pack[:, span(core * packed_half, packed_half, 128)]
    c_down.third()
    c_more.second()
    wait_normed()
    wait_dpack()
    weight_grad(v.t_qkv, v.nb, v.dy_qkv, 256)
    c_qkv[0].first()
    c_out.second()
    c_qkv[1].first()
    c_up.third()
    c_more.third()
    wait_prod()

    def finish(rows):
        produced = (v.own_prod[rows, :] + v.got_prod[rows, :].astype(F32)).astype(BF16).astype(F32)
        scaled = produced * (v.keep[rows, :] * v.router[rows, :])
        v.output[rows, :] = (v.middle[rows, :] + v.mod[5:6] * scaled).astype(BF16)
        v.sums[0] += fold(v.g_v[rows, :].astype(F32) * scaled)

    by_rows(tokens, finish)
    head_back = dot(
        jnp.broadcast_to(jnp.sum(v.sums[5], axis=0, keepdims=True), (8, width)), v.expand[...], NT, exact=True
    )
    head_back = head_back[0:1] * head_mask * head_sigmoid * (1.0 - head_sigmoid)
    v.early_f[...] = jnp.zeros(v.early_f.shape, F32)
    rows_out = [jnp.sum(v.sums[k], axis=0, keepdims=True) for k in (4, 3, 2, 0, 1)]
    cut = width // 2
    for slot, values in zip((0, 1, 2, 3, 5, 6), (*rows_out, v.condition[...])):
        v.early_f[2 * slot : 2 * slot + 1, :] = values[:, 0:cut]
        v.early_f[2 * slot + 1 : 2 * slot + 2, :] = values[:, cut:width]
    v.early_f[8:9, 0:128] = head_back
    v.early_out[...] = v.early_f[...].astype(BF16)
    early = gather_far(v.early_out, v.early)

    @pl.loop(0, width // 256)
    def _(index):
        columns = span(index * 256, 256, 128)
        v.tmp[:, columns] = dot(v.grad_pack[...], v.fq[columns, :], NT)

    c_up.fourth()
    c_qkv[0].second()
    c_qkv[2].first()

    def first_back(rows):
        back = v.tmp[rows, :]
        values = v.x_v[rows, :].astype(F32)
        centre = values - jnp.mean(values, axis=1, keepdims=True)
        spread = jnp.mean(centre * centre, axis=1, keepdims=True)
        scale = lax.rsqrt(spread + epsilon)
        normal = centre * scale
        v.sums[6] += fold(back * normal)
        v.sums[7] += fold(back)
        inside = back * (1.0 + v.mod[1:2])
        level = jnp.mean(inside, axis=1, keepdims=True)
        slope = jnp.mean(inside * normal, axis=1, keepdims=True)
        v.grad_input[rows, :] = v.grad_mid[rows, :] + scale * (inside - level - normal * slope)

    by_rows(tokens, first_back)
    shift = jnp.sum(v.sums[7], axis=0, keepdims=True)
    scale = jnp.sum(v.sums[6], axis=0, keepdims=True)
    v.late_f[...] = jnp.zeros(v.late_f.shape, F32)
    for k in range(width // 128):
        v.late_f[k : k + 1, :] = shift[:, k * 128 : (k + 1) * 128]
        v.late_f[8 + k : 9 + k, :] = scale[:, k * 128 : (k + 1) * 128]
    v.late_out[...] = v.late_f[...].astype(BF16)
    late = gather_far(v.late_out, v.late)
    c_more.fourth()
    c_down.fifth()
    early = gather_near(v.early, early)
    c_out.third()
    c_qkv[1].second()
    early = gather_one(v.early, early)
    late = gather_near(v.late, late)
    c_up.fifth()
    c_qkv[0].third()
    c_qkv[2].second()
    c_more.fifth()
    c_out.fourth()
    c_qkv[1].third()
    early = gather_two(v.early, early)
    late = gather_dp(v.late, late)
    c_qkv[0].fourth()
    c_qkv[2].third()
    c_qkv[1].fourth()
    c_out.fifth()
    early = gather_pair(v.early, early)
    late = gather_pair(v.late, late)
    early()
    offset = dp * quarter + (here.seq % BLOCK) * SHARE
    pick = (
        lax.broadcasted_iota(jnp.int32, (width, SHARE), 0)
        == lax.broadcasted_iota(jnp.int32, (width, SHARE), 1) + offset
    ).astype(F32)

    every = v.early[...].reshape(512, cut).astype(F32).reshape(32, 16, cut)
    conditions = (
        dot(every[:, 12, :].astype(BF16), pick[0:cut].astype(BF16), NN)
        + dot(every[:, 13, :].astype(BF16), pick[cut:width].astype(BF16), NN)
    ).astype(BF16)
    for slot, piece in enumerate((2, 3, 4, 5)):
        for side in range(2):
            start = piece * width + side * cut
            v.o_ada[:, start : start + cut] = dot(
                conditions, every[:, 2 * slot + side, :].astype(BF16), TN
            )
    v.o_head[...] = dot(every[:, 8, 0:128].astype(BF16), conditions, TN)[0:heads]
    totals = [jnp.sum(every[:, 10 + side, :], axis=0, keepdims=True) for side in range(2)]
    v.o_token[...] = (
        dot(jnp.broadcast_to(totals[0], (8, cut)), pick[0:cut], NN, exact=True)
        + dot(jnp.broadcast_to(totals[1], (8, cut)), pick[cut:width], NN, exact=True)
    )[0:1]

    c_qkv[0].fifth()
    c_qkv[1].fifth()
    for chunk in (c_down, c_up, c_more):
        chunk.end()
    late()
    tail = v.late[...].reshape(512, 128).astype(F32).reshape(32, 16, 128)
    for base in (0, 8):
        row = jnp.concatenate([tail[:, base + k, :] for k in range(width // 128)], axis=1)
        start = base // 8 * width
        v.o_ada[:, start : start + width] = dot(conditions, row.astype(BF16), TN)
    c_qkv[2].fifth()
    for chunk in (c_out, *c_qkv):
        chunk.end()
    net.finish()


def layer(time_table, time_index, w_token, w_head, token_keep, head_keep, inputs, cotangent, w_ada, wq, wo, wu, wd):
    tokens, width = inputs.shape
    hidden_width = wu.shape[1]
    heads = head_keep.shape[1]
    widths = [wq.shape[1], wo.shape[1], wu.shape[1], wd.shape[1]]
    depths = [4 * w.shape[0] for w in (wq, wo, wu, wd)]
    chunks = chunk_list(widths)
    operands = dict(
        time_table=time_table, time_index=time_index, w_token=w_token, w_head=w_head, token_keep=token_keep, head_keep=head_keep,
        inputs=inputs, cotangent=cotangent, w_ada=w_ada, wq=wq, wo=wo, wu=wu, wd=wd,
    )
    outs = dict(
        ada=((SHARE, 6 * width), F32),
        qkv=((depths[0] // 32, widths[0]), F32),
        out=((depths[1] // 32, widths[1]), F32),
        up=((depths[2] // 32, widths[2]), F32),
        down=((depths[3] // 32, widths[3]), F32),
        head=((heads, SHARE), F32),
        token=((1, SHARE), F32),
    )
    results = dict(output=((tokens, width), BF16), grad_input=((tokens, width), F32))
    results.update({"o_" + k: s for k, s in outs.items()})
    space = dict(
        table_v=(time_table.shape, BF16),
        index_v=(time_index.shape, jnp.int32),
        small_v=((16, 128), F32),
        condition=((1, width), F32),
        token_v=(w_token.shape, BF16),
        keep_v=(token_keep.shape, jnp.int32),
        head_keep_v=(head_keep.shape, jnp.int32),
        head_mask=((1, 128), F32),
        head_v=(w_head.shape, BF16),
        ada_v=(w_ada.shape, BF16),
        x_v=((tokens, width), BF16),
        g_v=((2 * tokens, width), BF16),
        mod_near=((8, width), F32),
        keep_near=((tokens, 1), F32),
        fq=((depths[0], widths[0]), BF16),
        fo=((depths[1], widths[1]), BF16),
        fu=((depths[2], widths[2] // 2), BF16),
        fd=((depths[3] // 2, widths[3]), BF16),
        cond_buf=((4, 16, 128), F32),
        part=((4, 8, width), F32),
        part_buf=((3, 8, width), F32),
        mod=((8, width), F32),
        token=((1, width), F32),
        keep=((tokens, 1), F32),
        expand=((128, width), F32),
        gate_row=((1, width), F32),
        nb=((2 * tokens, width), BF16),
        packed=((tokens, 3 * width), BF16),
        probs=((heads, tokens, tokens), F32),
        attended=((tokens, width), F32),
        gated=((2 * tokens, width), BF16),
        branch=((tokens, width), F32),
        middle=((tokens, width), F32),
        z2=((tokens, width), F32),
        scale2=((tokens, 1), F32),
        second=((4 * tokens, width), BF16),
        router=((tokens, 1), F32),
        logit=((tokens, 1), F32),
        grad_prod=((2 * tokens, width), BF16),
        dy_down=((4 * tokens, width // 2), BF16),
        tmp=((tokens, width), F32),
        hidden=((4 * tokens, hidden_width // 2), BF16),
        slope=((2 * tokens, hidden_width // 2), F32),
        grad_u=((2 * tokens, hidden_width // 2), BF16),
        dy_up=((4 * tokens, hidden_width // 4), BF16),
        own_prod=((tokens, width), F32),
        own_back=((tokens, width), F32),
        near_prod=((tokens, width), BF16),
        near_back=((tokens, width), BF16),
        got_prod=((tokens, width), BF16),
        got_back=((tokens, width), BF16),
        level=((tokens, 1), F32),
        level_out=((8, tokens), F32),
        level_in=((8, tokens), F32),
        grad_mid=((tokens, width), F32),
        grad_branch=((tokens, width), BF16),
        dy_out=((2 * tokens, width // 2), BF16),
        grad_att=((tokens, width), BF16),
        grad_pack=((tokens, 3 * width), BF16),
        dy_qkv=((2 * tokens, 3 * width // 2), BF16),
        sums=((8, 8, width), F32),
        early_f=((16, width // 2), F32),
        early_out=((16, width // 2), BF16),
        early=((2, Z_CHIPS, 4, 16, width // 2), BF16),
        late_f=((16, 128), F32),
        late_out=((16, 128), BF16),
        late=((2, Z_CHIPS, 4, 16, 128), BF16),
        t_qkv=((depths[0], widths[0] // 2), BF16),
        t_out=((depths[1], widths[1] // 2), BF16),
        t_up=((depths[2], widths[2] // 4), BF16),
        t_down=((depths[3] // 2, widths[3] // 2), BF16),
    )
    for number, (index, _, wide, kind) in enumerate(chunks):
        shapes = kind.shapes(depths[index] // 16, wide)
        for k, shape in enumerate(shapes):
            space[f"c{number}_{k}"] = (shape, BF16)
        space[f"c{number}_6"] = (kind.sums(depths[index] // 16, wide), F32)
    copies = 6 + 4 * 13 + 32 + len(chunks) * 14 + 14
    names = list(operands) + list(results) + list(space) + ["send_sems", "recv_sems", "local_sems"]
    return pl.pallas_call(
        functools.partial(layer_kernel, names, chunks, (tokens, width, heads, hidden_width)),
        out_shape=[pltpu.VMEM(*r) for r in results.values()],
        in_specs=[ANY] * len(operands),
        out_specs=[VMEM] * len(results),
        scratch_shapes=[pltpu.VMEM(*s) for s in space.values()]
        + [
            pltpu.SemaphoreType.DMA((copies,)),
            pltpu.SemaphoreType.DMA((copies,)),
            pltpu.SemaphoreType.DMA((16,)),
        ],
        compiler_params=pltpu.CompilerParams(
            collective_id=0, has_side_effects=True, vmem_limit_bytes=61 * 2**20
        ),
    )(*operands.values())


def copy_kernel(count, *refs):
    copies = [
        pltpu.make_async_copy(refs[k], refs[count + k], refs[2 * count].at[k]) for k in range(count)
    ]
    for copy in copies:
        copy.start()
    for copy in copies:
        copy.wait()


def copy_all(arrays):
    count = len(arrays)
    return pl.pallas_call(
        functools.partial(copy_kernel, count),
        out_shape=[jax.ShapeDtypeStruct(a.shape, a.dtype) for a in arrays],
        in_specs=[VMEM] * count,
        out_specs=[ANY] * count,
        scratch_shapes=[pltpu.SemaphoreType.DMA((count,))],
        compiler_params=pltpu.CompilerParams(vmem_limit_bytes=16 * 2**20),
    )(*(pltpu.with_memory_space_constraint(a, pltpu.VMEM) for a in arrays))


def across_blocks(part, seq_size):
    blocks = seq_size // BLOCK
    if blocks == 1:
        return part
    groups = [[b * BLOCK + j for b in range(blocks)] for j in range(BLOCK)]
    mine = lax.psum_scatter(
        part, "seq", scatter_dimension=0, axis_index_groups=groups, tiled=True
    )
    moves = [(b * BLOCK + j, j * blocks + b) for b in range(blocks) for j in range(BLOCK)]
    return lax.ppermute(mine, "seq", moves)


def per_device(
    seq_size, inputs, time_table, time_index, token_keep, head_keep, cotangent,
    w_ada, w_qkv, w_out, w_up, w_down, w_head, w_token,
):
    out = layer(
        time_table, time_index[None], w_token, w_head.T, token_keep, head_keep,
        inputs[0], cotangent[0], w_ada, w_qkv, w_out, w_up, w_down,
    )
    output, grad_input, ada, qkv, outw, up, down, head, token = copy_all(out)
    parts = (ada, qkv, outw, up, down, head.T, token[0])
    parts = tuple(across_blocks(part, seq_size) for part in parts)
    return (output[None], grad_input[None]) + parts


def solution(mesh):
    both = ("dp", "seq")
    in_specs = (
        P(both, None, None), P(), P(both), P(both, None), P(both, None), P(both, None, None),
        P("dp", None), P("dp", None), P("dp", None), P("dp", None), P("dp", None), P("dp", None), P("dp"),
    )
    out_specs = (P(both, None, None), P(both, None, None)) + (P(both, None),) * 6 + (P(both),)
    return jax.shard_map(
        functools.partial(per_device, mesh.shape["seq"]),
        mesh=mesh, in_specs=in_specs, out_specs=out_specs, check_vma=False,
    )
```

```python
import functools
import math
import types

import jax
import jax.numpy as jnp
from jax import lax
from jax.experimental import pallas as pl
from jax.experimental.pallas import tpu as pltpu
from jax.sharding import PartitionSpec as P

epsilon = 1e-06
MESH = pl.DeviceIdType.MESH
ANY = pl.BlockSpec(memory_space=pl.ANY)
VMEM = pl.BlockSpec(memory_space=pltpu.VMEM)
Z_CHIPS = 4
BLOCK = 2 * Z_CHIPS
F32, BF16 = jnp.float32, jnp.bfloat16
NN, NT, TN = ((1,), (0,)), ((1,), (1,)), ((0,), (0,))
ROWS = 32
SHARE = 24


def dot(left, right, dims, exact=False):
    return lax.dot_general(
        left, right, (dims, ((), ())), preferred_element_type=F32,
        precision=lax.Precision.HIGHEST if exact else None,
    )


def span(start, size, unit):
    return pl.ds(pl.multiple_of(start, unit), size)


def by_rows(total, body, step=ROWS):
    @pl.loop(0, total // step)
    def _(index):
        body(span(index * step, step, step))


def fold(values):
    return jnp.sum(values.reshape(-1, 8, values.shape[-1]), axis=0)


class Place:
    def __init__(self):
        self.dp = lax.axis_index("dp")
        self.seq = lax.axis_index("seq")
        self.x = self.dp % 2
        self.y = self.dp // 2
        self.core = self.seq % 2
        self.z = (self.seq // 2) % Z_CHIPS
        self.side = self.z % 2
        self.high = self.z // 2
        self.outer = self.seq // BLOCK

    def z_of(self, step):
        return (self.z + step) % Z_CHIPS

    def peer_x(self):
        return (self.y * 2 + 1 - self.x, self.seq)

    def peer_y(self):
        return ((1 - self.y) * 2 + self.x, self.seq)

    def peer_d(self):
        return ((1 - self.y) * 2 + 1 - self.x, self.seq)

    def peer_core(self):
        return (self.dp, self.seq + 1 - 2 * self.core)

    def peer_z(self, step):
        return (self.dp, self.outer * BLOCK + self.z_of(step) * 2 + self.core)

    def peer_z1(self):
        return (self.dp, self.seq + 2 - 4 * (self.z % 2))

    def peer_z2(self):
        return (self.dp, self.seq + 4 - 8 * (self.z // 2))

    def dp_peers(self):
        return (self.peer_x(), self.peer_y(), self.peer_d())

    def greet(self):
        peers = list(self.dp_peers()) + [self.peer_core()]
        for k in range(1, Z_CHIPS):
            same = self.peer_z(k)
            peers += [same, (same[0], same[1] + 1 - 2 * self.core)]
        for peer in peers:
            pl.semaphore_signal(
                pltpu.get_barrier_semaphore(), inc=1, device_id=peer, device_id_type=MESH
            )
        self.peers = len(peers)

    def meet(self):
        pl.semaphore_wait(pltpu.get_barrier_semaphore(), self.peers)


class Net:
    def __init__(self, send_sems, recv_sems):
        self.send_sems = send_sems
        self.recv_sems = recv_sems
        self.used = 0
        self.sent = []

    def send(self, src, dst, peer, landing=None):
        slot = self.used
        self.used += 1

        def copy_to(target):
            return pltpu.make_async_remote_copy(
                src_ref=src,
                dst_ref=target,
                send_sem=self.send_sems.at[slot],
                recv_sem=self.recv_sems.at[slot],
                device_id=peer,
                device_id_type=MESH,
            )

        copy = copy_to(dst)
        copy.start()
        self.sent.append(copy)
        arrival = copy if landing is None else copy_to(landing)
        return arrival.wait_recv

    def plan(self, src, dst, peer):
        slot = self.used
        self.used += 1
        return pltpu.make_async_remote_copy(
            src_ref=src,
            dst_ref=dst,
            send_sem=self.send_sems.at[slot],
            recv_sem=self.recv_sems.at[slot],
            device_id=peer,
            device_id_type=MESH,
        )

    def finish(self):
        for copy in self.sent:
            copy.wait_send()


class Weight:
    def __init__(self, net, here, own, full):
        self.net, self.here, self.own, self.full = net, here, own, full
        self.depth = own.shape[0]
        self.piece = self.depth // Z_CHIPS
        self.width = own.shape[1] // 2
        self.wait_xy, self.last = [], []

    def columns(self, core):
        return span(core * self.width, self.width, 128)

    def quarter(self, dp):
        return span(dp * self.depth, self.depth, 16)

    def part(self, dp, z):
        return span(dp * self.depth + z * self.piece, self.piece, 16)

    def keep(self, sem):
        self.local = pltpu.make_async_copy(self.own, self.full.at[self.quarter(self.here.dp)], sem)
        self.local.start()

    def send_diagonal(self):
        here, columns = self.here, self.columns(self.here.core)
        peer = here.peer_d()
        self.wait_d = self.net.send(
            self.own.at[span(here.z * self.piece, self.piece, 16), columns],
            self.full.at[self.part(here.dp, here.z), columns],
            peer,
            self.full.at[self.part(peer[0], here.z), columns],
        )

    def rows(self, dp, side):
        half = self.depth // 2
        return span(dp * self.depth + side * half, half, 16)

    def send_straight(self, sides=(0, 1)):
        here, columns = self.here, self.columns(self.here.core)
        self.wait_xy += [
            [
                self.net.send(
                    self.own.at[self.rows(0, side), columns],
                    self.full.at[self.rows(here.dp, side), columns],
                    peer,
                    self.full.at[self.rows(peer[0], side), columns],
                )
                for peer in (here.peer_x(), here.peer_y())
            ]
            for side in sides
        ]

    def spread(self):
        here, columns = self.here, self.columns(self.here.core)
        diagonal = here.peer_d()[0]
        self.wait_d()
        piece = self.full.at[self.part(diagonal, here.z), columns]
        self.wait_z = [
            self.net.send(
                piece, piece, here.peer_z(step),
                self.full.at[self.part(diagonal, here.z_of(Z_CHIPS - step)), columns],
            )
            for step in range(1, Z_CHIPS)
        ]

    def hand(self, rows):
        here = self.here
        block = self.full.at[rows, self.columns(here.core)]
        landing = self.full.at[rows, self.columns(1 - here.core)]
        self.last.append(self.net.send(block, block, here.peer_core(), landing))

    def share_straight(self, side):
        here = self.here
        for wait, peer in zip(self.wait_xy[side], (here.peer_x(), here.peer_y())):
            wait()
            self.hand(self.rows(peer[0], side))

    def share_diagonal(self):
        for wait in self.wait_z:
            wait()
        self.hand(self.quarter(self.here.peer_d()[0]))

    def ready(self):
        for wait in self.last:
            wait()
        self.local.wait()


class HalfWeight(Weight):
    def __init__(self, net, here, own, full, by_columns):
        self.net, self.here, self.own, self.full, self.by_columns = net, here, own, full, by_columns
        self.last = []

    def source(self, part):
        here = self.here
        if self.by_columns:
            return self.own.at[:, span((2 * here.core + part) * 768 + here.side * 384, 384, 128)]
        return self.own.at[span(here.side * 384 + part * 192, 192, 16), span(here.core * 384, 384, 128)]

    def block(self, dp, part, core):
        if self.by_columns:
            return self.full.at[span(dp * 192, 192, 16), span((2 * core + part) * 384, 384, 128)]
        return self.full.at[span(dp * 384 + part * 192, 192, 16), span(core * 384, 384, 128)]

    def whole(self, dp, core):
        if self.by_columns:
            return self.full.at[span(dp * 192, 192, 16), span(core * 768, 768, 128)]
        return self.full.at[span(dp * 384, 384, 16), span(core * 384, 384, 128)]

    def keep(self, sems):
        dp, side = self.here.dp, self.here.side
        if self.by_columns:
            moves = [
                (
                    self.own.at[:, span(k * 768 + side * 384, 384, 128)],
                    self.full.at[span(dp * 192, 192, 16), span(k * 384, 384, 128)],
                )
                for k in range(4)
            ]
        else:
            moves = [(self.own.at[span(side * 384, 384, 16)], self.full.at[span(dp * 384, 384, 16)])]
        self.locals = [
            pltpu.make_async_copy(source, target, sem) for (source, target), sem in zip(moves, sems)
        ]
        for copy in self.locals:
            copy.start()

    def send_diagonal(self):
        here = self.here
        peer = here.peer_d()
        self.wait_d = self.net.send(
            self.source(here.high),
            self.block(here.dp, here.high, here.core),
            peer,
            self.block(peer[0], here.high, here.core),
        )

    def send_straight(self):
        here = self.here
        self.wait_xy = [
            [
                self.net.send(
                    self.source(part),
                    self.block(here.dp, part, here.core),
                    peer,
                    self.block(peer[0], part, here.core),
                )
                for peer in (here.peer_x(), here.peer_y())
            ]
            for part in range(2)
        ]

    def spread(self):
        here = self.here
        diagonal = here.peer_d()[0]
        self.wait_d()
        piece = self.block(diagonal, here.high, here.core)
        self.wait_z = [
            self.net.send(
                piece, piece, here.peer_z2(), self.block(diagonal, 1 - here.high, here.core)
            )
        ]

    def pass_core(self, block, landing):
        self.last.append(self.net.send(block, block, self.here.peer_core(), landing))

    def share_straight(self, part):
        here = self.here
        for wait, peer in zip(self.wait_xy[part], (here.peer_x(), here.peer_y())):
            wait()
            self.pass_core(self.block(peer[0], part, here.core), self.block(peer[0], part, 1 - here.core))

    def share_diagonal(self):
        here = self.here
        diagonal = here.peer_d()[0]
        for wait in self.wait_z:
            wait()
        self.pass_core(self.whole(diagonal, here.core), self.whole(diagonal, 1 - here.core))

    def ready(self):
        for wait in self.last:
            wait()
        for copy in self.locals:
            copy.wait()


class WholeWeight(HalfWeight):
    def send_diagonal(self):
        here = self.here
        peer = here.peer_d()
        self.wait_d = [
            self.net.send(
                self.source(part),
                self.block(here.dp, part, here.core),
                peer,
                self.block(peer[0], part, here.core),
            )
            for part in range(2)
        ]

    def share_diagonal(self):
        here = self.here
        diagonal = here.peer_d()[0]
        for wait in self.wait_d:
            wait()
        self.pass_core(self.whole(diagonal, here.core), self.whole(diagonal, 1 - here.core))


class Chunk:
    @staticmethod
    def shapes(rows, wide):
        return ((2, 2 * rows, wide),) * 2 + ((2 * rows, wide),) * 2 + ((2, rows, wide), (rows, wide))

    def __init__(self, net, here, total, out, bufs, column, width):
        self.net, self.here, self.out = net, here, out
        self.total = total.at[:, span(column, width, 128)]
        self.block = total.shape[0] // 16
        self.column, self.width = column, width
        self.r1a, self.r1b, self.r2a, self.r2b, self.r3a, self.r3b, self.f32 = bufs

    @staticmethod
    def sums(rows, wide):
        return (rows, wide)

    def columns(self, core):
        return span(core * (self.out.shape[1] // 2) + self.column, self.width, 128)

    def upper(self, dp):
        return self.total.at[span(dp * 4 * self.block, 2 * self.block, 16)]

    def lower(self, dp):
        return self.total.at[span(dp * 4 * self.block + 2 * self.block, 2 * self.block, 16)]

    def add(self, total, extra):
        def body(rows):
            total[rows, :] = (total[rows, :].astype(F32) + extra[rows, :].astype(F32)).astype(BF16)

        by_rows(total.shape[0], body, 16)

    def first_diagonal(self):
        here, dp = self.here, self.here.peer_d()[0]
        self.wait_a = [self.net.send(self.upper(dp), self.r1a.at[1 - here.y], here.peer_x())]
        self.wait_b = [self.net.send(self.lower(dp), self.r1b.at[1 - here.x], here.peer_y())]

    def first_x(self):
        here, peer = self.here, self.here.peer_x()
        self.wait_a.append(self.net.send(self.upper(peer[0]), self.r1a.at[here.y], peer))

    def first_y(self):
        here, peer = self.here, self.here.peer_y()
        self.wait_b.append(self.net.send(self.lower(peer[0]), self.r1b.at[here.x], peer))

    def first(self):
        self.first_diagonal()
        self.first_x()
        self.first_y()

    def second(self):
        here = self.here
        for wait in self.wait_a:
            wait()
        away = self.upper((1 - here.y) * 2 + here.x)
        self.add(away, self.r1a.at[1 - here.y])
        next_a = self.net.send(away, self.r2a.at[span(0, away.shape[0], 16)], here.peer_y())
        for wait in self.wait_b:
            wait()
        away = self.lower(here.y * 2 + 1 - here.x)
        self.add(away, self.r1b.at[1 - here.x])
        next_b = self.net.send(away, self.r2b, here.peer_x())
        self.add(self.upper(here.dp), self.r1a.at[here.y])
        self.add(self.lower(here.dp), self.r1b.at[here.x])
        self.wait_a, self.wait_b = next_a, next_b

    def mine(self, z):
        return self.total.at[span((self.here.dp * 4 + z) * self.block, self.block, 16)]

    def third(self):
        here = self.here
        self.wait_a()
        self.add(self.upper(here.dp), self.r2a)
        self.wait_b()
        self.add(self.lower(here.dp), self.r2b)
        odd = 1 - here.z % 2
        self.waits = [
            self.net.send(self.mine(odd + 2 * k), self.r3a.at[k], here.peer_z1()) for k in range(2)
        ]

    def fourth(self):
        here = self.here
        far = (here.z + 2) % Z_CHIPS
        for wait in self.waits:
            wait()
        self.add(self.mine(far), self.r3a.at[far // 2])
        self.wait = self.net.send(self.mine(far), self.r3b, here.peer_z2())
        self.add(self.mine(here.z), self.r3a.at[here.z // 2])

    def fifth(self):
        here = self.here
        self.wait()
        own = self.mine(here.z)

        def body(rows):
            self.f32[rows, :] = own[rows, :].astype(F32) + self.r3b[rows, :].astype(F32)

        by_rows(self.block, body, 16)
        self.pass_on()

    def pass_on(self):
        here = self.here
        part = self.block // 2
        self.wait = self.net.send(
            self.f32.at[span((1 - here.core) * part, part, 8)],
            self.out.at[:, self.columns(here.core)],
            here.peer_core(),
            self.out.at[:, self.columns(1 - here.core)],
        )
        self.out[:, self.columns(here.core)] = self.f32[span(here.core * part, part, 8), :]

    def end(self):
        self.wait()


class LastChunk(Chunk):
    @staticmethod
    def shapes(rows, wide):
        return ((2, 2 * rows, wide),) * 2 + ((2 * rows, wide),) * 2 + ((3, rows, wide), (16, 128))

    def third(self):
        here = self.here
        self.wait_a()
        self.add(self.upper(here.dp), self.r2a)
        self.wait_b()
        self.add(self.lower(here.dp), self.r2b)
        self.waits = [
            self.net.send(self.mine(here.z_of(k)), self.r3a.at[k - 1], here.peer_z(k))
            for k in range(1, Z_CHIPS)
        ]

    def fifth(self):
        for wait in self.waits:
            wait()
        own = self.mine(self.here.z)

        def body(rows):
            total = own[rows, :].astype(F32)
            for k in range(Z_CHIPS - 1):
                total += self.r3a[k, rows, :].astype(F32)
            self.f32[rows, :] = total

        by_rows(self.block, body, 16)
        self.pass_on()


class UpChunk(LastChunk):
    @staticmethod
    def sums(rows, wide):
        return (2, rows, wide)

    def place(self, core, side):
        return span((2 * core + self.column // self.width) * 768 + side * 384, 384, 128)

    def fifth(self):
        here = self.here
        for wait in self.waits:
            wait()
        part = self.block // 2
        self.waits = []
        for k, (left, right, side) in enumerate(
            (
                (self.mine(here.z), self.r3a.at[1], here.side),
                (self.r3a.at[0], self.r3a.at[2], 1 - here.side),
            )
        ):

            def body(rows):
                self.f32[k, rows, :] = left[rows, :].astype(F32) + right[rows, :].astype(F32)

            by_rows(self.block, body, 16)
            self.waits.append(
                self.net.send(
                    self.f32.at[k, span((1 - here.core) * part, part, 8)],
                    self.out.at[:, self.place(here.core, side)],
                    here.peer_core(),
                    self.out.at[:, self.place(1 - here.core, side)],
                )
            )
            self.out[:, self.place(here.core, side)] = self.f32[k, span(here.core * part, part, 8), :]

    def end(self):
        for wait in self.waits:
            wait()


class DownChunk(Chunk):
    @staticmethod
    def shapes(rows, wide):
        return ((2, rows, wide),) * 2 + ((rows, wide),) * 2 + ((16, 128), (2, rows, wide))

    def __init__(self, net, here, total, out, bufs, column, width):
        super().__init__(net, here, total, out, bufs, column, width)
        self.block = total.shape[0] // 8

    def part(self, dp, which):
        return self.total.at[span((dp * 2 + which) * self.block, self.block, 16)]

    def upper(self, dp):
        return self.part(dp, 0)

    def lower(self, dp):
        return self.part(dp, 1)

    def third(self):
        here = self.here
        self.wait_a()
        self.add(self.upper(here.dp), self.r2a)
        self.wait_b()
        self.add(self.lower(here.dp), self.r2b)
        inner = (here.side - here.high) * (here.side - here.high)
        there = here.seq + (1 - inner) * (2 - 4 * here.side) + inner * (4 - 8 * here.high)
        self.wait = self.net.send(
            self.part(here.dp, 1 - here.high), self.r3b.at[0], (here.dp, there)
        )
        self.across = self.net.plan(
            self.part(here.dp, here.high), self.r3b.at[1], (here.dp, here.seq + 6 - 4 * here.z)
        )

        @pl.when(here.side != here.high)
        def _():
            self.across.start()

    def fifth(self):
        here = self.here
        self.wait()

        def total(left):
            def body(rows):
                self.f32[rows, :] = left[rows, :].astype(F32) + self.r3b[0, rows, :].astype(F32)

            by_rows(self.block, body, 16)

        @pl.when(here.side == here.high)
        def _():
            total(self.part(here.dp, here.high))

        @pl.when(here.side != here.high)
        def _():
            self.across.wait()
            total(self.r3b.at[1])

        self.pass_on()


def chunk_list(widths):
    cuts = (
        (3, (384,), (DownChunk,)),
        (2, (384, 384), (UpChunk, UpChunk)),
        (1, (384,), (Chunk,)),
        (0, (512, 384, 256), (Chunk, Chunk, LastChunk)),
    )
    chunks = []
    for index, parts, kinds in cuts:
        column = 0
        for part, kind in zip(parts, kinds):
            chunks.append((index, column, part, kind))
            column += part
    return chunks


def layer_kernel(names, chunks, sizes, *refs):
    v = types.SimpleNamespace(**dict(zip(names, refs)))
    tokens, width, heads, hidden_width = sizes
    quarter = width // 4
    size = width // heads
    factor = size ** (-0.5)
    here = Place()
    core, dp = here.core, here.dp
    net = Net(v.send_sems, v.recv_sems)
    mine, theirs = slice(0, tokens), slice(tokens, 2 * tokens)
    near_rows = theirs
    both, pair_both = slice(0, 2 * tokens), slice(2 * tokens, 4 * tokens)

    here.greet()
    loads = []
    for number, (source, target) in enumerate(
        (
            (v.time_table, v.table_v), (v.w_token, v.token_v), (v.w_head, v.head_v), (v.w_ada, v.ada_v),
            (v.token_keep, v.keep_v), (v.head_keep, v.head_keep_v), (v.inputs, v.x_v), (v.cotangent, v.g_v.at[mine]),
            (v.time_index, v.index_v),
        )
    ):
        copy = pltpu.make_async_copy(source, target, v.local_sems.at[7 + number])
        copy.start()
        loads.append(copy)
    w_q, w_o = Weight(net, here, v.wq, v.fq), Weight(net, here, v.wo, v.fo)
    w_u, w_d = HalfWeight(net, here, v.wu, v.fu, True), WholeWeight(net, here, v.wd, v.fd, False)
    weights = [w_q, w_o, w_u, w_d]
    w_q.keep(v.local_sems.at[0])
    w_o.keep(v.local_sems.at[1])
    w_u.keep([v.local_sems.at[2 + k] for k in range(4)])
    w_d.keep([v.local_sems.at[6]])
    select = (
        lax.broadcasted_iota(jnp.int32, (width, quarter), 0)
        == lax.broadcasted_iota(jnp.int32, (width, quarter), 1) + dp * quarter
    ).astype(F32).astype(BF16)
    loads[1].wait()
    token = jnp.broadcast_to(v.token_v[...].astype(F32).reshape(1, quarter), (16, quarter))
    placed = dot(token.astype(BF16), select, NT)
    loads[8].wait()
    loads[0].wait()
    rows = v.table_v.shape[0]
    whole = rows // 128 * 128
    index_row = jnp.broadcast_to(v.index_v[...], (16, whole))
    hot = (lax.broadcasted_iota(jnp.int32, (16, whole), 1) == index_row).astype(F32).astype(BF16)
    row = dot(hot, v.table_v[0:whole, :], NN)[0:1]
    rest = lax.broadcasted_iota(jnp.int32, (rows - whole, width), 0) + whole
    rest = jnp.where(
        rest == jnp.broadcast_to(v.index_v[...], rest.shape), v.table_v[whole:rows, :].astype(F32), 0.0
    )
    row += jnp.sum(rest, axis=0, keepdims=True)
    condition = (row * jax.nn.sigmoid(row)).astype(BF16).astype(F32)
    v.condition[...] = condition
    v.small_v[...] = jnp.zeros(v.small_v.shape, F32)
    for k in range(width // 128):
        v.small_v[k : k + 1, :] = condition[:, k * 128 : (k + 1) * 128]
        v.small_v[8 + k : 9 + k, :] = placed[0:1, k * 128 : (k + 1) * 128]
    here.meet()

    w_q.send_diagonal()
    bit = tokens // 2
    wait_cotangent = []

    def send_cotangent(k):
        block = slice(k * bit, k * bit + bit)
        landing = v.g_v.at[slice(tokens + k * bit, tokens + k * bit + bit)]
        wait_cotangent.append(net.send(v.cotangent.at[block], landing, here.peer_z1()))

    send_cotangent(0)
    waits = [
        net.send(v.small_v, v.cond_buf.at[dp], peer, v.cond_buf.at[peer[0]])
        for peer in here.dp_peers()
    ]
    w_q.send_straight((0,))
    v.cond_buf[pl.ds(dp, 1)] = v.small_v[...][None]
    head_of = lax.broadcasted_iota(jnp.int32, (128, width), 0) * size
    lane = lax.broadcasted_iota(jnp.int32, (128, width), 1)
    v.expand[...] = ((lane >= head_of) & (lane < head_of + size)).astype(F32)
    for load in loads[2:6]:
        load.wait()
    diagonal = lax.broadcasted_iota(jnp.int32, (tokens, tokens), 0) == lax.broadcasted_iota(
        jnp.int32, (tokens, tokens), 1
    )
    v.keep[...] = jnp.sum(jnp.where(diagonal, v.keep_v[...].astype(F32), 0.0), axis=1, keepdims=True)
    v.head_mask[...] = jnp.zeros(v.head_mask.shape, F32)
    v.head_mask[:, 0:heads] = v.head_keep_v[...].astype(F32)
    v.part[...] = jnp.zeros(v.part.shape, F32)
    w_q.spread()
    send_cotangent(1)
    for wait in waits:
        wait()
    def wide(first):
        return jnp.concatenate([v.cond_buf[:, first + k, :] for k in range(width // 128)], axis=1)

    stacked = jnp.concatenate([wide(0), jnp.zeros((12, width), F32)], axis=0).astype(BF16)
    left = dot(stacked, select, NN).astype(BF16)
    for piece in range(7):
        if piece < 6:
            product = dot(left, v.ada_v[:, piece * width : (piece + 1) * width], NN)
        else:
            product = dot(left, v.head_v[...], NT)
        for image in range(4):
            v.part[image, piece : piece + 1, 0 : product.shape[1]] = product[image : image + 1]
    waits = [
        net.send(v.part.at[peer[0]], v.part_buf.at[index], peer)
        for index, peer in enumerate(here.dp_peers())
    ]
    w_q.send_straight((1,))
    w_o.send_diagonal()
    w_u.send_diagonal()
    w_o.send_straight()
    v.token[...] = jnp.sum(wide(8), axis=0, keepdims=True)
    for wait in waits:
        wait()
    v.mod[...] = v.part[dp] + v.part_buf[0] + v.part_buf[1] + v.part_buf[2]
    v.mod[7:8, 0:tokens] = v.keep_v[...].astype(F32)
    head_sigmoid = jax.nn.sigmoid(v.mod[6:7, 0:128])
    head_mask = v.head_mask[...]
    gate = dot(jnp.broadcast_to(head_mask * head_sigmoid, (8, 128)), v.expand[...], NN, exact=True)
    v.gate_row[...] = gate[0:1]

    loads[6].wait()

    def first_norm(rows):
        values = v.x_v[rows, :].astype(F32)
        centre = values - jnp.mean(values, axis=1, keepdims=True)
        spread = jnp.mean(centre * centre, axis=1, keepdims=True)
        normal = centre * lax.rsqrt(spread + epsilon)
        v.nb[rows, :] = (normal * (1.0 + v.mod[1:2]) + v.mod[0:1]).astype(BF16)

    by_rows(tokens, first_norm)
    wait_normed = net.send(v.nb.at[mine], v.nb.at[theirs], here.peer_core())

    w_q.share_straight(0)
    w_q.share_straight(1)
    w_u.send_straight()
    w_d.send_diagonal()
    w_d.send_straight()
    w_o.spread()
    w_q.share_diagonal()
    wait_mod = net.send(v.mod, v.mod_near, here.peer_z1())
    w_q.ready()

    @pl.loop(0, 3 * width // 384)
    def _(index):
        columns = span(index * 384, 384, 128)
        v.packed[:, columns] = dot(v.nb[mine, :], v.fq[:, columns], NN).astype(BF16)

    w_u.spread()

    lanes = lax.broadcasted_iota(jnp.int32, (1, 2 * size), 1)
    masks = ((lanes < size).astype(F32).astype(BF16), (lanes >= size).astype(F32).astype(BF16))
    scaled_masks = tuple(mask * jnp.asarray(factor, BF16) for mask in masks)
    low_lane = lax.broadcasted_iota(jnp.int32, (tokens, 2 * size), 1) < size

    def three(pair, block):
        return [block[:, span(part * width + pair * 2 * size, 2 * size, 128)] for part in range(3)]

    def attend(pair):
        queries, key_rows, value_rows = three(pair, v.packed)
        found = []
        for which in range(2):
            scores = dot(queries * scaled_masks[which], key_rows, NT)
            powers = jnp.exp(scores - jnp.max(scores, axis=1, keepdims=True))
            probs = powers * (1.0 / jnp.sum(powers, axis=1, keepdims=True))
            v.probs[pair * 2 + which] = probs
            found.append(dot(probs.astype(BF16), value_rows, NN))
        attended = jnp.where(low_lane, found[0], found[1])
        columns = span(pair * 2 * size, 2 * size, 128)
        v.attended[:, columns] = attended
        v.gated[mine, columns] = (attended * v.gate_row[:, columns]).astype(BF16)

    pl.loop(0, heads // 3)(attend)
    attend(heads // 3)
    w_o.share_straight(0)
    w_o.share_straight(1)
    w_o.share_diagonal()
    pl.loop(heads // 3 + 1, heads // 2)(attend)
    wait_gated = net.send(v.gated.at[mine], v.gated.at[theirs], here.peer_core())
    w_o.ready()

    @pl.loop(0, width // 256)
    def _(index):
        columns = span(index * 256, 256, 128)
        v.branch[:, columns] = dot(v.gated[mine, :], v.fo[:, columns], NN)

    loads[7].wait()

    def weigh(rows, second, modulation, keep):
        logit = jnp.sum(second.astype(F32) * v.token[...], axis=1, keepdims=True)
        router = jax.nn.sigmoid(logit)
        weight = keep * router
        v.grad_prod[rows, :] = (v.g_v[rows, :].astype(F32) * modulation[5:6] * weight).astype(BF16)
        return router

    def second_norm(rows):
        middle = v.x_v[rows, :].astype(F32) + v.mod[2:3] * v.branch[rows, :]
        v.middle[rows, :] = middle
        centre = middle - jnp.mean(middle, axis=1, keepdims=True)
        spread = jnp.mean(centre * centre, axis=1, keepdims=True)
        scale = lax.rsqrt(spread + epsilon)
        normal = centre * scale
        v.z2[rows, :] = normal
        v.scale2[rows, :] = scale
        second = (normal * (1.0 + v.mod[4:5]) + v.mod[3:4]).astype(BF16)
        v.second[rows, :] = second
        v.router[rows, :] = weigh(rows, second, v.mod, v.keep[rows, :])

    def some_rows(start, count, body):
        @pl.loop(0, count // ROWS)
        def _(index):
            body(span(start + index * ROWS, ROWS, ROWS))

    wait_near = []
    for k in range(2):
        some_rows(k * bit, bit, second_norm)
        block = slice(k * bit, k * bit + bit)
        landing = v.second.at[slice(tokens + k * bit, tokens + k * bit + bit)]
        wait_near.append(net.send(v.second.at[block], landing, here.peer_z1()))
    w_u.share_diagonal()
    w_u.share_straight(0)
    w_u.share_straight(1)
    half = width // 2
    other = span((1 - core) * half, half, 128)
    own = span(core * half, half, 128)
    wait_pair = [
        net.send(v.second.at[mine], v.second.at[slice(2 * tokens, 3 * tokens)], here.peer_core()),
        net.send(
            v.grad_prod.at[mine, other], v.dy_down.at[slice(2 * tokens, 3 * tokens)], here.peer_core()
        ),
    ]
    v.dy_down[mine, :] = v.grad_prod[mine, own]

    w_u.ready()
    inner = math.sqrt(2.0 / math.pi)
    units = hidden_width // 2

    def feed(start, count):
        tokens_of = slice(start, start + count)
        for index in range(units // 512):
            columns = slice(index * 512, index * 512 + 512)
            v.tmp[0:count, 0:512] = dot(v.second[tokens_of, :], v.fu[:, columns], NN)

            @pl.loop(0, count // ROWS)
            def _(step):
                rows = span(step * ROWS, ROWS, ROWS)
                there = span(start + step * ROWS, ROWS, ROWS)
                u = v.tmp[rows, 0:512]
                square = u * u
                t = jnp.tanh(u * (inner + (inner * 0.044715) * square))
                a = 0.5 + 0.5 * t
                value = u * a
                v.hidden[there, columns] = value.astype(BF16)
                v.slope[there, columns] = a + value * (1.0 - a) * (
                    2.0 * inner + (6.0 * inner * 0.044715) * square
                )

    def feed_back(start, count):
        tokens_of = slice(start, start + count)

        @pl.loop(0, units // 512)
        def _(index):
            columns = span(index * 512, 512, 128)
            back = dot(v.grad_prod[tokens_of, :], v.fd[columns, :], NT)
            v.grad_u[tokens_of, columns] = (back * v.slope[tokens_of, columns]).astype(BF16)

    def down(start, count, target, at, kind):
        @pl.loop(0, width // 256)
        def _(index):
            columns = span(index * 256, 256, 128)
            target[at, columns] = dot(v.hidden[start : start + count, :], v.fd[:, columns], NN).astype(kind)

    def up_back(start, count, target, at, kind):
        @pl.loop(0, width // 256)
        def _(index):
            columns = span(index * 256, 256, 128)
            target[at, columns] = dot(v.grad_u[start : start + count, :], v.fu[columns, :], NT).astype(kind)

    wait_units = []
    quarter_units = units // 2
    other_units = span((1 - core) * quarter_units, quarter_units, 128)
    own_units = span(core * quarter_units, quarter_units, 128)

    def hand_over(block, landing):
        wait_units.append(net.send(v.grad_u.at[block, other_units], v.dy_up.at[landing], here.peer_core()))
        v.dy_up[block, :] = v.grad_u[block, own_units]

    feed(0, tokens)
    wait_pair.append(
        net.send(v.hidden.at[mine], v.hidden.at[slice(2 * tokens, 3 * tokens)], here.peer_core())
    )
    pieces = []
    for number, (index, column, wide, kind) in enumerate(chunks):
        total = (v.t_qkv, v.t_out, v.t_up, v.t_down)[index]
        out = (v.o_qkv, v.o_out, v.o_up, v.o_down)[index]
        bufs = [getattr(v, f"c{number}_{k}") for k in range(7)]
        pieces.append(kind(net, here, total, out, bufs, column, wide))
    c_down, c_up, c_more, c_out = pieces[:4]
    c_qkv = pieces[4:]

    def weight_grad(total, left, right, step):
        @pl.loop(0, total.shape[0] // step)
        def _(index):
            rows = span(index * step, step, 128)
            total[rows, :] = dot(left[:, rows], right[...], TN).astype(BF16)

    wait_mod()
    v.keep_near[...] = jnp.sum(
        jnp.where(diagonal, v.mod_near[7:8, 0:tokens], 0.0), axis=1, keepdims=True
    )

    def weigh_near(rows):
        kept = v.keep_near[span(rows.start - tokens, ROWS, ROWS), :]
        weigh(rows, v.second[rows, :], v.mod_near, kept)

    def take_near(k):
        wait_near[k]()
        wait_cotangent[k]()
        some_rows(tokens + k * bit, bit, weigh_near)
        feed(tokens + k * bit, bit)

    take_near(0)
    w_d.share_diagonal()
    w_d.share_straight(0)
    w_d.share_straight(1)
    take_near(1)
    w_d.ready()
    last_rows = slice(3 * tokens, 4 * tokens)
    wait_pair.append(net.send(v.hidden.at[near_rows], v.hidden.at[last_rows], here.peer_core()))
    wait_pair.append(net.send(v.second.at[near_rows], v.second.at[last_rows], here.peer_core()))
    wait_pair.append(net.send(v.grad_prod.at[near_rows, other], v.dy_down.at[last_rows], here.peer_core()))
    feed_back(tokens, tokens)
    hand_over(near_rows, last_rows)
    wait_back = []
    for k in range(width // 256):
        columns = slice(k * 256, k * 256 + 256)
        v.near_back[:, columns] = dot(v.grad_u[near_rows, :], v.fu[columns, :], NT).astype(BF16)
        wait_back.append(
            net.send(v.near_back.at[:, columns], v.got_back.at[:, columns], here.peer_z1())
        )
    v.dy_down[near_rows, :] = v.grad_prod[near_rows, own]

    def down_quarter(place):
        rows = span(place * 384, 384, 128)
        v.t_down[rows, :] = dot(v.hidden[:, rows], v.dy_down[...], TN).astype(BF16)

    for wait in wait_pair:
        wait()
    down_quarter(here.peer_d()[0])
    c_down.first_diagonal()
    down_quarter(here.peer_x()[0])
    c_down.first_x()
    down_quarter(here.peer_y()[0])
    c_down.first_y()
    down_quarter(dp)
    feed_back(0, tokens)
    hand_over(mine, slice(2 * tokens, 3 * tokens))
    down(tokens, tokens, v.near_prod, mine, BF16)

    def near_level(rows):
        grad = v.g_v[span(rows.start + tokens, ROWS, ROWS), :].astype(F32)
        produced = v.near_prod[rows, :].astype(F32)
        v.level[rows, :] = jnp.sum(grad * v.mod_near[5:6] * produced, axis=1, keepdims=True)

    by_rows(tokens, near_level)
    v.level_out[...] = jnp.broadcast_to(
        jnp.sum(jnp.where(diagonal, v.level[...], 0.0), axis=0, keepdims=True), v.level_out.shape
    )
    wait_level = net.send(v.level_out, v.level_in, here.peer_z1())
    wait_prod = net.send(v.near_prod, v.got_prod, here.peer_z1())
    for wait in wait_units:
        wait()
    weight_grad(v.t_up, v.second, v.dy_up, 256)
    c_up.first()
    c_more.first()
    up_back(0, tokens, v.own_back, mine, F32)
    down(0, tokens, v.own_prod, mine, F32)

    def own_level(rows):
        grad = v.g_v[rows, :].astype(F32)
        v.level[rows, :] = jnp.sum(grad * v.mod[5:6] * v.own_prod[rows, :], axis=1, keepdims=True)

    by_rows(tokens, own_level)

    v.sums[...] = jnp.zeros(v.sums.shape, F32)
    wait_level()
    got = jnp.sum(jnp.where(diagonal, v.level_in[0:1, :], 0.0), axis=1, keepdims=True)
    router, keep = v.router[...], v.keep[...]
    v.logit[...] = (v.level[...] + got) * keep * router * (1.0 - router)

    def second_back(rows):
        logit = v.logit[rows, :]
        back = (v.own_back[rows, :] + v.got_back[rows, :].astype(F32)).astype(BF16).astype(F32)
        back += logit * v.token[...]
        normal = v.z2[rows, :]
        v.sums[1] += fold(logit * v.second[rows, :].astype(F32))
        v.sums[2] += fold(back * normal)
        v.sums[3] += fold(back)
        inside = back * (1.0 + v.mod[4:5])
        level = jnp.mean(inside, axis=1, keepdims=True)
        slope = jnp.mean(inside * normal, axis=1, keepdims=True)
        grad = v.g_v[rows, :].astype(F32) + v.scale2[rows, :] * (inside - level - normal * slope)
        v.grad_mid[rows, :] = grad
        v.sums[4] += fold(grad * v.branch[rows, :])
        v.grad_branch[rows, :] = (v.mod[2:3] * grad).astype(BF16)

    for wait in wait_back:
        wait()
    by_rows(tokens, second_back)
    wait_dbranch = net.send(v.grad_branch.at[:, other], v.dy_out.at[theirs], here.peer_core())
    v.dy_out[mine, :] = v.grad_branch[:, own]

    @pl.loop(0, width // 256)
    def _(index):
        columns = span(index * 256, 256, 128)
        v.tmp[:, columns] = dot(v.grad_branch[...], v.fo[columns, :], NT)


    def gate_back(rows):
        grad = v.tmp[rows, :]
        v.sums[5] += fold(grad * v.attended[rows, :])
        v.grad_att[rows, :] = (grad * v.gate_row[...]).astype(BF16)

    by_rows(tokens, gate_back)
    c_down.second()
    c_up.second()

    def gather_far(piece, block):
        block[pl.ds(core, 1), pl.ds(here.z, 1), pl.ds(dp, 1)] = piece[...][None, None, None]
        far = (here.z + 2) % Z_CHIPS
        return [net.send(piece, block.at[core, here.z, dp], here.peer_z2(), block.at[core, far, dp])]

    def gather_near(block, waits):
        for wait in waits:
            wait()
        near = here.z + 1 - 2 * (here.z % 2)
        moves = []
        for k in range(2):
            z, other = (here.z + 2 * k) % Z_CHIPS, (near + 2 * k) % Z_CHIPS
            tile = block.at[core, z, dp]
            moves.append(net.send(tile, tile, here.peer_z1(), block.at[core, other, dp]))
        return moves

    def gather_dp(block, waits):
        for wait in waits:
            wait()
        tiles = block.at[core, pl.ds(0, Z_CHIPS), dp]
        return [
            net.send(tiles, tiles, peer, block.at[core, pl.ds(0, Z_CHIPS), peer[0]])
            for peer in here.dp_peers()
        ]

    one_way = (dp + (1 - core) * (1 - 2 * here.x) + core * (2 - 4 * here.y), here.seq)
    other_way = (dp + core * (1 - 2 * here.x) + (1 - core) * (2 - 4 * here.y), here.seq)

    def gather_one(block, waits):
        for wait in waits:
            wait()
        tiles = block.at[core, pl.ds(0, Z_CHIPS), dp]
        return [net.send(tiles, tiles, one_way, block.at[core, pl.ds(0, Z_CHIPS), one_way[0]])]

    def gather_two(block, waits):
        for wait in waits:
            wait()
        moves = []
        for mine_dp, their_dp in ((dp, other_way[0]), (one_way[0], here.peer_d()[0])):
            tiles = block.at[core, pl.ds(0, Z_CHIPS), mine_dp]
            moves.append(
                net.send(tiles, tiles, other_way, block.at[core, pl.ds(0, Z_CHIPS), their_dp])
            )
        return moves

    def gather_pair(block, waits):
        for wait in waits:
            wait()
        return net.send(block.at[core], block.at[core], here.peer_core(), block.at[1 - core])

    def back_pair(pair):
        queries, key_rows, value_rows = three(pair, v.packed)
        columns = span(pair * 2 * size, 2 * size, 128)
        grad_att = v.grad_att[:, columns]
        gq, gk, gv = [], [], []
        for which in range(2):
            probs = v.probs[pair * 2 + which]
            grad_probs = dot(grad_att * masks[which], value_rows, NT)
            level = jnp.sum(probs * grad_probs, axis=1, keepdims=True)
            grad_scores = (probs * (grad_probs - level)).astype(BF16)
            gq.append(dot(grad_scores, key_rows, NN))
            gk.append(dot(grad_scores, queries, TN))
            gv.append(dot(probs.astype(BF16), grad_att, TN))
        for part, (grads, scale) in enumerate(((gq, factor), (gk, factor), (gv, 1.0))):
            both = jnp.where(low_lane, grads[0], grads[1]) * scale
            v.grad_pack[:, span(part * width + pair * 2 * size, 2 * size, 128)] = both.astype(BF16)

    head_back = dot(
        jnp.broadcast_to(jnp.sum(v.sums[5], axis=0, keepdims=True), (8, width)), v.expand[...], NT, exact=True
    )
    head_back = head_back[0:1] * head_mask * head_sigmoid * (1.0 - head_sigmoid)
    v.early_f[...] = jnp.zeros(v.early_f.shape, F32)
    rows_out = [jnp.sum(v.sums[k], axis=0, keepdims=True) for k in (4, 3, 2, 1)]
    cut = width // 2
    for slot, values in zip((0, 1, 2, 5, 6), (*rows_out, v.condition[...])):
        v.early_f[2 * slot : 2 * slot + 1, :] = values[:, 0:cut]
        v.early_f[2 * slot + 1 : 2 * slot + 2, :] = values[:, cut:width]
    v.early_f[8:9, 0:128] = head_back
    v.early_out[...] = v.early_f[...].astype(BF16)
    early = gather_far(v.early_out, v.early)
    pl.loop(0, heads // 4)(back_pair)
    early = gather_near(v.early, early)
    wait_gated()
    wait_dbranch()
    weight_grad(v.t_out, v.gated, v.dy_out, 256)
    c_out.first()
    pl.loop(heads // 4, heads // 2)(back_pair)
    packed_half = 3 * width // 2
    wait_dpack = net.send(
        v.grad_pack.at[:, span((1 - core) * packed_half, packed_half, 128)],
        v.dy_qkv.at[theirs],
        here.peer_core(),
    )
    v.dy_qkv[mine, :] = v.grad_pack[:, span(core * packed_half, packed_half, 128)]
    early = gather_one(v.early, early)
    c_down.third()
    c_more.second()
    wait_normed()
    wait_dpack()

    def qkv_grad(start, count):
        columns = slice(start, start + count)

        @pl.loop(0, width // 256)
        def _(index):
            rows = span(index * 256, 256, 128)
            v.t_qkv[rows, columns] = dot(v.nb[:, rows], v.dy_qkv[:, columns], TN).astype(BF16)

    c_out.second()
    qkv_grad(0, 512)
    c_qkv[0].first()
    qkv_grad(512, 384)
    c_qkv[1].first()
    early = gather_two(v.early, early)
    qkv_grad(896, 256)
    c_up.third()
    c_more.third()
    wait_prod()

    def finish(rows):
        produced = (v.own_prod[rows, :] + v.got_prod[rows, :].astype(F32)).astype(BF16).astype(F32)
        scaled = produced * (v.keep[rows, :] * v.router[rows, :])
        v.output[rows, :] = (v.middle[rows, :] + v.mod[5:6] * scaled).astype(BF16)
        v.sums[0] += fold(v.g_v[rows, :].astype(F32) * scaled)

    by_rows(tokens, finish)

    @pl.loop(0, width // 256)
    def _(index):
        columns = span(index * 256, 256, 128)
        v.tmp[:, columns] = dot(v.grad_pack[...], v.fq[columns, :], NT)

    c_qkv[0].second()
    c_qkv[2].first()

    def first_back(rows):
        back = v.tmp[rows, :]
        values = v.x_v[rows, :].astype(F32)
        centre = values - jnp.mean(values, axis=1, keepdims=True)
        spread = jnp.mean(centre * centre, axis=1, keepdims=True)
        scale = lax.rsqrt(spread + epsilon)
        normal = centre * scale
        v.sums[6] += fold(back * normal)
        v.sums[7] += fold(back)
        inside = back * (1.0 + v.mod[1:2])
        level = jnp.mean(inside, axis=1, keepdims=True)
        slope = jnp.mean(inside * normal, axis=1, keepdims=True)
        v.grad_input[rows, :] = v.grad_mid[rows, :] + scale * (inside - level - normal * slope)

    by_rows(tokens, first_back)
    shift = jnp.sum(v.sums[7], axis=0, keepdims=True)
    scale = jnp.sum(v.sums[6], axis=0, keepdims=True)
    v.late_f[...] = jnp.zeros(v.late_f.shape, F32)
    for k in range(width // 128):
        v.late_f[k : k + 1, :] = shift[:, k * 128 : (k + 1) * 128]
        v.late_f[8 + k : 9 + k, :] = scale[:, k * 128 : (k + 1) * 128]
    gate_two = jnp.sum(v.sums[0], axis=0, keepdims=True)
    for k in range(width // 128):
        v.late_f[16 + k : 17 + k, :] = gate_two[:, k * 128 : (k + 1) * 128]
    v.late_out[...] = v.late_f[...].astype(BF16)
    late = gather_far(v.late_out, v.late)
    c_down.fifth()
    c_up.fifth()
    c_qkv[1].second()
    early = gather_pair(v.early, early)
    c_out.third()
    late = gather_near(v.late, late)
    c_qkv[0].third()
    c_qkv[2].second()
    c_more.fifth()
    c_out.fourth()
    c_qkv[1].third()
    late = gather_dp(v.late, late)
    c_qkv[0].fourth()
    c_qkv[2].third()
    c_qkv[1].fourth()
    c_out.fifth()
    late = gather_pair(v.late, late)
    early()
    offset = dp * quarter + (here.seq % BLOCK) * SHARE
    pick = (
        lax.broadcasted_iota(jnp.int32, (width, SHARE), 0)
        == lax.broadcasted_iota(jnp.int32, (width, SHARE), 1) + offset
    ).astype(F32)

    every = v.early[...].reshape(512, cut).astype(F32).reshape(32, 16, cut)
    conditions = (
        dot(every[:, 12, :].astype(BF16), pick[0:cut].astype(BF16), NN)
        + dot(every[:, 13, :].astype(BF16), pick[cut:width].astype(BF16), NN)
    ).astype(BF16)
    for slot, piece in enumerate((2, 3, 4)):
        for side in range(2):
            start = piece * width + side * cut
            v.o_ada[:, start : start + cut] = dot(
                conditions, every[:, 2 * slot + side, :].astype(BF16), TN
            )
    v.o_head[...] = dot(every[:, 8, 0:128].astype(BF16), conditions, TN)[0:heads]
    totals = [jnp.sum(every[:, 10 + side, :], axis=0, keepdims=True) for side in range(2)]
    v.o_token[...] = (
        dot(jnp.broadcast_to(totals[0], (8, cut)), pick[0:cut], NN, exact=True)
        + dot(jnp.broadcast_to(totals[1], (8, cut)), pick[cut:width], NN, exact=True)
    )[0:1]

    c_qkv[0].fifth()
    c_qkv[1].fifth()
    for chunk in (c_down, c_up, c_more):
        chunk.end()
    late()
    tail = v.late[...].reshape(1024, 128).astype(F32).reshape(32, 32, 128)
    for base, piece in ((0, 0), (8, 1), (16, 5)):
        row = jnp.concatenate([tail[:, base + k, :] for k in range(width // 128)], axis=1)
        start = piece * width
        v.o_ada[:, start : start + width] = dot(conditions, row.astype(BF16), TN)
    c_qkv[2].fifth()
    for chunk in (c_out, *c_qkv):
        chunk.end()
    net.finish()


def layer(time_table, time_index, w_token, w_head, token_keep, head_keep, inputs, cotangent, w_ada, wq, wo, wu, wd):
    tokens, width = inputs.shape
    hidden_width = wu.shape[1]
    heads = head_keep.shape[1]
    widths = [wq.shape[1], wo.shape[1], wu.shape[1], wd.shape[1]]
    depths = [4 * w.shape[0] for w in (wq, wo, wu, wd)]
    chunks = chunk_list(widths)
    operands = dict(
        time_table=time_table, time_index=time_index, w_token=w_token, w_head=w_head, token_keep=token_keep, head_keep=head_keep,
        inputs=inputs, cotangent=cotangent, w_ada=w_ada, wq=wq, wo=wo, wu=wu, wd=wd,
    )
    outs = dict(
        ada=((SHARE, 6 * width), F32),
        qkv=((depths[0] // 32, widths[0]), F32),
        out=((depths[1] // 32, widths[1]), F32),
        up=((depths[2] // 32, widths[2]), F32),
        down=((depths[3] // 32, widths[3]), F32),
        head=((heads, SHARE), F32),
        token=((1, SHARE), F32),
    )
    results = dict(output=((tokens, width), BF16), grad_input=((tokens, width), F32))
    results.update({"o_" + k: s for k, s in outs.items()})
    space = dict(
        table_v=(time_table.shape, BF16),
        index_v=(time_index.shape, jnp.int32),
        small_v=((16, 128), F32),
        condition=((1, width), F32),
        token_v=(w_token.shape, BF16),
        keep_v=(token_keep.shape, jnp.int32),
        head_keep_v=(head_keep.shape, jnp.int32),
        head_mask=((1, 128), F32),
        head_v=(w_head.shape, BF16),
        ada_v=(w_ada.shape, BF16),
        x_v=((tokens, width), BF16),
        g_v=((2 * tokens, width), BF16),
        mod_near=((8, width), F32),
        keep_near=((tokens, 1), F32),
        fq=((depths[0], widths[0]), BF16),
        fo=((depths[1], widths[1]), BF16),
        fu=((depths[2], widths[2] // 2), BF16),
        fd=((depths[3] // 2, widths[3]), BF16),
        cond_buf=((4, 16, 128), F32),
        part=((4, 8, width), F32),
        part_buf=((3, 8, width), F32),
        mod=((8, width), F32),
        token=((1, width), F32),
        keep=((tokens, 1), F32),
        expand=((128, width), F32),
        gate_row=((1, width), F32),
        nb=((2 * tokens, width), BF16),
        packed=((tokens, 3 * width), BF16),
        probs=((heads, tokens, tokens), F32),
        attended=((tokens, width), F32),
        gated=((2 * tokens, width), BF16),
        branch=((tokens, width), F32),
        middle=((tokens, width), F32),
        z2=((tokens, width), F32),
        scale2=((tokens, 1), F32),
        second=((4 * tokens, width), BF16),
        router=((tokens, 1), F32),
        logit=((tokens, 1), F32),
        grad_prod=((2 * tokens, width), BF16),
        dy_down=((4 * tokens, width // 2), BF16),
        tmp=((tokens, width), F32),
        hidden=((4 * tokens, hidden_width // 2), BF16),
        slope=((2 * tokens, hidden_width // 2), F32),
        grad_u=((2 * tokens, hidden_width // 2), BF16),
        dy_up=((4 * tokens, hidden_width // 4), BF16),
        own_prod=((tokens, width), F32),
        own_back=((tokens, width), F32),
        near_prod=((tokens, width), BF16),
        near_back=((tokens, width), BF16),
        got_prod=((tokens, width), BF16),
        got_back=((tokens, width), BF16),
        level=((tokens, 1), F32),
        level_out=((8, tokens), F32),
        level_in=((8, tokens), F32),
        grad_mid=((tokens, width), F32),
        grad_branch=((tokens, width), BF16),
        dy_out=((2 * tokens, width // 2), BF16),
        grad_att=((tokens, width), BF16),
        grad_pack=((tokens, 3 * width), BF16),
        dy_qkv=((2 * tokens, 3 * width // 2), BF16),
        sums=((8, 8, width), F32),
        early_f=((16, width // 2), F32),
        early_out=((16, width // 2), BF16),
        early=((2, Z_CHIPS, 4, 16, width // 2), BF16),
        late_f=((32, 128), F32),
        late_out=((32, 128), BF16),
        late=((2, Z_CHIPS, 4, 32, 128), BF16),
        t_qkv=((depths[0], widths[0] // 2), BF16),
        t_out=((depths[1], widths[1] // 2), BF16),
        t_up=((depths[2], widths[2] // 4), BF16),
        t_down=((depths[3] // 2, widths[3] // 2), BF16),
    )
    for number, (index, _, wide, kind) in enumerate(chunks):
        shapes = kind.shapes(depths[index] // 16, wide)
        for k, shape in enumerate(shapes):
            space[f"c{number}_{k}"] = (shape, BF16)
        space[f"c{number}_6"] = (kind.sums(depths[index] // 16, wide), F32)
    copies = 6 + 4 * 13 + 32 + len(chunks) * 14 + 14
    names = list(operands) + list(results) + list(space) + ["send_sems", "recv_sems", "local_sems"]
    return pl.pallas_call(
        functools.partial(layer_kernel, names, chunks, (tokens, width, heads, hidden_width)),
        out_shape=[pltpu.VMEM(*r) for r in results.values()],
        in_specs=[ANY] * len(operands),
        out_specs=[VMEM] * len(results),
        scratch_shapes=[pltpu.VMEM(*s) for s in space.values()]
        + [
            pltpu.SemaphoreType.DMA((copies,)),
            pltpu.SemaphoreType.DMA((copies,)),
            pltpu.SemaphoreType.DMA((16,)),
        ],
        compiler_params=pltpu.CompilerParams(
            collective_id=0, has_side_effects=True, vmem_limit_bytes=61 * 2**20
        ),
    )(*operands.values())


def copy_kernel(count, *refs):
    copies = [
        pltpu.make_async_copy(refs[k], refs[count + k], refs[2 * count].at[k]) for k in range(count)
    ]
    for copy in copies:
        copy.start()
    for copy in copies:
        copy.wait()


def copy_all(arrays):
    count = len(arrays)
    return pl.pallas_call(
        functools.partial(copy_kernel, count),
        out_shape=[jax.ShapeDtypeStruct(a.shape, a.dtype) for a in arrays],
        in_specs=[VMEM] * count,
        out_specs=[ANY] * count,
        scratch_shapes=[pltpu.SemaphoreType.DMA((count,))],
        compiler_params=pltpu.CompilerParams(vmem_limit_bytes=16 * 2**20),
    )(*(pltpu.with_memory_space_constraint(a, pltpu.VMEM) for a in arrays))


def across_blocks(part, seq_size):
    blocks = seq_size // BLOCK
    if blocks == 1:
        return part
    groups = [[b * BLOCK + j for b in range(blocks)] for j in range(BLOCK)]
    mine = lax.psum_scatter(
        part, "seq", scatter_dimension=0, axis_index_groups=groups, tiled=True
    )
    moves = [(b * BLOCK + j, j * blocks + b) for b in range(blocks) for j in range(BLOCK)]
    return lax.ppermute(mine, "seq", moves)


def per_device(
    seq_size, inputs, time_table, time_index, token_keep, head_keep, cotangent,
    w_ada, w_qkv, w_out, w_up, w_down, w_head, w_token,
):
    out = layer(
        time_table, time_index[None], w_token, w_head.T, token_keep, head_keep,
        inputs[0], cotangent[0], w_ada, w_qkv, w_out, w_up, w_down,
    )
    output, grad_input, ada, qkv, outw, up, down, head, token = copy_all(out)
    parts = (ada, qkv, outw, up, down, head.T, token[0])
    parts = tuple(across_blocks(part, seq_size) for part in parts)
    return (output[None], grad_input[None]) + parts


def solution(mesh):
    both = ("dp", "seq")
    in_specs = (
        P(both, None, None), P(), P(both), P(both, None), P(both, None), P(both, None, None),
        P("dp", None), P("dp", None), P("dp", None), P("dp", None), P("dp", None), P("dp", None), P("dp"),
    )
    out_specs = (P(both, None, None), P(both, None, None)) + (P(both, None),) * 6 + (P(both),)
    return jax.shard_map(
        functools.partial(per_device, mesh.shape["seq"]),
        mesh=mesh, in_specs=in_specs, out_specs=out_specs, check_vma=False,
    )
```

```python
import functools
import math
import types

import jax
import jax.numpy as jnp
from jax import lax
from jax.experimental import pallas as pl
from jax.experimental.pallas import tpu as pltpu
from jax.sharding import PartitionSpec as P

epsilon = 1e-06
MESH = pl.DeviceIdType.MESH
ANY = pl.BlockSpec(memory_space=pl.ANY)
VMEM = pl.BlockSpec(memory_space=pltpu.VMEM)
Z_CHIPS = 4
BLOCK = 2 * Z_CHIPS
F32, BF16 = jnp.float32, jnp.bfloat16
NN, NT, TN = ((1,), (0,)), ((1,), (1,)), ((0,), (0,))
ROWS = 32
SHARE = 24


def dot(left, right, dims, exact=False):
    return lax.dot_general(
        left, right, (dims, ((), ())), preferred_element_type=F32,
        precision=lax.Precision.HIGHEST if exact else None,
    )


def span(start, size, unit):
    return pl.ds(pl.multiple_of(start, unit), size)


def by_rows(total, body, step=ROWS):
    @pl.loop(0, total // step)
    def _(index):
        body(span(index * step, step, step))


def fold(values):
    return jnp.sum(values.reshape(-1, 8, values.shape[-1]), axis=0)


class Place:
    def __init__(self):
        self.dp = lax.axis_index("dp")
        self.seq = lax.axis_index("seq")
        self.x = self.dp % 2
        self.y = self.dp // 2
        self.core = self.seq % 2
        self.z = (self.seq // 2) % Z_CHIPS
        self.side = self.z % 2
        self.high = self.z // 2
        self.outer = self.seq // BLOCK

    def z_of(self, step):
        return (self.z + step) % Z_CHIPS

    def peer_x(self):
        return (self.y * 2 + 1 - self.x, self.seq)

    def peer_y(self):
        return ((1 - self.y) * 2 + self.x, self.seq)

    def peer_d(self):
        return ((1 - self.y) * 2 + 1 - self.x, self.seq)

    def peer_core(self):
        return (self.dp, self.seq + 1 - 2 * self.core)

    def peer_z(self, step):
        return (self.dp, self.outer * BLOCK + self.z_of(step) * 2 + self.core)

    def peer_z1(self):
        return (self.dp, self.seq + 2 - 4 * (self.z % 2))

    def peer_z2(self):
        return (self.dp, self.seq + 4 - 8 * (self.z // 2))

    def dp_peers(self):
        return (self.peer_x(), self.peer_y(), self.peer_d())

    def greet(self):
        peers = list(self.dp_peers()) + [self.peer_core()]
        for k in range(1, Z_CHIPS):
            same = self.peer_z(k)
            peers += [same, (same[0], same[1] + 1 - 2 * self.core)]
        for peer in peers:
            pl.semaphore_signal(
                pltpu.get_barrier_semaphore(), inc=1, device_id=peer, device_id_type=MESH
            )
        self.peers = len(peers)

    def meet(self):
        pl.semaphore_wait(pltpu.get_barrier_semaphore(), self.peers)


class Net:
    def __init__(self, send_sems, recv_sems):
        self.send_sems = send_sems
        self.recv_sems = recv_sems
        self.used = 0
        self.sent = []

    def send(self, src, dst, peer, landing=None):
        slot = self.used
        self.used += 1

        def copy_to(target):
            return pltpu.make_async_remote_copy(
                src_ref=src,
                dst_ref=target,
                send_sem=self.send_sems.at[slot],
                recv_sem=self.recv_sems.at[slot],
                device_id=peer,
                device_id_type=MESH,
            )

        copy = copy_to(dst)
        copy.start()
        self.sent.append(copy)
        arrival = copy if landing is None else copy_to(landing)
        return arrival.wait_recv

    def plan(self, src, dst, peer):
        slot = self.used
        self.used += 1
        return pltpu.make_async_remote_copy(
            src_ref=src,
            dst_ref=dst,
            send_sem=self.send_sems.at[slot],
            recv_sem=self.recv_sems.at[slot],
            device_id=peer,
            device_id_type=MESH,
        )

    def finish(self):
        for copy in self.sent:
            copy.wait_send()


class Weight:
    def __init__(self, net, here, own, full):
        self.net, self.here, self.own, self.full = net, here, own, full
        self.depth = own.shape[0]
        self.piece = self.depth // Z_CHIPS
        self.width = own.shape[1] // 2
        self.wait_xy, self.last = [], []

    def columns(self, core):
        return span(core * self.width, self.width, 128)

    def quarter(self, dp):
        return span(dp * self.depth, self.depth, 16)

    def part(self, dp, z):
        return span(dp * self.depth + z * self.piece, self.piece, 16)

    def keep(self, sem):
        self.local = pltpu.make_async_copy(self.own, self.full.at[self.quarter(self.here.dp)], sem)
        self.local.start()

    def send_diagonal(self):
        here, columns = self.here, self.columns(self.here.core)
        peer = here.peer_d()
        self.wait_d = self.net.send(
            self.own.at[span(here.z * self.piece, self.piece, 16), columns],
            self.full.at[self.part(here.dp, here.z), columns],
            peer,
            self.full.at[self.part(peer[0], here.z), columns],
        )

    def rows(self, dp, side):
        half = self.depth // 2
        return span(dp * self.depth + side * half, half, 16)

    def send_straight(self, sides=(0, 1)):
        here, columns = self.here, self.columns(self.here.core)
        self.wait_xy += [
            [
                self.net.send(
                    self.own.at[self.rows(0, side), columns],
                    self.full.at[self.rows(here.dp, side), columns],
                    peer,
                    self.full.at[self.rows(peer[0], side), columns],
                )
                for peer in (here.peer_x(), here.peer_y())
            ]
            for side in sides
        ]

    def spread(self):
        here, columns = self.here, self.columns(self.here.core)
        diagonal = here.peer_d()[0]
        self.wait_d()
        piece = self.full.at[self.part(diagonal, here.z), columns]
        self.wait_z = [
            self.net.send(
                piece, piece, here.peer_z(step),
                self.full.at[self.part(diagonal, here.z_of(Z_CHIPS - step)), columns],
            )
            for step in range(1, Z_CHIPS)
        ]

    def hand(self, rows):
        here = self.here
        block = self.full.at[rows, self.columns(here.core)]
        landing = self.full.at[rows, self.columns(1 - here.core)]
        self.last.append(self.net.send(block, block, here.peer_core(), landing))

    def share_straight(self, side):
        here = self.here
        for wait, peer in zip(self.wait_xy[side], (here.peer_x(), here.peer_y())):
            wait()
            self.hand(self.rows(peer[0], side))

    def share_diagonal(self):
        for wait in self.wait_z:
            wait()
        self.hand(self.quarter(self.here.peer_d()[0]))

    def ready(self):
        for wait in self.last:
            wait()
        self.local.wait()


class HalfWeight(Weight):
    def __init__(self, net, here, own, full, by_columns):
        self.net, self.here, self.own, self.full, self.by_columns = net, here, own, full, by_columns
        self.last = []

    def source(self, part):
        here = self.here
        if self.by_columns:
            return self.own.at[:, span((2 * here.core + part) * 768 + here.side * 384, 384, 128)]
        return self.own.at[span(here.side * 384 + part * 192, 192, 16), span(here.core * 384, 384, 128)]

    def block(self, dp, part, core):
        if self.by_columns:
            return self.full.at[span(dp * 192, 192, 16), span((2 * core + part) * 384, 384, 128)]
        return self.full.at[span(dp * 384 + part * 192, 192, 16), span(core * 384, 384, 128)]

    def whole(self, dp, core):
        if self.by_columns:
            return self.full.at[span(dp * 192, 192, 16), span(core * 768, 768, 128)]
        return self.full.at[span(dp * 384, 384, 16), span(core * 384, 384, 128)]

    def keep(self, sems):
        dp, side = self.here.dp, self.here.side
        if self.by_columns:
            moves = [
                (
                    self.own.at[:, span(k * 768 + side * 384, 384, 128)],
                    self.full.at[span(dp * 192, 192, 16), span(k * 384, 384, 128)],
                )
                for k in range(4)
            ]
        else:
            moves = [(self.own.at[span(side * 384, 384, 16)], self.full.at[span(dp * 384, 384, 16)])]
        self.locals = [
            pltpu.make_async_copy(source, target, sem) for (source, target), sem in zip(moves, sems)
        ]
        for copy in self.locals:
            copy.start()

    def send_diagonal(self):
        here = self.here
        peer = here.peer_d()
        self.wait_d = self.net.send(
            self.source(here.high),
            self.block(here.dp, here.high, here.core),
            peer,
            self.block(peer[0], here.high, here.core),
        )

    def send_straight(self):
        here = self.here
        self.wait_xy = [
            [
                self.net.send(
                    self.source(part),
                    self.block(here.dp, part, here.core),
                    peer,
                    self.block(peer[0], part, here.core),
                )
                for peer in (here.peer_x(), here.peer_y())
            ]
            for part in range(2)
        ]

    def spread(self):
        here = self.here
        diagonal = here.peer_d()[0]
        self.wait_d()
        piece = self.block(diagonal, here.high, here.core)
        self.wait_z = [
            self.net.send(
                piece, piece, here.peer_z2(), self.block(diagonal, 1 - here.high, here.core)
            )
        ]

    def pass_core(self, block, landing):
        self.last.append(self.net.send(block, block, self.here.peer_core(), landing))

    def share_straight(self, part):
        here = self.here
        for wait, peer in zip(self.wait_xy[part], (here.peer_x(), here.peer_y())):
            wait()
            self.pass_core(self.block(peer[0], part, here.core), self.block(peer[0], part, 1 - here.core))

    def share_diagonal(self):
        here = self.here
        diagonal = here.peer_d()[0]
        for wait in self.wait_z:
            wait()
        self.pass_core(self.whole(diagonal, here.core), self.whole(diagonal, 1 - here.core))

    def ready(self):
        for wait in self.last:
            wait()
        for copy in self.locals:
            copy.wait()


class WholeWeight(HalfWeight):
    def send_diagonal(self):
        here = self.here
        peer = here.peer_d()
        self.wait_d = [
            self.net.send(
                self.source(part),
                self.block(here.dp, part, here.core),
                peer,
                self.block(peer[0], part, here.core),
            )
            for part in range(2)
        ]

    def share_diagonal(self):
        here = self.here
        diagonal = here.peer_d()[0]
        for wait in self.wait_d:
            wait()
        self.pass_core(self.whole(diagonal, here.core), self.whole(diagonal, 1 - here.core))


class Chunk:
    @staticmethod
    def shapes(rows, wide):
        return ((2, 2 * rows, wide),) * 2 + ((2 * rows, wide),) * 2 + ((2, rows, wide), (rows, wide))

    def __init__(self, net, here, total, out, bufs, column, width):
        self.net, self.here, self.out = net, here, out
        self.total = total.at[:, span(column, width, 128)]
        self.block = total.shape[0] // 16
        self.column, self.width = column, width
        self.r1a, self.r1b, self.r2a, self.r2b, self.r3a, self.r3b, self.f32 = bufs

    @staticmethod
    def sums(rows, wide):
        return (rows, wide)

    def columns(self, core):
        return span(core * (self.out.shape[1] // 2) + self.column, self.width, 128)

    def upper(self, dp):
        return self.total.at[span(dp * 4 * self.block, 2 * self.block, 16)]

    def lower(self, dp):
        return self.total.at[span(dp * 4 * self.block + 2 * self.block, 2 * self.block, 16)]

    def add(self, total, extra):
        def body(rows):
            total[rows, :] = (total[rows, :].astype(F32) + extra[rows, :].astype(F32)).astype(BF16)

        by_rows(total.shape[0], body, 16)

    def first_diagonal(self):
        here, dp = self.here, self.here.peer_d()[0]
        self.wait_a = [self.net.send(self.upper(dp), self.r1a.at[1 - here.y], here.peer_x())]
        self.wait_b = [self.net.send(self.lower(dp), self.r1b.at[1 - here.x], here.peer_y())]

    def first_x(self):
        here, peer = self.here, self.here.peer_x()
        self.wait_a.append(self.net.send(self.upper(peer[0]), self.r1a.at[here.y], peer))

    def first_y(self):
        here, peer = self.here, self.here.peer_y()
        self.wait_b.append(self.net.send(self.lower(peer[0]), self.r1b.at[here.x], peer))

    def first(self):
        self.first_diagonal()
        self.first_x()
        self.first_y()

    def second(self):
        here = self.here
        for wait in self.wait_a:
            wait()
        away = self.upper((1 - here.y) * 2 + here.x)
        self.add(away, self.r1a.at[1 - here.y])
        next_a = self.net.send(away, self.r2a.at[span(0, away.shape[0], 16)], here.peer_y())
        for wait in self.wait_b:
            wait()
        away = self.lower(here.y * 2 + 1 - here.x)
        self.add(away, self.r1b.at[1 - here.x])
        next_b = self.net.send(away, self.r2b, here.peer_x())
        self.add(self.upper(here.dp), self.r1a.at[here.y])
        self.add(self.lower(here.dp), self.r1b.at[here.x])
        self.wait_a, self.wait_b = next_a, next_b

    def mine(self, z):
        return self.total.at[span((self.here.dp * 4 + z) * self.block, self.block, 16)]

    def third(self):
        here = self.here
        self.wait_a()
        self.add(self.upper(here.dp), self.r2a)
        self.wait_b()
        self.add(self.lower(here.dp), self.r2b)
        odd = 1 - here.z % 2
        self.waits = [
            self.net.send(self.mine(odd + 2 * k), self.r3a.at[k], here.peer_z1()) for k in range(2)
        ]

    def fourth(self):
        here = self.here
        far = (here.z + 2) % Z_CHIPS
        for wait in self.waits:
            wait()
        self.add(self.mine(far), self.r3a.at[far // 2])
        self.wait = self.net.send(self.mine(far), self.r3b, here.peer_z2())
        self.add(self.mine(here.z), self.r3a.at[here.z // 2])

    def fifth(self):
        here = self.here
        self.wait()
        own = self.mine(here.z)

        def body(rows):
            self.f32[rows, :] = own[rows, :].astype(F32) + self.r3b[rows, :].astype(F32)

        by_rows(self.block, body, 16)
        self.pass_on()

    def pass_on(self):
        here = self.here
        part = self.block // 2
        self.wait = self.net.send(
            self.f32.at[span((1 - here.core) * part, part, 8)],
            self.out.at[:, self.columns(here.core)],
            here.peer_core(),
            self.out.at[:, self.columns(1 - here.core)],
        )
        self.out[:, self.columns(here.core)] = self.f32[span(here.core * part, part, 8), :]

    def end(self):
        self.wait()


class LastChunk(Chunk):
    @staticmethod
    def shapes(rows, wide):
        return ((2, 2 * rows, wide),) * 2 + ((2 * rows, wide),) * 2 + ((3, rows, wide), (16, 128))

    def third(self):
        here = self.here
        self.wait_a()
        self.add(self.upper(here.dp), self.r2a)
        self.wait_b()
        self.add(self.lower(here.dp), self.r2b)
        self.waits = [
            self.net.send(self.mine(here.z_of(k)), self.r3a.at[k - 1], here.peer_z(k))
            for k in range(1, Z_CHIPS)
        ]

    def fifth(self):
        for wait in self.waits:
            wait()
        own = self.mine(self.here.z)

        def body(rows):
            total = own[rows, :].astype(F32)
            for k in range(Z_CHIPS - 1):
                total += self.r3a[k, rows, :].astype(F32)
            self.f32[rows, :] = total

        by_rows(self.block, body, 16)
        self.pass_on()


class UpChunk(LastChunk):
    @staticmethod
    def sums(rows, wide):
        return (2, rows, wide)

    def place(self, core, side):
        return span((2 * core + self.column // self.width) * 768 + side * 384, 384, 128)

    def fifth(self):
        here = self.here
        for wait in self.waits:
            wait()
        part = self.block // 2
        self.waits = []
        for k, (left, right, side) in enumerate(
            (
                (self.mine(here.z), self.r3a.at[1], here.side),
                (self.r3a.at[0], self.r3a.at[2], 1 - here.side),
            )
        ):

            def body(rows):
                self.f32[k, rows, :] = left[rows, :].astype(F32) + right[rows, :].astype(F32)

            by_rows(self.block, body, 16)
            self.waits.append(
                self.net.send(
                    self.f32.at[k, span((1 - here.core) * part, part, 8)],
                    self.out.at[:, self.place(here.core, side)],
                    here.peer_core(),
                    self.out.at[:, self.place(1 - here.core, side)],
                )
            )
            self.out[:, self.place(here.core, side)] = self.f32[k, span(here.core * part, part, 8), :]

    def end(self):
        for wait in self.waits:
            wait()


class DownChunk(Chunk):
    @staticmethod
    def shapes(rows, wide):
        return ((2, rows, wide),) * 2 + ((rows, wide),) * 2 + ((16, 128), (2, rows, wide))

    def __init__(self, net, here, total, out, bufs, column, width):
        super().__init__(net, here, total, out, bufs, column, width)
        self.block = total.shape[0] // 8

    def part(self, dp, which):
        return self.total.at[span((dp * 2 + which) * self.block, self.block, 16)]

    def upper(self, dp):
        return self.part(dp, 0)

    def lower(self, dp):
        return self.part(dp, 1)

    def third(self):
        here = self.here
        self.wait_a()
        self.add(self.upper(here.dp), self.r2a)
        self.wait_b()
        self.add(self.lower(here.dp), self.r2b)
        inner = (here.side - here.high) * (here.side - here.high)
        there = here.seq + (1 - inner) * (2 - 4 * here.side) + inner * (4 - 8 * here.high)
        self.wait = self.net.send(
            self.part(here.dp, 1 - here.high), self.r3b.at[0], (here.dp, there)
        )
        self.across = self.net.plan(
            self.part(here.dp, here.high), self.r3b.at[1], (here.dp, here.seq + 6 - 4 * here.z)
        )

        @pl.when(here.side != here.high)
        def _():
            self.across.start()

    def fifth(self):
        here = self.here
        self.wait()

        def total(left):
            def body(rows):
                self.f32[rows, :] = left[rows, :].astype(F32) + self.r3b[0, rows, :].astype(F32)

            by_rows(self.block, body, 16)

        @pl.when(here.side == here.high)
        def _():
            total(self.part(here.dp, here.high))

        @pl.when(here.side != here.high)
        def _():
            self.across.wait()
            total(self.r3b.at[1])

        self.pass_on()


class HeadColumns:
    def columns(self, core):
        return span(self.column // self.width * 768 + core * 384, 384, 128)


class HeadChunk(HeadColumns, Chunk):
    pass


class LastHeadChunk(HeadColumns, LastChunk):
    pass


def chunk_list(widths):
    cuts = (
        (3, (384,), (DownChunk,)),
        (2, (384, 384), (UpChunk, UpChunk)),
        (1, (384,), (Chunk,)),
        (0, (384, 384, 384), (HeadChunk, HeadChunk, LastHeadChunk)),
    )
    chunks = []
    for index, parts, kinds in cuts:
        column = 0
        for part, kind in zip(parts, kinds):
            chunks.append((index, column, part, kind))
            column += part
    return chunks


def layer_kernel(names, chunks, sizes, *refs):
    v = types.SimpleNamespace(**dict(zip(names, refs)))
    tokens, width, heads, hidden_width = sizes
    quarter = width // 4
    size = width // heads
    factor = size ** (-0.5)
    here = Place()
    core, dp = here.core, here.dp
    net = Net(v.send_sems, v.recv_sems)
    mine, theirs = slice(0, tokens), slice(tokens, 2 * tokens)
    near_rows = theirs
    both, pair_both = slice(0, 2 * tokens), slice(2 * tokens, 4 * tokens)

    here.greet()
    loads = []
    for number, (source, target) in enumerate(
        (
            (v.time_table, v.table_v), (v.w_token, v.token_v), (v.w_head, v.head_v), (v.w_ada, v.ada_v),
            (v.token_keep, v.keep_v), (v.head_keep, v.head_keep_v), (v.inputs, v.x_v), (v.cotangent, v.g_v.at[mine]),
            (v.time_index, v.index_v),
        )
    ):
        copy = pltpu.make_async_copy(source, target, v.local_sems.at[7 + number])
        copy.start()
        loads.append(copy)
    w_q, w_o = Weight(net, here, v.wq, v.fq), Weight(net, here, v.wo, v.fo)
    w_u, w_d = HalfWeight(net, here, v.wu, v.fu, True), WholeWeight(net, here, v.wd, v.fd, False)
    weights = [w_q, w_o, w_u, w_d]
    w_q.keep(v.local_sems.at[0])
    w_o.keep(v.local_sems.at[1])
    w_u.keep([v.local_sems.at[2 + k] for k in range(4)])
    w_d.keep([v.local_sems.at[6]])
    select = (
        lax.broadcasted_iota(jnp.int32, (width, quarter), 0)
        == lax.broadcasted_iota(jnp.int32, (width, quarter), 1) + dp * quarter
    ).astype(F32).astype(BF16)
    loads[1].wait()
    token = jnp.broadcast_to(v.token_v[...].astype(F32).reshape(1, quarter), (16, quarter))
    placed = dot(token.astype(BF16), select, NT)
    loads[8].wait()
    loads[0].wait()
    rows = v.table_v.shape[0]
    whole = rows // 128 * 128
    index_row = jnp.broadcast_to(v.index_v[...], (16, whole))
    hot = (lax.broadcasted_iota(jnp.int32, (16, whole), 1) == index_row).astype(F32).astype(BF16)
    row = dot(hot, v.table_v[0:whole, :], NN)[0:1]
    rest = lax.broadcasted_iota(jnp.int32, (rows - whole, width), 0) + whole
    rest = jnp.where(
        rest == jnp.broadcast_to(v.index_v[...], rest.shape), v.table_v[whole:rows, :].astype(F32), 0.0
    )
    row += jnp.sum(rest, axis=0, keepdims=True)
    condition = (row * jax.nn.sigmoid(row)).astype(BF16).astype(F32)
    v.condition[...] = condition
    v.small_v[...] = jnp.zeros(v.small_v.shape, F32)
    for k in range(width // 128):
        v.small_v[k : k + 1, :] = condition[:, k * 128 : (k + 1) * 128]
        v.small_v[8 + k : 9 + k, :] = placed[0:1, k * 128 : (k + 1) * 128]
    here.meet()

    w_q.send_diagonal()
    bit = tokens // 2
    wait_cotangent = []

    def send_cotangent(k):
        block = slice(k * bit, k * bit + bit)
        landing = v.g_v.at[slice(tokens + k * bit, tokens + k * bit + bit)]
        wait_cotangent.append(net.send(v.cotangent.at[block], landing, here.peer_z1()))

    send_cotangent(0)
    waits = [
        net.send(v.small_v, v.cond_buf.at[dp], peer, v.cond_buf.at[peer[0]])
        for peer in here.dp_peers()
    ]
    w_q.send_straight((0,))
    v.cond_buf[pl.ds(dp, 1)] = v.small_v[...][None]
    head_of = lax.broadcasted_iota(jnp.int32, (128, width), 0) * size
    lane = lax.broadcasted_iota(jnp.int32, (128, width), 1)
    v.expand[...] = ((lane >= head_of) & (lane < head_of + size)).astype(F32)
    for load in loads[2:6]:
        load.wait()
    diagonal = lax.broadcasted_iota(jnp.int32, (tokens, tokens), 0) == lax.broadcasted_iota(
        jnp.int32, (tokens, tokens), 1
    )
    v.keep[...] = jnp.sum(jnp.where(diagonal, v.keep_v[...].astype(F32), 0.0), axis=1, keepdims=True)
    v.head_mask[...] = jnp.zeros(v.head_mask.shape, F32)
    v.head_mask[:, 0:heads] = v.head_keep_v[...].astype(F32)
    v.part[...] = jnp.zeros(v.part.shape, F32)
    w_q.spread()
    send_cotangent(1)
    for wait in waits:
        wait()
    def wide(first):
        return jnp.concatenate([v.cond_buf[:, first + k, :] for k in range(width // 128)], axis=1)

    stacked = jnp.concatenate([wide(0), jnp.zeros((12, width), F32)], axis=0).astype(BF16)
    left = dot(stacked, select, NN).astype(BF16)
    for piece in range(7):
        if piece < 6:
            product = dot(left, v.ada_v[:, piece * width : (piece + 1) * width], NN)
        else:
            product = dot(left, v.head_v[...], NT)
        for image in range(4):
            v.part[image, piece : piece + 1, 0 : product.shape[1]] = product[image : image + 1]
    waits = [
        net.send(v.part.at[peer[0]], v.part_buf.at[index], peer)
        for index, peer in enumerate(here.dp_peers())
    ]
    w_q.send_straight((1,))
    w_o.send_diagonal()
    w_u.send_diagonal()
    w_o.send_straight()
    v.token[...] = jnp.sum(wide(8), axis=0, keepdims=True)
    for wait in waits:
        wait()
    v.mod[...] = v.part[dp] + v.part_buf[0] + v.part_buf[1] + v.part_buf[2]
    v.mod[7:8, 0:tokens] = v.keep_v[...].astype(F32)
    head_sigmoid = jax.nn.sigmoid(v.mod[6:7, 0:128])
    head_mask = v.head_mask[...]
    gate = dot(jnp.broadcast_to(head_mask * head_sigmoid, (8, 128)), v.expand[...], NN, exact=True)
    v.gate_row[...] = gate[0:1]

    loads[6].wait()

    def first_norm(rows):
        values = v.x_v[rows, :].astype(F32)
        centre = values - jnp.mean(values, axis=1, keepdims=True)
        spread = jnp.mean(centre * centre, axis=1, keepdims=True)
        normal = centre * lax.rsqrt(spread + epsilon)
        v.nb[rows, :] = (normal * (1.0 + v.mod[1:2]) + v.mod[0:1]).astype(BF16)

    by_rows(tokens, first_norm)
    wait_normed = net.send(v.nb.at[mine], v.nb.at[theirs], here.peer_core())

    w_q.share_straight(0)
    w_q.share_straight(1)
    w_u.send_straight()
    w_d.send_diagonal()
    w_d.send_straight()
    w_o.spread()
    w_q.share_diagonal()
    wait_mod = net.send(v.mod, v.mod_near, here.peer_z1())
    w_q.ready()

    @pl.loop(0, 3 * width // 384)
    def _(index):
        columns = span(index * 384, 384, 128)
        v.packed[:, columns] = dot(v.nb[mine, :], v.fq[:, columns], NN).astype(BF16)

    w_u.spread()

    lanes = lax.broadcasted_iota(jnp.int32, (1, 2 * size), 1)
    masks = ((lanes < size).astype(F32).astype(BF16), (lanes >= size).astype(F32).astype(BF16))
    scaled_masks = tuple(mask * jnp.asarray(factor, BF16) for mask in masks)
    low_lane = lax.broadcasted_iota(jnp.int32, (tokens, 2 * size), 1) < size

    def three(pair, block):
        return [block[:, span(part * width + pair * 2 * size, 2 * size, 128)] for part in range(3)]

    def attend(pair):
        queries, key_rows, value_rows = three(pair, v.packed)
        found = []
        for which in range(2):
            scores = dot(queries * scaled_masks[which], key_rows, NT)
            powers = jnp.exp(scores - jnp.max(scores, axis=1, keepdims=True))
            probs = powers * (1.0 / jnp.sum(powers, axis=1, keepdims=True))
            v.probs[pair * 2 + which] = probs
            found.append(dot(probs.astype(BF16), value_rows, NN))
        attended = jnp.where(low_lane, found[0], found[1])
        columns = span(pair * 2 * size, 2 * size, 128)
        v.attended[:, columns] = attended
        v.gated[mine, columns] = (attended * v.gate_row[:, columns]).astype(BF16)

    pl.loop(0, heads // 3)(attend)
    attend(heads // 3)
    w_o.share_straight(0)
    w_o.share_straight(1)
    w_o.share_diagonal()
    pl.loop(heads // 3 + 1, heads // 2)(attend)
    wait_gated = net.send(v.gated.at[mine], v.gated.at[theirs], here.peer_core())
    w_o.ready()

    @pl.loop(0, width // 256)
    def _(index):
        columns = span(index * 256, 256, 128)
        v.branch[:, columns] = dot(v.gated[mine, :], v.fo[:, columns], NN)

    loads[7].wait()

    def weigh(rows, second, modulation, keep):
        logit = jnp.sum(second.astype(F32) * v.token[...], axis=1, keepdims=True)
        router = jax.nn.sigmoid(logit)
        weight = keep * router
        v.grad_prod[rows, :] = (v.g_v[rows, :].astype(F32) * modulation[5:6] * weight).astype(BF16)
        return router

    def second_norm(rows):
        middle = v.x_v[rows, :].astype(F32) + v.mod[2:3] * v.branch[rows, :]
        v.middle[rows, :] = middle
        centre = middle - jnp.mean(middle, axis=1, keepdims=True)
        spread = jnp.mean(centre * centre, axis=1, keepdims=True)
        scale = lax.rsqrt(spread + epsilon)
        normal = centre * scale
        v.z2[rows, :] = normal
        v.scale2[rows, :] = scale
        second = (normal * (1.0 + v.mod[4:5]) + v.mod[3:4]).astype(BF16)
        v.second[rows, :] = second
        v.router[rows, :] = weigh(rows, second, v.mod, v.keep[rows, :])

    def some_rows(start, count, body):
        @pl.loop(0, count // ROWS)
        def _(index):
            body(span(start + index * ROWS, ROWS, ROWS))

    wait_near = []
    for k in range(2):
        some_rows(k * bit, bit, second_norm)
        block = slice(k * bit, k * bit + bit)
        landing = v.second.at[slice(tokens + k * bit, tokens + k * bit + bit)]
        wait_near.append(net.send(v.second.at[block], landing, here.peer_z1()))
    w_u.share_diagonal()
    w_u.share_straight(0)
    w_u.share_straight(1)
    half = width // 2
    other = span((1 - core) * half, half, 128)
    own = span(core * half, half, 128)
    wait_pair = [
        net.send(v.second.at[mine], v.second.at[slice(2 * tokens, 3 * tokens)], here.peer_core()),
        net.send(
            v.grad_prod.at[mine, other], v.dy_down.at[slice(2 * tokens, 3 * tokens)], here.peer_core()
        ),
    ]
    v.dy_down[mine, :] = v.grad_prod[mine, own]

    w_u.ready()
    inner = math.sqrt(2.0 / math.pi)
    units = hidden_width // 2

    def feed(start, count):
        tokens_of = slice(start, start + count)
        for index in range(units // 512):
            columns = slice(index * 512, index * 512 + 512)
            v.tmp[0:count, 0:512] = dot(v.second[tokens_of, :], v.fu[:, columns], NN)

            @pl.loop(0, count // ROWS)
            def _(step):
                rows = span(step * ROWS, ROWS, ROWS)
                there = span(start + step * ROWS, ROWS, ROWS)
                u = v.tmp[rows, 0:512]
                square = u * u
                t = jnp.tanh(u * (inner + (inner * 0.044715) * square))
                a = 0.5 + 0.5 * t
                value = u * a
                v.hidden[there, columns] = value.astype(BF16)
                v.slope[there, columns] = a + value * (1.0 - a) * (
                    2.0 * inner + (6.0 * inner * 0.044715) * square
                )

    def feed_back(start, count):
        tokens_of = slice(start, start + count)

        @pl.loop(0, units // 512)
        def _(index):
            columns = span(index * 512, 512, 128)
            back = dot(v.grad_prod[tokens_of, :], v.fd[columns, :], NT)
            v.grad_u[tokens_of, columns] = (back * v.slope[tokens_of, columns]).astype(BF16)

    def down(start, count, target, at, kind):
        @pl.loop(0, width // 256)
        def _(index):
            columns = span(index * 256, 256, 128)
            target[at, columns] = dot(v.hidden[start : start + count, :], v.fd[:, columns], NN).astype(kind)

    def up_back(start, count, target, at, kind):
        @pl.loop(0, width // 256)
        def _(index):
            columns = span(index * 256, 256, 128)
            target[at, columns] = dot(v.grad_u[start : start + count, :], v.fu[columns, :], NT).astype(kind)

    wait_units = []
    quarter_units = units // 2
    other_units = span((1 - core) * quarter_units, quarter_units, 128)
    own_units = span(core * quarter_units, quarter_units, 128)

    def hand_over(block, landing):
        wait_units.append(net.send(v.grad_u.at[block, other_units], v.dy_up.at[landing], here.peer_core()))
        v.dy_up[block, :] = v.grad_u[block, own_units]

    feed(0, tokens)
    wait_pair.append(
        net.send(v.hidden.at[mine], v.hidden.at[slice(2 * tokens, 3 * tokens)], here.peer_core())
    )
    pieces = []
    for number, (index, column, wide, kind) in enumerate(chunks):
        total = (v.t_qkv, v.t_out, v.t_up, v.t_down)[index]
        out = (v.o_qkv, v.o_out, v.o_up, v.o_down)[index]
        bufs = [getattr(v, f"c{number}_{k}") for k in range(7)]
        pieces.append(kind(net, here, total, out, bufs, column, wide))
    c_down, c_up, c_more, c_out = pieces[:4]
    c_qkv = pieces[4:]

    def weight_grad(total, left, right, step):
        @pl.loop(0, total.shape[0] // step)
        def _(index):
            rows = span(index * step, step, 128)
            total[rows, :] = dot(left[:, rows], right[...], TN).astype(BF16)

    wait_mod()
    v.keep_near[...] = jnp.sum(
        jnp.where(diagonal, v.mod_near[7:8, 0:tokens], 0.0), axis=1, keepdims=True
    )

    def weigh_near(rows):
        kept = v.keep_near[span(rows.start - tokens, ROWS, ROWS), :]
        weigh(rows, v.second[rows, :], v.mod_near, kept)

    def take_near(k):
        wait_near[k]()
        wait_cotangent[k]()
        some_rows(tokens + k * bit, bit, weigh_near)
        feed(tokens + k * bit, bit)

    take_near(0)
    w_d.share_diagonal()
    w_d.share_straight(0)
    w_d.share_straight(1)
    take_near(1)
    w_d.ready()
    last_rows = slice(3 * tokens, 4 * tokens)
    wait_pair.append(net.send(v.hidden.at[near_rows], v.hidden.at[last_rows], here.peer_core()))
    wait_pair.append(net.send(v.second.at[near_rows], v.second.at[last_rows], here.peer_core()))
    wait_pair.append(net.send(v.grad_prod.at[near_rows, other], v.dy_down.at[last_rows], here.peer_core()))
    feed_back(tokens, tokens)
    hand_over(near_rows, last_rows)
    wait_back = []
    for k in range(width // 256):
        columns = slice(k * 256, k * 256 + 256)
        v.near_back[:, columns] = dot(v.grad_u[near_rows, :], v.fu[columns, :], NT).astype(BF16)
        wait_back.append(
            net.send(v.near_back.at[:, columns], v.got_back.at[:, columns], here.peer_z1())
        )
    v.dy_down[near_rows, :] = v.grad_prod[near_rows, own]

    def down_quarter(place):
        rows = span(place * 384, 384, 128)
        v.t_down[rows, :] = dot(v.hidden[:, rows], v.dy_down[...], TN).astype(BF16)

    for wait in wait_pair:
        wait()
    down_quarter(here.peer_d()[0])
    c_down.first_diagonal()
    down_quarter(here.peer_x()[0])
    c_down.first_x()
    down_quarter(here.peer_y()[0])
    c_down.first_y()
    down_quarter(dp)
    feed_back(0, tokens)
    hand_over(mine, slice(2 * tokens, 3 * tokens))
    down(tokens, tokens, v.near_prod, mine, BF16)

    def near_level(rows):
        grad = v.g_v[span(rows.start + tokens, ROWS, ROWS), :].astype(F32)
        produced = v.near_prod[rows, :].astype(F32)
        v.level[rows, :] = jnp.sum(grad * v.mod_near[5:6] * produced, axis=1, keepdims=True)

    by_rows(tokens, near_level)
    v.level_out[...] = jnp.broadcast_to(
        jnp.sum(jnp.where(diagonal, v.level[...], 0.0), axis=0, keepdims=True), v.level_out.shape
    )
    wait_level = net.send(v.level_out, v.level_in, here.peer_z1())
    wait_prod = net.send(v.near_prod, v.got_prod, here.peer_z1())
    for wait in wait_units:
        wait()
    weight_grad(v.t_up, v.second, v.dy_up, 256)
    c_up.first()
    c_more.first()
    up_back(0, tokens, v.own_back, mine, F32)
    down(0, tokens, v.own_prod, mine, F32)

    def own_level(rows):
        grad = v.g_v[rows, :].astype(F32)
        v.level[rows, :] = jnp.sum(grad * v.mod[5:6] * v.own_prod[rows, :], axis=1, keepdims=True)

    by_rows(tokens, own_level)

    v.sums[...] = jnp.zeros(v.sums.shape, F32)
    wait_level()
    got = jnp.sum(jnp.where(diagonal, v.level_in[0:1, :], 0.0), axis=1, keepdims=True)
    router, keep = v.router[...], v.keep[...]
    v.logit[...] = (v.level[...] + got) * keep * router * (1.0 - router)

    def second_back(rows):
        logit = v.logit[rows, :]
        back = (v.own_back[rows, :] + v.got_back[rows, :].astype(F32)).astype(BF16).astype(F32)
        back += logit * v.token[...]
        normal = v.z2[rows, :]
        v.sums[1] += fold(logit * v.second[rows, :].astype(F32))
        v.sums[2] += fold(back * normal)
        v.sums[3] += fold(back)
        inside = back * (1.0 + v.mod[4:5])
        level = jnp.mean(inside, axis=1, keepdims=True)
        slope = jnp.mean(inside * normal, axis=1, keepdims=True)
        grad = v.g_v[rows, :].astype(F32) + v.scale2[rows, :] * (inside - level - normal * slope)
        v.grad_mid[rows, :] = grad
        v.sums[4] += fold(grad * v.branch[rows, :])
        v.grad_branch[rows, :] = (v.mod[2:3] * grad).astype(BF16)

    for wait in wait_back:
        wait()
    by_rows(tokens, second_back)
    wait_dbranch = net.send(v.grad_branch.at[:, other], v.dy_out.at[theirs], here.peer_core())
    v.dy_out[mine, :] = v.grad_branch[:, own]

    @pl.loop(0, width // 256)
    def _(index):
        columns = span(index * 256, 256, 128)
        v.tmp[:, columns] = dot(v.grad_branch[...], v.fo[columns, :], NT)


    def gate_back(rows):
        grad = v.tmp[rows, :]
        v.sums[5] += fold(grad * v.attended[rows, :])
        v.grad_att[rows, :] = (grad * v.gate_row[...]).astype(BF16)

    by_rows(tokens, gate_back)
    c_down.second()
    c_up.second()

    def gather_far(piece, block):
        block[pl.ds(core, 1), pl.ds(here.z, 1), pl.ds(dp, 1)] = piece[...][None, None, None]
        far = (here.z + 2) % Z_CHIPS
        return [net.send(piece, block.at[core, here.z, dp], here.peer_z2(), block.at[core, far, dp])]

    def gather_near(block, waits):
        for wait in waits:
            wait()
        near = here.z + 1 - 2 * (here.z % 2)
        moves = []
        for k in range(2):
            z, other = (here.z + 2 * k) % Z_CHIPS, (near + 2 * k) % Z_CHIPS
            tile = block.at[core, z, dp]
            moves.append(net.send(tile, tile, here.peer_z1(), block.at[core, other, dp]))
        return moves

    def gather_dp(block, waits):
        for wait in waits:
            wait()
        tiles = block.at[core, pl.ds(0, Z_CHIPS), dp]
        return [
            net.send(tiles, tiles, peer, block.at[core, pl.ds(0, Z_CHIPS), peer[0]])
            for peer in here.dp_peers()
        ]

    one_way = (dp + (1 - core) * (1 - 2 * here.x) + core * (2 - 4 * here.y), here.seq)
    other_way = (dp + core * (1 - 2 * here.x) + (1 - core) * (2 - 4 * here.y), here.seq)

    def gather_one(block, waits):
        for wait in waits:
            wait()
        tiles = block.at[core, pl.ds(0, Z_CHIPS), dp]
        return [net.send(tiles, tiles, one_way, block.at[core, pl.ds(0, Z_CHIPS), one_way[0]])]

    def gather_two(block, waits):
        for wait in waits:
            wait()
        moves = []
        for mine_dp, their_dp in ((dp, other_way[0]), (one_way[0], here.peer_d()[0])):
            tiles = block.at[core, pl.ds(0, Z_CHIPS), mine_dp]
            moves.append(
                net.send(tiles, tiles, other_way, block.at[core, pl.ds(0, Z_CHIPS), their_dp])
            )
        return moves

    def gather_pair(block, waits):
        for wait in waits:
            wait()
        return net.send(block.at[core], block.at[core], here.peer_core(), block.at[1 - core])

    def back_pair(pair):
        queries, key_rows, value_rows = three(pair, v.packed)
        columns = span(pair * 2 * size, 2 * size, 128)
        grad_att = v.grad_att[:, columns]
        gq, gk, gv = [], [], []
        for which in range(2):
            probs = v.probs[pair * 2 + which]
            grad_probs = dot(grad_att * masks[which], value_rows, NT)
            level = jnp.sum(probs * grad_probs, axis=1, keepdims=True)
            grad_scores = (probs * (grad_probs - level)).astype(BF16)
            gq.append(dot(grad_scores, key_rows, NN))
            gk.append(dot(grad_scores, queries, TN))
            gv.append(dot(probs.astype(BF16), grad_att, TN))
        for part, (grads, scale) in enumerate(((gq, factor), (gk, factor), (gv, 1.0))):
            both = jnp.where(low_lane, grads[0], grads[1]) * scale
            v.grad_pack[:, span(part * width + pair * 2 * size, 2 * size, 128)] = both.astype(BF16)

    head_back = dot(
        jnp.broadcast_to(jnp.sum(v.sums[5], axis=0, keepdims=True), (8, width)), v.expand[...], NT, exact=True
    )
    head_back = head_back[0:1] * head_mask * head_sigmoid * (1.0 - head_sigmoid)
    v.early_f[...] = jnp.zeros(v.early_f.shape, F32)
    rows_out = [jnp.sum(v.sums[k], axis=0, keepdims=True) for k in (4, 3, 2, 1)]
    cut = width // 2
    for slot, values in zip((0, 1, 2, 5, 6), (*rows_out, v.condition[...])):
        v.early_f[2 * slot : 2 * slot + 1, :] = values[:, 0:cut]
        v.early_f[2 * slot + 1 : 2 * slot + 2, :] = values[:, cut:width]
    v.early_f[8:9, 0:128] = head_back
    v.early_out[...] = v.early_f[...].astype(BF16)
    early = gather_far(v.early_out, v.early)
    def back_group(group):
        @pl.loop(0, heads // 4)
        def _(index):
            back_pair(group * (heads // 4) + index)

    back_group(1 - core)
    wait_dpack = [
        net.send(
            v.grad_pack.at[:, span(part * width + (1 - core) * half, half, 128)],
            v.dy_qkv.at[theirs, slice(part * half, part * half + half)],
            here.peer_core(),
        )
        for part in range(3)
    ]
    early = gather_near(v.early, early)
    wait_gated()
    wait_dbranch()
    weight_grad(v.t_out, v.gated, v.dy_out, 256)
    c_out.first()
    back_group(core)
    for part in range(3):
        v.dy_qkv[mine, part * half : part * half + half] = v.grad_pack[
            :, span(part * width + core * half, half, 128)
        ]
    early = gather_one(v.early, early)
    c_more.second()
    wait_normed()
    for wait in wait_dpack:
        wait()

    def qkv_grad(start, count):
        columns = slice(start, start + count)

        @pl.loop(0, width // 256)
        def _(index):
            rows = span(index * 256, 256, 128)
            v.t_qkv[rows, columns] = dot(v.nb[:, rows], v.dy_qkv[:, columns], TN).astype(BF16)

    qkv_grad(0, 384)
    c_qkv[0].first()
    c_down.third()
    c_out.second()
    qkv_grad(384, 384)
    c_qkv[1].first()
    early = gather_two(v.early, early)
    qkv_grad(768, 384)
    c_up.third()
    c_more.third()
    wait_prod()

    def finish(rows):
        produced = (v.own_prod[rows, :] + v.got_prod[rows, :].astype(F32)).astype(BF16).astype(F32)
        scaled = produced * (v.keep[rows, :] * v.router[rows, :])
        v.output[rows, :] = (v.middle[rows, :] + v.mod[5:6] * scaled).astype(BF16)
        v.sums[0] += fold(v.g_v[rows, :].astype(F32) * scaled)

    by_rows(tokens, finish)

    @pl.loop(0, width // 256)
    def _(index):
        columns = span(index * 256, 256, 128)
        v.tmp[:, columns] = dot(v.grad_pack[...], v.fq[columns, :], NT)

    c_qkv[0].second()
    c_qkv[2].first()

    def first_back(rows):
        back = v.tmp[rows, :]
        values = v.x_v[rows, :].astype(F32)
        centre = values - jnp.mean(values, axis=1, keepdims=True)
        spread = jnp.mean(centre * centre, axis=1, keepdims=True)
        scale = lax.rsqrt(spread + epsilon)
        normal = centre * scale
        v.sums[6] += fold(back * normal)
        v.sums[7] += fold(back)
        inside = back * (1.0 + v.mod[1:2])
        level = jnp.mean(inside, axis=1, keepdims=True)
        slope = jnp.mean(inside * normal, axis=1, keepdims=True)
        v.grad_input[rows, :] = v.grad_mid[rows, :] + scale * (inside - level - normal * slope)

    by_rows(tokens, first_back)
    shift = jnp.sum(v.sums[7], axis=0, keepdims=True)
    scale = jnp.sum(v.sums[6], axis=0, keepdims=True)
    v.late_f[...] = jnp.zeros(v.late_f.shape, F32)
    for k in range(width // 128):
        v.late_f[k : k + 1, :] = shift[:, k * 128 : (k + 1) * 128]
        v.late_f[8 + k : 9 + k, :] = scale[:, k * 128 : (k + 1) * 128]
    gate_two = jnp.sum(v.sums[0], axis=0, keepdims=True)
    for k in range(width // 128):
        v.late_f[16 + k : 17 + k, :] = gate_two[:, k * 128 : (k + 1) * 128]
    v.late_out[...] = v.late_f[...].astype(BF16)
    late = gather_far(v.late_out, v.late)
    c_down.fifth()
    c_up.fifth()
    c_qkv[1].second()
    early = gather_pair(v.early, early)
    c_out.third()
    late = gather_near(v.late, late)
    c_qkv[0].third()
    c_qkv[2].second()
    c_more.fifth()
    c_out.fourth()
    c_qkv[1].third()
    late = gather_dp(v.late, late)
    c_qkv[0].fourth()
    c_qkv[2].third()
    c_qkv[1].fourth()
    c_out.fifth()
    late = gather_pair(v.late, late)
    early()
    offset = dp * quarter + (here.seq % BLOCK) * SHARE
    pick = (
        lax.broadcasted_iota(jnp.int32, (width, SHARE), 0)
        == lax.broadcasted_iota(jnp.int32, (width, SHARE), 1) + offset
    ).astype(F32)

    every = v.early[...].reshape(512, cut).astype(F32).reshape(32, 16, cut)
    conditions = (
        dot(every[:, 12, :].astype(BF16), pick[0:cut].astype(BF16), NN)
        + dot(every[:, 13, :].astype(BF16), pick[cut:width].astype(BF16), NN)
    ).astype(BF16)
    for slot, piece in enumerate((2, 3, 4)):
        for side in range(2):
            start = piece * width + side * cut
            v.o_ada[:, start : start + cut] = dot(
                conditions, every[:, 2 * slot + side, :].astype(BF16), TN
            )
    v.o_head[...] = dot(every[:, 8, 0:128].astype(BF16), conditions, TN)[0:heads]
    totals = [jnp.sum(every[:, 10 + side, :], axis=0, keepdims=True) for side in range(2)]
    v.o_token[...] = (
        dot(jnp.broadcast_to(totals[0], (8, cut)), pick[0:cut], NN, exact=True)
        + dot(jnp.broadcast_to(totals[1], (8, cut)), pick[cut:width], NN, exact=True)
    )[0:1]

    c_qkv[0].fifth()
    c_qkv[1].fifth()
    for chunk in (c_down, c_up, c_more):
        chunk.end()
    late()
    tail = v.late[...].reshape(1024, 128).astype(F32).reshape(32, 32, 128)
    for base, piece in ((0, 0), (8, 1), (16, 5)):
        row = jnp.concatenate([tail[:, base + k, :] for k in range(width // 128)], axis=1)
        start = piece * width
        v.o_ada[:, start : start + width] = dot(conditions, row.astype(BF16), TN)
    c_qkv[2].fifth()
    for chunk in (c_out, *c_qkv):
        chunk.end()
    net.finish()


def layer(time_table, time_index, w_token, w_head, token_keep, head_keep, inputs, cotangent, w_ada, wq, wo, wu, wd):
    tokens, width = inputs.shape
    hidden_width = wu.shape[1]
    heads = head_keep.shape[1]
    widths = [wq.shape[1], wo.shape[1], wu.shape[1], wd.shape[1]]
    depths = [4 * w.shape[0] for w in (wq, wo, wu, wd)]
    chunks = chunk_list(widths)
    operands = dict(
        time_table=time_table, time_index=time_index, w_token=w_token, w_head=w_head, token_keep=token_keep, head_keep=head_keep,
        inputs=inputs, cotangent=cotangent, w_ada=w_ada, wq=wq, wo=wo, wu=wu, wd=wd,
    )
    outs = dict(
        ada=((SHARE, 6 * width), F32),
        qkv=((depths[0] // 32, widths[0]), F32),
        out=((depths[1] // 32, widths[1]), F32),
        up=((depths[2] // 32, widths[2]), F32),
        down=((depths[3] // 32, widths[3]), F32),
        head=((heads, SHARE), F32),
        token=((1, SHARE), F32),
    )
    results = dict(output=((tokens, width), BF16), grad_input=((tokens, width), F32))
    results.update({"o_" + k: s for k, s in outs.items()})
    space = dict(
        table_v=(time_table.shape, BF16),
        index_v=(time_index.shape, jnp.int32),
        small_v=((16, 128), F32),
        condition=((1, width), F32),
        token_v=(w_token.shape, BF16),
        keep_v=(token_keep.shape, jnp.int32),
        head_keep_v=(head_keep.shape, jnp.int32),
        head_mask=((1, 128), F32),
        head_v=(w_head.shape, BF16),
        ada_v=(w_ada.shape, BF16),
        x_v=((tokens, width), BF16),
        g_v=((2 * tokens, width), BF16),
        mod_near=((8, width), F32),
        keep_near=((tokens, 1), F32),
        fq=((depths[0], widths[0]), BF16),
        fo=((depths[1], widths[1]), BF16),
        fu=((depths[2], widths[2] // 2), BF16),
        fd=((depths[3] // 2, widths[3]), BF16),
        cond_buf=((4, 16, 128), F32),
        part=((4, 8, width), F32),
        part_buf=((3, 8, width), F32),
        mod=((8, width), F32),
        token=((1, width), F32),
        keep=((tokens, 1), F32),
        expand=((128, width), F32),
        gate_row=((1, width), F32),
        nb=((2 * tokens, width), BF16),
        packed=((tokens, 3 * width), BF16),
        probs=((heads, tokens, tokens), F32),
        attended=((tokens, width), F32),
        gated=((2 * tokens, width), BF16),
        branch=((tokens, width), F32),
        middle=((tokens, width), F32),
        z2=((tokens, width), F32),
        scale2=((tokens, 1), F32),
        second=((4 * tokens, width), BF16),
        router=((tokens, 1), F32),
        logit=((tokens, 1), F32),
        grad_prod=((2 * tokens, width), BF16),
        dy_down=((4 * tokens, width // 2), BF16),
        tmp=((tokens, width), F32),
        hidden=((4 * tokens, hidden_width // 2), BF16),
        slope=((2 * tokens, hidden_width // 2), F32),
        grad_u=((2 * tokens, hidden_width // 2), BF16),
        dy_up=((4 * tokens, hidden_width // 4), BF16),
        own_prod=((tokens, width), F32),
        own_back=((tokens, width), F32),
        near_prod=((tokens, width), BF16),
        near_back=((tokens, width), BF16),
        got_prod=((tokens, width), BF16),
        got_back=((tokens, width), BF16),
        level=((tokens, 1), F32),
        level_out=((8, tokens), F32),
        level_in=((8, tokens), F32),
        grad_mid=((tokens, width), F32),
        grad_branch=((tokens, width), BF16),
        dy_out=((2 * tokens, width // 2), BF16),
        grad_att=((tokens, width), BF16),
        grad_pack=((tokens, 3 * width), BF16),
        dy_qkv=((2 * tokens, 3 * width // 2), BF16),
        sums=((8, 8, width), F32),
        early_f=((16, width // 2), F32),
        early_out=((16, width // 2), BF16),
        early=((2, Z_CHIPS, 4, 16, width // 2), BF16),
        late_f=((32, 128), F32),
        late_out=((32, 128), BF16),
        late=((2, Z_CHIPS, 4, 32, 128), BF16),
        t_qkv=((depths[0], widths[0] // 2), BF16),
        t_out=((depths[1], widths[1] // 2), BF16),
        t_up=((depths[2], widths[2] // 4), BF16),
        t_down=((depths[3] // 2, widths[3] // 2), BF16),
    )
    for number, (index, _, wide, kind) in enumerate(chunks):
        shapes = kind.shapes(depths[index] // 16, wide)
        for k, shape in enumerate(shapes):
            space[f"c{number}_{k}"] = (shape, BF16)
        space[f"c{number}_6"] = (kind.sums(depths[index] // 16, wide), F32)
    copies = 6 + 4 * 13 + 32 + len(chunks) * 14 + 14
    names = list(operands) + list(results) + list(space) + ["send_sems", "recv_sems", "local_sems"]
    return pl.pallas_call(
        functools.partial(layer_kernel, names, chunks, (tokens, width, heads, hidden_width)),
        out_shape=[pltpu.VMEM(*r) for r in results.values()],
        in_specs=[ANY] * len(operands),
        out_specs=[VMEM] * len(results),
        scratch_shapes=[pltpu.VMEM(*s) for s in space.values()]
        + [
            pltpu.SemaphoreType.DMA((copies,)),
            pltpu.SemaphoreType.DMA((copies,)),
            pltpu.SemaphoreType.DMA((16,)),
        ],
        compiler_params=pltpu.CompilerParams(
            collective_id=0, has_side_effects=True, vmem_limit_bytes=61 * 2**20
        ),
    )(*operands.values())


def copy_kernel(count, *refs):
    copies = [
        pltpu.make_async_copy(refs[k], refs[count + k], refs[2 * count].at[k]) for k in range(count)
    ]
    for copy in copies:
        copy.start()
    for copy in copies:
        copy.wait()


def copy_all(arrays):
    count = len(arrays)
    return pl.pallas_call(
        functools.partial(copy_kernel, count),
        out_shape=[jax.ShapeDtypeStruct(a.shape, a.dtype) for a in arrays],
        in_specs=[VMEM] * count,
        out_specs=[ANY] * count,
        scratch_shapes=[pltpu.SemaphoreType.DMA((count,))],
        compiler_params=pltpu.CompilerParams(vmem_limit_bytes=16 * 2**20),
    )(*(pltpu.with_memory_space_constraint(a, pltpu.VMEM) for a in arrays))


def across_blocks(part, seq_size):
    blocks = seq_size // BLOCK
    if blocks == 1:
        return part
    groups = [[b * BLOCK + j for b in range(blocks)] for j in range(BLOCK)]
    mine = lax.psum_scatter(
        part, "seq", scatter_dimension=0, axis_index_groups=groups, tiled=True
    )
    moves = [(b * BLOCK + j, j * blocks + b) for b in range(blocks) for j in range(BLOCK)]
    return lax.ppermute(mine, "seq", moves)


def per_device(
    seq_size, inputs, time_table, time_index, token_keep, head_keep, cotangent,
    w_ada, w_qkv, w_out, w_up, w_down, w_head, w_token,
):
    out = layer(
        time_table, time_index[None], w_token, w_head.T, token_keep, head_keep,
        inputs[0], cotangent[0], w_ada, w_qkv, w_out, w_up, w_down,
    )
    output, grad_input, ada, qkv, outw, up, down, head, token = copy_all(out)
    parts = (ada, qkv, outw, up, down, head.T, token[0])
    parts = tuple(across_blocks(part, seq_size) for part in parts)
    return (output[None], grad_input[None]) + parts


def solution(mesh):
    both = ("dp", "seq")
    in_specs = (
        P(both, None, None), P(), P(both), P(both, None), P(both, None), P(both, None, None),
        P("dp", None), P("dp", None), P("dp", None), P("dp", None), P("dp", None), P("dp", None), P("dp"),
    )
    out_specs = (P(both, None, None), P(both, None, None)) + (P(both, None),) * 6 + (P(both),)
    return jax.shard_map(
        functools.partial(per_device, mesh.shape["seq"]),
        mesh=mesh, in_specs=in_specs, out_specs=out_specs, check_vma=False,
    )
```

```python
import functools
import math
import types

import jax
import jax.numpy as jnp
from jax import lax
from jax.experimental import pallas as pl
from jax.experimental.pallas import tpu as pltpu
from jax.sharding import PartitionSpec as P

epsilon = 1e-06
MESH = pl.DeviceIdType.MESH
ANY = pl.BlockSpec(memory_space=pl.ANY)
VMEM = pl.BlockSpec(memory_space=pltpu.VMEM)
Z_CHIPS = 4
BLOCK = 2 * Z_CHIPS
F32, BF16 = jnp.float32, jnp.bfloat16
NN, NT, TN = ((1,), (0,)), ((1,), (1,)), ((0,), (0,))
ROWS = 64
BEND_ROWS = 32
SHARE = 24


def dot(left, right, dims, exact=False):
    return lax.dot_general(
        left, right, (dims, ((), ())), preferred_element_type=F32,
        precision=lax.Precision.HIGHEST if exact else None,
    )


def span(start, size, unit):
    return pl.ds(pl.multiple_of(start, unit), size)


def by_rows(total, body, step=ROWS):
    @pl.loop(0, total // step)
    def _(index):
        body(span(index * step, step, step))


def fold(values):
    return jnp.sum(values.reshape(-1, 8, values.shape[-1]), axis=0)


class Place:
    def __init__(self):
        self.dp = lax.axis_index("dp")
        self.seq = lax.axis_index("seq")
        self.x = self.dp % 2
        self.y = self.dp // 2
        self.core = self.seq % 2
        self.z = (self.seq // 2) % Z_CHIPS
        self.side = self.z % 2
        self.high = self.z // 2
        self.outer = self.seq // BLOCK

    def z_of(self, step):
        return (self.z + step) % Z_CHIPS

    def peer_x(self):
        return (self.y * 2 + 1 - self.x, self.seq)

    def peer_y(self):
        return ((1 - self.y) * 2 + self.x, self.seq)

    def peer_d(self):
        return ((1 - self.y) * 2 + 1 - self.x, self.seq)

    def peer_core(self):
        return (self.dp, self.seq + 1 - 2 * self.core)

    def peer_z(self, step):
        return (self.dp, self.outer * BLOCK + self.z_of(step) * 2 + self.core)

    def peer_z1(self):
        return (self.dp, self.seq + 2 - 4 * (self.z % 2))

    def peer_z2(self):
        return (self.dp, self.seq + 4 - 8 * (self.z // 2))

    def dp_peers(self):
        return (self.peer_x(), self.peer_y(), self.peer_d())

    def greet(self):
        peers = list(self.dp_peers()) + [self.peer_core()]
        for k in range(1, Z_CHIPS):
            same = self.peer_z(k)
            peers += [same, (same[0], same[1] + 1 - 2 * self.core)]
        for peer in peers:
            pl.semaphore_signal(
                pltpu.get_barrier_semaphore(), inc=1, device_id=peer, device_id_type=MESH
            )
        self.peers = len(peers)

    def meet(self):
        pl.semaphore_wait(pltpu.get_barrier_semaphore(), self.peers)


class Net:
    def __init__(self, send_sems, recv_sems):
        self.send_sems = send_sems
        self.recv_sems = recv_sems
        self.used = 0
        self.sent = []

    def send(self, src, dst, peer, landing=None):
        slot = self.used
        self.used += 1

        def copy_to(target):
            return pltpu.make_async_remote_copy(
                src_ref=src,
                dst_ref=target,
                send_sem=self.send_sems.at[slot],
                recv_sem=self.recv_sems.at[slot],
                device_id=peer,
                device_id_type=MESH,
            )

        copy = copy_to(dst)
        copy.start()
        self.sent.append(copy)
        arrival = copy if landing is None else copy_to(landing)
        return arrival.wait_recv

    def plan(self, src, dst, peer):
        slot = self.used
        self.used += 1
        return pltpu.make_async_remote_copy(
            src_ref=src,
            dst_ref=dst,
            send_sem=self.send_sems.at[slot],
            recv_sem=self.recv_sems.at[slot],
            device_id=peer,
            device_id_type=MESH,
        )

    def finish(self):
        for copy in self.sent:
            copy.wait_send()


class Weight:
    def __init__(self, net, here, own, full):
        self.net, self.here, self.own, self.full = net, here, own, full
        self.depth = own.shape[0]
        self.piece = self.depth // Z_CHIPS
        self.width = own.shape[1] // 2
        self.wait_xy, self.last = [], []

    def columns(self, core):
        return span(core * self.width, self.width, 128)

    def quarter(self, dp):
        return span(dp * self.depth, self.depth, 16)

    def part(self, dp, z):
        return span(dp * self.depth + z * self.piece, self.piece, 16)

    def keep(self, sem):
        self.local = pltpu.make_async_copy(self.own, self.full.at[self.quarter(self.here.dp)], sem)
        self.local.start()

    def send_diagonal(self):
        here, columns = self.here, self.columns(self.here.core)
        peer = here.peer_d()
        self.wait_d = self.net.send(
            self.own.at[span(here.z * self.piece, self.piece, 16), columns],
            self.full.at[self.part(here.dp, here.z), columns],
            peer,
            self.full.at[self.part(peer[0], here.z), columns],
        )

    def rows(self, dp, side):
        half = self.depth // 2
        return span(dp * self.depth + side * half, half, 16)

    def send_straight(self, sides=(0, 1)):
        here, columns = self.here, self.columns(self.here.core)
        self.wait_xy += [
            [
                self.net.send(
                    self.own.at[self.rows(0, side), columns],
                    self.full.at[self.rows(here.dp, side), columns],
                    peer,
                    self.full.at[self.rows(peer[0], side), columns],
                )
                for peer in (here.peer_x(), here.peer_y())
            ]
            for side in sides
        ]

    def spread(self):
        here, columns = self.here, self.columns(self.here.core)
        diagonal = here.peer_d()[0]
        self.wait_d()
        piece = self.full.at[self.part(diagonal, here.z), columns]
        self.wait_z = [
            self.net.send(
                piece, piece, here.peer_z(step),
                self.full.at[self.part(diagonal, here.z_of(Z_CHIPS - step)), columns],
            )
            for step in range(1, Z_CHIPS)
        ]

    def hand(self, rows):
        here = self.here
        block = self.full.at[rows, self.columns(here.core)]
        landing = self.full.at[rows, self.columns(1 - here.core)]
        self.last.append(self.net.send(block, block, here.peer_core(), landing))

    def share_straight(self, side):
        here = self.here
        for wait, peer in zip(self.wait_xy[side], (here.peer_x(), here.peer_y())):
            wait()
            self.hand(self.rows(peer[0], side))

    def share_diagonal(self):
        for wait in self.wait_z:
            wait()
        self.hand(self.quarter(self.here.peer_d()[0]))

    def ready(self):
        for wait in self.last:
            wait()
        self.local.wait()


class HalfWeight(Weight):
    def __init__(self, net, here, own, full, by_columns):
        self.net, self.here, self.own, self.full, self.by_columns = net, here, own, full, by_columns
        self.last = []

    def source(self, part):
        here = self.here
        if self.by_columns:
            return self.own.at[:, span((2 * here.core + part) * 768 + here.side * 384, 384, 128)]
        return self.own.at[span(here.side * 384 + part * 192, 192, 16), span(here.core * 384, 384, 128)]

    def block(self, dp, part, core):
        if self.by_columns:
            return self.full.at[span(dp * 192, 192, 16), span((2 * core + part) * 384, 384, 128)]
        return self.full.at[span(dp * 384 + part * 192, 192, 16), span(core * 384, 384, 128)]

    def whole(self, dp, core):
        if self.by_columns:
            return self.full.at[span(dp * 192, 192, 16), span(core * 768, 768, 128)]
        return self.full.at[span(dp * 384, 384, 16), span(core * 384, 384, 128)]

    def keep(self, sems):
        dp, side = self.here.dp, self.here.side
        if self.by_columns:
            moves = [
                (
                    self.own.at[:, span(k * 768 + side * 384, 384, 128)],
                    self.full.at[span(dp * 192, 192, 16), span(k * 384, 384, 128)],
                )
                for k in range(4)
            ]
        else:
            moves = [(self.own.at[span(side * 384, 384, 16)], self.full.at[span(dp * 384, 384, 16)])]
        self.locals = [
            pltpu.make_async_copy(source, target, sem) for (source, target), sem in zip(moves, sems)
        ]
        for copy in self.locals:
            copy.start()

    def send_diagonal(self):
        here = self.here
        peer = here.peer_d()
        self.wait_d = self.net.send(
            self.source(here.high),
            self.block(here.dp, here.high, here.core),
            peer,
            self.block(peer[0], here.high, here.core),
        )

    def send_straight(self):
        here = self.here
        self.wait_xy = [
            [
                self.net.send(
                    self.source(part),
                    self.block(here.dp, part, here.core),
                    peer,
                    self.block(peer[0], part, here.core),
                )
                for peer in (here.peer_x(), here.peer_y())
            ]
            for part in range(2)
        ]

    def spread(self):
        here = self.here
        diagonal = here.peer_d()[0]
        self.wait_d()
        piece = self.block(diagonal, here.high, here.core)
        self.wait_z = [
            self.net.send(
                piece, piece, here.peer_z2(), self.block(diagonal, 1 - here.high, here.core)
            )
        ]

    def pass_core(self, block, landing):
        self.last.append(self.net.send(block, block, self.here.peer_core(), landing))

    def share_straight(self, part):
        here = self.here
        for wait, peer in zip(self.wait_xy[part], (here.peer_x(), here.peer_y())):
            wait()
            self.pass_core(self.block(peer[0], part, here.core), self.block(peer[0], part, 1 - here.core))

    def share_diagonal(self):
        here = self.here
        diagonal = here.peer_d()[0]
        for wait in self.wait_z:
            wait()
        self.pass_core(self.whole(diagonal, here.core), self.whole(diagonal, 1 - here.core))

    def ready(self):
        for wait in self.last:
            wait()
        for copy in self.locals:
            copy.wait()


class WholeWeight(HalfWeight):
    def send_diagonal(self):
        here = self.here
        peer = here.peer_d()
        self.wait_d = [
            self.net.send(
                self.source(part),
                self.block(here.dp, part, here.core),
                peer,
                self.block(peer[0], part, here.core),
            )
            for part in range(2)
        ]

    def share_diagonal(self):
        here = self.here
        diagonal = here.peer_d()[0]
        for wait in self.wait_d:
            wait()
        self.pass_core(self.whole(diagonal, here.core), self.whole(diagonal, 1 - here.core))


class Chunk:
    @staticmethod
    def shapes(rows, wide):
        return ((2, 2 * rows, wide),) * 2 + ((2 * rows, wide),) * 2 + ((2, rows, wide), (rows, wide))

    def __init__(self, net, here, total, out, bufs, column, width):
        self.net, self.here, self.out = net, here, out
        self.total = total.at[:, span(column, width, 128)]
        self.block = total.shape[0] // 16
        self.column, self.width = column, width
        self.r1a, self.r1b, self.r2a, self.r2b, self.r3a, self.r3b, self.f32 = bufs

    @staticmethod
    def sums(rows, wide):
        return (rows, wide)

    def columns(self, core):
        return span(core * (self.out.shape[1] // 2) + self.column, self.width, 128)

    def upper(self, dp):
        return self.total.at[span(dp * 4 * self.block, 2 * self.block, 16)]

    def lower(self, dp):
        return self.total.at[span(dp * 4 * self.block + 2 * self.block, 2 * self.block, 16)]

    def add(self, total, extra):
        def body(rows):
            total[rows, :] = (total[rows, :].astype(F32) + extra[rows, :].astype(F32)).astype(BF16)

        by_rows(total.shape[0], body, 16)

    def first_diagonal(self):
        here, dp = self.here, self.here.peer_d()[0]
        self.wait_a = [self.net.send(self.upper(dp), self.r1a.at[1 - here.y], here.peer_x())]
        self.wait_b = [self.net.send(self.lower(dp), self.r1b.at[1 - here.x], here.peer_y())]

    def first_x(self):
        here, peer = self.here, self.here.peer_x()
        self.wait_a.append(self.net.send(self.upper(peer[0]), self.r1a.at[here.y], peer))

    def first_y(self):
        here, peer = self.here, self.here.peer_y()
        self.wait_b.append(self.net.send(self.lower(peer[0]), self.r1b.at[here.x], peer))

    def first(self):
        self.first_diagonal()
        self.first_x()
        self.first_y()

    def second(self):
        here = self.here
        for wait in self.wait_a:
            wait()
        away = self.upper((1 - here.y) * 2 + here.x)
        self.add(away, self.r1a.at[1 - here.y])
        next_a = self.net.send(away, self.r2a.at[span(0, away.shape[0], 16)], here.peer_y())
        for wait in self.wait_b:
            wait()
        away = self.lower(here.y * 2 + 1 - here.x)
        self.add(away, self.r1b.at[1 - here.x])
        next_b = self.net.send(away, self.r2b, here.peer_x())
        self.add(self.upper(here.dp), self.r1a.at[here.y])
        self.add(self.lower(here.dp), self.r1b.at[here.x])
        self.wait_a, self.wait_b = next_a, next_b

    def mine(self, z):
        return self.total.at[span((self.here.dp * 4 + z) * self.block, self.block, 16)]

    def third(self):
        here = self.here
        self.wait_a()
        self.add(self.upper(here.dp), self.r2a)
        self.wait_b()
        self.add(self.lower(here.dp), self.r2b)
        odd = 1 - here.z % 2
        self.waits = [
            self.net.send(self.mine(odd + 2 * k), self.r3a.at[k], here.peer_z1()) for k in range(2)
        ]

    def fourth(self):
        here = self.here
        far = (here.z + 2) % Z_CHIPS
        for wait in self.waits:
            wait()
        self.add(self.mine(far), self.r3a.at[far // 2])
        self.wait = self.net.send(self.mine(far), self.r3b, here.peer_z2())
        self.add(self.mine(here.z), self.r3a.at[here.z // 2])

    def fifth(self):
        here = self.here
        self.wait()
        own = self.mine(here.z)

        def body(rows):
            self.f32[rows, :] = own[rows, :].astype(F32) + self.r3b[rows, :].astype(F32)

        by_rows(self.block, body, 16)
        self.pass_on()

    def pass_on(self):
        here = self.here
        part = self.block // 2
        self.wait = self.net.send(
            self.f32.at[span((1 - here.core) * part, part, 8)],
            self.out.at[:, self.columns(here.core)],
            here.peer_core(),
            self.out.at[:, self.columns(1 - here.core)],
        )
        self.out[:, self.columns(here.core)] = self.f32[span(here.core * part, part, 8), :]

    def end(self):
        self.wait()


class LastChunk(Chunk):
    @staticmethod
    def shapes(rows, wide):
        return ((2, 2 * rows, wide),) * 2 + ((2 * rows, wide),) * 2 + ((3, rows, wide), (16, 128))

    def third(self):
        here = self.here
        self.wait_a()
        self.add(self.upper(here.dp), self.r2a)
        self.wait_b()
        self.add(self.lower(here.dp), self.r2b)
        self.waits = [
            self.net.send(self.mine(here.z_of(k)), self.r3a.at[k - 1], here.peer_z(k))
            for k in range(1, Z_CHIPS)
        ]

    def fifth(self):
        for wait in self.waits:
            wait()
        own = self.mine(self.here.z)

        def body(rows):
            total = own[rows, :].astype(F32)
            for k in range(Z_CHIPS - 1):
                total += self.r3a[k, rows, :].astype(F32)
            self.f32[rows, :] = total

        by_rows(self.block, body, 16)
        self.pass_on()


class UpChunk(LastChunk):
    @staticmethod
    def sums(rows, wide):
        return (2, rows, wide)

    def place(self, core, side):
        return span((2 * core + self.column // self.width) * 768 + side * 384, 384, 128)

    def fifth(self):
        here = self.here
        for wait in self.waits:
            wait()
        part = self.block // 2
        self.waits = []
        for k, (left, right, side) in enumerate(
            (
                (self.mine(here.z), self.r3a.at[1], here.side),
                (self.r3a.at[0], self.r3a.at[2], 1 - here.side),
            )
        ):

            def body(rows):
                self.f32[k, rows, :] = left[rows, :].astype(F32) + right[rows, :].astype(F32)

            by_rows(self.block, body, 16)
            self.waits.append(
                self.net.send(
                    self.f32.at[k, span((1 - here.core) * part, part, 8)],
                    self.out.at[:, self.place(here.core, side)],
                    here.peer_core(),
                    self.out.at[:, self.place(1 - here.core, side)],
                )
            )
            self.out[:, self.place(here.core, side)] = self.f32[k, span(here.core * part, part, 8), :]

    def end(self):
        for wait in self.waits:
            wait()


class DownChunk(Chunk):
    @staticmethod
    def shapes(rows, wide):
        return ((2, rows, wide),) * 2 + ((rows, wide),) * 2 + ((16, 128), (2, rows, wide))

    def __init__(self, net, here, total, out, bufs, column, width):
        super().__init__(net, here, total, out, bufs, column, width)
        self.block = total.shape[0] // 8

    def part(self, dp, which):
        return self.total.at[span((dp * 2 + which) * self.block, self.block, 16)]

    def upper(self, dp):
        return self.part(dp, 0)

    def lower(self, dp):
        return self.part(dp, 1)

    def third(self):
        here = self.here
        self.wait_a()
        self.add(self.upper(here.dp), self.r2a)
        self.wait_b()
        self.add(self.lower(here.dp), self.r2b)
        inner = (here.side - here.high) * (here.side - here.high)
        there = here.seq + (1 - inner) * (2 - 4 * here.side) + inner * (4 - 8 * here.high)
        self.wait = self.net.send(
            self.part(here.dp, 1 - here.high), self.r3b.at[0], (here.dp, there)
        )
        self.across = self.net.plan(
            self.part(here.dp, here.high), self.r3b.at[1], (here.dp, here.seq + 6 - 4 * here.z)
        )

        @pl.when(here.side != here.high)
        def _():
            self.across.start()

    def fifth(self):
        here = self.here
        self.wait()

        def total(left):
            def body(rows):
                self.f32[rows, :] = left[rows, :].astype(F32) + self.r3b[0, rows, :].astype(F32)

            by_rows(self.block, body, 16)

        @pl.when(here.side == here.high)
        def _():
            total(self.part(here.dp, here.high))

        @pl.when(here.side != here.high)
        def _():
            self.across.wait()
            total(self.r3b.at[1])

        self.pass_on()


class HeadColumns:
    def columns(self, core):
        return span(self.column // self.width * 768 + core * 384, 384, 128)


class HeadChunk(HeadColumns, Chunk):
    pass


class LastHeadChunk(HeadColumns, LastChunk):
    pass


def chunk_list(widths):
    cuts = (
        (3, (384,), (DownChunk,)),
        (2, (384, 384), (UpChunk, UpChunk)),
        (1, (384,), (Chunk,)),
        (0, (384, 384, 384), (HeadChunk, HeadChunk, LastHeadChunk)),
    )
    chunks = []
    for index, parts, kinds in cuts:
        column = 0
        for part, kind in zip(parts, kinds):
            chunks.append((index, column, part, kind))
            column += part
    return chunks


def layer_kernel(names, chunks, sizes, *refs):
    v = types.SimpleNamespace(**dict(zip(names, refs)))
    tokens, width, heads, hidden_width = sizes
    quarter = width // 4
    size = width // heads
    factor = size ** (-0.5)
    here = Place()
    core, dp = here.core, here.dp
    net = Net(v.send_sems, v.recv_sems)
    mine, theirs = slice(0, tokens), slice(tokens, 2 * tokens)
    near_rows = theirs
    both, pair_both = slice(0, 2 * tokens), slice(2 * tokens, 4 * tokens)

    here.greet()
    loads = []
    for number, (source, target) in enumerate(
        (
            (v.time_table, v.table_v), (v.w_token, v.token_v), (v.w_head, v.head_v), (v.w_ada, v.ada_v),
            (v.token_keep, v.keep_v), (v.head_keep, v.head_keep_v), (v.inputs, v.x_v), (v.cotangent, v.g_v.at[mine]),
            (v.time_index, v.index_v),
        )
    ):
        copy = pltpu.make_async_copy(source, target, v.local_sems.at[7 + number])
        copy.start()
        loads.append(copy)
    w_q, w_o = Weight(net, here, v.wq, v.fq), Weight(net, here, v.wo, v.fo)
    w_u, w_d = HalfWeight(net, here, v.wu, v.fu, True), WholeWeight(net, here, v.wd, v.fd, False)
    weights = [w_q, w_o, w_u, w_d]
    w_q.keep(v.local_sems.at[0])
    w_o.keep(v.local_sems.at[1])
    w_u.keep([v.local_sems.at[2 + k] for k in range(4)])
    w_d.keep([v.local_sems.at[6]])
    select = (
        lax.broadcasted_iota(jnp.int32, (width, quarter), 0)
        == lax.broadcasted_iota(jnp.int32, (width, quarter), 1) + dp * quarter
    ).astype(F32).astype(BF16)
    loads[1].wait()
    token = jnp.broadcast_to(v.token_v[...].astype(F32).reshape(1, quarter), (16, quarter))
    placed = dot(token.astype(BF16), select, NT)
    loads[8].wait()
    loads[0].wait()
    rows = v.table_v.shape[0]
    whole = rows // 128 * 128
    index_row = jnp.broadcast_to(v.index_v[...], (16, whole))
    hot = (lax.broadcasted_iota(jnp.int32, (16, whole), 1) == index_row).astype(F32).astype(BF16)
    row = dot(hot, v.table_v[0:whole, :], NN)[0:1]
    rest = lax.broadcasted_iota(jnp.int32, (rows - whole, width), 0) + whole
    rest = jnp.where(
        rest == jnp.broadcast_to(v.index_v[...], rest.shape), v.table_v[whole:rows, :].astype(F32), 0.0
    )
    row += jnp.sum(rest, axis=0, keepdims=True)
    condition = (row * jax.nn.sigmoid(row)).astype(BF16).astype(F32)
    v.condition[...] = condition
    v.small_v[...] = jnp.zeros(v.small_v.shape, F32)
    for k in range(width // 128):
        v.small_v[k : k + 1, :] = condition[:, k * 128 : (k + 1) * 128]
        v.small_v[8 + k : 9 + k, :] = placed[0:1, k * 128 : (k + 1) * 128]
    here.meet()

    w_q.send_diagonal()
    bit = tokens // 2
    wait_cotangent = []

    def send_cotangent(k):
        block = slice(k * bit, k * bit + bit)
        landing = v.g_v.at[slice(tokens + k * bit, tokens + k * bit + bit)]
        wait_cotangent.append(net.send(v.cotangent.at[block], landing, here.peer_z1()))

    send_cotangent(0)
    waits = [
        net.send(v.small_v, v.cond_buf.at[dp], peer, v.cond_buf.at[peer[0]])
        for peer in here.dp_peers()
    ]
    w_q.send_straight((0,))
    v.cond_buf[pl.ds(dp, 1)] = v.small_v[...][None]
    head_of = lax.broadcasted_iota(jnp.int32, (128, width), 0) * size
    lane = lax.broadcasted_iota(jnp.int32, (128, width), 1)
    v.expand[...] = ((lane >= head_of) & (lane < head_of + size)).astype(F32)
    for load in loads[2:6]:
        load.wait()
    diagonal = lax.broadcasted_iota(jnp.int32, (tokens, tokens), 0) == lax.broadcasted_iota(
        jnp.int32, (tokens, tokens), 1
    )
    v.keep[...] = jnp.sum(jnp.where(diagonal, v.keep_v[...].astype(F32), 0.0), axis=1, keepdims=True)
    v.head_mask[...] = jnp.zeros(v.head_mask.shape, F32)
    v.head_mask[:, 0:heads] = v.head_keep_v[...].astype(F32)
    v.part[...] = jnp.zeros(v.part.shape, F32)
    w_q.spread()
    send_cotangent(1)
    for wait in waits:
        wait()
    def wide(first):
        return jnp.concatenate([v.cond_buf[:, first + k, :] for k in range(width // 128)], axis=1)

    stacked = jnp.concatenate([wide(0), jnp.zeros((12, width), F32)], axis=0).astype(BF16)
    left = dot(stacked, select, NN).astype(BF16)
    for piece in range(7):
        if piece < 6:
            product = dot(left, v.ada_v[:, piece * width : (piece + 1) * width], NN)
        else:
            product = dot(left, v.head_v[...], NT)
        for image in range(4):
            v.part[image, piece : piece + 1, 0 : product.shape[1]] = product[image : image + 1]
    waits = [
        net.send(v.part.at[peer[0]], v.part_buf.at[index], peer)
        for index, peer in enumerate(here.dp_peers())
    ]
    w_q.send_straight((1,))
    w_o.send_diagonal()
    w_u.send_diagonal()
    w_o.send_straight()
    v.token[...] = jnp.sum(wide(8), axis=0, keepdims=True)
    for wait in waits:
        wait()
    v.mod[...] = v.part[dp] + v.part_buf[0] + v.part_buf[1] + v.part_buf[2]
    v.mod[7:8, 0:tokens] = v.keep_v[...].astype(F32)
    head_sigmoid = jax.nn.sigmoid(v.mod[6:7, 0:128])
    head_mask = v.head_mask[...]
    gate = dot(jnp.broadcast_to(head_mask * head_sigmoid, (8, 128)), v.expand[...], NN, exact=True)
    v.gate_row[...] = gate[0:1]

    loads[6].wait()

    def first_norm(rows):
        values = v.x_v[rows, :].astype(F32)
        centre = values - jnp.mean(values, axis=1, keepdims=True)
        spread = jnp.mean(centre * centre, axis=1, keepdims=True)
        normal = centre * lax.rsqrt(spread + epsilon)
        v.nb[rows, :] = (normal * (1.0 + v.mod[1:2]) + v.mod[0:1]).astype(BF16)

    by_rows(tokens, first_norm)
    wait_normed = net.send(v.nb.at[mine], v.nb.at[theirs], here.peer_core())

    w_q.share_straight(0)
    w_q.share_straight(1)
    w_u.send_straight()
    w_d.send_diagonal()
    w_d.send_straight()
    w_o.spread()
    w_q.share_diagonal()
    wait_mod = net.send(v.mod, v.mod_near, here.peer_z1())
    w_q.ready()

    @pl.loop(0, 3 * width // 384)
    def _(index):
        columns = span(index * 384, 384, 128)
        v.packed[:, columns] = dot(v.nb[mine, :], v.fq[:, columns], NN).astype(BF16)

    w_u.spread()

    lanes = lax.broadcasted_iota(jnp.int32, (1, 2 * size), 1)
    masks = ((lanes < size).astype(F32).astype(BF16), (lanes >= size).astype(F32).astype(BF16))
    scaled_masks = tuple(mask * jnp.asarray(factor, BF16) for mask in masks)
    low_lane = lax.broadcasted_iota(jnp.int32, (tokens, 2 * size), 1) < size

    def three(pair, block):
        return [block[:, span(part * width + pair * 2 * size, 2 * size, 128)] for part in range(3)]

    def attend(pair):
        queries, key_rows, value_rows = three(pair, v.packed)
        found = []
        for which in range(2):
            scores = dot(queries * scaled_masks[which], key_rows, NT)
            powers = jnp.exp(scores - jnp.max(scores, axis=1, keepdims=True))
            probs = powers * (1.0 / jnp.sum(powers, axis=1, keepdims=True))
            v.probs[pair * 2 + which] = probs
            found.append(dot(probs.astype(BF16), value_rows, NN))
        attended = jnp.where(low_lane, found[0], found[1])
        columns = span(pair * 2 * size, 2 * size, 128)
        v.attended[:, columns] = attended
        v.gated[mine, columns] = (attended * v.gate_row[:, columns]).astype(BF16)

    pl.loop(0, heads // 3)(attend)
    attend(heads // 3)
    w_o.share_straight(0)
    w_o.share_straight(1)
    w_o.share_diagonal()
    pl.loop(heads // 3 + 1, heads // 2)(attend)
    wait_gated = net.send(v.gated.at[mine], v.gated.at[theirs], here.peer_core())
    w_o.ready()

    @pl.loop(0, width // 256)
    def _(index):
        columns = span(index * 256, 256, 128)
        v.branch[:, columns] = dot(v.gated[mine, :], v.fo[:, columns], NN)

    loads[7].wait()

    def weigh(rows, second, modulation, keep):
        logit = jnp.sum(second.astype(F32) * v.token[...], axis=1, keepdims=True)
        router = jax.nn.sigmoid(logit)
        weight = keep * router
        v.grad_prod[rows, :] = (v.g_v[rows, :].astype(F32) * modulation[5:6] * weight).astype(BF16)
        return router

    def second_norm(rows):
        middle = v.x_v[rows, :].astype(F32) + v.mod[2:3] * v.branch[rows, :]
        v.middle[rows, :] = middle
        centre = middle - jnp.mean(middle, axis=1, keepdims=True)
        spread = jnp.mean(centre * centre, axis=1, keepdims=True)
        scale = lax.rsqrt(spread + epsilon)
        normal = centre * scale
        v.z2[rows, :] = normal
        v.scale2[rows, :] = scale
        second = (normal * (1.0 + v.mod[4:5]) + v.mod[3:4]).astype(BF16)
        v.second[rows, :] = second
        v.router[rows, :] = weigh(rows, second, v.mod, v.keep[rows, :])

    def some_rows(start, count, body):
        @pl.loop(0, count // ROWS)
        def _(index):
            body(span(start + index * ROWS, ROWS, ROWS))

    wait_near = []
    for k in range(2):
        some_rows(k * bit, bit, second_norm)
        block = slice(k * bit, k * bit + bit)
        landing = v.second.at[slice(tokens + k * bit, tokens + k * bit + bit)]
        wait_near.append(net.send(v.second.at[block], landing, here.peer_z1()))
    w_u.share_diagonal()
    w_u.share_straight(0)
    w_u.share_straight(1)
    half = width // 2
    other = span((1 - core) * half, half, 128)
    own = span(core * half, half, 128)
    wait_pair = [
        net.send(v.second.at[mine], v.second.at[slice(2 * tokens, 3 * tokens)], here.peer_core()),
        net.send(
            v.grad_prod.at[mine, other], v.dy_down.at[slice(2 * tokens, 3 * tokens)], here.peer_core()
        ),
    ]
    v.dy_down[mine, :] = v.grad_prod[mine, own]

    w_u.ready()
    inner = math.sqrt(2.0 / math.pi)
    units = hidden_width // 2

    def feed(start, count):
        tokens_of = slice(start, start + count)
        for index in range(units // 512):
            columns = slice(index * 512, index * 512 + 512)
            v.tmp[0:count, 0:512] = dot(v.second[tokens_of, :], v.fu[:, columns], NN)

            @pl.loop(0, count // BEND_ROWS)
            def _(step):
                rows = span(step * BEND_ROWS, BEND_ROWS, BEND_ROWS)
                there = span(start + step * BEND_ROWS, BEND_ROWS, BEND_ROWS)
                u = v.tmp[rows, 0:512]
                square = u * u
                t = jnp.tanh(u * (inner + (inner * 0.044715) * square))
                a = 0.5 + 0.5 * t
                value = u * a
                v.hidden[there, columns] = value.astype(BF16)
                v.slope[there, columns] = a + value * (1.0 - a) * (
                    2.0 * inner + (6.0 * inner * 0.044715) * square
                )

    def feed_back(start, count):
        tokens_of = slice(start, start + count)

        @pl.loop(0, units // 512)
        def _(index):
            columns = span(index * 512, 512, 128)
            back = dot(v.grad_prod[tokens_of, :], v.fd[columns, :], NT)
            v.grad_u[tokens_of, columns] = (back * v.slope[tokens_of, columns]).astype(BF16)

    def down(start, count, target, at, kind):
        @pl.loop(0, width // 256)
        def _(index):
            columns = span(index * 256, 256, 128)
            target[at, columns] = dot(v.hidden[start : start + count, :], v.fd[:, columns], NN).astype(kind)

    def up_back(start, count, target, at, kind):
        @pl.loop(0, width // 256)
        def _(index):
            columns = span(index * 256, 256, 128)
            target[at, columns] = dot(v.grad_u[start : start + count, :], v.fu[columns, :], NT).astype(kind)

    wait_units = []
    quarter_units = units // 2
    other_units = span((1 - core) * quarter_units, quarter_units, 128)
    own_units = span(core * quarter_units, quarter_units, 128)

    def hand_over(block, landing):
        wait_units.append(net.send(v.grad_u.at[block, other_units], v.dy_up.at[landing], here.peer_core()))
        v.dy_up[block, :] = v.grad_u[block, own_units]

    feed(0, tokens)
    wait_pair.append(
        net.send(v.hidden.at[mine], v.hidden.at[slice(2 * tokens, 3 * tokens)], here.peer_core())
    )
    pieces = []
    for number, (index, column, wide, kind) in enumerate(chunks):
        total = (v.t_qkv, v.t_out, v.t_up, v.t_down)[index]
        out = (v.o_qkv, v.o_out, v.o_up, v.o_down)[index]
        bufs = [getattr(v, f"c{number}_{k}") for k in range(7)]
        pieces.append(kind(net, here, total, out, bufs, column, wide))
    c_down, c_up, c_more, c_out = pieces[:4]
    c_qkv = pieces[4:]

    def weight_grad(total, left, right, step):
        @pl.loop(0, total.shape[0] // step)
        def _(index):
            rows = span(index * step, step, 128)
            total[rows, :] = dot(left[:, rows], right[...], TN).astype(BF16)

    wait_mod()
    v.keep_near[...] = jnp.sum(
        jnp.where(diagonal, v.mod_near[7:8, 0:tokens], 0.0), axis=1, keepdims=True
    )

    def weigh_near(rows):
        kept = v.keep_near[span(rows.start - tokens, ROWS, ROWS), :]
        weigh(rows, v.second[rows, :], v.mod_near, kept)

    def take_near(k):
        wait_near[k]()
        wait_cotangent[k]()
        some_rows(tokens + k * bit, bit, weigh_near)
        feed(tokens + k * bit, bit)

    take_near(0)
    w_d.share_diagonal()
    w_d.share_straight(0)
    w_d.share_straight(1)
    take_near(1)
    w_d.ready()
    last_rows = slice(3 * tokens, 4 * tokens)
    wait_pair.append(net.send(v.hidden.at[near_rows], v.hidden.at[last_rows], here.peer_core()))
    wait_pair.append(net.send(v.second.at[near_rows], v.second.at[last_rows], here.peer_core()))
    wait_pair.append(net.send(v.grad_prod.at[near_rows, other], v.dy_down.at[last_rows], here.peer_core()))
    feed_back(tokens, tokens)
    hand_over(near_rows, last_rows)
    wait_back = []
    for k in range(width // 256):
        columns = slice(k * 256, k * 256 + 256)
        v.near_back[:, columns] = dot(v.grad_u[near_rows, :], v.fu[columns, :], NT).astype(BF16)
        wait_back.append(
            net.send(v.near_back.at[:, columns], v.got_back.at[:, columns], here.peer_z1())
        )
    v.dy_down[near_rows, :] = v.grad_prod[near_rows, own]

    def down_quarter(place):
        rows = span(place * 384, 384, 128)
        v.t_down[rows, :] = dot(v.hidden[:, rows], v.dy_down[...], TN).astype(BF16)

    for wait in wait_pair:
        wait()
    down_quarter(here.peer_d()[0])
    c_down.first_diagonal()
    down_quarter(here.peer_x()[0])
    c_down.first_x()
    down_quarter(here.peer_y()[0])
    c_down.first_y()
    down_quarter(dp)
    feed_back(0, tokens)
    hand_over(mine, slice(2 * tokens, 3 * tokens))
    down(tokens, tokens, v.near_prod, mine, BF16)

    def near_level(rows):
        grad = v.g_v[span(rows.start + tokens, ROWS, ROWS), :].astype(F32)
        produced = v.near_prod[rows, :].astype(F32)
        v.level[rows, :] = jnp.sum(grad * v.mod_near[5:6] * produced, axis=1, keepdims=True)

    by_rows(tokens, near_level)
    v.level_out[...] = jnp.broadcast_to(
        jnp.sum(jnp.where(diagonal, v.level[...], 0.0), axis=0, keepdims=True), v.level_out.shape
    )
    wait_level = net.send(v.level_out, v.level_in, here.peer_z1())
    wait_prod = net.send(v.near_prod, v.got_prod, here.peer_z1())
    for wait in wait_units:
        wait()
    weight_grad(v.t_up, v.second, v.dy_up, 256)
    c_up.first()
    c_more.first()
    up_back(0, tokens, v.own_back, mine, F32)
    down(0, tokens, v.own_prod, mine, F32)

    def own_level(rows):
        grad = v.g_v[rows, :].astype(F32)
        v.level[rows, :] = jnp.sum(grad * v.mod[5:6] * v.own_prod[rows, :], axis=1, keepdims=True)

    by_rows(tokens, own_level)

    v.sums[...] = jnp.zeros(v.sums.shape, F32)
    wait_level()
    got = jnp.sum(jnp.where(diagonal, v.level_in[0:1, :], 0.0), axis=1, keepdims=True)
    router, keep = v.router[...], v.keep[...]
    v.logit[...] = (v.level[...] + got) * keep * router * (1.0 - router)

    def second_back(rows):
        logit = v.logit[rows, :]
        back = (v.own_back[rows, :] + v.got_back[rows, :].astype(F32)).astype(BF16).astype(F32)
        back += logit * v.token[...]
        normal = v.z2[rows, :]
        v.sums[1] += fold(logit * v.second[rows, :].astype(F32))
        v.sums[2] += fold(back * normal)
        v.sums[3] += fold(back)
        inside = back * (1.0 + v.mod[4:5])
        level = jnp.mean(inside, axis=1, keepdims=True)
        slope = jnp.mean(inside * normal, axis=1, keepdims=True)
        grad = v.g_v[rows, :].astype(F32) + v.scale2[rows, :] * (inside - level - normal * slope)
        v.grad_mid[rows, :] = grad
        v.sums[4] += fold(grad * v.branch[rows, :])
        v.grad_branch[rows, :] = (v.mod[2:3] * grad).astype(BF16)

    for wait in wait_back:
        wait()
    by_rows(tokens, second_back)
    wait_dbranch = net.send(v.grad_branch.at[:, other], v.dy_out.at[theirs], here.peer_core())
    v.dy_out[mine, :] = v.grad_branch[:, own]

    @pl.loop(0, width // 256)
    def _(index):
        columns = span(index * 256, 256, 128)
        v.tmp[:, columns] = dot(v.grad_branch[...], v.fo[columns, :], NT)


    def gate_back(rows):
        grad = v.tmp[rows, :]
        v.sums[5] += fold(grad * v.attended[rows, :])
        v.grad_att[rows, :] = (grad * v.gate_row[...]).astype(BF16)

    by_rows(tokens, gate_back)
    c_down.second()
    c_up.second()

    def gather_far(piece, block):
        block[pl.ds(core, 1), pl.ds(here.z, 1), pl.ds(dp, 1)] = piece[...][None, None, None]
        far = (here.z + 2) % Z_CHIPS
        return [net.send(piece, block.at[core, here.z, dp], here.peer_z2(), block.at[core, far, dp])]

    def gather_near(block, waits):
        for wait in waits:
            wait()
        near = here.z + 1 - 2 * (here.z % 2)
        moves = []
        for k in range(2):
            z, other = (here.z + 2 * k) % Z_CHIPS, (near + 2 * k) % Z_CHIPS
            tile = block.at[core, z, dp]
            moves.append(net.send(tile, tile, here.peer_z1(), block.at[core, other, dp]))
        return moves

    def gather_dp(block, waits):
        for wait in waits:
            wait()
        tiles = block.at[core, pl.ds(0, Z_CHIPS), dp]
        return [
            net.send(tiles, tiles, peer, block.at[core, pl.ds(0, Z_CHIPS), peer[0]])
            for peer in here.dp_peers()
        ]

    one_way = (dp + (1 - core) * (1 - 2 * here.x) + core * (2 - 4 * here.y), here.seq)
    other_way = (dp + core * (1 - 2 * here.x) + (1 - core) * (2 - 4 * here.y), here.seq)

    def gather_one(block, waits):
        for wait in waits:
            wait()
        tiles = block.at[core, pl.ds(0, Z_CHIPS), dp]
        return [net.send(tiles, tiles, one_way, block.at[core, pl.ds(0, Z_CHIPS), one_way[0]])]

    def gather_two(block, waits):
        for wait in waits:
            wait()
        moves = []
        for mine_dp, their_dp in ((dp, other_way[0]), (one_way[0], here.peer_d()[0])):
            tiles = block.at[core, pl.ds(0, Z_CHIPS), mine_dp]
            moves.append(
                net.send(tiles, tiles, other_way, block.at[core, pl.ds(0, Z_CHIPS), their_dp])
            )
        return moves

    def gather_pair(block, waits):
        for wait in waits:
            wait()
        return net.send(block.at[core], block.at[core], here.peer_core(), block.at[1 - core])

    def back_pair(pair):
        queries, key_rows, value_rows = three(pair, v.packed)
        columns = span(pair * 2 * size, 2 * size, 128)
        grad_att = v.grad_att[:, columns]
        gq, gk, gv = [], [], []
        for which in range(2):
            probs = v.probs[pair * 2 + which]
            grad_probs = dot(grad_att * masks[which], value_rows, NT)
            level = jnp.sum(probs * grad_probs, axis=1, keepdims=True)
            grad_scores = (probs * (grad_probs - level)).astype(BF16)
            gq.append(dot(grad_scores, key_rows, NN))
            gk.append(dot(grad_scores, queries, TN))
            gv.append(dot(probs.astype(BF16), grad_att, TN))
        for part, (grads, scale) in enumerate(((gq, factor), (gk, factor), (gv, 1.0))):
            both = jnp.where(low_lane, grads[0], grads[1]) * scale
            v.grad_pack[:, span(part * width + pair * 2 * size, 2 * size, 128)] = both.astype(BF16)

    head_back = dot(
        jnp.broadcast_to(jnp.sum(v.sums[5], axis=0, keepdims=True), (8, width)), v.expand[...], NT, exact=True
    )
    head_back = head_back[0:1] * head_mask * head_sigmoid * (1.0 - head_sigmoid)
    v.early_f[...] = jnp.zeros(v.early_f.shape, F32)
    rows_out = [jnp.sum(v.sums[k], axis=0, keepdims=True) for k in (4, 3, 2, 1)]
    cut = width // 2
    for slot, values in zip((0, 1, 2, 5, 6), (*rows_out, v.condition[...])):
        v.early_f[2 * slot : 2 * slot + 1, :] = values[:, 0:cut]
        v.early_f[2 * slot + 1 : 2 * slot + 2, :] = values[:, cut:width]
    v.early_f[8:9, 0:128] = head_back
    v.early_out[...] = v.early_f[...].astype(BF16)
    early = gather_far(v.early_out, v.early)
    def back_group(group):
        @pl.loop(0, heads // 4)
        def _(index):
            back_pair(group * (heads // 4) + index)

    back_group(1 - core)
    wait_dpack = [
        net.send(
            v.grad_pack.at[:, span(part * width + (1 - core) * half, half, 128)],
            v.dy_qkv.at[theirs, slice(part * half, part * half + half)],
            here.peer_core(),
        )
        for part in range(3)
    ]
    early = gather_near(v.early, early)
    wait_gated()
    wait_dbranch()
    weight_grad(v.t_out, v.gated, v.dy_out, 256)
    c_out.first()
    back_group(core)
    for part in range(3):
        v.dy_qkv[mine, part * half : part * half + half] = v.grad_pack[
            :, span(part * width + core * half, half, 128)
        ]
    early = gather_one(v.early, early)
    c_more.second()
    wait_normed()
    for wait in wait_dpack:
        wait()

    def qkv_grad(start, count):
        columns = slice(start, start + count)

        @pl.loop(0, width // 256)
        def _(index):
            rows = span(index * 256, 256, 128)
            v.t_qkv[rows, columns] = dot(v.nb[:, rows], v.dy_qkv[:, columns], TN).astype(BF16)

    qkv_grad(0, 384)
    c_qkv[0].first()
    c_down.third()
    c_out.second()
    qkv_grad(384, 384)
    c_qkv[1].first()
    early = gather_two(v.early, early)
    qkv_grad(768, 384)
    c_up.third()
    c_more.third()
    wait_prod()

    def finish(rows):
        produced = (v.own_prod[rows, :] + v.got_prod[rows, :].astype(F32)).astype(BF16).astype(F32)
        scaled = produced * (v.keep[rows, :] * v.router[rows, :])
        v.output[rows, :] = (v.middle[rows, :] + v.mod[5:6] * scaled).astype(BF16)
        v.sums[0] += fold(v.g_v[rows, :].astype(F32) * scaled)

    by_rows(tokens, finish)

    @pl.loop(0, width // 256)
    def _(index):
        columns = span(index * 256, 256, 128)
        v.tmp[:, columns] = dot(v.grad_pack[...], v.fq[columns, :], NT)

    c_qkv[0].second()
    c_qkv[2].first()

    def first_back(rows):
        back = v.tmp[rows, :]
        values = v.x_v[rows, :].astype(F32)
        centre = values - jnp.mean(values, axis=1, keepdims=True)
        spread = jnp.mean(centre * centre, axis=1, keepdims=True)
        scale = lax.rsqrt(spread + epsilon)
        normal = centre * scale
        v.sums[6] += fold(back * normal)
        v.sums[7] += fold(back)
        inside = back * (1.0 + v.mod[1:2])
        level = jnp.mean(inside, axis=1, keepdims=True)
        slope = jnp.mean(inside * normal, axis=1, keepdims=True)
        v.grad_input[rows, :] = v.grad_mid[rows, :] + scale * (inside - level - normal * slope)

    by_rows(tokens, first_back)
    shift = jnp.sum(v.sums[7], axis=0, keepdims=True)
    scale = jnp.sum(v.sums[6], axis=0, keepdims=True)
    v.late_f[...] = jnp.zeros(v.late_f.shape, F32)
    for k in range(width // 128):
        v.late_f[k : k + 1, :] = shift[:, k * 128 : (k + 1) * 128]
        v.late_f[8 + k : 9 + k, :] = scale[:, k * 128 : (k + 1) * 128]
    gate_two = jnp.sum(v.sums[0], axis=0, keepdims=True)
    for k in range(width // 128):
        v.late_f[16 + k : 17 + k, :] = gate_two[:, k * 128 : (k + 1) * 128]
    v.late_out[...] = v.late_f[...].astype(BF16)
    late = gather_far(v.late_out, v.late)
    c_down.fifth()
    c_up.fifth()
    c_qkv[1].second()
    early = gather_pair(v.early, early)
    c_out.third()
    late = gather_near(v.late, late)
    c_qkv[0].third()
    c_qkv[2].second()
    c_more.fifth()
    c_out.fourth()
    c_qkv[1].third()
    late = gather_dp(v.late, late)
    c_qkv[0].fourth()
    c_qkv[2].third()
    c_qkv[1].fourth()
    c_out.fifth()
    late = gather_pair(v.late, late)
    early()
    offset = dp * quarter + (here.seq % BLOCK) * SHARE
    pick = (
        lax.broadcasted_iota(jnp.int32, (width, SHARE), 0)
        == lax.broadcasted_iota(jnp.int32, (width, SHARE), 1) + offset
    ).astype(F32)

    every = v.early[...].reshape(512, cut).astype(F32).reshape(32, 16, cut)
    conditions = (
        dot(every[:, 12, :].astype(BF16), pick[0:cut].astype(BF16), NN)
        + dot(every[:, 13, :].astype(BF16), pick[cut:width].astype(BF16), NN)
    ).astype(BF16)
    for slot, piece in enumerate((2, 3, 4)):
        for side in range(2):
            start = piece * width + side * cut
            v.o_ada[:, start : start + cut] = dot(
                conditions, every[:, 2 * slot + side, :].astype(BF16), TN
            )
    v.o_head[...] = dot(every[:, 8, 0:128].astype(BF16), conditions, TN)[0:heads]
    totals = [jnp.sum(every[:, 10 + side, :], axis=0, keepdims=True) for side in range(2)]
    v.o_token[...] = (
        dot(jnp.broadcast_to(totals[0], (8, cut)), pick[0:cut], NN, exact=True)
        + dot(jnp.broadcast_to(totals[1], (8, cut)), pick[cut:width], NN, exact=True)
    )[0:1]

    c_qkv[0].fifth()
    c_qkv[1].fifth()
    for chunk in (c_down, c_up, c_more):
        chunk.end()
    late()
    tail = v.late[...].reshape(1024, 128).astype(F32).reshape(32, 32, 128)
    for base, piece in ((0, 0), (8, 1), (16, 5)):
        row = jnp.concatenate([tail[:, base + k, :] for k in range(width // 128)], axis=1)
        start = piece * width
        v.o_ada[:, start : start + width] = dot(conditions, row.astype(BF16), TN)
    c_qkv[2].fifth()
    for chunk in (c_out, *c_qkv):
        chunk.end()
    net.finish()


def layer(time_table, time_index, w_token, w_head, token_keep, head_keep, inputs, cotangent, w_ada, wq, wo, wu, wd):
    tokens, width = inputs.shape
    hidden_width = wu.shape[1]
    heads = head_keep.shape[1]
    widths = [wq.shape[1], wo.shape[1], wu.shape[1], wd.shape[1]]
    depths = [4 * w.shape[0] for w in (wq, wo, wu, wd)]
    chunks = chunk_list(widths)
    operands = dict(
        time_table=time_table, time_index=time_index, w_token=w_token, w_head=w_head, token_keep=token_keep, head_keep=head_keep,
        inputs=inputs, cotangent=cotangent, w_ada=w_ada, wq=wq, wo=wo, wu=wu, wd=wd,
    )
    outs = dict(
        ada=((SHARE, 6 * width), F32),
        qkv=((depths[0] // 32, widths[0]), F32),
        out=((depths[1] // 32, widths[1]), F32),
        up=((depths[2] // 32, widths[2]), F32),
        down=((depths[3] // 32, widths[3]), F32),
        head=((heads, SHARE), F32),
        token=((1, SHARE), F32),
    )
    results = dict(output=((tokens, width), BF16), grad_input=((tokens, width), F32))
    results.update({"o_" + k: s for k, s in outs.items()})
    space = dict(
        table_v=(time_table.shape, BF16),
        index_v=(time_index.shape, jnp.int32),
        small_v=((16, 128), F32),
        condition=((1, width), F32),
        token_v=(w_token.shape, BF16),
        keep_v=(token_keep.shape, jnp.int32),
        head_keep_v=(head_keep.shape, jnp.int32),
        head_mask=((1, 128), F32),
        head_v=(w_head.shape, BF16),
        ada_v=(w_ada.shape, BF16),
        x_v=((tokens, width), BF16),
        g_v=((2 * tokens, width), BF16),
        mod_near=((8, width), F32),
        keep_near=((tokens, 1), F32),
        fq=((depths[0], widths[0]), BF16),
        fo=((depths[1], widths[1]), BF16),
        fu=((depths[2], widths[2] // 2), BF16),
        fd=((depths[3] // 2, widths[3]), BF16),
        cond_buf=((4, 16, 128), F32),
        part=((4, 8, width), F32),
        part_buf=((3, 8, width), F32),
        mod=((8, width), F32),
        token=((1, width), F32),
        keep=((tokens, 1), F32),
        expand=((128, width), F32),
        gate_row=((1, width), F32),
        nb=((2 * tokens, width), BF16),
        packed=((tokens, 3 * width), BF16),
        probs=((heads, tokens, tokens), F32),
        attended=((tokens, width), F32),
        gated=((2 * tokens, width), BF16),
        branch=((tokens, width), F32),
        middle=((tokens, width), F32),
        z2=((tokens, width), F32),
        scale2=((tokens, 1), F32),
        second=((4 * tokens, width), BF16),
        router=((tokens, 1), F32),
        logit=((tokens, 1), F32),
        grad_prod=((2 * tokens, width), BF16),
        dy_down=((4 * tokens, width // 2), BF16),
        tmp=((tokens, width), F32),
        hidden=((4 * tokens, hidden_width // 2), BF16),
        slope=((2 * tokens, hidden_width // 2), F32),
        grad_u=((2 * tokens, hidden_width // 2), BF16),
        dy_up=((4 * tokens, hidden_width // 4), BF16),
        own_prod=((tokens, width), F32),
        own_back=((tokens, width), F32),
        near_prod=((tokens, width), BF16),
        near_back=((tokens, width), BF16),
        got_prod=((tokens, width), BF16),
        got_back=((tokens, width), BF16),
        level=((tokens, 1), F32),
        level_out=((8, tokens), F32),
        level_in=((8, tokens), F32),
        grad_mid=((tokens, width), F32),
        grad_branch=((tokens, width), BF16),
        dy_out=((2 * tokens, width // 2), BF16),
        grad_att=((tokens, width), BF16),
        grad_pack=((tokens, 3 * width), BF16),
        dy_qkv=((2 * tokens, 3 * width // 2), BF16),
        sums=((8, 8, width), F32),
        early_f=((16, width // 2), F32),
        early_out=((16, width // 2), BF16),
        early=((2, Z_CHIPS, 4, 16, width // 2), BF16),
        late_f=((32, 128), F32),
        late_out=((32, 128), BF16),
        late=((2, Z_CHIPS, 4, 32, 128), BF16),
        t_qkv=((depths[0], widths[0] // 2), BF16),
        t_out=((depths[1], widths[1] // 2), BF16),
        t_up=((depths[2], widths[2] // 4), BF16),
        t_down=((depths[3] // 2, widths[3] // 2), BF16),
    )
    for number, (index, _, wide, kind) in enumerate(chunks):
        shapes = kind.shapes(depths[index] // 16, wide)
        for k, shape in enumerate(shapes):
            space[f"c{number}_{k}"] = (shape, BF16)
        space[f"c{number}_6"] = (kind.sums(depths[index] // 16, wide), F32)
    copies = 6 + 4 * 13 + 32 + len(chunks) * 14 + 14
    names = list(operands) + list(results) + list(space) + ["send_sems", "recv_sems", "local_sems"]
    return pl.pallas_call(
        functools.partial(layer_kernel, names, chunks, (tokens, width, heads, hidden_width)),
        out_shape=[pltpu.VMEM(*r) for r in results.values()],
        in_specs=[ANY] * len(operands),
        out_specs=[VMEM] * len(results),
        scratch_shapes=[pltpu.VMEM(*s) for s in space.values()]
        + [
            pltpu.SemaphoreType.DMA((copies,)),
            pltpu.SemaphoreType.DMA((copies,)),
            pltpu.SemaphoreType.DMA((16,)),
        ],
        compiler_params=pltpu.CompilerParams(
            collective_id=0, has_side_effects=True, vmem_limit_bytes=61 * 2**20
        ),
    )(*operands.values())


def copy_kernel(count, *refs):
    copies = [
        pltpu.make_async_copy(refs[k], refs[count + k], refs[2 * count].at[k]) for k in range(count)
    ]
    for copy in copies:
        copy.start()
    for copy in copies:
        copy.wait()


def copy_all(arrays):
    count = len(arrays)
    return pl.pallas_call(
        functools.partial(copy_kernel, count),
        out_shape=[jax.ShapeDtypeStruct(a.shape, a.dtype) for a in arrays],
        in_specs=[VMEM] * count,
        out_specs=[ANY] * count,
        scratch_shapes=[pltpu.SemaphoreType.DMA((count,))],
        compiler_params=pltpu.CompilerParams(vmem_limit_bytes=16 * 2**20),
    )(*(pltpu.with_memory_space_constraint(a, pltpu.VMEM) for a in arrays))


def across_blocks(part, seq_size):
    blocks = seq_size // BLOCK
    if blocks == 1:
        return part
    groups = [[b * BLOCK + j for b in range(blocks)] for j in range(BLOCK)]
    mine = lax.psum_scatter(
        part, "seq", scatter_dimension=0, axis_index_groups=groups, tiled=True
    )
    moves = [(b * BLOCK + j, j * blocks + b) for b in range(blocks) for j in range(BLOCK)]
    return lax.ppermute(mine, "seq", moves)


def per_device(
    seq_size, inputs, time_table, time_index, token_keep, head_keep, cotangent,
    w_ada, w_qkv, w_out, w_up, w_down, w_head, w_token,
):
    out = layer(
        time_table, time_index[None], w_token, w_head.T, token_keep, head_keep,
        inputs[0], cotangent[0], w_ada, w_qkv, w_out, w_up, w_down,
    )
    output, grad_input, ada, qkv, outw, up, down, head, token = copy_all(out)
    parts = (ada, qkv, outw, up, down, head.T, token[0])
    parts = tuple(across_blocks(part, seq_size) for part in parts)
    return (output[None], grad_input[None]) + parts


def solution(mesh):
    both = ("dp", "seq")
    in_specs = (
        P(both, None, None), P(), P(both), P(both, None), P(both, None), P(both, None, None),
        P("dp", None), P("dp", None), P("dp", None), P("dp", None), P("dp", None), P("dp", None), P("dp"),
    )
    out_specs = (P(both, None, None), P(both, None, None)) + (P(both, None),) * 6 + (P(both),)
    return jax.shard_map(
        functools.partial(per_device, mesh.shape["seq"]),
        mesh=mesh, in_specs=in_specs, out_specs=out_specs, check_vma=False,
    )
```
